32 devices in a mesh: dp: 4 (over y, x), mp: 8 (over z, core).
Axes of the slice: x: 2, y: 2, z: 4, core: 2. Of those that a mesh axis runs over, the one named last changes fastest.
Arguments:
- tokens: bfloat16 [8192, 2304], P(('dp', 'mp')), may hold values from -6 to 6
- ada_ffn: float32 [8, 2, 2304], P('dp'), may hold values from -4 to 4
- ffn_gate: float32 [8, 2304], P('dp'), may hold values from 0.5 to 1.5
- up_weight: bfloat16 [2304, 9216], P(None, 'mp'), may hold values from -0.125 to 0.125
- up_bias: float32 [9216], P('mp'), may hold values from -6 to 6
- down_weight: bfloat16 [9216, 2304], P('mp'), may hold values from -0.125 to 0.125
- down_bias: float32 [2304], replicated, may hold values from -6 to 6
- ada_head: float32 [8, 2, 2304], P('dp'), may hold values from -4 to 4
- head_weight: bfloat16 [2304, 4096], P(None, 'mp'), may hold values from -0.125 to 0.125
- head_bias: float32 [4096], P('mp'), may hold values from -6 to 6
- gumbel_noise: float32 [4, 1024, 4096], P('dp', None, 'mp'), as said below
- codebook: bfloat16 [4096, 32], P('mp'), may hold values from -16 to 16
- phi_weight: float32 [32, 32, 3, 3], replicated, may hold values from -0.375 to 0.375
- phi_bias: float32 [32], replicated, may hold values from -6 to 6
- f_hat: float32 [4, 32, 1024], P('dp', None, 'mp'), may hold values from -6 to 6
Outputs:
- block_out: bfloat16 [8192, 2304], P(('dp', 'mp'))
- f_hat_out: float32 [4, 32, 1024], P('dp', None, 'mp')
The draws below stay inside these ranges and needn't reach their ends.
Inputs may be any that keep to these rules, and one draw needn't show every extreme that they name: `gumbel_noise`: noise added to the guided logits.
All inputs are finite; a program needn't handle non-finite values.
Results may differ from the reference program's by a relative error of at most 0.024.
Values may be sent and summed in bfloat16 or wider, within the bound.
No kernel may reach another device: no remote copies, remote signals or barrier semaphores. Data moves between devices by JAX's collectives and lax.ppermute only.
A program may use at most 256 MiB of HBM per device.

```python
import jax
import jax.numpy as jnp
from jax import lax

D = 2304
FF = 9216
VOCAB = 4096
CVAE = 32
SIDE = 32
NEW = 1024
IMGS = 8
TOKENS = 8192
HALF = 1
PAIRS = 4
CONDS = 2
VB = 512
N_MP = 8


def draw_gumbel_noise(key, part):
    key_list = jax.random.split(key, 1)
    full_shape = (PAIRS, NEW, VOCAB)
    uniform_draw = jax.random.uniform(key_list[0], full_shape, jnp.float32, 1e-06, 1.0 - 1e-06)
    return -jnp.log(-jnp.log(uniform_draw))


def steps_of(key, shape, shards, least, largest):
    factor_of, own = 1.0, jax.random.fold_in(key, 6)
    for dim, shards_of in shards:
        draws = jnp.exp(jax.random.uniform(jax.random.fold_in(own, dim), (shards_of,), jnp.float32, least / len(shards), largest / len(shards)))
        factor_of = factor_of * jnp.repeat(draws, shape[dim] // shards_of).reshape([-1 if axis == dim else 1 for axis in range(len(shape))])
    return factor_of


def noise(own_key, shape, scale, limit, pieces=(), kind=jnp.bfloat16):
    loudness = steps_of(own_key, shape, pieces, -0.22, 0.18) if pieces else 1.0
    entries = jax.random.normal(own_key, shape, jnp.float32) * scale * loudness
    return jnp.minimum(jnp.maximum(entries, -limit), limit).astype(kind)


def setup_inputs(seed: int = 0) -> dict:
    splits = jax.random.split(jax.random.key(seed), 16)
    tokens = noise(splits[0], (TOKENS, D), 1.0, 6.0, ((0, 32),))
    ada_ffn = noise(splits[1], (IMGS, 2, D), 0.3, 4.0, ((0, 4),), jnp.float32)
    ffn_gate = jnp.clip(0.5 + 1.0 * jax.random.uniform(splits[2], (IMGS, D), jnp.float32) ** steps_of(splits[2], (IMGS, D), ((0, 4),), -0.2, 0.2), 0.5, 1.5)
    up_weight = noise(splits[3], (D, FF), D ** -0.5, 0.125, ((1, 8),))
    up_bias = noise(splits[4], (FF,), 0.5, 6.0, ((0, 8),), jnp.float32)
    down_weight = noise(splits[5], (FF, D), (FF // 4) ** -0.5, 0.125, ((0, 8),))
    down_bias = noise(splits[6], (D,), 0.5, 6.0, (), jnp.float32)
    ada_head = noise(splits[7], (IMGS, 2, D), 0.3, 4.0, ((0, 4),), jnp.float32)
    head_weight = noise(splits[8], (D, VOCAB), D ** -0.5, 0.125, ((1, 8),))
    head_bias = noise(splits[9], (VOCAB,), 1.0, 6.0, ((0, 8),), jnp.float32)
    gumbel_noise = draw_gumbel_noise(jax.random.fold_in(splits[15], 71), 0)
    codebook = noise(splits[11], (VOCAB, CVAE), 3.0, 16.0, ((0, 8),))
    phi_weight = noise(splits[12], (CVAE, CVAE, 3, 3), (9 * CVAE) ** -0.5, 0.375, (), jnp.float32)
    phi_bias = noise(splits[13], (CVAE,), 0.5, 6.0, (), jnp.float32)
    f_hat = noise(splits[14], (PAIRS, CVAE, NEW), 1.0, 6.0, ((0, 4), (2, 8)), jnp.float32)
    return dict(tokens=tokens, ada_ffn=ada_ffn, ffn_gate=ffn_gate, up_weight=up_weight, up_bias=up_bias, down_weight=down_weight, down_bias=down_bias, ada_head=ada_head, head_weight=head_weight, head_bias=head_bias, gumbel_noise=gumbel_noise, codebook=codebook, phi_weight=phi_weight, phi_bias=phi_bias, f_hat=f_hat)


GUIDE = 1.5

def norm_rows(values):
    row_mean = lax.optimization_barrier(jnp.mean(values, axis=-1, keepdims=True))
    centred = values - row_mean
    spread = lax.optimization_barrier(jnp.mean(centred * centred, axis=-1, keepdims=True))
    return centred * lax.rsqrt(spread + 1e-06)

def modulate(values, ada_one):
    return norm_rows(values) * (1.0 + ada_one[1]) + ada_one[0]

def reference(tokens, ada_ffn, ffn_gate, up_weight, up_bias, down_weight, down_bias, ada_head, head_weight, head_bias, gumbel_noise, codebook, phi_weight, phi_bias, f_hat):

    def one_image(inputs):
        image_rows, ffn_ada, gate_row, head_ada = inputs
        normed = modulate(image_rows.astype(jnp.float32), ffn_ada).astype(jnp.bfloat16)
        hidden = jax.nn.gelu(jnp.dot(normed, up_weight, preferred_element_type=jnp.float32) + up_bias, approximate=True).astype(jnp.bfloat16)
        ffn_sum = jnp.dot(hidden, down_weight, preferred_element_type=jnp.float32)
        image_out = (image_rows.astype(jnp.float32) + gate_row * (ffn_sum + down_bias)).astype(jnp.bfloat16)
        head_in = modulate(image_out.astype(jnp.float32), head_ada).astype(jnp.bfloat16)
        logits = jnp.dot(head_in, head_weight, preferred_element_type=jnp.float32) + head_bias
        return (image_out, logits)
    stream_out, logits = lax.map(one_image, (tokens.reshape(IMGS, NEW, D), ada_ffn, ffn_gate, ada_head))
    logits = logits.reshape(2, CONDS, 2, HALF, NEW, VOCAB)
    guided = (1.0 + GUIDE) * logits[0] - GUIDE * logits[1]
    guided = jnp.transpose(guided, (1, 0, 2, 3, 4)).reshape(PAIRS, NEW, VOCAB)
    scores = guided + gumbel_noise
    code_blocks = codebook.reshape(N_MP, VB, CVAE).astype(jnp.float32)

    def sample(score_rows):
        blocks = score_rows.reshape(NEW, N_MP, VB)
        peak_part = lax.optimization_barrier(jnp.max(blocks, axis=2))
        weights = jnp.exp(blocks - peak_part[:, :, None]).astype(jnp.bfloat16)
        total_part = lax.optimization_barrier(jnp.sum(weights.astype(jnp.float32), axis=2))
        code_part = jnp.einsum('tbv,bvc->tbc', weights.astype(jnp.float32), code_blocks, precision=lax.Precision.HIGHEST)
        peak = lax.optimization_barrier(jnp.max(peak_part, axis=1))
        factor = jnp.exp(peak_part - peak[:, None])
        return lax.optimization_barrier(jnp.sum(code_part * factor[:, :, None], axis=1)) / lax.optimization_barrier(jnp.sum(total_part * factor, axis=1))[:, None]
    soft_code = lax.map(sample, scores)
    code_maps = soft_code.reshape(PAIRS, SIDE, SIDE, CVAE)
    padded = jnp.pad(code_maps, ((0, 0), (1, 1), (1, 1), (0, 0)))
    conv_out = jnp.zeros((PAIRS, CVAE, SIDE, SIDE), jnp.float32) + phi_bias[None, :, None, None]
    for row_step in range(3):
        for col_step in range(3):
            conv_out = conv_out + jnp.einsum('pyxc,oc->poyx', padded[:, row_step:row_step + SIDE, col_step:col_step + SIDE, :], phi_weight[:, :, row_step, col_step], precision=lax.Precision.HIGHEST)
    own_cells = jnp.transpose(code_maps, (0, 3, 1, 2))
    f_hat_out = f_hat + (0.5 * own_cells + 0.5 * conv_out).reshape(PAIRS, CVAE, NEW)
    return (stream_out.reshape(TOKENS, D), f_hat_out)
```

```python
import jax
import jax.numpy as jnp
from jax import lax
from jax.sharding import PartitionSpec as P

SIDE = 32
NEW = 1024
GUIDE = 1.5
CHUNKS = 4
HEAD_CHUNKS = 2


def norm_rows(values):
    row_mean = jnp.mean(values, axis=-1, keepdims=True)
    centred = values - row_mean
    spread = jnp.mean(centred * centred, axis=-1, keepdims=True)
    return centred * lax.rsqrt(spread + 1e-06)


def modulate(values, ada):
    return norm_rows(values.astype(jnp.float32)) * (1.0 + ada[1]) + ada[0]


def permute_devices(value, dp, mp, target):
    pairs = []
    for d in range(dp):
        for m in range(mp):
            to = target(d, m)
            if to is not None:
                pairs.append((d * mp + m, to[0] * mp + to[1]))
    return lax.ppermute(value, ("dp", "mp"), pairs)


def body(
    tokens,
    ada_ffn,
    ffn_gate,
    up_weight,
    up_bias,
    down_weight,
    down_bias,
    ada_head,
    head_weight,
    head_bias,
    gumbel_noise,
    codebook,
    phi_weight,
    phi_bias,
    f_hat,
):
    rows, width = tokens.shape
    dp, mp = lax.axis_size("dp"), lax.axis_size("mp")
    d_index, m_index = lax.axis_index("dp"), lax.axis_index("mp")
    images = ada_ffn.shape[0]
    pairs = f_hat.shape[0]
    channels = f_hat.shape[1]
    vocab = head_weight.shape[1]
    own_image = (m_index * rows) // NEW
    ada_own = lax.dynamic_index_in_dim(ada_ffn, own_image, 0, keepdims=False)
    gate_own = lax.dynamic_index_in_dim(ffn_gate, own_image, 0, keepdims=False)
    head_own = lax.dynamic_index_in_dim(ada_head, own_image, 0, keepdims=False)
    half_dp, half_mp = dp // 2, mp // 2
    upper = d_index // half_dp

    def swap(d, m):
        return ((d + half_dp) % dp, m)

    def cross(d, m):
        if d // half_dp == m // half_mp:
            return None
        return ((d + half_dp) % dp, (m + half_mp) % mp)

    stays = upper == m_index // half_mp
    head_twin = permute_devices(head_own, dp, mp, swap)
    head_cond = jnp.where(upper == 0, head_own, head_twin)
    head_uncond = jnp.where(upper == 0, head_twin, head_own)

    step = rows // CHUNKS
    normed = modulate(tokens, ada_own).astype(jnp.bfloat16)
    outs = []
    for c in range(CHUNKS):
        part = lax.slice_in_dim(normed, c * step, (c + 1) * step, axis=0)
        gathered = lax.all_gather(part, "mp", axis=0, tiled=True)
        hidden = jax.nn.gelu(
            jnp.dot(gathered, up_weight, preferred_element_type=jnp.float32) + up_bias,
            approximate=True,
        ).astype(jnp.bfloat16)
        partial = jnp.dot(hidden, down_weight, preferred_element_type=jnp.float32).astype(jnp.bfloat16)
        summed = lax.psum_scatter(partial, "mp", scatter_dimension=0, tiled=True).astype(jnp.float32)
        own = lax.slice_in_dim(tokens, c * step, (c + 1) * step, axis=0).astype(jnp.float32)
        outs.append((own + gate_own * (summed + down_bias)).astype(jnp.bfloat16))
    block_out = jnp.concatenate(outs, axis=0)

    group = CHUNKS // HEAD_CHUNKS
    half = rows // HEAD_CHUNKS // 2
    noise = gumbel_noise.reshape(pairs, NEW // rows, HEAD_CHUNKS, 2, half, vocab)
    peaks, totals, codes = [], [], []
    for c in range(HEAD_CHUNKS):
        part = jnp.concatenate(outs[c * group : (c + 1) * group], axis=0)
        first, second = part[:half], part[half:]
        kept = jnp.where(upper == 0, first, second)
        sent = jnp.where(upper == 0, second, first)
        came = permute_devices(sent, dp, mp, swap)
        cond = jnp.where(upper == 0, kept, came)
        uncond = jnp.where(upper == 0, came, kept)
        mixed = (
            (1.0 + GUIDE) * modulate(cond, head_cond) - GUIDE * modulate(uncond, head_uncond)
        ).astype(jnp.bfloat16)
        crossed = permute_devices(mixed, dp, mp, cross)
        mixed = jnp.where(stays, mixed, crossed)
        gathered = lax.all_gather(mixed, "mp", axis=0, tiled=True)
        logits = jnp.dot(gathered, head_weight, preferred_element_type=jnp.float32) + head_bias
        logits = logits.reshape(2, half_mp, half, vocab)
        order = jnp.transpose(logits, (1, 0, 2, 3)).reshape(pairs, NEW // rows, 2, half, vocab)
        scores = order + noise[:, :, c]
        peak = jnp.max(scores, axis=-1)
        weights = jnp.exp(scores - peak[..., None]).astype(jnp.bfloat16)
        totals.append(jnp.sum(weights.astype(jnp.float32), axis=-1))
        codes.append(jnp.dot(weights, codebook, preferred_element_type=jnp.float32))
        peaks.append(peak)
    stack = lambda parts: jnp.stack(parts, axis=2)
    peak = stack(peaks).reshape(pairs, 1, NEW)
    total = stack(totals).reshape(pairs, 1, NEW)
    code = stack(codes).reshape(pairs, NEW, channels).transpose(0, 2, 1)
    stats = jnp.concatenate([code, total, peak], axis=1)

    cells = f_hat.shape[2]
    band = cells // SIDE
    padded = jnp.pad(stats, ((0, 0), (0, 0), (SIDE, SIDE)))
    windows = jnp.stack(
        [padded[:, :, m * cells : m * cells + cells + 2 * SIDE] for m in range(mp)], axis=0
    )
    parts = lax.all_to_all(windows, "mp", 0, 0, tiled=True)
    top = jnp.max(parts[:, :, channels + 1], axis=0)
    factor = jnp.exp(parts[:, :, channels + 1] - top[None])[:, :, None]
    sums = jnp.sum(parts[:, :, : channels + 1] * factor, axis=0)
    cell_index = m_index * cells - SIDE + jnp.arange(cells + 2 * SIDE)
    inside = (cell_index >= 0) & (cell_index < NEW)
    soft = jnp.where(inside, sums[:, :channels] / jnp.where(inside, sums[:, channels:], 1.0), 0.0)
    code_map = soft.reshape(pairs, channels, band + 2, SIDE)
    wide = jnp.pad(code_map, ((0, 0), (0, 0), (0, 0), (1, 1)))
    taps = jnp.stack(
        [wide[:, :, i : i + band, j : j + SIDE] for i in range(3) for j in range(3)], axis=2
    ).reshape(pairs, channels * 9, cells)
    conv = jnp.einsum(
        "ok,pkn->pon",
        phi_weight.reshape(channels, channels * 9),
        taps,
        precision=lax.Precision.HIGHEST,
        preferred_element_type=jnp.float32,
    ) + phi_bias[None, :, None]
    f_hat_out = f_hat + 0.5 * soft[:, :, SIDE : SIDE + cells] + 0.5 * conv
    return (block_out, f_hat_out)


def solution(mesh):
    in_specs = (
        P(("dp", "mp"), None),
        P("dp", None, None),
        P("dp", None),
        P(None, "mp"),
        P("mp"),
        P("mp", None),
        P(),
        P("dp", None, None),
        P(None, "mp"),
        P("mp"),
        P("dp", None, "mp"),
        P("mp", None),
        P(),
        P(),
        P("dp", None, "mp"),
    )
    out_specs = (P(("dp", "mp"), None), P("dp", None, "mp"))
    return jax.shard_map(body, mesh=mesh, in_specs=in_specs, out_specs=out_specs, check_vma=False)
```

```python
import functools

import jax
import jax.numpy as jnp
from jax import lax
from jax.experimental import pallas as pl
from jax.experimental.pallas import tpu as pltpu
from jax.sharding import PartitionSpec as P

SIDE = 32
NEW = 1024
GUIDE = 1.5
CHUNKS = 2
FLOWS = 4
HEAD_FLOWS = 2


def norm_rows(values):
    row_mean = jnp.mean(values, axis=-1, keepdims=True)
    centred = values - row_mean
    spread = jnp.mean(centred * centred, axis=-1, keepdims=True)
    return centred * lax.rsqrt(spread + 1e-06)


def modulate(values, ada):
    return norm_rows(values.astype(jnp.float32)) * (1.0 + ada[1]) + ada[0]


def permute_devices(value, dp, mp, target):
    pairs = []
    for d in range(dp):
        for m in range(mp):
            to = target(d, m)
            if to is not None:
                pairs.append((d * mp + m, to[0] * mp + to[1]))
    return lax.ppermute(value, ("dp", "mp"), pairs)


def general_body(
    tokens,
    ada_ffn,
    ffn_gate,
    up_weight,
    up_bias,
    down_weight,
    down_bias,
    ada_head,
    head_weight,
    head_bias,
    gumbel_noise,
    codebook,
    phi_weight,
    phi_bias,
    f_hat,
):
    rows, width = tokens.shape
    dp, mp = lax.axis_size("dp"), lax.axis_size("mp")
    d_index, m_index = lax.axis_index("dp"), lax.axis_index("mp")
    images = ada_ffn.shape[0]
    pairs = f_hat.shape[0]
    channels = f_hat.shape[1]
    vocab = head_weight.shape[1]
    own_image = (m_index * rows) // NEW
    ada_own = lax.dynamic_index_in_dim(ada_ffn, own_image, 0, keepdims=False)
    gate_own = lax.dynamic_index_in_dim(ffn_gate, own_image, 0, keepdims=False)
    head_own = lax.dynamic_index_in_dim(ada_head, own_image, 0, keepdims=False)
    half_dp, half_mp = dp // 2, mp // 2
    upper = d_index // half_dp

    def swap(d, m):
        return ((d + half_dp) % dp, m)

    def cross(d, m):
        if d // half_dp == m // half_mp:
            return None
        return ((d + half_dp) % dp, (m + half_mp) % mp)

    stays = upper == m_index // half_mp
    head_twin = permute_devices(head_own, dp, mp, swap)
    head_cond = jnp.where(upper == 0, head_own, head_twin)
    head_uncond = jnp.where(upper == 0, head_twin, head_own)

    step = rows // FLOWS
    normed = modulate(tokens, ada_own).astype(jnp.bfloat16)
    outs = []
    for c in range(FLOWS):
        part = lax.slice_in_dim(normed, c * step, (c + 1) * step, axis=0)
        gathered = lax.all_gather(part, "mp", axis=0, tiled=True)
        hidden = jax.nn.gelu(
            jnp.dot(gathered, up_weight, preferred_element_type=jnp.float32) + up_bias,
            approximate=True,
        ).astype(jnp.bfloat16)
        partial = jnp.dot(hidden, down_weight, preferred_element_type=jnp.float32).astype(jnp.bfloat16)
        summed = lax.psum_scatter(partial, "mp", scatter_dimension=0, tiled=True).astype(jnp.float32)
        own = lax.slice_in_dim(tokens, c * step, (c + 1) * step, axis=0).astype(jnp.float32)
        outs.append((own + gate_own * (summed + down_bias)).astype(jnp.bfloat16))
    block_out = jnp.concatenate(outs, axis=0)

    group = FLOWS // HEAD_FLOWS
    half = rows // HEAD_FLOWS // 2
    noise = gumbel_noise.reshape(pairs, NEW // rows, HEAD_FLOWS, 2, half, vocab)
    peaks, totals, codes = [], [], []
    for c in range(HEAD_FLOWS):
        part = jnp.concatenate(outs[c * group : (c + 1) * group], axis=0)
        first, second = part[:half], part[half:]
        kept = jnp.where(upper == 0, first, second)
        sent = jnp.where(upper == 0, second, first)
        came = permute_devices(sent, dp, mp, swap)
        cond = jnp.where(upper == 0, kept, came)
        uncond = jnp.where(upper == 0, came, kept)
        mixed = (
            (1.0 + GUIDE) * modulate(cond, head_cond) - GUIDE * modulate(uncond, head_uncond)
        ).astype(jnp.bfloat16)
        crossed = permute_devices(mixed, dp, mp, cross)
        mixed = jnp.where(stays, mixed, crossed)
        gathered = lax.all_gather(mixed, "mp", axis=0, tiled=True)
        logits = jnp.dot(gathered, head_weight, preferred_element_type=jnp.float32) + head_bias
        logits = logits.reshape(2, half_mp, half, vocab)
        order = jnp.transpose(logits, (1, 0, 2, 3)).reshape(pairs, NEW // rows, 2, half, vocab)
        scores = order + noise[:, :, c]
        peak = jnp.max(scores, axis=-1)
        weights = jnp.exp(scores - peak[..., None]).astype(jnp.bfloat16)
        totals.append(jnp.sum(weights.astype(jnp.float32), axis=-1))
        codes.append(jnp.dot(weights, codebook, preferred_element_type=jnp.float32))
        peaks.append(peak)
    stack = lambda parts: jnp.stack(parts, axis=2)
    peak = stack(peaks).reshape(pairs, 1, NEW)
    total = stack(totals).reshape(pairs, 1, NEW)
    code = stack(codes).reshape(pairs, NEW, channels).transpose(0, 2, 1)
    stats = jnp.concatenate([code, total, peak], axis=1)

    cells = f_hat.shape[2]
    band = cells // SIDE
    padded = jnp.pad(stats, ((0, 0), (0, 0), (SIDE, SIDE)))
    windows = jnp.stack(
        [padded[:, :, m * cells : m * cells + cells + 2 * SIDE] for m in range(mp)], axis=0
    )
    parts = lax.all_to_all(windows, "mp", 0, 0, tiled=True)
    top = jnp.max(parts[:, :, channels + 1], axis=0)
    factor = jnp.exp(parts[:, :, channels + 1] - top[None])[:, :, None]
    sums = jnp.sum(parts[:, :, : channels + 1] * factor, axis=0)
    cell_index = m_index * cells - SIDE + jnp.arange(cells + 2 * SIDE)
    inside = (cell_index >= 0) & (cell_index < NEW)
    soft = jnp.where(inside, sums[:, :channels] / jnp.where(inside, sums[:, channels:], 1.0), 0.0)
    code_map = soft.reshape(pairs, channels, band + 2, SIDE)
    wide = jnp.pad(code_map, ((0, 0), (0, 0), (0, 0), (1, 1)))
    taps = jnp.stack(
        [wide[:, :, i : i + band, j : j + SIDE] for i in range(3) for j in range(3)], axis=2
    ).reshape(pairs, channels * 9, cells)
    conv = jnp.einsum(
        "ok,pkn->pon",
        phi_weight.reshape(channels, channels * 9),
        taps,
        precision=lax.Precision.HIGHEST,
        preferred_element_type=jnp.float32,
    ) + phi_bias[None, :, None]
    f_hat_out = f_hat + 0.5 * soft[:, :, SIDE : SIDE + cells] + 0.5 * conv
    return (block_out, f_hat_out)


def whole(shape):
    return pl.BlockSpec(shape, lambda: (0,) * len(shape))


SCALARS = pl.BlockSpec(memory_space=pltpu.SMEM)
LEFT_IN_PLACE = pl.BlockSpec(memory_space=pl.ANY)
VMEM_LIMIT = 56 * 1024 * 1024


def call(kernel, args, specs, outs, flops, scratch=(), transcendentals=0):
    moved = sum(a.size * a.dtype.itemsize for a in args) + sum(o.size * o.dtype.itemsize for o in outs)
    return pl.pallas_call(
        kernel,
        out_shape=outs,
        in_specs=specs,
        out_specs=[whole(o.shape) for o in outs],
        scratch_shapes=scratch,
        compiler_params=pltpu.CompilerParams(vmem_limit_bytes=VMEM_LIMIT),
        cost_estimate=pl.CostEstimate(
            flops=int(flops), bytes_accessed=int(moved), transcendentals=int(transcendentals)
        ),
    )(*args)


def shape_of(shape, kind=jnp.bfloat16):
    return jax.ShapeDtypeStruct(shape, kind)


def norm_kernel(chunks, tokens_ref, ada_ref, *outs):
    step = tokens_ref.shape[0] // chunks
    for c in range(chunks):
        values = tokens_ref[c * step : (c + 1) * step, :].astype(jnp.float32)
        outs[c][...] = (norm_rows(values) * (1.0 + ada_ref[1:2, :]) + ada_ref[0:1, :]).astype(jnp.bfloat16)


def norm_chunks(tokens, ada, chunks):
    rows, width = tokens.shape
    outs = [shape_of((rows // chunks, width))] * chunks
    return call(
        functools.partial(norm_kernel, chunks),
        (tokens, ada),
        [whole(tokens.shape), whole(ada.shape)],
        outs,
        10 * tokens.size,
    )


def strips(panel, tile):
    tiles = []
    for begin in range(0, 2 * panel, tile):
        end = begin + tile
        pieces = []
        if begin < panel:
            pieces.append((0, begin, min(end, panel) - begin))
        if end > panel:
            start = max(begin, panel) - panel
            pieces.append((1, start, end - panel - start))
        tiles.append(pieces)
    return tiles


def ffn_kernel(groups, tile, *refs):
    count = sum(groups)
    parts = refs[:count]
    up_refs, down_refs = refs[count : count + 2], refs[count + 2 : count + 4]
    bias_ref = refs[count + 4]
    outs = refs[count + 5 : count + 5 + len(groups)]
    x_ref, hidden_ref, up_ref, down_ref, up_sems, down_sems = refs[count + 5 + len(groups) :]
    panel, width = down_refs[0].shape
    tiles = strips(panel, tile)
    up_copies, down_copies = [], []
    place = 0
    for pieces in tiles:
        mine = []
        for which, start, size in pieces:
            at = which * panel + start
            copy = pltpu.make_async_copy(
                up_refs[which].at[:, pl.ds(start, size)], up_ref.at[:, pl.ds(at, size)], up_sems.at[place]
            )
            copy.start()
            mine.append(copy)
            place += 1
        up_copies.append(mine)
    for which in range(2):
        copy = pltpu.make_async_copy(
            down_refs[which], down_ref.at[pl.ds(which * panel, panel), :], down_sems.at[which]
        )
        copy.start()
        down_copies.append(copy)
    step = outs[0].shape[0]
    place = 0
    for g, size in enumerate(groups):
        value = parts[place][...]
        for other in range(1, size):
            value = value + parts[place + other][...]
        x_ref[g * step : (g + 1) * step, :] = value
        place += size
    for t, copies in enumerate(up_copies):
        for copy in copies:
            copy.wait()
        cols = slice(t * tile, (t + 1) * tile)
        v = jnp.dot(x_ref[...], up_ref[:, cols], preferred_element_type=jnp.float32) + bias_ref[:, cols]
        hidden_ref[:, cols] = jax.nn.gelu(v, approximate=True).astype(jnp.bfloat16)
    for copy in down_copies:
        copy.wait()
    for t in range(width // tile):
        cols = slice(t * tile, (t + 1) * tile)
        result = jnp.dot(hidden_ref[...], down_ref[:, cols], preferred_element_type=jnp.float32)
        for g in range(len(groups)):
            outs[g][:, cols] = result[g * step : (g + 1) * step].astype(jnp.bfloat16)


def ffn(slots, ups, downs, bias):
    groups = tuple(len(slot) for slot in slots)
    parts = [part for slot in slots for part in slot]
    rows, width = parts[0].shape
    panel = ups[0].shape[1]
    total = rows * len(slots)
    tile = 256
    pieces = sum(len(p) for p in strips(panel, tile))
    return call(
        functools.partial(ffn_kernel, groups, tile),
        (*parts, *ups, *downs, bias),
        [whole(p.shape) for p in parts] + [LEFT_IN_PLACE] * 4 + [whole(bias.shape)],
        [shape_of((rows, width))] * len(slots),
        8 * total * width * panel,
        scratch=[
            pltpu.VMEM((total, width), jnp.bfloat16),
            pltpu.VMEM((total, 2 * panel), jnp.bfloat16),
            pltpu.VMEM((width, 2 * panel), jnp.bfloat16),
            pltpu.VMEM((2 * panel, width), jnp.bfloat16),
            pltpu.SemaphoreType.DMA((pieces,)),
            pltpu.SemaphoreType.DMA((2,)),
        ],
        transcendentals=2 * total * panel,
    )


def out_kernel(chunk, where_ref, own_ref, near_ref, mid_ref, tokens_ref, gate_ref, bias_ref, out_ref, kept_ref, sent_ref):
    summed = own_ref[...].astype(jnp.float32) + near_ref[...].astype(jnp.float32) + mid_ref[...].astype(jnp.float32)
    rows = out_ref.shape[0]
    tokens = tokens_ref[chunk * rows : (chunk + 1) * rows, :].astype(jnp.float32)
    value = (tokens + gate_ref[...] * (summed + bias_ref[...])).astype(jnp.bfloat16)
    out_ref[...] = value
    half = rows // 2
    lower = where_ref[0] == 0
    kept_ref[...] = jnp.where(lower, value[:half], value[half:])
    sent_ref[...] = jnp.where(lower, value[half:], value[:half])


def block_rows(chunk, where, own, near, mid, tokens, gate, bias):
    rows, width = own.shape
    args = (where, own, near, mid, tokens, gate, bias)
    return call(
        functools.partial(out_kernel, chunk),
        args,
        [SCALARS] + [whole(a.shape) for a in args[1:]],
        [shape_of((rows, width)), shape_of((rows // 2, width)), shape_of((rows // 2, width))],
        6 * own.size,
    )


def mix_kernel(share_ref, kept_ref, came_ref, ada_ref, twin_ref, out_ref):
    kept = norm_rows(kept_ref[...].astype(jnp.float32)) * (1.0 + ada_ref[1:2, :]) + ada_ref[0:1, :]
    came = norm_rows(came_ref[...].astype(jnp.float32)) * (1.0 + twin_ref[1:2, :]) + twin_ref[0:1, :]
    out_ref[...] = (share_ref[0] * kept + share_ref[1] * came).astype(jnp.bfloat16)


def mix_twins(shares, kept, came, ada, twin):
    args = (shares, kept, came, ada, twin)
    return call(
        mix_kernel,
        args,
        [SCALARS] + [whole(a.shape) for a in args[1:]],
        [shape_of(kept.shape)],
        20 * kept.size,
    )[0]


def head_kernel(
    chunk, where_ref, own_ref, near_ref, far_a, far_b, last_a, last_b, weight_a, weight_b, bias_ref, code_ref,
    same_a, same_b, other_a, other_b, stats_ref, x_ref
):
    step = own_ref.shape[0]
    panel = weight_a.shape[1]
    x_ref[0:step, :] = own_ref[...]
    x_ref[step : 2 * step, :] = near_ref[...]
    x_ref[2 * step : 3 * step, :] = far_a[...] + far_b[...]
    x_ref[3 * step : 4 * step, :] = last_a[...] + last_b[...]
    x = x_ref[...]
    odd = where_ref[1]
    even = 1 - odd
    scores = []
    for which, weight, same, other in ((0, weight_a, same_a, other_a), (1, weight_b, same_b, other_b)):
        noise = jnp.concatenate([same[odd, chunk], same[even, chunk], other[odd, chunk], other[even, chunk]], axis=0)
        logits = jnp.dot(x, weight[...], preferred_element_type=jnp.float32)
        scores.append(logits + bias_ref[:, which * panel : (which + 1) * panel] + noise)
    peak = jnp.max(jnp.maximum(scores[0], scores[1]), axis=1, keepdims=True)
    sums = 0.0
    total = 0.0
    for which in range(2):
        weights = jnp.exp(scores[which] - peak).astype(jnp.bfloat16)
        total = total + jnp.sum(weights.astype(jnp.float32), axis=1, keepdims=True)
        codes = code_ref[which * panel : (which + 1) * panel, :].astype(jnp.bfloat16)
        sums = sums + jnp.dot(weights, codes, preferred_element_type=jnp.float32)
    channels = code_ref.shape[1]
    pad = jnp.zeros((4 * step, 128 - channels), jnp.float32)
    table = jnp.concatenate([sums, pad], axis=1)
    lane = lax.broadcasted_iota(jnp.int32, table.shape, 1)
    table = jnp.where(lane == channels, total, table)
    table = jnp.where(lane == channels + 1, peak, table)
    stats_ref[...] = jnp.transpose(table)[: stats_ref.shape[0], :]


def head_stats(chunk, where, slots, weights, bias, codes, noises):
    step, width = slots[0].shape
    panel = weights[0].shape[1]
    height = -(-(codes.shape[1] + 2) // 8) * 8
    args = (where, *slots, *weights, bias, codes, *noises)
    return call(
        functools.partial(head_kernel, chunk),
        args,
        [SCALARS] + [whole(a.shape) for a in args[1:]],
        [shape_of((height, 4 * step), jnp.float32)],
        16 * step * width * panel,
        scratch=[pltpu.VMEM((4 * step, width), jnp.bfloat16)],
        transcendentals=8 * step * panel,
    )[0]


def soft_kernel(channels, *refs):
    parts, out_ref = refs[:-1], refs[-1]
    tops = [part[channels + 1 : channels + 2, :] for part in parts]
    top = functools.reduce(jnp.maximum, tops)
    code = 0.0
    total = 0.0
    for part, peak in zip(parts, tops):
        factor = jnp.exp(peak - top)
        code = code + part[0:channels, :] * factor
        total = total + part[channels : channels + 1, :] * factor
    out_ref[...] = code / total


def soft_codes(parts, channels):
    return call(
        functools.partial(soft_kernel, channels),
        tuple(parts),
        [whole(p.shape) for p in parts],
        [shape_of((channels, parts[0].shape[1]), jnp.float32)],
        10 * parts[0].size,
    )[0]


def line_body(
    tokens,
    ada_ffn,
    ffn_gate,
    up_weight,
    up_bias,
    down_weight,
    down_bias,
    ada_head,
    head_weight,
    head_bias,
    gumbel_noise,
    codebook,
    phi_weight,
    phi_bias,
    f_hat,
):
    rows, width = tokens.shape
    dp, mp = lax.axis_size("dp"), lax.axis_size("mp")
    d_index, m_index = lax.axis_index("dp"), lax.axis_index("mp")
    channels = f_hat.shape[1]
    half_dp = dp // 2
    upper = d_index // half_dp
    z_index, core = m_index // 2, m_index % 2
    is_same = z_index // 2 == upper

    def along_z(value, target):
        def to(d, m):
            z = target(m // 2)
            return None if z is None else (d, 2 * z + m % 2)

        return permute_devices(value, dp, mp, to)

    def near(value):
        return along_z(value, lambda z: z ^ 1)

    def middle(value):
        return along_z(value, lambda z: 3 - z if z in (1, 2) else None)

    def outward(value):
        return along_z(value, lambda z: {1: 0, 2: 3}.get(z))

    def inward(value):
        return along_z(value, lambda z: {0: 1, 3: 2}.get(z))

    def swap_cores(value):
        return permute_devices(value, dp, mp, lambda d, m: (d, m ^ 1))

    def swap_twins(value):
        return permute_devices(value, dp, mp, lambda d, m: ((d + half_dp) % dp, m))

    def swap_both(value):
        return permute_devices(value, dp, mp, lambda d, m: ((d + half_dp) % dp, m ^ 1))

    own_image = (m_index * rows) // NEW
    ada_own = lax.dynamic_index_in_dim(ada_ffn, own_image, 0, keepdims=False)
    gate_own = lax.dynamic_index_in_dim(ffn_gate, own_image, 0, keepdims=True)
    head_own = lax.dynamic_index_in_dim(ada_head, own_image, 0, keepdims=False)

    def gather(own):
        from_near = near(own)
        from_mid = middle(own)
        far_mid = middle(from_near)
        far_end = outward(from_mid)
        last_end = outward(far_mid)
        return from_near, (far_mid, far_end), (from_mid, last_end)

    normed = norm_chunks(tokens, ada_own, CHUNKS)
    gathered = [gather(part) for part in normed]
    up_other, down_other = swap_cores(up_weight), swap_cores(down_weight)
    small = jnp.concatenate([up_bias, head_bias, codebook.astype(jnp.float32).reshape(-1)])
    small_other = swap_cores(small)
    head_other = swap_cores(head_weight)
    head_twin = swap_twins(head_own)
    hid, voc = up_bias.shape[0], head_bias.shape[0]
    bias_up = jnp.concatenate([up_bias, small_other[:hid]])[None]
    bias_head = jnp.concatenate([head_bias, small_other[hid : hid + voc]])[None]
    codes = jnp.concatenate(
        [codebook.astype(jnp.float32), small_other[hid + voc :].reshape(codebook.shape)], axis=0
    )

    half = rows // CHUNKS // 2
    noise = gumbel_noise.reshape(2, 2, CHUNKS, 2, half, voc)

    def noise_for(to_core, to_upper):
        picked = lax.dynamic_slice(
            noise, (0, to_core, 0, to_upper, 0, 0), (2, 1, CHUNKS, 1, half, voc)
        )
        return picked.reshape(2, CHUNKS, half, voc)

    noise_own = noise_for(core, upper)
    noise_core = swap_cores(noise_for(1 - core, upper))
    noise_twin = swap_twins(noise_for(core, 1 - upper))
    noise_both = swap_both(noise_for(1 - core, 1 - upper))
    noises = (
        jnp.where(is_same, noise_own, noise_twin),
        jnp.where(is_same, noise_core, noise_both),
        jnp.where(is_same, noise_twin, noise_own),
        jnp.where(is_same, noise_both, noise_core),
    )

    where = jnp.stack([upper, z_index % 2]).astype(jnp.int32)
    shares = jnp.where(upper == 0, jnp.array([1.0 + GUIDE, -GUIDE]), jnp.array([-GUIDE, 1.0 + GUIDE]))
    shares = shares.astype(jnp.float32)
    ups, downs = (up_weight, up_other), (down_weight, down_other)

    def add(a, b):
        return (a.astype(jnp.float32) + b.astype(jnp.float32)).astype(jnp.bfloat16)

    outs, stats = [], []
    for c in range(CHUNKS):
        from_near, far, last = gathered[c]
        sum_own, sum_near, sum_far = ffn([[normed[c]], [from_near], list(far)], ups, downs, bias_up)
        (sum_last,) = ffn([list(last)], ups, downs, bias_up)
        came_far = inward(sum_far)
        came_last = inward(sum_last)
        went_last = middle(add(sum_last, came_far))
        went_far = middle(add(sum_far, came_last))
        came_near = near(add(sum_near, went_far))
        rows_out, kept, sent = block_rows(
            c, where, sum_own, came_near, went_last, tokens, gate_own, down_bias[None]
        )
        outs.append(rows_out)
        came = swap_twins(sent)
        mixed = mix_twins(shares, kept, came, head_own, head_twin)
        mix_near, mix_far, mix_last = gather(mixed)
        stats.append(
            head_stats(
                c, where, (mixed, mix_near, *mix_far, *mix_last), (head_weight, head_other), bias_head, codes, noises
            )
        )
    block_out = jnp.concatenate(outs, axis=0)

    slots = [
        jnp.concatenate([part[:, r * half : (r + 1) * half] for part in stats], axis=1) for r in range(4)
    ]
    parts = [slots[0]] + [along_z(slots[r], lambda z, r=r: z ^ r) for r in (1, 2, 3)]
    soft = soft_codes(parts, channels)

    def to_cells(d, m, core_of):
        y, x = d // half_dp, d % half_dp
        z, c = m // 2, m % 2
        return ((z // 2) * half_dp + x, 2 * (2 * (z % 2) + c) + core_of(y))

    def to_halo(d, m):
        y, x = d // half_dp, d % half_dp
        z, c = m // 2, m % 2
        block = 2 * (z % 2) + c + (1 if y == 1 else -1)
        if block < 0 or block > 3:
            return None
        return ((z // 2) * half_dp + x, 2 * block + (0 if y == 1 else 1))

    first = permute_devices(soft, dp, mp, lambda d, m: to_cells(d, m, lambda y: y))
    second = permute_devices(soft, dp, mp, lambda d, m: to_cells(d, m, lambda y: 1 - y))
    halo = permute_devices(soft, dp, mp, to_halo)
    lower, higher = jnp.where(core == 0, first, second), jnp.where(core == 0, second, first)
    window = jnp.where(
        core == 0,
        jnp.concatenate([halo[:, -SIDE:], lower[:, :half], higher[:, :half], lower[:, half : half + SIDE]], axis=1),
        jnp.concatenate([higher[:, half - SIDE : half], lower[:, half:], higher[:, half:], halo[:, :SIDE]], axis=1),
    )
    cells = f_hat.shape[2]
    band = cells // SIDE
    code_map = window.reshape(channels, band + 2, SIDE)
    wide = jnp.pad(code_map, ((0, 0), (0, 0), (1, 1)))
    taps = jnp.stack(
        [wide[:, i : i + band, j : j + SIDE] for i in range(3) for j in range(3)], axis=1
    ).reshape(channels * 9, cells)
    conv = jnp.dot(
        phi_weight.reshape(channels, channels * 9),
        taps,
        precision=lax.Precision.HIGHEST,
        preferred_element_type=jnp.float32,
    ) + phi_bias[:, None]
    f_hat_out = f_hat + (0.5 * window[:, SIDE : SIDE + cells] + 0.5 * conv)[None]
    return (block_out, f_hat_out)


def solution(mesh):
    in_specs = (
        P(("dp", "mp"), None),
        P("dp", None, None),
        P("dp", None),
        P(None, "mp"),
        P("mp"),
        P("mp", None),
        P(),
        P("dp", None, None),
        P(None, "mp"),
        P("mp"),
        P("dp", None, "mp"),
        P("mp", None),
        P(),
        P(),
        P("dp", None, "mp"),
    )
    out_specs = (P(("dp", "mp"), None), P("dp", None, "mp"))
    line = mesh.shape["dp"] == 4 and mesh.shape["mp"] == 8
    body = line_body if line else general_body
    return jax.shard_map(body, mesh=mesh, in_specs=in_specs, out_specs=out_specs, check_vma=False)
```

```python
import functools

import jax
import jax.numpy as jnp
from jax import lax
from jax.experimental import pallas as pl
from jax.experimental.pallas import tpu as pltpu
from jax.sharding import PartitionSpec as P

SIDE = 32
NEW = 1024
GUIDE = 1.5
CHUNKS = 2
FLOWS = 4
HEAD_FLOWS = 2


def norm_rows(values):
    row_mean = jnp.mean(values, axis=-1, keepdims=True)
    centred = values - row_mean
    spread = jnp.mean(centred * centred, axis=-1, keepdims=True)
    return centred * lax.rsqrt(spread + 1e-06)


def modulate(values, ada):
    return norm_rows(values.astype(jnp.float32)) * (1.0 + ada[1]) + ada[0]


def permute_devices(value, dp, mp, target):
    pairs = []
    for d in range(dp):
        for m in range(mp):
            to = target(d, m)
            if to is not None:
                pairs.append((d * mp + m, to[0] * mp + to[1]))
    return lax.ppermute(value, ("dp", "mp"), pairs)


def general_body(
    tokens,
    ada_ffn,
    ffn_gate,
    up_weight,
    up_bias,
    down_weight,
    down_bias,
    ada_head,
    head_weight,
    head_bias,
    gumbel_noise,
    codebook,
    phi_weight,
    phi_bias,
    f_hat,
):
    rows, width = tokens.shape
    dp, mp = lax.axis_size("dp"), lax.axis_size("mp")
    d_index, m_index = lax.axis_index("dp"), lax.axis_index("mp")
    images = ada_ffn.shape[0]
    pairs = f_hat.shape[0]
    channels = f_hat.shape[1]
    vocab = head_weight.shape[1]
    own_image = (m_index * rows) // NEW
    ada_own = lax.dynamic_index_in_dim(ada_ffn, own_image, 0, keepdims=False)
    gate_own = lax.dynamic_index_in_dim(ffn_gate, own_image, 0, keepdims=False)
    head_own = lax.dynamic_index_in_dim(ada_head, own_image, 0, keepdims=False)
    half_dp, half_mp = dp // 2, mp // 2
    upper = d_index // half_dp

    def swap(d, m):
        return ((d + half_dp) % dp, m)

    def cross(d, m):
        if d // half_dp == m // half_mp:
            return None
        return ((d + half_dp) % dp, (m + half_mp) % mp)

    stays = upper == m_index // half_mp
    head_twin = permute_devices(head_own, dp, mp, swap)
    head_cond = jnp.where(upper == 0, head_own, head_twin)
    head_uncond = jnp.where(upper == 0, head_twin, head_own)

    step = rows // FLOWS
    normed = modulate(tokens, ada_own).astype(jnp.bfloat16)
    outs = []
    for c in range(FLOWS):
        part = lax.slice_in_dim(normed, c * step, (c + 1) * step, axis=0)
        gathered = lax.all_gather(part, "mp", axis=0, tiled=True)
        hidden = jax.nn.gelu(
            jnp.dot(gathered, up_weight, preferred_element_type=jnp.float32) + up_bias,
            approximate=True,
        ).astype(jnp.bfloat16)
        partial = jnp.dot(hidden, down_weight, preferred_element_type=jnp.float32).astype(jnp.bfloat16)
        summed = lax.psum_scatter(partial, "mp", scatter_dimension=0, tiled=True).astype(jnp.float32)
        own = lax.slice_in_dim(tokens, c * step, (c + 1) * step, axis=0).astype(jnp.float32)
        outs.append((own + gate_own * (summed + down_bias)).astype(jnp.bfloat16))
    block_out = jnp.concatenate(outs, axis=0)

    group = FLOWS // HEAD_FLOWS
    half = rows // HEAD_FLOWS // 2
    noise = gumbel_noise.reshape(pairs, NEW // rows, HEAD_FLOWS, 2, half, vocab)
    peaks, totals, codes = [], [], []
    for c in range(HEAD_FLOWS):
        part = jnp.concatenate(outs[c * group : (c + 1) * group], axis=0)
        first, second = part[:half], part[half:]
        kept = jnp.where(upper == 0, first, second)
        sent = jnp.where(upper == 0, second, first)
        came = permute_devices(sent, dp, mp, swap)
        cond = jnp.where(upper == 0, kept, came)
        uncond = jnp.where(upper == 0, came, kept)
        mixed = (
            (1.0 + GUIDE) * modulate(cond, head_cond) - GUIDE * modulate(uncond, head_uncond)
        ).astype(jnp.bfloat16)
        crossed = permute_devices(mixed, dp, mp, cross)
        mixed = jnp.where(stays, mixed, crossed)
        gathered = lax.all_gather(mixed, "mp", axis=0, tiled=True)
        logits = jnp.dot(gathered, head_weight, preferred_element_type=jnp.float32) + head_bias
        logits = logits.reshape(2, half_mp, half, vocab)
        order = jnp.transpose(logits, (1, 0, 2, 3)).reshape(pairs, NEW // rows, 2, half, vocab)
        scores = order + noise[:, :, c]
        peak = jnp.max(scores, axis=-1)
        weights = jnp.exp(scores - peak[..., None]).astype(jnp.bfloat16)
        totals.append(jnp.sum(weights.astype(jnp.float32), axis=-1))
        codes.append(jnp.dot(weights, codebook, preferred_element_type=jnp.float32))
        peaks.append(peak)
    stack = lambda parts: jnp.stack(parts, axis=2)
    peak = stack(peaks).reshape(pairs, 1, NEW)
    total = stack(totals).reshape(pairs, 1, NEW)
    code = stack(codes).reshape(pairs, NEW, channels).transpose(0, 2, 1)
    stats = jnp.concatenate([code, total, peak], axis=1)

    cells = f_hat.shape[2]
    band = cells // SIDE
    padded = jnp.pad(stats, ((0, 0), (0, 0), (SIDE, SIDE)))
    windows = jnp.stack(
        [padded[:, :, m * cells : m * cells + cells + 2 * SIDE] for m in range(mp)], axis=0
    )
    parts = lax.all_to_all(windows, "mp", 0, 0, tiled=True)
    top = jnp.max(parts[:, :, channels + 1], axis=0)
    factor = jnp.exp(parts[:, :, channels + 1] - top[None])[:, :, None]
    sums = jnp.sum(parts[:, :, : channels + 1] * factor, axis=0)
    cell_index = m_index * cells - SIDE + jnp.arange(cells + 2 * SIDE)
    inside = (cell_index >= 0) & (cell_index < NEW)
    soft = jnp.where(inside, sums[:, :channels] / jnp.where(inside, sums[:, channels:], 1.0), 0.0)
    code_map = soft.reshape(pairs, channels, band + 2, SIDE)
    wide = jnp.pad(code_map, ((0, 0), (0, 0), (0, 0), (1, 1)))
    taps = jnp.stack(
        [wide[:, :, i : i + band, j : j + SIDE] for i in range(3) for j in range(3)], axis=2
    ).reshape(pairs, channels * 9, cells)
    conv = jnp.einsum(
        "ok,pkn->pon",
        phi_weight.reshape(channels, channels * 9),
        taps,
        precision=lax.Precision.HIGHEST,
        preferred_element_type=jnp.float32,
    ) + phi_bias[None, :, None]
    f_hat_out = f_hat + 0.5 * soft[:, :, SIDE : SIDE + cells] + 0.5 * conv
    return (block_out, f_hat_out)


SCALARS = pl.BlockSpec(memory_space=pltpu.SMEM)
ON_CHIP = pl.BlockSpec(memory_space=pltpu.VMEM)
VMEM_LIMIT = 16 * 1024 * 1024


def call(kernel, args, outs, scalars=0, scratch=()):
    return pl.pallas_call(
        kernel,
        out_shape=outs,
        in_specs=[SCALARS] * scalars + [ON_CHIP] * (len(args) - scalars),
        out_specs=[ON_CHIP] * len(outs),
        scratch_shapes=scratch,
        compiler_params=pltpu.CompilerParams(vmem_limit_bytes=VMEM_LIMIT),
        cost_estimate=pl.CostEstimate(flops=0, bytes_accessed=0, transcendentals=0),
    )(*args)


def shape_of(shape, kind=jnp.bfloat16):
    return jax.ShapeDtypeStruct(shape, kind)


def after(value, *others):
    return lax.optimization_barrier((value, *others))[0]


def modulated(ref, ada_ref):
    return norm_rows(ref[...].astype(jnp.float32)) * (1.0 + ada_ref[1:2, :]) + ada_ref[0:1, :]


def norm_kernel(tokens_ref, ada_ref, out_ref):
    out_ref[...] = modulated(tokens_ref, ada_ref).astype(jnp.bfloat16)


def norm_part(tokens, ada):
    return call(norm_kernel, (tokens, ada), [shape_of(tokens.shape)])[0]


def ffn_kernel(groups, tile, where_ref, *refs):
    count = sum(groups)
    parts = refs[:count]
    up_refs, down_refs = refs[count : count + 2], refs[count + 2 : count + 4]
    bias_ref = refs[count + 4]
    outs = refs[count + 5 : count + 5 + len(groups)]
    x_ref, hidden_ref = refs[count + 5 + len(groups) :]
    panel, width = down_refs[0].shape
    step = outs[0].shape[0]
    place = 0
    for g, size in enumerate(groups):
        if size == 1:
            value = parts[place][...]
        else:
            value = jnp.where(where_ref[0] == 1, parts[place][...], parts[place + 1][...])
        x_ref[g * step : (g + 1) * step, :] = value
        place += size
    for begin in range(0, 2 * panel, tile):
        end = begin + tile
        if end <= panel:
            weight = up_refs[0][:, begin:end]
        elif begin >= panel:
            weight = up_refs[1][:, begin - panel : end - panel]
        else:
            weight = jnp.concatenate([up_refs[0][:, begin:], up_refs[1][:, : end - panel]], axis=1)
        v = jnp.dot(x_ref[...], weight, preferred_element_type=jnp.float32) + bias_ref[:, begin:end]
        hidden_ref[:, begin:end] = jax.nn.gelu(v, approximate=True).astype(jnp.bfloat16)
    for begin in range(0, width, tile):
        cols = slice(begin, begin + tile)
        weight = jnp.concatenate([down_refs[0][:, cols], down_refs[1][:, cols]], axis=0)
        result = jnp.dot(hidden_ref[...], weight, preferred_element_type=jnp.float32)
        for g in range(len(groups)):
            outs[g][:, cols] = result[g * step : (g + 1) * step].astype(jnp.bfloat16)


def ffn(where, slots, ups, downs, bias):
    groups = tuple(len(slot) for slot in slots)
    parts = [part for slot in slots for part in slot]
    rows, width = parts[0].shape
    panel = ups[0].shape[1]
    total = rows * len(slots)
    return call(
        functools.partial(ffn_kernel, groups, 256),
        (where, *parts, *ups, *downs, bias),
        [shape_of((rows, width))] * len(slots),
        scalars=1,
        scratch=[
            pltpu.VMEM((total, width), jnp.bfloat16),
            pltpu.VMEM((total, 2 * panel), jnp.bfloat16),
        ],
    )


def add_kernel(where_ref, a_ref, b_ref, out_ref):
    b = jnp.where(where_ref[0] == 1, b_ref[...].astype(jnp.float32), 0.0)
    out_ref[...] = (a_ref[...].astype(jnp.float32) + b).astype(jnp.bfloat16)


def add_mid(where, a, b):
    return call(add_kernel, (where, a, b), [shape_of(a.shape)], scalars=1)[0]


def out_kernel(where_ref, own_ref, near_ref, mid_ref, tokens_ref, gate_ref, bias_ref, out_ref, kept_ref, sent_ref):
    from_mid = jnp.where(where_ref[0] == 1, mid_ref[...].astype(jnp.float32), 0.0)
    summed = own_ref[...].astype(jnp.float32) + near_ref[...].astype(jnp.float32) + from_mid
    value = tokens_ref[...].astype(jnp.float32) + gate_ref[...] * (summed + bias_ref[...])
    value = value.astype(jnp.bfloat16)
    out_ref[...] = value
    half = value.shape[0] // 2
    lower = where_ref[1] == 0
    kept_ref[...] = jnp.where(lower, value[:half], value[half:])
    sent_ref[...] = jnp.where(lower, value[half:], value[:half])


def block_rows(where, own, near, mid, tokens, gate, bias):
    rows, width = own.shape
    return call(
        out_kernel,
        (where, own, near, mid, tokens, gate, bias),
        [shape_of((rows, width)), shape_of((rows // 2, width)), shape_of((rows // 2, width))],
        scalars=1,
    )


def mix_kernel(where_ref, kept_ref, came_ref, ada_ref, twin_ref, out_ref):
    kept, came = modulated(kept_ref, ada_ref), modulated(came_ref, twin_ref)
    lower = where_ref[1] == 0
    share = jnp.where(lower, 1.0 + GUIDE, -GUIDE)
    other = jnp.where(lower, -GUIDE, 1.0 + GUIDE)
    out_ref[...] = (share * kept + other * came).astype(jnp.bfloat16)


def mix_twins(where, kept, came, ada, twin):
    return call(mix_kernel, (where, kept, came, ada, twin), [shape_of(kept.shape)], scalars=1)[0]


def head_kernel(
    chunk, where_ref, own_ref, near_ref, far_a, far_b, last_a, last_b, weight_a, weight_b, bias_ref, code_ref,
    noise_own, noise_core, noise_twin, noise_both, stats_ref, x_ref
):
    step = own_ref.shape[0]
    panel = weight_a.shape[1]
    mid = where_ref[0] == 1
    x_ref[0:step, :] = own_ref[...]
    x_ref[step : 2 * step, :] = near_ref[...]
    x_ref[2 * step : 3 * step, :] = jnp.where(mid, far_a[...], far_b[...])
    x_ref[3 * step : 4 * step, :] = jnp.where(mid, last_a[...], last_b[...])
    x = x_ref[...]
    odd = where_ref[2]
    even = 1 - odd
    same = where_ref[3] == 1
    scores = []
    for which, weight, ours, theirs in ((0, weight_a, noise_own, noise_twin), (1, weight_b, noise_core, noise_both)):
        picked = []
        for first in (True, False):
            for block in (odd, even):
                a, b = ours[block, chunk], theirs[block, chunk]
                picked.append(jnp.where(same, a, b) if first else jnp.where(same, b, a))
        logits = jnp.dot(x, weight[...], preferred_element_type=jnp.float32)
        scores.append(
            logits + bias_ref[:, which * panel : (which + 1) * panel] + jnp.concatenate(picked, axis=0)
        )
    peak = jnp.max(jnp.maximum(scores[0], scores[1]), axis=1, keepdims=True)
    sums = 0.0
    total = 0.0
    for which in range(2):
        weights = jnp.exp(scores[which] - peak).astype(jnp.bfloat16)
        total = total + jnp.sum(weights.astype(jnp.float32), axis=1, keepdims=True)
        codes = code_ref[which * panel : (which + 1) * panel, :].astype(jnp.bfloat16)
        sums = sums + jnp.dot(weights, codes, preferred_element_type=jnp.float32)
    channels = code_ref.shape[1]
    pad = jnp.zeros((4 * step, 128 - channels), jnp.float32)
    table = jnp.concatenate([sums, pad], axis=1)
    lane = lax.broadcasted_iota(jnp.int32, table.shape, 1)
    table = jnp.where(lane == channels, total, table)
    table = jnp.where(lane == channels + 1, peak, table)
    stats_ref[...] = jnp.transpose(table)[: stats_ref.shape[0], :]


def head_stats(chunk, where, slots, weights, bias, codes, noises):
    step, width = slots[0].shape
    panel = weights[0].shape[1]
    height = -(-(codes.shape[1] + 2) // 8) * 8
    return call(
        functools.partial(head_kernel, chunk),
        (where, *slots, *weights, bias, codes, *noises),
        [shape_of((height, 4 * step), jnp.float32)],
        scalars=1,
        scratch=[pltpu.VMEM((4 * step, width), jnp.bfloat16)],
    )[0]


def soft_kernel(channels, *refs):
    parts, out_ref = refs[:-1], refs[-1]
    tops = [part[channels + 1 : channels + 2, :] for part in parts]
    top = functools.reduce(jnp.maximum, tops)
    code = 0.0
    total = 0.0
    for part, peak in zip(parts, tops):
        factor = jnp.exp(peak - top)
        code = code + part[0:channels, :] * factor
        total = total + part[channels : channels + 1, :] * factor
    out_ref[...] = code / total


def soft_codes(parts, channels):
    return call(
        functools.partial(soft_kernel, channels),
        tuple(parts),
        [shape_of((channels, parts[0].shape[1]), jnp.float32)],
    )[0]


def line_body(
    tokens,
    ada_ffn,
    ffn_gate,
    up_weight,
    up_bias,
    down_weight,
    down_bias,
    ada_head,
    head_weight,
    head_bias,
    gumbel_noise,
    codebook,
    phi_weight,
    phi_bias,
    f_hat,
):
    rows, width = tokens.shape
    dp, mp = lax.axis_size("dp"), lax.axis_size("mp")
    d_index, m_index = lax.axis_index("dp"), lax.axis_index("mp")
    channels = f_hat.shape[1]
    half_dp = dp // 2
    upper = d_index // half_dp
    z_index, core = m_index // 2, m_index % 2
    where = jnp.stack(
        [(z_index == 1) | (z_index == 2), upper, z_index % 2, z_index // 2 == upper]
    ).astype(jnp.int32)

    def along_z(value, target):
        def to(d, m):
            z = target(m // 2)
            return None if z is None else (d, 2 * z + m % 2)

        return permute_devices(value, dp, mp, to)

    def near(value):
        return along_z(value, lambda z: z ^ 1)

    def middle(value):
        return along_z(value, lambda z: 3 - z if z in (1, 2) else z)

    def outward(value):
        return along_z(value, lambda z: {1: 0, 2: 3}.get(z))

    def inward(value):
        return along_z(value, lambda z: {0: 1, 3: 2}.get(z))

    def swap_cores(value):
        return permute_devices(value, dp, mp, lambda d, m: (d, m ^ 1))

    def swap_twins(value):
        return permute_devices(value, dp, mp, lambda d, m: ((d + half_dp) % dp, m))

    def swap_both(value):
        return permute_devices(value, dp, mp, lambda d, m: ((d + half_dp) % dp, m ^ 1))

    own_image = (m_index * rows) // NEW
    ada_own = lax.dynamic_index_in_dim(ada_ffn, own_image, 0, keepdims=False)
    gate_own = lax.dynamic_index_in_dim(ffn_gate, own_image, 0, keepdims=True)
    head_own = lax.dynamic_index_in_dim(ada_head, own_image, 0, keepdims=False)

    ups, downs = (up_weight, swap_cores(up_weight)), (down_weight, swap_cores(down_weight))
    small = jnp.concatenate([up_bias, head_bias, codebook.astype(jnp.float32).reshape(-1)])
    small_other = swap_cores(small)
    head_twin = swap_twins(head_own)
    hid, voc = up_bias.shape[0], head_bias.shape[0]
    bias_up = jnp.concatenate([up_bias, small_other[:hid]])[None]
    bias_head = jnp.concatenate([head_bias, small_other[hid : hid + voc]])[None]
    codes = jnp.concatenate(
        [codebook.astype(jnp.float32), small_other[hid + voc :].reshape(codebook.shape)], axis=0
    )

    half = rows // CHUNKS // 2
    noise = gumbel_noise.reshape(2, 2, CHUNKS, 2, half, voc)

    def noise_for(to_core, to_upper):
        picked = lax.dynamic_slice(
            noise, (0, to_core, 0, to_upper, 0, 0), (2, 1, CHUNKS, 1, half, voc)
        )
        return picked.reshape(2, CHUNKS, half, voc)

    step = rows // CHUNKS
    rows_a, rows_b = tokens[:step], tokens[step:]
    own_a = norm_part(rows_a, ada_own)
    near_a, mid_a = near(own_a), middle(own_a)
    own_b = norm_part(rows_b, ada_own)
    far_mid_a, far_end_a = middle(near_a), outward(mid_a)
    near_b = near(after(own_b, near_a))
    noises = (
        noise_for(core, upper),
        swap_cores(after(noise_for(1 - core, upper), mid_a)),
        swap_twins(after(noise_for(core, 1 - upper), mid_a)),
        swap_both(after(noise_for(1 - core, 1 - upper), mid_a)),
    )
    sum_own_a, sum_near_a = ffn(where, [[own_a], [near_a]], ups, downs, bias_up)
    head_other = swap_cores(after(head_weight, ups[1], downs[1]))
    far_a = (after(far_mid_a, sum_near_a), far_end_a)
    last_end_a = outward(far_a[0])
    mid_b = middle(after(own_b, far_a[0]))
    (sum_far_a,) = ffn(where, [far_a], ups, downs, bias_up)
    came_far_a = inward(sum_far_a)
    near_b, mid_b = after(near_b, sum_far_a), after(mid_b, sum_far_a)
    far_mid_b, far_end_b = middle(near_b), outward(mid_b)
    (sum_last_a,) = ffn(where, [(mid_a, after(last_end_a, sum_far_a))], ups, downs, bias_up)
    came_last_a = inward(sum_last_a)
    sum_own_b, sum_near_b = ffn(where, [[after(own_b, sum_last_a, came_far_a, *noises)], [near_b]], ups, downs, bias_up)
    far_b = (after(far_mid_b, sum_near_b), far_end_b)
    last_end_b = outward(far_b[0])
    both_last_a = add_mid(where, after(sum_last_a, far_b[0]), came_far_a)
    went_last_a = middle(both_last_a)
    (sum_far_b,) = ffn(where, [(after(far_b[0], both_last_a), far_b[1])], ups, downs, bias_up)
    came_far_b = inward(sum_far_b)
    both_far_a = add_mid(where, after(sum_far_a, sum_far_b), came_last_a)
    went_far_a = middle(both_far_a)
    (sum_last_b,) = ffn(where, [(after(mid_b, went_last_a, both_far_a), after(last_end_b, sum_far_b))], ups, downs, bias_up)
    came_last_b = inward(sum_last_b)
    came_near_a = near(add_mid(where, sum_near_a, went_far_a))
    went_last_b = middle(add_mid(where, sum_last_b, came_far_b))
    went_far_b = middle(add_mid(where, sum_far_b, came_last_b))

    def finish(own, came_near, went_last, part):
        return block_rows(where, own, came_near, went_last, part, gate_own, down_bias[None])

    def gather(own):
        from_near, from_mid = near(own), middle(own)
        far_mid, far_end = middle(from_near), outward(from_mid)
        return own, from_near, far_mid, far_end, from_mid, outward(far_mid)

    out_a, kept_a, sent_a = finish(sum_own_a, came_near_a, went_last_a, rows_a)
    came_a = swap_twins(sent_a)
    mixed_a = mix_twins(where, kept_a, came_a, head_own, head_twin)
    came_near_b = near(add_mid(where, sum_near_b, went_far_b))
    slots_a = gather(mixed_a)
    out_b, kept_b, sent_b = finish(sum_own_b, came_near_b, went_last_b, rows_b)
    came_b = swap_twins(sent_b)
    mixed_b = mix_twins(where, kept_b, came_b, head_own, head_twin)
    slots_b = gather(mixed_b)
    heads = (head_weight, head_other)
    stats = [
        head_stats(0, where, slots_a, heads, bias_head, codes, noises),
        head_stats(1, where, slots_b, heads, bias_head, codes, noises),
    ]
    block_out = jnp.concatenate([out_a, out_b], axis=0)

    slots = [
        jnp.concatenate([part[:, r * half : (r + 1) * half] for part in stats], axis=1) for r in range(4)
    ]
    parts = [slots[0]] + [along_z(slots[r], lambda z, r=r: z ^ r) for r in (1, 2, 3)]
    soft = soft_codes(parts, channels)

    def to_cells(d, m, core_of):
        y, x = d // half_dp, d % half_dp
        z, c = m // 2, m % 2
        return ((z // 2) * half_dp + x, 2 * (2 * (z % 2) + c) + core_of(y))

    def to_halo(d, m):
        y, x = d // half_dp, d % half_dp
        z, c = m // 2, m % 2
        block = 2 * (z % 2) + c + (1 if y == 1 else -1)
        if block < 0 or block > 3:
            return None
        return ((z // 2) * half_dp + x, 2 * block + (0 if y == 1 else 1))

    first = permute_devices(soft, dp, mp, lambda d, m: to_cells(d, m, lambda y: y))
    second = permute_devices(soft, dp, mp, lambda d, m: to_cells(d, m, lambda y: 1 - y))
    halo = permute_devices(soft, dp, mp, to_halo)
    lower, higher = jnp.where(core == 0, first, second), jnp.where(core == 0, second, first)
    window = jnp.where(
        core == 0,
        jnp.concatenate([halo[:, -SIDE:], lower[:, :half], higher[:, :half], lower[:, half : half + SIDE]], axis=1),
        jnp.concatenate([higher[:, half - SIDE : half], lower[:, half:], higher[:, half:], halo[:, :SIDE]], axis=1),
    )
    cells = f_hat.shape[2]
    band = cells // SIDE
    code_map = window.reshape(channels, band + 2, SIDE)
    wide = jnp.pad(code_map, ((0, 0), (0, 0), (1, 1)))
    taps = jnp.stack(
        [wide[:, i : i + band, j : j + SIDE] for i in range(3) for j in range(3)], axis=1
    ).reshape(channels * 9, cells)
    conv = jnp.dot(
        phi_weight.reshape(channels, channels * 9),
        taps,
        precision=lax.Precision.HIGHEST,
        preferred_element_type=jnp.float32,
    ) + phi_bias[:, None]
    f_hat_out = f_hat + (0.5 * window[:, SIDE : SIDE + cells] + 0.5 * conv)[None]
    return (block_out, f_hat_out)


def solution(mesh):
    in_specs = (
        P(("dp", "mp"), None),
        P("dp", None, None),
        P("dp", None),
        P(None, "mp"),
        P("mp"),
        P("mp", None),
        P(),
        P("dp", None, None),
        P(None, "mp"),
        P("mp"),
        P("dp", None, "mp"),
        P("mp", None),
        P(),
        P(),
        P("dp", None, "mp"),
    )
    out_specs = (P(("dp", "mp"), None), P("dp", None, "mp"))
    line = mesh.shape["dp"] == 4 and mesh.shape["mp"] == 8
    body = line_body if line else general_body
    return jax.shard_map(body, mesh=mesh, in_specs=in_specs, out_specs=out_specs, check_vma=False)
```

```python
import functools

import jax
import jax.numpy as jnp
from jax import lax
from jax.experimental import pallas as pl
from jax.experimental.pallas import tpu as pltpu
from jax.sharding import PartitionSpec as P

SIDE = 32
NEW = 1024
GUIDE = 1.5
CHUNKS = 2
FLOWS = 4
HEAD_FLOWS = 2


def norm_rows(values):
    row_mean = jnp.mean(values, axis=-1, keepdims=True)
    centred = values - row_mean
    spread = jnp.mean(centred * centred, axis=-1, keepdims=True)
    return centred * lax.rsqrt(spread + 1e-06)


def modulate(values, ada):
    return norm_rows(values.astype(jnp.float32)) * (1.0 + ada[1]) + ada[0]


def permute_devices(value, dp, mp, target):
    pairs = []
    for d in range(dp):
        for m in range(mp):
            to = target(d, m)
            if to is not None:
                pairs.append((d * mp + m, to[0] * mp + to[1]))
    return lax.ppermute(value, ("dp", "mp"), pairs)


def general_body(
    tokens,
    ada_ffn,
    ffn_gate,
    up_weight,
    up_bias,
    down_weight,
    down_bias,
    ada_head,
    head_weight,
    head_bias,
    gumbel_noise,
    codebook,
    phi_weight,
    phi_bias,
    f_hat,
):
    rows, width = tokens.shape
    dp, mp = lax.axis_size("dp"), lax.axis_size("mp")
    d_index, m_index = lax.axis_index("dp"), lax.axis_index("mp")
    images = ada_ffn.shape[0]
    pairs = f_hat.shape[0]
    channels = f_hat.shape[1]
    vocab = head_weight.shape[1]
    own_image = (m_index * rows) // NEW
    ada_own = lax.dynamic_index_in_dim(ada_ffn, own_image, 0, keepdims=False)
    gate_own = lax.dynamic_index_in_dim(ffn_gate, own_image, 0, keepdims=False)
    head_own = lax.dynamic_index_in_dim(ada_head, own_image, 0, keepdims=False)
    half_dp, half_mp = dp // 2, mp // 2
    upper = d_index // half_dp

    def swap(d, m):
        return ((d + half_dp) % dp, m)

    def cross(d, m):
        if d // half_dp == m // half_mp:
            return None
        return ((d + half_dp) % dp, (m + half_mp) % mp)

    stays = upper == m_index // half_mp
    head_twin = permute_devices(head_own, dp, mp, swap)
    head_cond = jnp.where(upper == 0, head_own, head_twin)
    head_uncond = jnp.where(upper == 0, head_twin, head_own)

    step = rows // FLOWS
    normed = modulate(tokens, ada_own).astype(jnp.bfloat16)
    outs = []
    for c in range(FLOWS):
        part = lax.slice_in_dim(normed, c * step, (c + 1) * step, axis=0)
        gathered = lax.all_gather(part, "mp", axis=0, tiled=True)
        hidden = jax.nn.gelu(
            jnp.dot(gathered, up_weight, preferred_element_type=jnp.float32) + up_bias,
            approximate=True,
        ).astype(jnp.bfloat16)
        partial = jnp.dot(hidden, down_weight, preferred_element_type=jnp.float32).astype(jnp.bfloat16)
        summed = lax.psum_scatter(partial, "mp", scatter_dimension=0, tiled=True).astype(jnp.float32)
        own = lax.slice_in_dim(tokens, c * step, (c + 1) * step, axis=0).astype(jnp.float32)
        outs.append((own + gate_own * (summed + down_bias)).astype(jnp.bfloat16))
    block_out = jnp.concatenate(outs, axis=0)

    group = FLOWS // HEAD_FLOWS
    half = rows // HEAD_FLOWS // 2
    noise = gumbel_noise.reshape(pairs, NEW // rows, HEAD_FLOWS, 2, half, vocab)
    peaks, totals, codes = [], [], []
    for c in range(HEAD_FLOWS):
        part = jnp.concatenate(outs[c * group : (c + 1) * group], axis=0)
        first, second = part[:half], part[half:]
        kept = jnp.where(upper == 0, first, second)
        sent = jnp.where(upper == 0, second, first)
        came = permute_devices(sent, dp, mp, swap)
        cond = jnp.where(upper == 0, kept, came)
        uncond = jnp.where(upper == 0, came, kept)
        mixed = (
            (1.0 + GUIDE) * modulate(cond, head_cond) - GUIDE * modulate(uncond, head_uncond)
        ).astype(jnp.bfloat16)
        crossed = permute_devices(mixed, dp, mp, cross)
        mixed = jnp.where(stays, mixed, crossed)
        gathered = lax.all_gather(mixed, "mp", axis=0, tiled=True)
        logits = jnp.dot(gathered, head_weight, preferred_element_type=jnp.float32) + head_bias
        logits = logits.reshape(2, half_mp, half, vocab)
        order = jnp.transpose(logits, (1, 0, 2, 3)).reshape(pairs, NEW // rows, 2, half, vocab)
        scores = order + noise[:, :, c]
        peak = jnp.max(scores, axis=-1)
        weights = jnp.exp(scores - peak[..., None]).astype(jnp.bfloat16)
        totals.append(jnp.sum(weights.astype(jnp.float32), axis=-1))
        codes.append(jnp.dot(weights, codebook, preferred_element_type=jnp.float32))
        peaks.append(peak)
    stack = lambda parts: jnp.stack(parts, axis=2)
    peak = stack(peaks).reshape(pairs, 1, NEW)
    total = stack(totals).reshape(pairs, 1, NEW)
    code = stack(codes).reshape(pairs, NEW, channels).transpose(0, 2, 1)
    stats = jnp.concatenate([code, total, peak], axis=1)

    cells = f_hat.shape[2]
    band = cells // SIDE
    padded = jnp.pad(stats, ((0, 0), (0, 0), (SIDE, SIDE)))
    windows = jnp.stack(
        [padded[:, :, m * cells : m * cells + cells + 2 * SIDE] for m in range(mp)], axis=0
    )
    parts = lax.all_to_all(windows, "mp", 0, 0, tiled=True)
    top = jnp.max(parts[:, :, channels + 1], axis=0)
    factor = jnp.exp(parts[:, :, channels + 1] - top[None])[:, :, None]
    sums = jnp.sum(parts[:, :, : channels + 1] * factor, axis=0)
    cell_index = m_index * cells - SIDE + jnp.arange(cells + 2 * SIDE)
    inside = (cell_index >= 0) & (cell_index < NEW)
    soft = jnp.where(inside, sums[:, :channels] / jnp.where(inside, sums[:, channels:], 1.0), 0.0)
    code_map = soft.reshape(pairs, channels, band + 2, SIDE)
    wide = jnp.pad(code_map, ((0, 0), (0, 0), (0, 0), (1, 1)))
    taps = jnp.stack(
        [wide[:, :, i : i + band, j : j + SIDE] for i in range(3) for j in range(3)], axis=2
    ).reshape(pairs, channels * 9, cells)
    conv = jnp.einsum(
        "ok,pkn->pon",
        phi_weight.reshape(channels, channels * 9),
        taps,
        precision=lax.Precision.HIGHEST,
        preferred_element_type=jnp.float32,
    ) + phi_bias[None, :, None]
    f_hat_out = f_hat + 0.5 * soft[:, :, SIDE : SIDE + cells] + 0.5 * conv
    return (block_out, f_hat_out)


SCALARS = pl.BlockSpec(memory_space=pltpu.SMEM)
ON_CHIP = pl.BlockSpec(memory_space=pltpu.VMEM)
VMEM_LIMIT = 16 * 1024 * 1024


def call(kernel, args, outs, scalars=0, scratch=()):
    return pl.pallas_call(
        kernel,
        out_shape=outs,
        in_specs=[SCALARS] * scalars + [ON_CHIP] * (len(args) - scalars),
        out_specs=[ON_CHIP] * len(outs),
        scratch_shapes=scratch,
        compiler_params=pltpu.CompilerParams(vmem_limit_bytes=VMEM_LIMIT),
        cost_estimate=pl.CostEstimate(flops=0, bytes_accessed=0, transcendentals=0),
    )(*args)


def shape_of(shape, kind=jnp.bfloat16):
    return jax.ShapeDtypeStruct(shape, kind)


def after(value, *others):
    return lax.optimization_barrier((value, *others))[0]


def modulated(ref, ada_ref):
    return norm_rows(ref[...].astype(jnp.float32)) * (1.0 + ada_ref[1:2, :]) + ada_ref[0:1, :]


def norm_kernel(tokens_ref, ada_ref, out_ref):
    out_ref[...] = modulated(tokens_ref, ada_ref).astype(jnp.bfloat16)


def norm_part(tokens, ada):
    return call(norm_kernel, (tokens, ada), [shape_of(tokens.shape)])[0]


def ffn_kernel(slots, tile, where_ref, rows_ref, up_a, up_b, down_a, down_b, bias_ref, *refs):
    outs, (x_ref, hidden_ref) = refs[: len(slots)], refs[len(slots) :]
    panel, width = down_a.shape
    step = outs[0].shape[0]
    for g, slot in enumerate(slots):
        place = where_ref[4 + slot] * step
        x_ref[g * step : (g + 1) * step, :] = rows_ref[pl.ds(pl.multiple_of(place, step), step), :]
    for begin in range(0, 2 * panel, tile):
        end = begin + tile
        if end <= panel:
            weight = up_a[:, begin:end]
        elif begin >= panel:
            weight = up_b[:, begin - panel : end - panel]
        else:
            weight = jnp.concatenate([up_a[:, begin:], up_b[:, : end - panel]], axis=1)
        v = jnp.dot(x_ref[...], weight, preferred_element_type=jnp.float32) + bias_ref[:, begin:end]
        hidden_ref[:, begin:end] = jax.nn.gelu(v, approximate=True).astype(jnp.bfloat16)
    for begin in range(0, width, tile):
        cols = slice(begin, begin + tile)
        weight = jnp.concatenate([down_a[:, cols], down_b[:, cols]], axis=0)
        result = jnp.dot(hidden_ref[...], weight, preferred_element_type=jnp.float32)
        for g in range(len(slots)):
            outs[g][:, cols] = result[g * step : (g + 1) * step].astype(jnp.bfloat16)


def ffn(where, gathered, slots, ups, downs, bias):
    rows, width = gathered.shape
    panel = ups[0].shape[1]
    step = rows // 4
    return call(
        functools.partial(ffn_kernel, slots, 256),
        (where, gathered, *ups, *downs, bias),
        [shape_of((step, width))] * len(slots),
        scalars=1,
        scratch=[
            pltpu.VMEM((step * len(slots), width), jnp.bfloat16),
            pltpu.VMEM((step * len(slots), 2 * panel), jnp.bfloat16),
        ],
    )


def add_kernel(a_ref, b_ref, out_ref):
    out_ref[...] = (a_ref[...].astype(jnp.float32) + b_ref[...].astype(jnp.float32)).astype(jnp.bfloat16)


def add(a, b):
    return call(add_kernel, (a, b), [shape_of(a.shape)])[0]


def out_kernel(where_ref, own_ref, near_ref, far_ref, tokens_ref, gate_ref, bias_ref, out_ref, kept_ref, sent_ref):
    summed = own_ref[...].astype(jnp.float32) + near_ref[...].astype(jnp.float32) + far_ref[...].astype(jnp.float32)
    value = tokens_ref[...].astype(jnp.float32) + gate_ref[...] * (summed + bias_ref[...])
    value = value.astype(jnp.bfloat16)
    out_ref[...] = value
    half = value.shape[0] // 2
    lower = where_ref[1] == 0
    kept_ref[...] = jnp.where(lower, value[:half], value[half:])
    sent_ref[...] = jnp.where(lower, value[half:], value[:half])


def block_rows(where, own, near, far, tokens, gate, bias):
    rows, width = own.shape
    return call(
        out_kernel,
        (where, own, near, far, tokens, gate, bias),
        [shape_of((rows, width)), shape_of((rows // 2, width)), shape_of((rows // 2, width))],
        scalars=1,
    )


def mix_kernel(where_ref, kept_ref, came_ref, ada_ref, twin_ref, out_ref):
    kept, came = modulated(kept_ref, ada_ref), modulated(came_ref, twin_ref)
    lower = where_ref[1] == 0
    share = jnp.where(lower, 1.0 + GUIDE, -GUIDE)
    other = jnp.where(lower, -GUIDE, 1.0 + GUIDE)
    out_ref[...] = (share * kept + other * came).astype(jnp.bfloat16)


def mix_twins(where, kept, came, ada, twin):
    return call(mix_kernel, (where, kept, came, ada, twin), [shape_of(kept.shape)], scalars=1)[0]


def head_kernel(
    chunk, where_ref, own_ref, near_ref, far_ref, last_ref, weight_a, weight_b, bias_ref, code_ref,
    noise_own, noise_core, noise_twin, noise_both, stats_ref, x_ref
):
    step = own_ref.shape[0]
    panel = weight_a.shape[1]
    x_ref[0:step, :] = own_ref[...]
    x_ref[step : 2 * step, :] = near_ref[...]
    x_ref[2 * step : 3 * step, :] = far_ref[...]
    x_ref[3 * step : 4 * step, :] = last_ref[...]
    x = x_ref[...]
    odd = where_ref[2]
    even = 1 - odd
    same = where_ref[3] == 1
    scores = []
    for which, weight, ours, theirs in ((0, weight_a, noise_own, noise_twin), (1, weight_b, noise_core, noise_both)):
        picked = []
        for first in (True, False):
            for block in (odd, even):
                a, b = ours[block, chunk], theirs[block, chunk]
                picked.append(jnp.where(same, a, b) if first else jnp.where(same, b, a))
        logits = jnp.dot(x, weight[...], preferred_element_type=jnp.float32)
        scores.append(
            logits + bias_ref[:, which * panel : (which + 1) * panel] + jnp.concatenate(picked, axis=0)
        )
    peak = jnp.max(jnp.maximum(scores[0], scores[1]), axis=1, keepdims=True)
    sums = 0.0
    total = 0.0
    for which in range(2):
        weights = jnp.exp(scores[which] - peak).astype(jnp.bfloat16)
        total = total + jnp.sum(weights.astype(jnp.float32), axis=1, keepdims=True)
        codes = code_ref[which * panel : (which + 1) * panel, :].astype(jnp.bfloat16)
        sums = sums + jnp.dot(weights, codes, preferred_element_type=jnp.float32)
    channels = code_ref.shape[1]
    pad = jnp.zeros((4 * step, 128 - channels), jnp.float32)
    table = jnp.concatenate([sums, pad], axis=1)
    lane = lax.broadcasted_iota(jnp.int32, table.shape, 1)
    table = jnp.where(lane == channels, total, table)
    table = jnp.where(lane == channels + 1, peak, table)
    stats_ref[...] = jnp.transpose(table)[: stats_ref.shape[0], :]


def head_stats(chunk, where, slots, weights, bias, codes, noises):
    step, width = slots[0].shape
    panel = weights[0].shape[1]
    height = -(-(codes.shape[1] + 2) // 8) * 8
    return call(
        functools.partial(head_kernel, chunk),
        (where, *slots, *weights, bias, codes, *noises),
        [shape_of((height, 4 * step), jnp.float32)],
        scalars=1,
        scratch=[pltpu.VMEM((4 * step, width), jnp.bfloat16)],
    )[0]


def soft_kernel(channels, *refs):
    parts, out_ref = refs[:-1], refs[-1]
    tops = [part[channels + 1 : channels + 2, :] for part in parts]
    top = functools.reduce(jnp.maximum, tops)
    code = 0.0
    total = 0.0
    for part, peak in zip(parts, tops):
        factor = jnp.exp(peak - top)
        code = code + part[0:channels, :] * factor
        total = total + part[channels : channels + 1, :] * factor
    out_ref[...] = code / total


def soft_codes(parts, channels):
    return call(
        functools.partial(soft_kernel, channels),
        tuple(parts),
        [shape_of((channels, parts[0].shape[1]), jnp.float32)],
    )[0]


def line_body(
    tokens,
    ada_ffn,
    ffn_gate,
    up_weight,
    up_bias,
    down_weight,
    down_bias,
    ada_head,
    head_weight,
    head_bias,
    gumbel_noise,
    codebook,
    phi_weight,
    phi_bias,
    f_hat,
):
    rows, width = tokens.shape
    dp, mp = lax.axis_size("dp"), lax.axis_size("mp")
    d_index, m_index = lax.axis_index("dp"), lax.axis_index("mp")
    channels = f_hat.shape[1]
    half_dp = dp // 2
    upper = d_index // half_dp
    z_index, core = m_index // 2, m_index % 2
    where = jnp.stack(
        [z_index, upper, z_index % 2, z_index // 2 == upper] + [z_index ^ r for r in range(4)]
    ).astype(jnp.int32)

    def along_z(value, target):
        def to(d, m):
            z = target(m // 2)
            return None if z is None else (d, 2 * z + m % 2)

        return permute_devices(value, dp, mp, to)

    def near(value):
        return along_z(value, lambda z: z ^ 1)

    def across(value):
        return along_z(value, lambda z: z ^ 2)

    def swap_cores(value):
        return permute_devices(value, dp, mp, lambda d, m: (d, m ^ 1))

    def swap_twins(value):
        return permute_devices(value, dp, mp, lambda d, m: ((d + half_dp) % dp, m))

    def swap_both(value):
        return permute_devices(value, dp, mp, lambda d, m: ((d + half_dp) % dp, m ^ 1))

    own_image = (m_index * rows) // NEW
    ada_own = lax.dynamic_index_in_dim(ada_ffn, own_image, 0, keepdims=False)
    gate_own = lax.dynamic_index_in_dim(ffn_gate, own_image, 0, keepdims=True)
    head_own = lax.dynamic_index_in_dim(ada_head, own_image, 0, keepdims=False)

    ups, downs = (up_weight, swap_cores(up_weight)), (down_weight, swap_cores(down_weight))
    small = jnp.concatenate([up_bias, head_bias, codebook.astype(jnp.float32).reshape(-1)])
    small_other = swap_cores(small)
    head_other = swap_cores(head_weight)
    head_twin = swap_twins(head_own)
    hid, voc = up_bias.shape[0], head_bias.shape[0]
    bias_up = jnp.concatenate([up_bias, small_other[:hid]])[None]
    bias_head = jnp.concatenate([head_bias, small_other[hid : hid + voc]])[None]
    codes = jnp.concatenate(
        [codebook.astype(jnp.float32), small_other[hid + voc :].reshape(codebook.shape)], axis=0
    )

    half = rows // CHUNKS // 2
    noise = gumbel_noise.reshape(2, 2, CHUNKS, 2, half, voc)

    def noise_for(to_core, to_upper):
        picked = lax.dynamic_slice(
            noise, (0, to_core, 0, to_upper, 0, 0), (2, 1, CHUNKS, 1, half, voc)
        )
        return picked.reshape(2, CHUNKS, half, voc)

    noises = (
        noise_for(core, upper),
        swap_cores(noise_for(1 - core, upper)),
        swap_twins(noise_for(core, 1 - upper)),
        swap_both(noise_for(1 - core, 1 - upper)),
    )
    phi = phi_weight.reshape(channels, channels * 9)

    step = rows // CHUNKS
    rows_a, rows_b = tokens[:step], tokens[step:]
    lanes = [[2 * z + c for z in range(mp // 2)] for c in range(2)]

    def gather_line(value):
        return lax.all_gather(value, "mp", axis=0, tiled=True, axis_index_groups=lanes)

    all_a = gather_line(norm_part(rows_a, ada_own))
    all_b = gather_line(norm_part(rows_b, ada_own))
    (
        all_a, ups, downs, noises, head_other, head_twin, bias_up, bias_head, codes, phi
    ) = lax.optimization_barrier(
        (all_a, ups, downs, noises, head_other, head_twin, bias_up, bias_head, codes, phi)
    )

    def spread(own):
        from_near, from_far = near(own), across(own)
        return own, from_near, from_far, near(from_far)

    def finish(own, came_near, came_far, part):
        out, kept, sent = block_rows(where, own, came_near, came_far, part, gate_own, down_bias[None])
        return out, mix_twins(where, kept, swap_twins(sent), head_own, head_twin)

    last_a, far_a, near_a, own_a = ffn(where, all_a, (3, 2, 1, 0), ups, downs, bias_up)
    came_last_a, came_near_a = near(last_a), near(near_a)
    came_far_a = across(add(far_a, came_last_a))
    last_b, far_b = ffn(where, after(all_b, own_a), (3, 2), ups, downs, bias_up)
    came_last_b = near(last_b)
    near_b, own_b = ffn(where, after(all_b, far_b), (1, 0), ups, downs, bias_up)
    came_far_b = across(add(far_b, came_last_b))
    came_near_b = near(near_b)
    out_a, mixed_a = finish(own_a, came_near_a, after(came_far_a, own_b), rows_a)
    slots_a = spread(mixed_a)
    out_b, mixed_b = finish(own_b, came_near_b, came_far_b, rows_b)
    slots_b = spread(mixed_b)
    heads = (head_weight, head_other)
    stats = [
        head_stats(0, where, slots_a, heads, bias_head, codes, noises),
        head_stats(1, where, slots_b, heads, bias_head, codes, noises),
    ]
    block_out = jnp.concatenate([out_a, out_b], axis=0)

    slots = [
        jnp.concatenate([part[:, r * half : (r + 1) * half] for part in stats], axis=1) for r in range(4)
    ]
    parts = [slots[0]] + [along_z(slots[r], lambda z, r=r: z ^ r) for r in (1, 2, 3)]
    soft = soft_codes(parts, channels)

    def to_cells(d, m, core_of):
        y, x = d // half_dp, d % half_dp
        z, c = m // 2, m % 2
        return ((z // 2) * half_dp + x, 2 * (2 * (z % 2) + c) + core_of(y))

    def to_halo(d, m):
        y, x = d // half_dp, d % half_dp
        z, c = m // 2, m % 2
        block = 2 * (z % 2) + c + (1 if y == 1 else -1)
        if block < 0 or block > 3:
            return None
        return ((z // 2) * half_dp + x, 2 * block + (0 if y == 1 else 1))

    first = permute_devices(soft, dp, mp, lambda d, m: to_cells(d, m, lambda y: y))
    second = permute_devices(soft, dp, mp, lambda d, m: to_cells(d, m, lambda y: 1 - y))
    halo = permute_devices(soft, dp, mp, to_halo)
    lower, higher = jnp.where(core == 0, first, second), jnp.where(core == 0, second, first)
    window = jnp.where(
        core == 0,
        jnp.concatenate([halo[:, -SIDE:], lower[:, :half], higher[:, :half], lower[:, half : half + SIDE]], axis=1),
        jnp.concatenate([higher[:, half - SIDE : half], lower[:, half:], higher[:, half:], halo[:, :SIDE]], axis=1),
    )
    cells = f_hat.shape[2]
    band = cells // SIDE
    code_map = window.reshape(channels, band + 2, SIDE)
    wide = jnp.pad(code_map, ((0, 0), (0, 0), (1, 1)))
    taps = jnp.stack(
        [wide[:, i : i + band, j : j + SIDE] for i in range(3) for j in range(3)], axis=1
    ).reshape(channels * 9, cells)
    conv = jnp.dot(
        phi,
        taps,
        precision=lax.Precision.HIGHEST,
        preferred_element_type=jnp.float32,
    ) + phi_bias[:, None]
    f_hat_out = f_hat + (0.5 * window[:, SIDE : SIDE + cells] + 0.5 * conv)[None]
    return (block_out, f_hat_out)


def solution(mesh):
    in_specs = (
        P(("dp", "mp"), None),
        P("dp", None, None),
        P("dp", None),
        P(None, "mp"),
        P("mp"),
        P("mp", None),
        P(),
        P("dp", None, None),
        P(None, "mp"),
        P("mp"),
        P("dp", None, "mp"),
        P("mp", None),
        P(),
        P(),
        P("dp", None, "mp"),
    )
    out_specs = (P(("dp", "mp"), None), P("dp", None, "mp"))
    line = mesh.shape["dp"] == 4 and mesh.shape["mp"] == 8
    body = line_body if line else general_body
    return jax.shard_map(body, mesh=mesh, in_specs=in_specs, out_specs=out_specs, check_vma=False)
```

```python
import functools

import jax
import jax.numpy as jnp
from jax import lax
from jax.experimental import pallas as pl
from jax.experimental.pallas import tpu as pltpu
from jax.sharding import PartitionSpec as P

SIDE = 32
NEW = 1024
GUIDE = 1.5
CHUNKS = 2
FLOWS = 4
HEAD_FLOWS = 2


def norm_rows(values):
    row_mean = jnp.mean(values, axis=-1, keepdims=True)
    centred = values - row_mean
    spread = jnp.mean(centred * centred, axis=-1, keepdims=True)
    return centred * lax.rsqrt(spread + 1e-06)


def modulate(values, ada):
    return norm_rows(values.astype(jnp.float32)) * (1.0 + ada[1]) + ada[0]


def permute_devices(value, dp, mp, target):
    pairs = []
    for d in range(dp):
        for m in range(mp):
            to = target(d, m)
            if to is not None:
                pairs.append((d * mp + m, to[0] * mp + to[1]))
    return lax.ppermute(value, ("dp", "mp"), pairs)


def general_body(
    tokens,
    ada_ffn,
    ffn_gate,
    up_weight,
    up_bias,
    down_weight,
    down_bias,
    ada_head,
    head_weight,
    head_bias,
    gumbel_noise,
    codebook,
    phi_weight,
    phi_bias,
    f_hat,
):
    rows, width = tokens.shape
    dp, mp = lax.axis_size("dp"), lax.axis_size("mp")
    d_index, m_index = lax.axis_index("dp"), lax.axis_index("mp")
    images = ada_ffn.shape[0]
    pairs = f_hat.shape[0]
    channels = f_hat.shape[1]
    vocab = head_weight.shape[1]
    own_image = (m_index * rows) // NEW
    ada_own = lax.dynamic_index_in_dim(ada_ffn, own_image, 0, keepdims=False)
    gate_own = lax.dynamic_index_in_dim(ffn_gate, own_image, 0, keepdims=False)
    head_own = lax.dynamic_index_in_dim(ada_head, own_image, 0, keepdims=False)
    half_dp, half_mp = dp // 2, mp // 2
    upper = d_index // half_dp

    def swap(d, m):
        return ((d + half_dp) % dp, m)

    def cross(d, m):
        if d // half_dp == m // half_mp:
            return None
        return ((d + half_dp) % dp, (m + half_mp) % mp)

    stays = upper == m_index // half_mp
    head_twin = permute_devices(head_own, dp, mp, swap)
    head_cond = jnp.where(upper == 0, head_own, head_twin)
    head_uncond = jnp.where(upper == 0, head_twin, head_own)

    step = rows // FLOWS
    normed = modulate(tokens, ada_own).astype(jnp.bfloat16)
    outs = []
    for c in range(FLOWS):
        part = lax.slice_in_dim(normed, c * step, (c + 1) * step, axis=0)
        gathered = lax.all_gather(part, "mp", axis=0, tiled=True)
        hidden = jax.nn.gelu(
            jnp.dot(gathered, up_weight, preferred_element_type=jnp.float32) + up_bias,
            approximate=True,
        ).astype(jnp.bfloat16)
        partial = jnp.dot(hidden, down_weight, preferred_element_type=jnp.float32).astype(jnp.bfloat16)
        summed = lax.psum_scatter(partial, "mp", scatter_dimension=0, tiled=True).astype(jnp.float32)
        own = lax.slice_in_dim(tokens, c * step, (c + 1) * step, axis=0).astype(jnp.float32)
        outs.append((own + gate_own * (summed + down_bias)).astype(jnp.bfloat16))
    block_out = jnp.concatenate(outs, axis=0)

    group = FLOWS // HEAD_FLOWS
    half = rows // HEAD_FLOWS // 2
    noise = gumbel_noise.reshape(pairs, NEW // rows, HEAD_FLOWS, 2, half, vocab)
    peaks, totals, codes = [], [], []
    for c in range(HEAD_FLOWS):
        part = jnp.concatenate(outs[c * group : (c + 1) * group], axis=0)
        first, second = part[:half], part[half:]
        kept = jnp.where(upper == 0, first, second)
        sent = jnp.where(upper == 0, second, first)
        came = permute_devices(sent, dp, mp, swap)
        cond = jnp.where(upper == 0, kept, came)
        uncond = jnp.where(upper == 0, came, kept)
        mixed = (
            (1.0 + GUIDE) * modulate(cond, head_cond) - GUIDE * modulate(uncond, head_uncond)
        ).astype(jnp.bfloat16)
        crossed = permute_devices(mixed, dp, mp, cross)
        mixed = jnp.where(stays, mixed, crossed)
        gathered = lax.all_gather(mixed, "mp", axis=0, tiled=True)
        logits = jnp.dot(gathered, head_weight, preferred_element_type=jnp.float32) + head_bias
        logits = logits.reshape(2, half_mp, half, vocab)
        order = jnp.transpose(logits, (1, 0, 2, 3)).reshape(pairs, NEW // rows, 2, half, vocab)
        scores = order + noise[:, :, c]
        peak = jnp.max(scores, axis=-1)
        weights = jnp.exp(scores - peak[..., None]).astype(jnp.bfloat16)
        totals.append(jnp.sum(weights.astype(jnp.float32), axis=-1))
        codes.append(jnp.dot(weights, codebook, preferred_element_type=jnp.float32))
        peaks.append(peak)
    stack = lambda parts: jnp.stack(parts, axis=2)
    peak = stack(peaks).reshape(pairs, 1, NEW)
    total = stack(totals).reshape(pairs, 1, NEW)
    code = stack(codes).reshape(pairs, NEW, channels).transpose(0, 2, 1)
    stats = jnp.concatenate([code, total, peak], axis=1)

    cells = f_hat.shape[2]
    band = cells // SIDE
    padded = jnp.pad(stats, ((0, 0), (0, 0), (SIDE, SIDE)))
    windows = jnp.stack(
        [padded[:, :, m * cells : m * cells + cells + 2 * SIDE] for m in range(mp)], axis=0
    )
    parts = lax.all_to_all(windows, "mp", 0, 0, tiled=True)
    top = jnp.max(parts[:, :, channels + 1], axis=0)
    factor = jnp.exp(parts[:, :, channels + 1] - top[None])[:, :, None]
    sums = jnp.sum(parts[:, :, : channels + 1] * factor, axis=0)
    cell_index = m_index * cells - SIDE + jnp.arange(cells + 2 * SIDE)
    inside = (cell_index >= 0) & (cell_index < NEW)
    soft = jnp.where(inside, sums[:, :channels] / jnp.where(inside, sums[:, channels:], 1.0), 0.0)
    code_map = soft.reshape(pairs, channels, band + 2, SIDE)
    wide = jnp.pad(code_map, ((0, 0), (0, 0), (0, 0), (1, 1)))
    taps = jnp.stack(
        [wide[:, :, i : i + band, j : j + SIDE] for i in range(3) for j in range(3)], axis=2
    ).reshape(pairs, channels * 9, cells)
    conv = jnp.einsum(
        "ok,pkn->pon",
        phi_weight.reshape(channels, channels * 9),
        taps,
        precision=lax.Precision.HIGHEST,
        preferred_element_type=jnp.float32,
    ) + phi_bias[None, :, None]
    f_hat_out = f_hat + 0.5 * soft[:, :, SIDE : SIDE + cells] + 0.5 * conv
    return (block_out, f_hat_out)


SCALARS = pl.BlockSpec(memory_space=pltpu.SMEM)
ON_CHIP = pl.BlockSpec(memory_space=pltpu.VMEM)
VMEM_LIMIT = 16 * 1024 * 1024
MID, UPPER, IMAGE, ODD, SAME, CORE = range(6)


def call(kernel, where, args, outs, scratch=()):
    return pl.pallas_call(
        kernel,
        out_shape=outs,
        in_specs=[SCALARS] + [ON_CHIP] * len(args),
        out_specs=[ON_CHIP] * len(outs),
        scratch_shapes=scratch,
        compiler_params=pltpu.CompilerParams(vmem_limit_bytes=VMEM_LIMIT),
        cost_estimate=pl.CostEstimate(flops=0, bytes_accessed=0, transcendentals=0),
    )(where, *args)


def shape_of(shape, kind=jnp.bfloat16):
    return jax.ShapeDtypeStruct(shape, kind)


def after(value, *others):
    return lax.optimization_barrier((value, *others))[0]


def modulated(values, ada_ref, image):
    shift, scale = ada_ref[image, 0:1, :], ada_ref[image, 1:2, :]
    return norm_rows(values.astype(jnp.float32)) * (1.0 + scale) + shift


def norm_kernel(begin, where_ref, tokens_ref, ada_ref, out_ref):
    values = tokens_ref[begin : begin + out_ref.shape[0], :]
    out_ref[...] = modulated(values, ada_ref, where_ref[IMAGE]).astype(jnp.bfloat16)


def norm_part(where, tokens, ada, begin, size):
    outs = [shape_of((size, tokens.shape[1]))]
    return call(functools.partial(norm_kernel, begin), where, (tokens, ada), outs)[0]


def ffn_kernel(groups, tile, where_ref, *refs):
    count = sum(groups)
    parts = refs[:count]
    up_a, up_b, down_a, down_b, bias_a, bias_b = refs[count : count + 6]
    outs = refs[count + 6 : count + 6 + len(groups)]
    x_ref, hidden_ref = refs[count + 6 + len(groups) :]
    panel, width = down_a.shape
    step = outs[0].shape[0]
    place = 0
    for g, size in enumerate(groups):
        if size == 1:
            value = parts[place][...]
        else:
            value = jnp.where(where_ref[MID] == 1, parts[place][...], parts[place + 1][...])
        x_ref[g * step : (g + 1) * step, :] = value
        place += size

    def columns(first, second, begin, end):
        if end <= panel:
            return first[:, begin:end]
        if begin >= panel:
            return second[:, begin - panel : end - panel]
        return jnp.concatenate([first[:, begin:panel], second[:, : end - panel]], axis=1)

    for begin in range(0, 2 * panel, tile):
        end = begin + tile
        v = jnp.dot(x_ref[...], columns(up_a, up_b, begin, end), preferred_element_type=jnp.float32)
        v = v + columns(bias_a, bias_b, begin, end)
        hidden_ref[:, begin:end] = jax.nn.gelu(v, approximate=True).astype(jnp.bfloat16)
    for begin in range(0, width, tile):
        cols = slice(begin, begin + tile)
        weight = jnp.concatenate([down_a[:, cols], down_b[:, cols]], axis=0)
        result = jnp.dot(hidden_ref[...], weight, preferred_element_type=jnp.float32)
        for g in range(len(groups)):
            outs[g][:, cols] = result[g * step : (g + 1) * step].astype(jnp.bfloat16)


def ffn(where, slots, panels):
    groups = tuple(len(slot) for slot in slots)
    parts = [part for slot in slots for part in slot]
    rows, width = parts[0].shape
    total = rows * len(slots)
    return call(
        functools.partial(ffn_kernel, groups, 256),
        where,
        (*parts, *panels),
        [shape_of((rows, width))] * len(slots),
        scratch=[
            pltpu.VMEM((total, width), jnp.bfloat16),
            pltpu.VMEM((total, 2 * panels[2].shape[0]), jnp.bfloat16),
        ],
    )


def add_kernel(always, where_ref, a_ref, b_ref, out_ref):
    b = b_ref[...].astype(jnp.float32)
    if not always:
        b = jnp.where(where_ref[MID] == 1, b, 0.0)
    out_ref[...] = (a_ref[...].astype(jnp.float32) + b).astype(jnp.bfloat16)


def add(where, a, b, always=False):
    return call(functools.partial(add_kernel, always), where, (a, b), [shape_of(a.shape)])[0]


def out_kernel(begin, always, where_ref, own_ref, near_ref, far_ref, tokens_ref, gate_ref, bias_ref, *refs):
    out_ref, kept_ref, sent_ref = refs[-3:]
    far = far_ref[...].astype(jnp.float32)
    if not always:
        far = jnp.where(where_ref[MID] == 1, far, 0.0)
    summed = own_ref[...].astype(jnp.float32) + near_ref[...].astype(jnp.float32) + far
    rows = summed.shape[0]
    tokens = tokens_ref[begin : begin + rows, :].astype(jnp.float32)
    gate = gate_ref[pl.ds(where_ref[IMAGE], 1), :]
    value = (tokens + gate * (summed + bias_ref[...])).astype(jnp.bfloat16)
    if len(refs) > 3:
        out_ref[0:begin, :] = refs[0][...]
        out_ref[begin : begin + rows, :] = value
    else:
        out_ref[...] = value
    half = rows // 2
    lower = where_ref[UPPER] == 0
    kept_ref[...] = jnp.where(lower, value[:half], value[half:])
    sent_ref[...] = jnp.where(lower, value[half:], value[:half])


def block_rows(where, begin, always, own, near, far, tokens, gate, bias, earlier=()):
    rows, width = own.shape
    full = rows + begin if earlier else rows
    return call(
        functools.partial(out_kernel, begin, always),
        where,
        (own, near, far, tokens, gate, bias, *earlier),
        [shape_of((full, width)), shape_of((rows // 2, width)), shape_of((rows // 2, width))],
    )


def mix_kernel(where_ref, kept_ref, came_ref, ada_ref, twin_ref, out_ref):
    image = where_ref[IMAGE]
    kept, came = modulated(kept_ref[...], ada_ref, image), modulated(came_ref[...], twin_ref, image)
    lower = where_ref[UPPER] == 0
    share = jnp.where(lower, 1.0 + GUIDE, -GUIDE)
    other = jnp.where(lower, -GUIDE, 1.0 + GUIDE)
    out_ref[...] = (share * kept + other * came).astype(jnp.bfloat16)


def mix_twins(where, kept, came, ada, twin):
    return call(mix_kernel, where, (kept, came, ada, twin), [shape_of(kept.shape)])[0]


def head_kernel(
    begin, where_ref, own_ref, near_ref, far_ref, last_ref, weight_a, weight_b, bias_a, bias_b, code_a, code_b,
    noise_own, noise_core, noise_twin, noise_both, stats_ref, x_ref
):
    step = own_ref.shape[0]
    for r, ref in enumerate((own_ref, near_ref, far_ref, last_ref)):
        x_ref[r * step : (r + 1) * step, :] = ref[...]
    x = x_ref[...]
    odd = where_ref[ODD]
    even = 1 - odd
    same = where_ref[SAME] == 1
    scores = []
    for weight, bias, ours, theirs in (
        (weight_a, bias_a, noise_own, noise_twin),
        (weight_b, bias_b, noise_core, noise_both),
    ):
        picked = []
        for first in (True, False):
            for block in (odd, even):
                a, b = ours[block, begin : begin + step, :], theirs[block, begin : begin + step, :]
                picked.append(jnp.where(same, a, b) if first else jnp.where(same, b, a))
        logits = jnp.dot(x, weight[...], preferred_element_type=jnp.float32)
        scores.append(logits + bias[:, bias.shape[1] - weight.shape[1] :] + jnp.concatenate(picked, axis=0))
    peak = jnp.max(jnp.maximum(scores[0], scores[1]), axis=1, keepdims=True)
    sums = 0.0
    total = 0.0
    for score, code in zip(scores, (code_a, code_b)):
        weights = jnp.exp(score - peak).astype(jnp.bfloat16)
        total = total + jnp.sum(weights.astype(jnp.float32), axis=1, keepdims=True)
        sums = sums + lax.dot_general(
            weights, code[...], (((1,), (1,)), ((), ())), preferred_element_type=jnp.float32
        )
    channels = code_a.shape[0]
    pad = jnp.zeros((4 * step, 128 - channels), jnp.float32)
    table = jnp.concatenate([sums, pad], axis=1)
    lane = lax.broadcasted_iota(jnp.int32, table.shape, 1)
    table = jnp.where(lane == channels, total, table)
    table = jnp.where(lane == channels + 1, peak, table)
    stats_ref[...] = jnp.transpose(table)[: stats_ref.shape[0], :]


def head_stats(where, begin, slots, heads, noises):
    step, width = slots[0].shape
    height = -(-(heads[-1].shape[0] + 2) // 8) * 8
    return call(
        functools.partial(head_kernel, begin),
        where,
        (*slots, *heads, *noises),
        [shape_of((height, 4 * step), jnp.float32)],
        scratch=[pltpu.VMEM((4 * step, width), jnp.bfloat16)],
    )[0]


def soft_kernel(channels, where_ref, *refs):
    parts, out_ref = refs[:-1], refs[-1]
    tops = [part[channels + 1 : channels + 2, :] for part in parts]
    top = functools.reduce(jnp.maximum, tops)
    code = 0.0
    total = 0.0
    for part, peak in zip(parts, tops):
        factor = jnp.exp(peak - top)
        code = code + part[0:channels, :] * factor
        total = total + part[channels : channels + 1, :] * factor
    out_ref[...] = code / total


def soft_codes(where, parts, channels):
    outs = [shape_of((channels, parts[0].shape[1]), jnp.float32)]
    return call(functools.partial(soft_kernel, channels), where, tuple(parts), outs)[0]


def refine_kernel(where_ref, first_ref, second_ref, halo_ref, phi_ref, bias_ref, map_ref, out_ref):
    first, second, halo = first_ref[...], second_ref[...], halo_ref[...]
    cells = first.shape[1]
    half = cells // 2
    lane = lax.broadcasted_iota(jnp.int32, first.shape, 1)
    shift = lambda value, by: pltpu.roll(value, by % cells, 1)
    early = where_ref[CORE] == 0
    lower, higher = jnp.where(early, first, second), jnp.where(early, second, first)
    centre = jnp.where(
        early,
        jnp.where(lane < half, lower, shift(higher, half)),
        jnp.where(lane < half, shift(lower, half), higher),
    )
    above = jnp.where(early, shift(halo, SIDE), shift(higher, SIDE - half))
    below = jnp.where(early, shift(lower, half - SIDE), shift(halo, -SIDE))
    rows = (
        jnp.where(lane < SIDE, above, shift(centre, SIDE)),
        centre,
        jnp.where(lane >= cells - SIDE, below, shift(centre, -SIDE)),
    )
    column = lane % SIDE
    conv = jnp.zeros(out_ref.shape, jnp.float32) + bias_ref[...]
    for i, row in enumerate(rows):
        left = jnp.where(column == 0, 0.0, shift(row, 1))
        right = jnp.where(column == SIDE - 1, 0.0, shift(row, -1))
        for j, tap in enumerate((left, row, right)):
            conv = conv + jnp.dot(
                phi_ref[i, j], tap, precision=lax.Precision.HIGHEST, preferred_element_type=jnp.float32
            )
    out_ref[...] = map_ref[...] + 0.5 * centre + 0.5 * conv


def line_body(
    tokens,
    ada_ffn,
    ffn_gate,
    up_weight,
    up_bias,
    down_weight,
    down_bias,
    ada_head,
    head_weight,
    head_bias,
    gumbel_noise,
    codebook,
    phi_weight,
    phi_bias,
    f_hat,
):
    rows = tokens.shape[0]
    dp, mp = lax.axis_size("dp"), lax.axis_size("mp")
    d_index, m_index = lax.axis_index("dp"), lax.axis_index("mp")
    channels = f_hat.shape[1]
    half_dp = dp // 2
    upper = d_index // half_dp
    z_index, core = m_index // 2, m_index % 2
    where = jnp.stack(
        [
            (z_index == 1) | (z_index == 2),
            upper,
            (m_index * rows) // NEW,
            z_index % 2,
            z_index // 2 == upper,
            core,
        ]
    ).astype(jnp.int32)

    def along_z(value, target):
        def to(d, m):
            z = target(m // 2)
            return None if z is None else (d, 2 * z + m % 2)

        return permute_devices(value, dp, mp, to)

    def near(value):
        return along_z(value, lambda z: z ^ 1)

    def across(value):
        return along_z(value, lambda z: z ^ 2)

    def middle(value):
        return along_z(value, lambda z: 3 - z if z in (1, 2) else z)

    def outward(value):
        return along_z(value, lambda z: {1: 0, 2: 3}.get(z))

    def inward(value):
        return along_z(value, lambda z: {0: 1, 3: 2}.get(z))

    def swap_cores(value):
        return permute_devices(value, dp, mp, lambda d, m: (d, m ^ 1))

    def swap_twins(value):
        return permute_devices(value, dp, mp, lambda d, m: ((d + half_dp) % dp, m))

    def swap_both(value):
        return permute_devices(value, dp, mp, lambda d, m: ((d + half_dp) % dp, m ^ 1))

    step = rows // CHUNKS
    half = step // 2
    voc = head_bias.shape[0]
    noise = gumbel_noise.reshape(2, 2, CHUNKS, 2, half, voc)

    def noise_for(to_core, to_upper):
        picked = lax.dynamic_slice(
            noise, (0, to_core, 0, to_upper, 0, 0), (2, 1, CHUNKS, 1, half, voc)
        )
        return picked.reshape(2, CHUNKS * half, voc)

    gate, bias_out = ffn_gate, down_bias[None]
    up_other, down_other = swap_cores(up_weight), swap_cores(down_weight)
    biases = jnp.concatenate([up_bias, head_bias])[None]
    codes = codebook.T
    bias_other = swap_cores(biases)

    own_a = norm_part(where, tokens, ada_ffn, 0, step)
    near_a, far_a = near(own_a), across(own_a)
    own_b = norm_part(where, tokens, ada_ffn, step, step)
    up_other, down_other, bias_other, near_a, far_a = lax.optimization_barrier(
        (up_other, down_other, bias_other, near_a, far_a)
    )
    panels = (up_weight, up_other, down_weight, down_other, biases, bias_other)
    last_a = near(far_a)
    mid_b = middle(after(own_b, far_a))
    noise_twin = swap_twins(after(noise_for(core, 1 - upper), far_a))
    sum_own_a, sum_near_a = ffn(where, [[own_a], [near_a]], panels)
    noise_core = swap_cores(after(noise_for(1 - core, upper), noise_twin))
    (sum_far_a,) = ffn(where, [[after(far_a, sum_near_a, noise_twin)]], panels)
    came_far_a = inward(sum_far_a)
    near_b = near(after(own_b, last_a))
    (sum_last_a,) = ffn(where, [[after(last_a, sum_far_a)]], panels)
    came_last_a = inward(sum_last_a)
    mid_b, near_b = lax.optimization_barrier((mid_b, near_b, sum_last_a))[:2]
    far_mid_b, far_end_b = middle(near_b), outward(mid_b)
    noise_both = swap_both(after(noise_for(1 - core, 1 - upper), noise_core))
    sum_own_b, sum_near_b = ffn(where, [[own_b], [after(near_b, noise_core)]], panels)
    both_last_a = add(where, after(sum_last_a, sum_near_b), came_far_a)
    went_last_a = middle(both_last_a)
    far_mid_b, far_end_b = lax.optimization_barrier((far_mid_b, far_end_b, both_last_a))[:2]
    last_end_b = outward(far_mid_b)
    (sum_far_b,) = ffn(where, [[far_mid_b, far_end_b]], panels)
    both_far_a = add(where, after(sum_far_a, sum_far_b), came_last_a)
    went_far_a = middle(both_far_a)
    (sum_last_b,) = ffn(where, [[after(mid_b, both_far_a, noise_both, went_last_a), last_end_b]], panels)
    came_last_b = near(sum_last_b)
    head_other = swap_cores(after(head_weight, sum_last_b))
    head_twin = swap_twins(after(ada_head, sum_last_b))
    code_other = swap_cores(after(codes, sum_last_b))
    both_far_b = add(where, sum_far_b, came_last_b, True)
    went_far_b = across(both_far_b)
    came_near_b = near(after(sum_near_b, both_far_b))
    both_near_a = add(where, sum_near_a, after(went_far_a, went_last_a, both_far_b))
    came_near_a = near(both_near_a)
    out_a, kept_a, sent_a = block_rows(
        where, 0, False, sum_own_a, after(came_near_a, head_twin), went_last_a, tokens, gate, bias_out
    )
    came_a = swap_twins(sent_a)
    mixed_a = mix_twins(where, kept_a, came_a, ada_head, head_twin)
    mix_near_a, mix_far_a = near(mixed_a), across(mixed_a)
    block_out, kept_b, sent_b = block_rows(
        where, step, True, sum_own_b, after(came_near_b, mix_far_a, mix_near_a, head_other, code_other), went_far_b, tokens, gate, bias_out, (out_a,)
    )
    came_b = swap_twins(sent_b)
    mix_last_a = near(after(mix_far_a, sent_b))
    mixed_b = mix_twins(where, kept_b, came_b, ada_head, head_twin)
    mix_near_b, mix_far_b = near(mixed_b), across(mixed_b)
    heads = (head_weight, head_other, biases, bias_other, codes, code_other)
    noises = (noise_for(core, upper), noise_core, noise_twin, noise_both)
    stats_a = head_stats(
        where, 0, (after(mixed_a, mixed_b), mix_near_a, mix_far_a, mix_last_a), heads, noises
    )
    mix_last_b = near(mix_far_b)
    stats_b = head_stats(where, half, (after(mixed_b, stats_a), mix_near_b, mix_far_b, mix_last_b), heads, noises)

    slots = [
        jnp.concatenate([part[:, r * half : (r + 1) * half] for part in (stats_a, stats_b)], axis=1) for r in range(4)
    ]
    parts = [slots[0]] + [along_z(slots[r], lambda z, r=r: z ^ r) for r in (1, 2, 3)]
    soft = soft_codes(where, parts, channels)

    def to_cells(d, m, core_of):
        y, x = d // half_dp, d % half_dp
        z, c = m // 2, m % 2
        return ((z // 2) * half_dp + x, 2 * (2 * (z % 2) + c) + core_of(y))

    def to_halo(d, m):
        y, x = d // half_dp, d % half_dp
        z, c = m // 2, m % 2
        block = 2 * (z % 2) + c + (1 if y == 1 else -1)
        if block < 0 or block > 3:
            return None
        return ((z // 2) * half_dp + x, 2 * block + (0 if y == 1 else 1))

    first = permute_devices(soft, dp, mp, lambda d, m: to_cells(d, m, lambda y: y))
    second = permute_devices(soft, dp, mp, lambda d, m: to_cells(d, m, lambda y: 1 - y))
    halo = permute_devices(soft, dp, mp, to_halo)
    f_hat_out = call(
        refine_kernel,
        where,
        (first, second, halo, jnp.transpose(phi_weight, (2, 3, 0, 1)), phi_bias[:, None], f_hat[0]),
        [shape_of(f_hat.shape[1:], jnp.float32)],
    )[0]
    return (block_out, f_hat_out[None])


def solution(mesh):
    in_specs = (
        P(("dp", "mp"), None),
        P("dp", None, None),
        P("dp", None),
        P(None, "mp"),
        P("mp"),
        P("mp", None),
        P(),
        P("dp", None, None),
        P(None, "mp"),
        P("mp"),
        P("dp", None, "mp"),
        P("mp", None),
        P(),
        P(),
        P("dp", None, "mp"),
    )
    out_specs = (P(("dp", "mp"), None), P("dp", None, "mp"))
    line = mesh.shape["dp"] == 4 and mesh.shape["mp"] == 8
    body = line_body if line else general_body
    return jax.shard_map(body, mesh=mesh, in_specs=in_specs, out_specs=out_specs, check_vma=False)
```

```python
import functools

import jax
import jax.numpy as jnp
from jax import lax
from jax.experimental import pallas as pl
from jax.experimental.pallas import tpu as pltpu
from jax.sharding import PartitionSpec as P

SIDE = 32
NEW = 1024
GUIDE = 1.5
CHUNKS = 2
FLOWS = 4
HEAD_FLOWS = 2


def norm_rows(values):
    row_mean = jnp.mean(values, axis=-1, keepdims=True)
    centred = values - row_mean
    spread = jnp.mean(centred * centred, axis=-1, keepdims=True)
    return centred * lax.rsqrt(spread + 1e-06)


def modulate(values, ada):
    return norm_rows(values.astype(jnp.float32)) * (1.0 + ada[1]) + ada[0]


def permute_devices(value, dp, mp, target):
    pairs = []
    for d in range(dp):
        for m in range(mp):
            to = target(d, m)
            if to is not None:
                pairs.append((d * mp + m, to[0] * mp + to[1]))
    return lax.ppermute(value, ("dp", "mp"), pairs)


def general_body(
    tokens,
    ada_ffn,
    ffn_gate,
    up_weight,
    up_bias,
    down_weight,
    down_bias,
    ada_head,
    head_weight,
    head_bias,
    gumbel_noise,
    codebook,
    phi_weight,
    phi_bias,
    f_hat,
):
    rows, width = tokens.shape
    dp, mp = lax.axis_size("dp"), lax.axis_size("mp")
    d_index, m_index = lax.axis_index("dp"), lax.axis_index("mp")
    images = ada_ffn.shape[0]
    pairs = f_hat.shape[0]
    channels = f_hat.shape[1]
    vocab = head_weight.shape[1]
    own_image = (m_index * rows) // NEW
    ada_own = lax.dynamic_index_in_dim(ada_ffn, own_image, 0, keepdims=False)
    gate_own = lax.dynamic_index_in_dim(ffn_gate, own_image, 0, keepdims=False)
    head_own = lax.dynamic_index_in_dim(ada_head, own_image, 0, keepdims=False)
    half_dp, half_mp = dp // 2, mp // 2
    upper = d_index // half_dp

    def swap(d, m):
        return ((d + half_dp) % dp, m)

    def cross(d, m):
        if d // half_dp == m // half_mp:
            return None
        return ((d + half_dp) % dp, (m + half_mp) % mp)

    stays = upper == m_index // half_mp
    head_twin = permute_devices(head_own, dp, mp, swap)
    head_cond = jnp.where(upper == 0, head_own, head_twin)
    head_uncond = jnp.where(upper == 0, head_twin, head_own)

    step = rows // FLOWS
    normed = modulate(tokens, ada_own).astype(jnp.bfloat16)
    outs = []
    for c in range(FLOWS):
        part = lax.slice_in_dim(normed, c * step, (c + 1) * step, axis=0)
        gathered = lax.all_gather(part, "mp", axis=0, tiled=True)
        hidden = jax.nn.gelu(
            jnp.dot(gathered, up_weight, preferred_element_type=jnp.float32) + up_bias,
            approximate=True,
        ).astype(jnp.bfloat16)
        partial = jnp.dot(hidden, down_weight, preferred_element_type=jnp.float32).astype(jnp.bfloat16)
        summed = lax.psum_scatter(partial, "mp", scatter_dimension=0, tiled=True).astype(jnp.float32)
        own = lax.slice_in_dim(tokens, c * step, (c + 1) * step, axis=0).astype(jnp.float32)
        outs.append((own + gate_own * (summed + down_bias)).astype(jnp.bfloat16))
    block_out = jnp.concatenate(outs, axis=0)

    group = FLOWS // HEAD_FLOWS
    half = rows // HEAD_FLOWS // 2
    noise = gumbel_noise.reshape(pairs, NEW // rows, HEAD_FLOWS, 2, half, vocab)
    peaks, totals, codes = [], [], []
    for c in range(HEAD_FLOWS):
        part = jnp.concatenate(outs[c * group : (c + 1) * group], axis=0)
        first, second = part[:half], part[half:]
        kept = jnp.where(upper == 0, first, second)
        sent = jnp.where(upper == 0, second, first)
        came = permute_devices(sent, dp, mp, swap)
        cond = jnp.where(upper == 0, kept, came)
        uncond = jnp.where(upper == 0, came, kept)
        mixed = (
            (1.0 + GUIDE) * modulate(cond, head_cond) - GUIDE * modulate(uncond, head_uncond)
        ).astype(jnp.bfloat16)
        crossed = permute_devices(mixed, dp, mp, cross)
        mixed = jnp.where(stays, mixed, crossed)
        gathered = lax.all_gather(mixed, "mp", axis=0, tiled=True)
        logits = jnp.dot(gathered, head_weight, preferred_element_type=jnp.float32) + head_bias
        logits = logits.reshape(2, half_mp, half, vocab)
        order = jnp.transpose(logits, (1, 0, 2, 3)).reshape(pairs, NEW // rows, 2, half, vocab)
        scores = order + noise[:, :, c]
        peak = jnp.max(scores, axis=-1)
        weights = jnp.exp(scores - peak[..., None]).astype(jnp.bfloat16)
        totals.append(jnp.sum(weights.astype(jnp.float32), axis=-1))
        codes.append(jnp.dot(weights, codebook, preferred_element_type=jnp.float32))
        peaks.append(peak)
    stack = lambda parts: jnp.stack(parts, axis=2)
    peak = stack(peaks).reshape(pairs, 1, NEW)
    total = stack(totals).reshape(pairs, 1, NEW)
    code = stack(codes).reshape(pairs, NEW, channels).transpose(0, 2, 1)
    stats = jnp.concatenate([code, total, peak], axis=1)

    cells = f_hat.shape[2]
    band = cells // SIDE
    padded = jnp.pad(stats, ((0, 0), (0, 0), (SIDE, SIDE)))
    windows = jnp.stack(
        [padded[:, :, m * cells : m * cells + cells + 2 * SIDE] for m in range(mp)], axis=0
    )
    parts = lax.all_to_all(windows, "mp", 0, 0, tiled=True)
    top = jnp.max(parts[:, :, channels + 1], axis=0)
    factor = jnp.exp(parts[:, :, channels + 1] - top[None])[:, :, None]
    sums = jnp.sum(parts[:, :, : channels + 1] * factor, axis=0)
    cell_index = m_index * cells - SIDE + jnp.arange(cells + 2 * SIDE)
    inside = (cell_index >= 0) & (cell_index < NEW)
    soft = jnp.where(inside, sums[:, :channels] / jnp.where(inside, sums[:, channels:], 1.0), 0.0)
    code_map = soft.reshape(pairs, channels, band + 2, SIDE)
    wide = jnp.pad(code_map, ((0, 0), (0, 0), (0, 0), (1, 1)))
    taps = jnp.stack(
        [wide[:, :, i : i + band, j : j + SIDE] for i in range(3) for j in range(3)], axis=2
    ).reshape(pairs, channels * 9, cells)
    conv = jnp.einsum(
        "ok,pkn->pon",
        phi_weight.reshape(channels, channels * 9),
        taps,
        precision=lax.Precision.HIGHEST,
        preferred_element_type=jnp.float32,
    ) + phi_bias[None, :, None]
    f_hat_out = f_hat + 0.5 * soft[:, :, SIDE : SIDE + cells] + 0.5 * conv
    return (block_out, f_hat_out)


SCALARS = pl.BlockSpec(memory_space=pltpu.SMEM)
ON_CHIP = pl.BlockSpec(memory_space=pltpu.VMEM)
VMEM_LIMIT = 16 * 1024 * 1024
MID, UPPER, IMAGE, ODD, SAME, CORE = range(6)


def call(kernel, where, args, outs, scratch=()):
    return pl.pallas_call(
        kernel,
        out_shape=outs,
        in_specs=[SCALARS] + [ON_CHIP] * len(args),
        out_specs=[ON_CHIP] * len(outs),
        scratch_shapes=scratch,
        compiler_params=pltpu.CompilerParams(vmem_limit_bytes=VMEM_LIMIT),
        cost_estimate=pl.CostEstimate(flops=0, bytes_accessed=0, transcendentals=0),
    )(where, *args)


def shape_of(shape, kind=jnp.bfloat16):
    return jax.ShapeDtypeStruct(shape, kind)


def after(value, *others):
    return lax.optimization_barrier((value, *others))[0]


def modulated(values, ada_ref, image):
    shift, scale = ada_ref[image, 0:1, :], ada_ref[image, 1:2, :]
    return norm_rows(values.astype(jnp.float32)) * (1.0 + scale) + shift


def norm_kernel(begin, where_ref, tokens_ref, ada_ref, out_ref):
    values = tokens_ref[begin : begin + out_ref.shape[0], :]
    out_ref[...] = modulated(values, ada_ref, where_ref[IMAGE]).astype(jnp.bfloat16)


def norm_part(where, tokens, ada, begin, size):
    outs = [shape_of((size, tokens.shape[1]))]
    return call(functools.partial(norm_kernel, begin), where, (tokens, ada), outs)[0]


def ffn_kernel(groups, tile, where_ref, *refs):
    count = sum(groups)
    parts = refs[:count]
    up_a, up_b, down_a, down_b, bias_a, bias_b = refs[count : count + 6]
    outs = refs[count + 6 : count + 6 + len(groups)]
    x_ref, hidden_ref = refs[count + 6 + len(groups) :]
    panel, width = down_a.shape
    step = outs[0].shape[0]
    place = 0
    for g, size in enumerate(groups):
        if size == 1:
            value = parts[place][...]
        else:
            value = jnp.where(where_ref[MID] == 1, parts[place][...], parts[place + 1][...])
        x_ref[g * step : (g + 1) * step, :] = value
        place += size

    def columns(first, second, begin, end):
        if end <= panel:
            return first[:, begin:end]
        if begin >= panel:
            return second[:, begin - panel : end - panel]
        return jnp.concatenate([first[:, begin:panel], second[:, : end - panel]], axis=1)

    for begin in range(0, 2 * panel, tile):
        end = begin + tile
        v = jnp.dot(x_ref[...], columns(up_a, up_b, begin, end), preferred_element_type=jnp.float32)
        v = v + columns(bias_a, bias_b, begin, end)
        hidden_ref[:, begin:end] = jax.nn.gelu(v, approximate=True).astype(jnp.bfloat16)
    for begin in range(0, width, tile):
        cols = slice(begin, begin + tile)
        weight = jnp.concatenate([down_a[:, cols], down_b[:, cols]], axis=0)
        result = jnp.dot(hidden_ref[...], weight, preferred_element_type=jnp.float32)
        for g in range(len(groups)):
            outs[g][:, cols] = result[g * step : (g + 1) * step].astype(jnp.bfloat16)


def ffn(where, slots, panels):
    groups = tuple(len(slot) for slot in slots)
    parts = [part for slot in slots for part in slot]
    rows, width = parts[0].shape
    total = rows * len(slots)
    return call(
        functools.partial(ffn_kernel, groups, 256),
        where,
        (*parts, *panels),
        [shape_of((rows, width))] * len(slots),
        scratch=[
            pltpu.VMEM((total, width), jnp.bfloat16),
            pltpu.VMEM((total, 2 * panels[2].shape[0]), jnp.bfloat16),
        ],
    )


def add_kernel(always, where_ref, a_ref, b_ref, out_ref):
    b = b_ref[...].astype(jnp.float32)
    if not always:
        b = jnp.where(where_ref[MID] == 1, b, 0.0)
    out_ref[...] = (a_ref[...].astype(jnp.float32) + b).astype(jnp.bfloat16)


def add(where, a, b, always=False):
    return call(functools.partial(add_kernel, always), where, (a, b), [shape_of(a.shape)])[0]


def out_kernel(begin, always, where_ref, own_ref, near_ref, far_ref, tokens_ref, gate_ref, bias_ref, *refs):
    out_ref, kept_ref, sent_ref = refs[-3:]
    far = far_ref[...].astype(jnp.float32)
    if not always:
        far = jnp.where(where_ref[MID] == 1, far, 0.0)
    summed = own_ref[...].astype(jnp.float32) + near_ref[...].astype(jnp.float32) + far
    rows = summed.shape[0]
    tokens = tokens_ref[begin : begin + rows, :].astype(jnp.float32)
    gate = gate_ref[pl.ds(where_ref[IMAGE], 1), :]
    value = (tokens + gate * (summed + bias_ref[...])).astype(jnp.bfloat16)
    if len(refs) > 3:
        out_ref[0:begin, :] = refs[0][...]
        out_ref[begin : begin + rows, :] = value
    else:
        out_ref[...] = value
    half = rows // 2
    lower = where_ref[UPPER] == 0
    kept_ref[...] = jnp.where(lower, value[:half], value[half:])
    sent_ref[...] = jnp.where(lower, value[half:], value[:half])


def block_rows(where, begin, always, own, near, far, tokens, gate, bias, earlier=()):
    rows, width = own.shape
    full = rows + begin if earlier else rows
    return call(
        functools.partial(out_kernel, begin, always),
        where,
        (own, near, far, tokens, gate, bias, *earlier),
        [shape_of((full, width)), shape_of((rows // 2, width)), shape_of((rows // 2, width))],
    )


def mix_kernel(where_ref, kept_ref, came_ref, ada_ref, twin_ref, out_ref):
    image = where_ref[IMAGE]
    kept, came = modulated(kept_ref[...], ada_ref, image), modulated(came_ref[...], twin_ref, image)
    lower = where_ref[UPPER] == 0
    share = jnp.where(lower, 1.0 + GUIDE, -GUIDE)
    other = jnp.where(lower, -GUIDE, 1.0 + GUIDE)
    out_ref[...] = (share * kept + other * came).astype(jnp.bfloat16)


def mix_twins(where, kept, came, ada, twin):
    return call(mix_kernel, where, (kept, came, ada, twin), [shape_of(kept.shape)])[0]


def head_kernel(
    begin, where_ref, own_ref, near_ref, far_ref, last_ref, weight_a, weight_b, bias_a, bias_b, code_a, code_b,
    noise_own, noise_core, noise_twin, noise_both, stats_ref, x_ref
):
    step = own_ref.shape[0]
    for r, ref in enumerate((own_ref, near_ref, far_ref, last_ref)):
        x_ref[r * step : (r + 1) * step, :] = ref[...]
    x = x_ref[...]
    odd = where_ref[ODD]
    even = 1 - odd
    same = where_ref[SAME] == 1
    scores = []
    for weight, bias, ours, theirs in (
        (weight_a, bias_a, noise_own, noise_twin),
        (weight_b, bias_b, noise_core, noise_both),
    ):
        picked = []
        for first in (True, False):
            for block in (odd, even):
                a, b = ours[block, begin : begin + step, :], theirs[block, begin : begin + step, :]
                picked.append(jnp.where(same, a, b) if first else jnp.where(same, b, a))
        logits = jnp.dot(x, weight[...], preferred_element_type=jnp.float32)
        scores.append(logits + bias[:, bias.shape[1] - weight.shape[1] :] + jnp.concatenate(picked, axis=0))
    peak = jnp.max(jnp.maximum(scores[0], scores[1]), axis=1, keepdims=True)
    sums = 0.0
    total = 0.0
    for score, code in zip(scores, (code_a, code_b)):
        weights = jnp.exp(score - peak).astype(jnp.bfloat16)
        total = total + jnp.sum(weights.astype(jnp.float32), axis=1, keepdims=True)
        sums = sums + lax.dot_general(
            weights, code[...], (((1,), (1,)), ((), ())), preferred_element_type=jnp.float32
        )
    channels = code_a.shape[0]
    pad = jnp.zeros((4 * step, 128 - channels), jnp.float32)
    table = jnp.concatenate([sums, pad], axis=1)
    lane = lax.broadcasted_iota(jnp.int32, table.shape, 1)
    table = jnp.where(lane == channels, total, table)
    table = jnp.where(lane == channels + 1, peak, table)
    stats_ref[...] = jnp.transpose(table)[: stats_ref.shape[0], :]


def head_stats(where, begin, slots, heads, noises):
    step, width = slots[0].shape
    height = -(-(heads[-1].shape[0] + 2) // 8) * 8
    return call(
        functools.partial(head_kernel, begin),
        where,
        (*slots, *heads, *noises),
        [shape_of((height, 4 * step), jnp.float32)],
        scratch=[pltpu.VMEM((4 * step, width), jnp.bfloat16)],
    )[0]


def soft_kernel(channels, where_ref, *refs):
    parts, out_ref = refs[:-1], refs[-1]
    tops = [part[channels + 1 : channels + 2, :] for part in parts]
    top = functools.reduce(jnp.maximum, tops)
    code = 0.0
    total = 0.0
    for part, peak in zip(parts, tops):
        factor = jnp.exp(peak - top)
        code = code + part[0:channels, :] * factor
        total = total + part[channels : channels + 1, :] * factor
    out_ref[...] = code / total


def soft_codes(where, parts, channels):
    outs = [shape_of((channels, parts[0].shape[1]), jnp.float32)]
    return call(functools.partial(soft_kernel, channels), where, tuple(parts), outs)[0]


def refine_kernel(where_ref, first_ref, second_ref, halo_ref, phi_ref, bias_ref, map_ref, out_ref):
    first, second, halo = first_ref[...], second_ref[...], halo_ref[...]
    cells = first.shape[1]
    half = cells // 2
    lane = lax.broadcasted_iota(jnp.int32, first.shape, 1)
    shift = lambda value, by: pltpu.roll(value, by % cells, 1)
    early = where_ref[CORE] == 0
    lower, higher = jnp.where(early, first, second), jnp.where(early, second, first)
    centre = jnp.where(
        early,
        jnp.where(lane < half, lower, shift(higher, half)),
        jnp.where(lane < half, shift(lower, half), higher),
    )
    above = jnp.where(early, shift(halo, SIDE), shift(higher, SIDE - half))
    below = jnp.where(early, shift(lower, half - SIDE), shift(halo, -SIDE))
    rows = (
        jnp.where(lane < SIDE, above, shift(centre, SIDE)),
        centre,
        jnp.where(lane >= cells - SIDE, below, shift(centre, -SIDE)),
    )
    column = lane % SIDE
    conv = jnp.zeros(out_ref.shape, jnp.float32) + bias_ref[...]
    for i, row in enumerate(rows):
        left = jnp.where(column == 0, 0.0, shift(row, 1))
        right = jnp.where(column == SIDE - 1, 0.0, shift(row, -1))
        for j, tap in enumerate((left, row, right)):
            conv = conv + jnp.dot(
                phi_ref[i, j], tap, precision=lax.Precision.HIGHEST, preferred_element_type=jnp.float32
            )
    out_ref[...] = map_ref[...] + 0.5 * centre + 0.5 * conv


def line_body(
    tokens,
    ada_ffn,
    ffn_gate,
    up_weight,
    up_bias,
    down_weight,
    down_bias,
    ada_head,
    head_weight,
    head_bias,
    gumbel_noise,
    codebook,
    phi_weight,
    phi_bias,
    f_hat,
):
    rows = tokens.shape[0]
    dp, mp = lax.axis_size("dp"), lax.axis_size("mp")
    d_index, m_index = lax.axis_index("dp"), lax.axis_index("mp")
    channels = f_hat.shape[1]
    half_dp = dp // 2
    upper = d_index // half_dp
    z_index, core = m_index // 2, m_index % 2
    where = jnp.stack(
        [
            (z_index == 1) | (z_index == 2),
            upper,
            (m_index * rows) // NEW,
            z_index % 2,
            z_index // 2 == upper,
            core,
        ]
    ).astype(jnp.int32)

    def along_z(value, target):
        def to(d, m):
            z = target(m // 2)
            return None if z is None else (d, 2 * z + m % 2)

        return permute_devices(value, dp, mp, to)

    def near(value):
        return along_z(value, lambda z: z ^ 1)

    def across(value):
        return along_z(value, lambda z: z ^ 2)

    def middle(value):
        return along_z(value, lambda z: 3 - z if z in (1, 2) else z)

    def outward(value):
        return along_z(value, lambda z: {1: 0, 2: 3}.get(z))

    def inward(value):
        return along_z(value, lambda z: {0: 1, 3: 2}.get(z))

    def swap_cores(value):
        return permute_devices(value, dp, mp, lambda d, m: (d, m ^ 1))

    def swap_twins(value):
        return permute_devices(value, dp, mp, lambda d, m: ((d + half_dp) % dp, m))

    def swap_both(value):
        return permute_devices(value, dp, mp, lambda d, m: ((d + half_dp) % dp, m ^ 1))

    step = rows // CHUNKS
    half = step // 2
    voc = head_bias.shape[0]
    noise = gumbel_noise.reshape(2, 2, CHUNKS, 2, half, voc)

    def noise_for(to_core, to_upper):
        picked = lax.dynamic_slice(
            noise, (0, to_core, 0, to_upper, 0, 0), (2, 1, CHUNKS, 1, half, voc)
        )
        return picked.reshape(2, CHUNKS * half, voc)

    gate, bias_out = ffn_gate, down_bias[None]
    up_other, down_other = swap_cores(up_weight), swap_cores(down_weight)
    biases = jnp.concatenate([up_bias, head_bias])[None]
    codes = codebook.T
    bias_other = swap_cores(biases)

    barrier = lax.optimization_barrier
    own_a = norm_part(where, tokens, ada_ffn, 0, step)
    near_a, mid_a = near(own_a), middle(own_a)
    own_b = norm_part(where, tokens, ada_ffn, step, step)
    noise_own, noise_twin, noise_core, noise_both = (
        noise_for(core, upper),
        noise_for(core, 1 - upper),
        noise_for(1 - core, upper),
        noise_for(1 - core, 1 - upper),
    )
    noise_twin, noise_core, noise_both, _ = barrier((noise_twin, noise_core, noise_both, own_b))
    noise_twin = swap_twins(noise_twin)
    up_other, down_other, bias_other, near_a = barrier((up_other, down_other, bias_other, near_a))
    panels = (up_weight, up_other, down_weight, down_other, biases, bias_other)
    far_mid_a = middle(near_a)
    near_b = near(after(own_b, near_a))
    mid_a = after(mid_a, near_a)
    far_end_a = outward(mid_a)
    sum_own_a, sum_near_a = ffn(where, [[own_a], [after(near_a, mid_a)]], panels)
    noise_core = swap_cores(after(noise_core, sum_near_a))
    far_mid_a = after(far_mid_a, sum_near_a)
    last_end_a = outward(far_mid_a)
    mid_b = middle(after(own_b, far_mid_a))
    (sum_far_a,) = ffn(where, [[far_mid_a, far_end_a]], panels)
    came_far_a = inward(sum_far_a)
    near_b, mid_b = barrier((near_b, mid_b, sum_far_a))[:2]
    far_mid_b, far_end_b = middle(near_b), outward(mid_b)
    (sum_last_a,) = ffn(where, [[mid_a, after(last_end_a, near_b, mid_b, noise_twin)]], panels)
    came_last_a = inward(sum_last_a)
    noise_both = swap_both(after(noise_both, sum_last_a))
    sum_own_b, sum_near_b = ffn(where, [[after(own_b, sum_last_a, noise_core)], [near_b]], panels)
    both_last_a = add(where, after(sum_last_a, sum_near_b), came_far_a)
    went_last_a = middle(both_last_a)
    far_mid_b, far_end_b = barrier((far_mid_b, far_end_b, both_last_a))[:2]
    last_end_b = outward(far_mid_b)
    (sum_far_b,) = ffn(where, [[far_mid_b, far_end_b]], panels)
    both_far_a = add(where, after(sum_far_a, sum_far_b), came_last_a)
    went_far_a = middle(both_far_a)
    (sum_last_b,) = ffn(where, [[after(mid_b, both_far_a, went_last_a), last_end_b]], panels)
    came_last_b = near(sum_last_b)
    head_other = swap_cores(after(head_weight, sum_last_b))
    head_twin = swap_twins(after(ada_head, sum_last_b))
    code_other = swap_cores(after(codes, sum_last_b))
    both_far_b = add(where, sum_far_b, came_last_b, True)
    went_far_b = across(both_far_b)
    came_near_b = near(after(sum_near_b, both_far_b))
    both_near_a = add(where, sum_near_a, after(went_far_a, went_last_a, both_far_b))
    came_near_a = near(both_near_a)
    out_a, kept_a, sent_a = block_rows(
        where, 0, False, sum_own_a, after(came_near_a, head_twin), went_last_a, tokens, gate, bias_out
    )
    came_a = swap_twins(sent_a)
    mixed_a = mix_twins(where, kept_a, came_a, ada_head, head_twin)
    mix_near_a, mix_far_a = near(mixed_a), across(mixed_a)
    block_out, kept_b, sent_b = block_rows(
        where, step, True, sum_own_b, after(came_near_b, mixed_a, head_other, code_other, noise_both), went_far_b, tokens, gate, bias_out, (out_a,)
    )
    came_b = swap_twins(sent_b)
    mix_last_a = near(mix_far_a)
    mixed_b = mix_twins(where, kept_b, came_b, ada_head, head_twin)
    mix_near_b, mix_far_b = near(mixed_b), across(mixed_b)
    heads = (head_weight, head_other, biases, bias_other, codes, code_other)
    noises = (noise_own, noise_core, noise_twin, noise_both)
    stats_a = head_stats(
        where, 0, (after(mixed_a, mixed_b), mix_near_a, mix_far_a, mix_last_a), heads, noises
    )
    mix_last_b = near(mix_far_b)
    stats_b = head_stats(where, half, (after(mixed_b, stats_a), mix_near_b, mix_far_b, mix_last_b), heads, noises)

    slots = [
        jnp.concatenate([part[:, r * half : (r + 1) * half] for part in (stats_a, stats_b)], axis=1) for r in range(4)
    ]
    parts = [slots[0]] + [along_z(slots[r], lambda z, r=r: z ^ r) for r in (1, 2, 3)]
    soft = soft_codes(where, parts, channels)

    def to_cells(d, m, core_of):
        y, x = d // half_dp, d % half_dp
        z, c = m // 2, m % 2
        return ((z // 2) * half_dp + x, 2 * (2 * (z % 2) + c) + core_of(y))

    def to_halo(d, m):
        y, x = d // half_dp, d % half_dp
        z, c = m // 2, m % 2
        block = 2 * (z % 2) + c + (1 if y == 1 else -1)
        if block < 0 or block > 3:
            return None
        return ((z // 2) * half_dp + x, 2 * block + (0 if y == 1 else 1))

    first = permute_devices(soft, dp, mp, lambda d, m: to_cells(d, m, lambda y: y))
    second = permute_devices(soft, dp, mp, lambda d, m: to_cells(d, m, lambda y: 1 - y))
    halo = permute_devices(soft, dp, mp, to_halo)
    f_hat_out = call(
        refine_kernel,
        where,
        (first, second, halo, jnp.transpose(phi_weight, (2, 3, 0, 1)), phi_bias[:, None], f_hat[0]),
        [shape_of(f_hat.shape[1:], jnp.float32)],
    )[0]
    return (block_out, f_hat_out[None])


def solution(mesh):
    in_specs = (
        P(("dp", "mp"), None),
        P("dp", None, None),
        P("dp", None),
        P(None, "mp"),
        P("mp"),
        P("mp", None),
        P(),
        P("dp", None, None),
        P(None, "mp"),
        P("mp"),
        P("dp", None, "mp"),
        P("mp", None),
        P(),
        P(),
        P("dp", None, "mp"),
    )
    out_specs = (P(("dp", "mp"), None), P("dp", None, "mp"))
    line = mesh.shape["dp"] == 4 and mesh.shape["mp"] == 8
    body = line_body if line else general_body
    return jax.shard_map(body, mesh=mesh, in_specs=in_specs, out_specs=out_specs, check_vma=False)
```

```python
import functools

import jax
import jax.numpy as jnp
from jax import lax
from jax.experimental import pallas as pl
from jax.experimental.pallas import tpu as pltpu
from jax.sharding import PartitionSpec as P

SIDE = 32
NEW = 1024
GUIDE = 1.5
CHUNKS = 2
FLOWS = 4
HEAD_FLOWS = 2


def norm_rows(values):
    row_mean = jnp.mean(values, axis=-1, keepdims=True)
    centred = values - row_mean
    spread = jnp.mean(centred * centred, axis=-1, keepdims=True)
    return centred * lax.rsqrt(spread + 1e-06)


def modulate(values, ada):
    return norm_rows(values.astype(jnp.float32)) * (1.0 + ada[1]) + ada[0]


def permute_devices(value, dp, mp, target):
    pairs = []
    for d in range(dp):
        for m in range(mp):
            to = target(d, m)
            if to is not None:
                pairs.append((d * mp + m, to[0] * mp + to[1]))
    return lax.ppermute(value, ("dp", "mp"), pairs)


def general_body(
    tokens,
    ada_ffn,
    ffn_gate,
    up_weight,
    up_bias,
    down_weight,
    down_bias,
    ada_head,
    head_weight,
    head_bias,
    gumbel_noise,
    codebook,
    phi_weight,
    phi_bias,
    f_hat,
):
    rows, width = tokens.shape
    dp, mp = lax.axis_size("dp"), lax.axis_size("mp")
    d_index, m_index = lax.axis_index("dp"), lax.axis_index("mp")
    images = ada_ffn.shape[0]
    pairs = f_hat.shape[0]
    channels = f_hat.shape[1]
    vocab = head_weight.shape[1]
    own_image = (m_index * rows) // NEW
    ada_own = lax.dynamic_index_in_dim(ada_ffn, own_image, 0, keepdims=False)
    gate_own = lax.dynamic_index_in_dim(ffn_gate, own_image, 0, keepdims=False)
    head_own = lax.dynamic_index_in_dim(ada_head, own_image, 0, keepdims=False)
    half_dp, half_mp = dp // 2, mp // 2
    upper = d_index // half_dp

    def swap(d, m):
        return ((d + half_dp) % dp, m)

    def cross(d, m):
        if d // half_dp == m // half_mp:
            return None
        return ((d + half_dp) % dp, (m + half_mp) % mp)

    stays = upper == m_index // half_mp
    head_twin = permute_devices(head_own, dp, mp, swap)
    head_cond = jnp.where(upper == 0, head_own, head_twin)
    head_uncond = jnp.where(upper == 0, head_twin, head_own)

    step = rows // FLOWS
    normed = modulate(tokens, ada_own).astype(jnp.bfloat16)
    outs = []
    for c in range(FLOWS):
        part = lax.slice_in_dim(normed, c * step, (c + 1) * step, axis=0)
        gathered = lax.all_gather(part, "mp", axis=0, tiled=True)
        hidden = jax.nn.gelu(
            jnp.dot(gathered, up_weight, preferred_element_type=jnp.float32) + up_bias,
            approximate=True,
        ).astype(jnp.bfloat16)
        partial = jnp.dot(hidden, down_weight, preferred_element_type=jnp.float32).astype(jnp.bfloat16)
        summed = lax.psum_scatter(partial, "mp", scatter_dimension=0, tiled=True).astype(jnp.float32)
        own = lax.slice_in_dim(tokens, c * step, (c + 1) * step, axis=0).astype(jnp.float32)
        outs.append((own + gate_own * (summed + down_bias)).astype(jnp.bfloat16))
    block_out = jnp.concatenate(outs, axis=0)

    group = FLOWS // HEAD_FLOWS
    half = rows // HEAD_FLOWS // 2
    noise = gumbel_noise.reshape(pairs, NEW // rows, HEAD_FLOWS, 2, half, vocab)
    peaks, totals, codes = [], [], []
    for c in range(HEAD_FLOWS):
        part = jnp.concatenate(outs[c * group : (c + 1) * group], axis=0)
        first, second = part[:half], part[half:]
        kept = jnp.where(upper == 0, first, second)
        sent = jnp.where(upper == 0, second, first)
        came = permute_devices(sent, dp, mp, swap)
        cond = jnp.where(upper == 0, kept, came)
        uncond = jnp.where(upper == 0, came, kept)
        mixed = (
            (1.0 + GUIDE) * modulate(cond, head_cond) - GUIDE * modulate(uncond, head_uncond)
        ).astype(jnp.bfloat16)
        crossed = permute_devices(mixed, dp, mp, cross)
        mixed = jnp.where(stays, mixed, crossed)
        gathered = lax.all_gather(mixed, "mp", axis=0, tiled=True)
        logits = jnp.dot(gathered, head_weight, preferred_element_type=jnp.float32) + head_bias
        logits = logits.reshape(2, half_mp, half, vocab)
        order = jnp.transpose(logits, (1, 0, 2, 3)).reshape(pairs, NEW // rows, 2, half, vocab)
        scores = order + noise[:, :, c]
        peak = jnp.max(scores, axis=-1)
        weights = jnp.exp(scores - peak[..., None]).astype(jnp.bfloat16)
        totals.append(jnp.sum(weights.astype(jnp.float32), axis=-1))
        codes.append(jnp.dot(weights, codebook, preferred_element_type=jnp.float32))
        peaks.append(peak)
    stack = lambda parts: jnp.stack(parts, axis=2)
    peak = stack(peaks).reshape(pairs, 1, NEW)
    total = stack(totals).reshape(pairs, 1, NEW)
    code = stack(codes).reshape(pairs, NEW, channels).transpose(0, 2, 1)
    stats = jnp.concatenate([code, total, peak], axis=1)

    cells = f_hat.shape[2]
    band = cells // SIDE
    padded = jnp.pad(stats, ((0, 0), (0, 0), (SIDE, SIDE)))
    windows = jnp.stack(
        [padded[:, :, m * cells : m * cells + cells + 2 * SIDE] for m in range(mp)], axis=0
    )
    parts = lax.all_to_all(windows, "mp", 0, 0, tiled=True)
    top = jnp.max(parts[:, :, channels + 1], axis=0)
    factor = jnp.exp(parts[:, :, channels + 1] - top[None])[:, :, None]
    sums = jnp.sum(parts[:, :, : channels + 1] * factor, axis=0)
    cell_index = m_index * cells - SIDE + jnp.arange(cells + 2 * SIDE)
    inside = (cell_index >= 0) & (cell_index < NEW)
    soft = jnp.where(inside, sums[:, :channels] / jnp.where(inside, sums[:, channels:], 1.0), 0.0)
    code_map = soft.reshape(pairs, channels, band + 2, SIDE)
    wide = jnp.pad(code_map, ((0, 0), (0, 0), (0, 0), (1, 1)))
    taps = jnp.stack(
        [wide[:, :, i : i + band, j : j + SIDE] for i in range(3) for j in range(3)], axis=2
    ).reshape(pairs, channels * 9, cells)
    conv = jnp.einsum(
        "ok,pkn->pon",
        phi_weight.reshape(channels, channels * 9),
        taps,
        precision=lax.Precision.HIGHEST,
        preferred_element_type=jnp.float32,
    ) + phi_bias[None, :, None]
    f_hat_out = f_hat + 0.5 * soft[:, :, SIDE : SIDE + cells] + 0.5 * conv
    return (block_out, f_hat_out)


SCALARS = pl.BlockSpec(memory_space=pltpu.SMEM)
ON_CHIP = pl.BlockSpec(memory_space=pltpu.VMEM)
VMEM_LIMIT = 16 * 1024 * 1024
MID, UPPER, IMAGE, ODD, SAME, CORE = range(6)


def call(kernel, where, args, outs, scratch=(), flops=0):
    return pl.pallas_call(
        kernel,
        out_shape=outs,
        in_specs=[SCALARS] + [ON_CHIP] * len(args),
        out_specs=[ON_CHIP] * len(outs),
        scratch_shapes=scratch,
        compiler_params=pltpu.CompilerParams(vmem_limit_bytes=VMEM_LIMIT),
        cost_estimate=pl.CostEstimate(flops=flops, bytes_accessed=0, transcendentals=0),
    )(where, *args)


def shape_of(shape, kind=jnp.bfloat16):
    return jax.ShapeDtypeStruct(shape, kind)


def after(value, *others):
    return lax.optimization_barrier((value, *others))[0]


def modulated(values, ada_ref, image):
    shift, scale = ada_ref[image, 0:1, :], ada_ref[image, 1:2, :]
    return norm_rows(values.astype(jnp.float32)) * (1.0 + scale) + shift


def norm_kernel(begin, where_ref, tokens_ref, ada_ref, out_ref):
    values = tokens_ref[begin : begin + out_ref.shape[0], :]
    out_ref[...] = modulated(values, ada_ref, where_ref[IMAGE]).astype(jnp.bfloat16)


def norm_part(where, tokens, ada, begin, size):
    outs = [shape_of((size, tokens.shape[1]))]
    return call(functools.partial(norm_kernel, begin), where, (tokens, ada), outs)[0]


def stage_kernel(where_ref, up_ref, down_ref, up_out, down_out, sems):
    copies = [
        pltpu.make_async_copy(up_ref, up_out, sems.at[0]),
        pltpu.make_async_copy(down_ref, down_out, sems.at[1]),
    ]
    for copy in copies:
        copy.start()
    for copy in copies:
        copy.wait()


def stage(where, up, down):
    return pl.pallas_call(
        stage_kernel,
        out_shape=[shape_of(up.shape), shape_of(down.shape)],
        in_specs=[SCALARS] + [pl.BlockSpec(memory_space=pltpu.HBM)] * 2,
        out_specs=[ON_CHIP] * 2,
        scratch_shapes=[pltpu.SemaphoreType.DMA((2,))],
        compiler_params=pltpu.CompilerParams(vmem_limit_bytes=VMEM_LIMIT),
        cost_estimate=pl.CostEstimate(flops=0, bytes_accessed=0, transcendentals=0),
    )(where, up, down)


def ffn_kernel(groups, tile, where_ref, *refs):
    count = sum(groups)
    parts = refs[:count]
    up_a, up_b, down_a, down_b, bias_a, bias_b = refs[count : count + 6]
    outs = refs[count + 6 : count + 6 + len(groups)]
    x_ref, hidden_ref = refs[count + 6 + len(groups) :]
    panel, width = down_a.shape
    step = outs[0].shape[0]
    place = 0
    for g, size in enumerate(groups):
        if size == 1:
            value = parts[place][...]
        else:
            value = jnp.where(where_ref[MID] == 1, parts[place][...], parts[place + 1][...])
        x_ref[g * step : (g + 1) * step, :] = value
        place += size

    def columns(first, second, begin, end):
        if end <= panel:
            return first[:, begin:end]
        if begin >= panel:
            return second[:, begin - panel : end - panel]
        return jnp.concatenate([first[:, begin:panel], second[:, : end - panel]], axis=1)

    for begin in range(0, 2 * panel, tile):
        end = begin + tile
        v = jnp.dot(x_ref[...], columns(up_a, up_b, begin, end), preferred_element_type=jnp.float32)
        v = v + columns(bias_a, bias_b, begin, end)
        hidden_ref[:, begin:end] = jax.nn.gelu(v, approximate=True).astype(jnp.bfloat16)
    for begin in range(0, width, tile):
        cols = slice(begin, begin + tile)
        weight = jnp.concatenate([down_a[:, cols], down_b[:, cols]], axis=0)
        result = jnp.dot(hidden_ref[...], weight, preferred_element_type=jnp.float32)
        for g in range(len(groups)):
            outs[g][:, cols] = result[g * step : (g + 1) * step].astype(jnp.bfloat16)


def ffn(where, slots, panels):
    groups = tuple(len(slot) for slot in slots)
    parts = [part for slot in slots for part in slot]
    rows, width = parts[0].shape
    total = rows * len(slots)
    return call(
        functools.partial(ffn_kernel, groups, 256),
        where,
        (*parts, *panels),
        [shape_of((rows, width))] * len(slots),
        scratch=[
            pltpu.VMEM((total, width), jnp.bfloat16),
            pltpu.VMEM((total, 2 * panels[2].shape[0]), jnp.bfloat16),
        ],
    )


def add_kernel(always, where_ref, a_ref, b_ref, out_ref):
    b = b_ref[...].astype(jnp.float32)
    if not always:
        b = jnp.where(where_ref[MID] == 1, b, 0.0)
    out_ref[...] = (a_ref[...].astype(jnp.float32) + b).astype(jnp.bfloat16)


def add(where, a, b, always=False, flops=0):
    return call(functools.partial(add_kernel, always), where, (a, b), [shape_of(a.shape)], flops=flops)[0]


def out_kernel(begin, always, where_ref, own_ref, near_ref, far_ref, tokens_ref, gate_ref, bias_ref, *refs):
    out_ref, kept_ref, sent_ref = refs[-3:]
    far = far_ref[...].astype(jnp.float32)
    if not always:
        far = jnp.where(where_ref[MID] == 1, far, 0.0)
    summed = own_ref[...].astype(jnp.float32) + near_ref[...].astype(jnp.float32) + far
    rows = summed.shape[0]
    tokens = tokens_ref[begin : begin + rows, :].astype(jnp.float32)
    gate = gate_ref[pl.ds(where_ref[IMAGE], 1), :]
    value = (tokens + gate * (summed + bias_ref[...])).astype(jnp.bfloat16)
    if len(refs) > 3:
        out_ref[0:begin, :] = refs[0][...]
        out_ref[begin : begin + rows, :] = value
    else:
        out_ref[...] = value
    half = rows // 2
    lower = where_ref[UPPER] == 0
    kept_ref[...] = jnp.where(lower, value[:half], value[half:])
    sent_ref[...] = jnp.where(lower, value[half:], value[:half])


def block_rows(where, begin, always, own, near, far, tokens, gate, bias, earlier=()):
    rows, width = own.shape
    full = rows + begin if earlier else rows
    return call(
        functools.partial(out_kernel, begin, always),
        where,
        (own, near, far, tokens, gate, bias, *earlier),
        [shape_of((full, width)), shape_of((rows // 2, width)), shape_of((rows // 2, width))],
    )


def mix_kernel(where_ref, kept_ref, came_ref, ada_ref, twin_ref, out_ref):
    image = where_ref[IMAGE]
    kept, came = modulated(kept_ref[...], ada_ref, image), modulated(came_ref[...], twin_ref, image)
    lower = where_ref[UPPER] == 0
    share = jnp.where(lower, 1.0 + GUIDE, -GUIDE)
    other = jnp.where(lower, -GUIDE, 1.0 + GUIDE)
    out_ref[...] = (share * kept + other * came).astype(jnp.bfloat16)


def mix_twins(where, kept, came, ada, twin):
    return call(mix_kernel, where, (kept, came, ada, twin), [shape_of(kept.shape)])[0]


def head_kernel(
    begin, where_ref, own_ref, near_ref, far_ref, last_ref, weight_a, weight_b, bias_a, bias_b, code_a, code_b,
    noise_own, noise_core, noise_twin, noise_both, stats_ref, x_ref
):
    step = own_ref.shape[0]
    for r, ref in enumerate((own_ref, near_ref, far_ref, last_ref)):
        x_ref[r * step : (r + 1) * step, :] = ref[...]
    x = x_ref[...]
    odd = where_ref[ODD]
    even = 1 - odd
    same = where_ref[SAME] == 1
    scores = []
    for weight, bias, ours, theirs in (
        (weight_a, bias_a, noise_own, noise_twin),
        (weight_b, bias_b, noise_core, noise_both),
    ):
        picked = []
        for first in (True, False):
            for block in (odd, even):
                a, b = ours[block, begin : begin + step, :], theirs[block, begin : begin + step, :]
                picked.append(jnp.where(same, a, b) if first else jnp.where(same, b, a))
        logits = jnp.dot(x, weight[...], preferred_element_type=jnp.float32)
        scores.append(logits + bias[:, bias.shape[1] - weight.shape[1] :] + jnp.concatenate(picked, axis=0))
    peak = jnp.max(jnp.maximum(scores[0], scores[1]), axis=1, keepdims=True)
    sums = 0.0
    total = 0.0
    for score, code in zip(scores, (code_a, code_b)):
        weights = jnp.exp(score - peak).astype(jnp.bfloat16)
        total = total + jnp.sum(weights.astype(jnp.float32), axis=1, keepdims=True)
        sums = sums + lax.dot_general(
            weights, code[...], (((1,), (1,)), ((), ())), preferred_element_type=jnp.float32
        )
    channels = code_a.shape[0]
    pad = jnp.zeros((4 * step, 128 - channels), jnp.float32)
    table = jnp.concatenate([sums, pad], axis=1)
    lane = lax.broadcasted_iota(jnp.int32, table.shape, 1)
    table = jnp.where(lane == channels, total, table)
    table = jnp.where(lane == channels + 1, peak, table)
    stats_ref[...] = jnp.transpose(table)[: stats_ref.shape[0], :]


def head_stats(where, begin, slots, heads, noises):
    step, width = slots[0].shape
    height = -(-(heads[-1].shape[0] + 2) // 8) * 8
    return call(
        functools.partial(head_kernel, begin),
        where,
        (*slots, *heads, *noises),
        [shape_of((height, 4 * step), jnp.float32)],
        scratch=[pltpu.VMEM((4 * step, width), jnp.bfloat16)],
    )[0]


def soft_kernel(channels, where_ref, *refs):
    parts, out_ref = refs[:-1], refs[-1]
    tops = [part[channels + 1 : channels + 2, :] for part in parts]
    top = functools.reduce(jnp.maximum, tops)
    code = 0.0
    total = 0.0
    for part, peak in zip(parts, tops):
        factor = jnp.exp(peak - top)
        code = code + part[0:channels, :] * factor
        total = total + part[channels : channels + 1, :] * factor
    out_ref[...] = code / total


def soft_codes(where, parts, channels):
    outs = [shape_of((channels, parts[0].shape[1]), jnp.float32)]
    return call(functools.partial(soft_kernel, channels), where, tuple(parts), outs)[0]


def refine_kernel(where_ref, first_ref, second_ref, halo_ref, phi_ref, bias_ref, map_ref, out_ref):
    first, second, halo = first_ref[...], second_ref[...], halo_ref[...]
    cells = first.shape[1]
    half = cells // 2
    lane = lax.broadcasted_iota(jnp.int32, first.shape, 1)
    shift = lambda value, by: pltpu.roll(value, by % cells, 1)
    early = where_ref[CORE] == 0
    lower, higher = jnp.where(early, first, second), jnp.where(early, second, first)
    centre = jnp.where(
        early,
        jnp.where(lane < half, lower, shift(higher, half)),
        jnp.where(lane < half, shift(lower, half), higher),
    )
    above = jnp.where(early, shift(halo, SIDE), shift(higher, SIDE - half))
    below = jnp.where(early, shift(lower, half - SIDE), shift(halo, -SIDE))
    rows = (
        jnp.where(lane < SIDE, above, shift(centre, SIDE)),
        centre,
        jnp.where(lane >= cells - SIDE, below, shift(centre, -SIDE)),
    )
    column = lane % SIDE
    conv = jnp.zeros(out_ref.shape, jnp.float32) + bias_ref[...]
    for i, row in enumerate(rows):
        left = jnp.where(column == 0, 0.0, shift(row, 1))
        right = jnp.where(column == SIDE - 1, 0.0, shift(row, -1))
        for j, tap in enumerate((left, row, right)):
            conv = conv + jnp.dot(
                phi_ref[i, j], tap, precision=lax.Precision.HIGHEST, preferred_element_type=jnp.float32
            )
    out_ref[...] = map_ref[...] + 0.5 * centre + 0.5 * conv


def line_body(
    tokens,
    ada_ffn,
    ffn_gate,
    up_weight,
    up_bias,
    down_weight,
    down_bias,
    ada_head,
    head_weight,
    head_bias,
    gumbel_noise,
    codebook,
    phi_weight,
    phi_bias,
    f_hat,
):
    rows = tokens.shape[0]
    dp, mp = lax.axis_size("dp"), lax.axis_size("mp")
    d_index, m_index = lax.axis_index("dp"), lax.axis_index("mp")
    channels = f_hat.shape[1]
    half_dp = dp // 2
    upper = d_index // half_dp
    z_index, core = m_index // 2, m_index % 2
    where = jnp.stack(
        [
            (z_index == 1) | (z_index == 2),
            upper,
            (m_index * rows) // NEW,
            z_index % 2,
            z_index // 2 == upper,
            core,
        ]
    ).astype(jnp.int32)

    def along_z(value, target):
        def to(d, m):
            z = target(m // 2)
            return None if z is None else (d, 2 * z + m % 2)

        return permute_devices(value, dp, mp, to)

    def near(value):
        return along_z(value, lambda z: z ^ 1)

    def across(value):
        return along_z(value, lambda z: z ^ 2)

    def middle(value):
        return along_z(value, lambda z: 3 - z if z in (1, 2) else z)

    def outward(value):
        return along_z(value, lambda z: {1: 0, 2: 3}.get(z))

    def inward(value):
        return along_z(value, lambda z: {0: 1, 3: 2}.get(z))

    def swap_cores(value):
        return permute_devices(value, dp, mp, lambda d, m: (d, m ^ 1))

    def swap_twins(value):
        return permute_devices(value, dp, mp, lambda d, m: ((d + half_dp) % dp, m))

    def swap_both(value):
        return permute_devices(value, dp, mp, lambda d, m: ((d + half_dp) % dp, m ^ 1))

    step = rows // CHUNKS
    half = step // 2
    voc = head_bias.shape[0]
    noise = gumbel_noise.reshape(2, 2, CHUNKS, 2, half, voc)

    def noise_for(to_core, to_upper):
        picked = lax.dynamic_slice(
            noise, (0, to_core, 0, to_upper, 0, 0), (2, 1, CHUNKS, 1, half, voc)
        )
        return picked.reshape(2, CHUNKS * half, voc)

    gate, bias_out = ffn_gate, down_bias[None]
    up_other, down_other = swap_cores(up_weight), swap_cores(down_weight)
    biases = jnp.concatenate([up_bias, head_bias])[None]
    codes = codebook.T
    bias_other = swap_cores(biases)

    barrier = lax.optimization_barrier
    own_a = norm_part(where, tokens, ada_ffn, 0, step)
    near_a, mid_a = near(own_a), middle(own_a)
    own_b = norm_part(where, tokens, ada_ffn, step, step)
    noise_own, noise_twin, noise_core, noise_both = (
        noise_for(core, upper),
        noise_for(core, 1 - upper),
        noise_for(1 - core, upper),
        noise_for(1 - core, 1 - upper),
    )
    noise_twin, noise_core, noise_both, _ = barrier((noise_twin, noise_core, noise_both, own_b))
    noise_twin = swap_twins(noise_twin)
    up_own, down_own = stage(where, up_weight, down_weight)
    up_own, down_own, up_other, down_other, bias_other, near_a, own_b = barrier(
        (up_own, down_own, up_other, down_other, bias_other, near_a, own_b)
    )
    panels = (up_own, up_other, down_own, down_other, biases, bias_other)
    far_mid_a = middle(near_a)
    near_b = near(after(own_b, near_a))
    mid_a = after(mid_a, near_a)
    far_end_a = outward(mid_a)
    sum_own_a, sum_near_a = ffn(where, [[own_a], [after(near_a, mid_a)]], panels)
    far_mid_a = after(far_mid_a, sum_near_a)
    last_end_a = outward(far_mid_a)
    mid_b = middle(after(own_b, far_mid_a))
    noise_core = swap_cores(after(noise_core, far_mid_a))
    (sum_far_a,) = ffn(where, [[far_mid_a, far_end_a]], panels)
    came_far_a = inward(sum_far_a)
    near_b, mid_b = barrier((near_b, mid_b, sum_far_a))[:2]
    far_mid_b, far_end_b = middle(near_b), outward(mid_b)
    (sum_last_a,) = ffn(where, [[mid_a, after(last_end_a, near_b, mid_b, noise_twin)]], panels)
    came_last_a = inward(sum_last_a)
    noise_both = swap_both(after(noise_both, sum_last_a))
    sum_own_b, sum_near_b = ffn(where, [[after(own_b, sum_last_a, noise_core)], [near_b]], panels)
    both_last_a = add(where, after(sum_last_a, sum_near_b), came_far_a)
    went_last_a = middle(both_last_a)
    far_mid_b, far_end_b = barrier((far_mid_b, far_end_b, both_last_a))[:2]
    last_end_b = outward(far_mid_b)
    (sum_far_b,) = ffn(where, [[far_mid_b, far_end_b]], panels)
    both_far_a = add(where, after(sum_far_a, sum_far_b), came_last_a)
    went_far_a = middle(both_far_a)
    (sum_last_b,) = ffn(where, [[after(mid_b, both_far_a, went_last_a), last_end_b]], panels)
    came_last_b = near(sum_last_b)
    came_near_b = near(after(sum_near_b, last_end_b))
    head_other = swap_cores(after(head_weight, sum_last_b))
    head_twin = swap_twins(after(ada_head, sum_last_b))
    code_other = swap_cores(after(codes, sum_last_b))
    both_near_a = add(where, sum_near_a, after(went_far_a, went_last_a, came_near_b), flops=40000000000)
    came_near_a = near(both_near_a)
    both_far_b = add(where, after(sum_far_b, both_near_a), came_last_b, True)
    went_far_b = across(both_far_b)
    out_a, kept_a, sent_a = block_rows(
        where, 0, False, sum_own_a, after(came_near_a, head_twin), went_last_a, tokens, gate, bias_out
    )
    came_a = swap_twins(sent_a)
    mixed_a = mix_twins(where, kept_a, came_a, ada_head, head_twin)
    mix_near_a, mix_far_a = near(mixed_a), across(mixed_a)
    block_out, kept_b, sent_b = block_rows(
        where, step, True, sum_own_b, after(came_near_b, mixed_a, head_other, code_other, noise_both), went_far_b, tokens, gate, bias_out, (out_a,)
    )
    came_b = after(swap_twins(sent_b), mix_far_a)
    mix_last_a = near(mix_far_a)
    mixed_b = mix_twins(where, kept_b, came_b, ada_head, head_twin)
    mix_near_b, mix_far_b = near(mixed_b), across(mixed_b)
    heads = (head_weight, head_other, biases, bias_other, codes, code_other)
    noises = (noise_own, noise_core, noise_twin, noise_both)
    stats_a = head_stats(
        where, 0, (after(mixed_a, mixed_b), mix_near_a, mix_far_a, mix_last_a), heads, noises
    )
    mix_last_b = near(mix_far_b)
    stats_b = head_stats(where, half, (after(mixed_b, stats_a), mix_near_b, mix_far_b, mix_last_b), heads, noises)

    slots = [
        jnp.concatenate([part[:, r * half : (r + 1) * half] for part in (stats_a, stats_b)], axis=1) for r in range(4)
    ]
    parts = [slots[0]] + [along_z(slots[r], lambda z, r=r: z ^ r) for r in (1, 2, 3)]
    soft = soft_codes(where, parts, channels)

    def to_cells(d, m, core_of):
        y, x = d // half_dp, d % half_dp
        z, c = m // 2, m % 2
        return ((z // 2) * half_dp + x, 2 * (2 * (z % 2) + c) + core_of(y))

    def to_halo(d, m):
        y, x = d // half_dp, d % half_dp
        z, c = m // 2, m % 2
        block = 2 * (z % 2) + c + (1 if y == 1 else -1)
        if block < 0 or block > 3:
            return None
        return ((z // 2) * half_dp + x, 2 * block + (0 if y == 1 else 1))

    first = permute_devices(soft, dp, mp, lambda d, m: to_cells(d, m, lambda y: y))
    second = permute_devices(soft, dp, mp, lambda d, m: to_cells(d, m, lambda y: 1 - y))
    halo = permute_devices(soft, dp, mp, to_halo)
    f_hat_out = call(
        refine_kernel,
        where,
        (first, second, halo, jnp.transpose(phi_weight, (2, 3, 0, 1)), phi_bias[:, None], f_hat[0]),
        [shape_of(f_hat.shape[1:], jnp.float32)],
    )[0]
    return (block_out, f_hat_out[None])


def solution(mesh):
    in_specs = (
        P(("dp", "mp"), None),
        P("dp", None, None),
        P("dp", None),
        P(None, "mp"),
        P("mp"),
        P("mp", None),
        P(),
        P("dp", None, None),
        P(None, "mp"),
        P("mp"),
        P("dp", None, "mp"),
        P("mp", None),
        P(),
        P(),
        P("dp", None, "mp"),
    )
    out_specs = (P(("dp", "mp"), None), P("dp", None, "mp"))
    line = mesh.shape["dp"] == 4 and mesh.shape["mp"] == 8
    body = line_body if line else general_body
    return jax.shard_map(body, mesh=mesh, in_specs=in_specs, out_specs=out_specs, check_vma=False)
```

```python
import functools

import jax
import jax.numpy as jnp
from jax import lax
from jax.experimental import pallas as pl
from jax.experimental.pallas import tpu as pltpu
from jax.sharding import PartitionSpec as P

SIDE = 32
NEW = 1024
GUIDE = 1.5
CHUNKS = 2
FLOWS = 4
HEAD_FLOWS = 2


def norm_rows(values):
    row_mean = jnp.mean(values, axis=-1, keepdims=True)
    centred = values - row_mean
    spread = jnp.mean(centred * centred, axis=-1, keepdims=True)
    return centred * lax.rsqrt(spread + 1e-06)


def modulate(values, ada):
    return norm_rows(values.astype(jnp.float32)) * (1.0 + ada[1]) + ada[0]


def permute_devices(value, dp, mp, target):
    pairs = []
    for d in range(dp):
        for m in range(mp):
            to = target(d, m)
            if to is not None:
                pairs.append((d * mp + m, to[0] * mp + to[1]))
    return lax.ppermute(value, ("dp", "mp"), pairs)


def general_body(
    tokens,
    ada_ffn,
    ffn_gate,
    up_weight,
    up_bias,
    down_weight,
    down_bias,
    ada_head,
    head_weight,
    head_bias,
    gumbel_noise,
    codebook,
    phi_weight,
    phi_bias,
    f_hat,
):
    rows, width = tokens.shape
    dp, mp = lax.axis_size("dp"), lax.axis_size("mp")
    d_index, m_index = lax.axis_index("dp"), lax.axis_index("mp")
    images = ada_ffn.shape[0]
    pairs = f_hat.shape[0]
    channels = f_hat.shape[1]
    vocab = head_weight.shape[1]
    own_image = (m_index * rows) // NEW
    ada_own = lax.dynamic_index_in_dim(ada_ffn, own_image, 0, keepdims=False)
    gate_own = lax.dynamic_index_in_dim(ffn_gate, own_image, 0, keepdims=False)
    head_own = lax.dynamic_index_in_dim(ada_head, own_image, 0, keepdims=False)
    half_dp, half_mp = dp // 2, mp // 2
    upper = d_index // half_dp

    def swap(d, m):
        return ((d + half_dp) % dp, m)

    def cross(d, m):
        if d // half_dp == m // half_mp:
            return None
        return ((d + half_dp) % dp, (m + half_mp) % mp)

    stays = upper == m_index // half_mp
    head_twin = permute_devices(head_own, dp, mp, swap)
    head_cond = jnp.where(upper == 0, head_own, head_twin)
    head_uncond = jnp.where(upper == 0, head_twin, head_own)

    step = rows // FLOWS
    normed = modulate(tokens, ada_own).astype(jnp.bfloat16)
    outs = []
    for c in range(FLOWS):
        part = lax.slice_in_dim(normed, c * step, (c + 1) * step, axis=0)
        gathered = lax.all_gather(part, "mp", axis=0, tiled=True)
        hidden = jax.nn.gelu(
            jnp.dot(gathered, up_weight, preferred_element_type=jnp.float32) + up_bias,
            approximate=True,
        ).astype(jnp.bfloat16)
        partial = jnp.dot(hidden, down_weight, preferred_element_type=jnp.float32).astype(jnp.bfloat16)
        summed = lax.psum_scatter(partial, "mp", scatter_dimension=0, tiled=True).astype(jnp.float32)
        own = lax.slice_in_dim(tokens, c * step, (c + 1) * step, axis=0).astype(jnp.float32)
        outs.append((own + gate_own * (summed + down_bias)).astype(jnp.bfloat16))
    block_out = jnp.concatenate(outs, axis=0)

    group = FLOWS // HEAD_FLOWS
    half = rows // HEAD_FLOWS // 2
    noise = gumbel_noise.reshape(pairs, NEW // rows, HEAD_FLOWS, 2, half, vocab)
    peaks, totals, codes = [], [], []
    for c in range(HEAD_FLOWS):
        part = jnp.concatenate(outs[c * group : (c + 1) * group], axis=0)
        first, second = part[:half], part[half:]
        kept = jnp.where(upper == 0, first, second)
        sent = jnp.where(upper == 0, second, first)
        came = permute_devices(sent, dp, mp, swap)
        cond = jnp.where(upper == 0, kept, came)
        uncond = jnp.where(upper == 0, came, kept)
        mixed = (
            (1.0 + GUIDE) * modulate(cond, head_cond) - GUIDE * modulate(uncond, head_uncond)
        ).astype(jnp.bfloat16)
        crossed = permute_devices(mixed, dp, mp, cross)
        mixed = jnp.where(stays, mixed, crossed)
        gathered = lax.all_gather(mixed, "mp", axis=0, tiled=True)
        logits = jnp.dot(gathered, head_weight, preferred_element_type=jnp.float32) + head_bias
        logits = logits.reshape(2, half_mp, half, vocab)
        order = jnp.transpose(logits, (1, 0, 2, 3)).reshape(pairs, NEW // rows, 2, half, vocab)
        scores = order + noise[:, :, c]
        peak = jnp.max(scores, axis=-1)
        weights = jnp.exp(scores - peak[..., None]).astype(jnp.bfloat16)
        totals.append(jnp.sum(weights.astype(jnp.float32), axis=-1))
        codes.append(jnp.dot(weights, codebook, preferred_element_type=jnp.float32))
        peaks.append(peak)
    stack = lambda parts: jnp.stack(parts, axis=2)
    peak = stack(peaks).reshape(pairs, 1, NEW)
    total = stack(totals).reshape(pairs, 1, NEW)
    code = stack(codes).reshape(pairs, NEW, channels).transpose(0, 2, 1)
    stats = jnp.concatenate([code, total, peak], axis=1)

    cells = f_hat.shape[2]
    band = cells // SIDE
    padded = jnp.pad(stats, ((0, 0), (0, 0), (SIDE, SIDE)))
    windows = jnp.stack(
        [padded[:, :, m * cells : m * cells + cells + 2 * SIDE] for m in range(mp)], axis=0
    )
    parts = lax.all_to_all(windows, "mp", 0, 0, tiled=True)
    top = jnp.max(parts[:, :, channels + 1], axis=0)
    factor = jnp.exp(parts[:, :, channels + 1] - top[None])[:, :, None]
    sums = jnp.sum(parts[:, :, : channels + 1] * factor, axis=0)
    cell_index = m_index * cells - SIDE + jnp.arange(cells + 2 * SIDE)
    inside = (cell_index >= 0) & (cell_index < NEW)
    soft = jnp.where(inside, sums[:, :channels] / jnp.where(inside, sums[:, channels:], 1.0), 0.0)
    code_map = soft.reshape(pairs, channels, band + 2, SIDE)
    wide = jnp.pad(code_map, ((0, 0), (0, 0), (0, 0), (1, 1)))
    taps = jnp.stack(
        [wide[:, :, i : i + band, j : j + SIDE] for i in range(3) for j in range(3)], axis=2
    ).reshape(pairs, channels * 9, cells)
    conv = jnp.einsum(
        "ok,pkn->pon",
        phi_weight.reshape(channels, channels * 9),
        taps,
        precision=lax.Precision.HIGHEST,
        preferred_element_type=jnp.float32,
    ) + phi_bias[None, :, None]
    f_hat_out = f_hat + 0.5 * soft[:, :, SIDE : SIDE + cells] + 0.5 * conv
    return (block_out, f_hat_out)


SCALARS = pl.BlockSpec(memory_space=pltpu.SMEM)
ON_CHIP = pl.BlockSpec(memory_space=pltpu.VMEM)
VMEM_LIMIT = 16 * 1024 * 1024
AHEAD = 40_000_000_000
MID, UPPER, IMAGE, ODD, SAME, CORE = range(6)


def call(kernel, where, args, outs, scratch=(), flops=0, specs=None, limit=VMEM_LIMIT):
    return pl.pallas_call(
        kernel,
        out_shape=outs,
        in_specs=[SCALARS] + (specs or [ON_CHIP] * len(args)),
        out_specs=[ON_CHIP] * len(outs),
        scratch_shapes=scratch,
        compiler_params=pltpu.CompilerParams(vmem_limit_bytes=limit),
        cost_estimate=pl.CostEstimate(flops=flops, bytes_accessed=0, transcendentals=0),
    )(where, *args)


def shape_of(shape, kind=jnp.bfloat16):
    return jax.ShapeDtypeStruct(shape, kind)


def after(value, *others):
    return lax.optimization_barrier((value, *others))[0]


def modulated(values, ada_ref, image):
    shift, scale = ada_ref[image, 0:1, :], ada_ref[image, 1:2, :]
    return norm_rows(values.astype(jnp.float32)) * (1.0 + scale) + shift


def norm_kernel(begin, where_ref, tokens_ref, ada_ref, out_ref):
    values = tokens_ref[begin : begin + out_ref.shape[0], :]
    out_ref[...] = modulated(values, ada_ref, where_ref[IMAGE]).astype(jnp.bfloat16)


def norm_part(where, tokens, ada, begin, size):
    outs = [shape_of((size, tokens.shape[1]))]
    return call(functools.partial(norm_kernel, begin), where, (tokens, ada), outs)[0]


def ffn_kernel(groups, tile, fetch, where_ref, *refs):
    count = sum(groups)
    parts = refs[:count]
    up_a, up_b, down_a, down_b, bias_a, bias_b = refs[count : count + 6]
    outs = refs[count + 6 : count + 6 + len(groups)]
    x_ref, hidden_ref, *own = refs[count + 6 + len(groups) :]
    order = list(range(0, 2 * down_a.shape[0], tile))
    copies = []
    if fetch:
        up_own, down_own, sems = own
        copies = [
            pltpu.make_async_copy(up_a, up_own, sems.at[0]),
            pltpu.make_async_copy(down_a, down_own, sems.at[1]),
        ]
        for copy in copies:
            copy.start()
        up_a, down_a = up_own, down_own
        order = [t for t in order if t >= down_a.shape[0]] + [t for t in order if t < down_a.shape[0]]
    panel, width = down_a.shape
    step = outs[0].shape[0]
    place = 0
    for g, size in enumerate(groups):
        if size == 1:
            value = parts[place][...]
        else:
            value = jnp.where(where_ref[MID] == 1, parts[place][...], parts[place + 1][...])
        x_ref[g * step : (g + 1) * step, :] = value
        place += size

    def columns(first, second, begin, end):
        if end <= panel:
            return first[:, begin:end]
        if begin >= panel:
            return second[:, begin - panel : end - panel]
        return jnp.concatenate([first[:, begin:panel], second[:, : end - panel]], axis=1)

    for begin in order:
        end = begin + tile
        if fetch and begin == 0:
            copies[0].wait()
        v = jnp.dot(x_ref[...], columns(up_a, up_b, begin, end), preferred_element_type=jnp.float32)
        v = v + columns(bias_a, bias_b, begin, end)
        hidden_ref[:, begin:end] = jax.nn.gelu(v, approximate=True).astype(jnp.bfloat16)
    if fetch:
        copies[1].wait()
    for begin in range(0, width, tile):
        cols = slice(begin, begin + tile)
        weight = jnp.concatenate([down_a[:, cols], down_b[:, cols]], axis=0)
        result = jnp.dot(hidden_ref[...], weight, preferred_element_type=jnp.float32)
        for g in range(len(groups)):
            outs[g][:, cols] = result[g * step : (g + 1) * step].astype(jnp.bfloat16)


def ffn(where, slots, panels, fetch=False):
    groups = tuple(len(slot) for slot in slots)
    parts = [part for slot in slots for part in slot]
    rows, width = parts[0].shape
    total = rows * len(slots)
    up, down = panels[0], panels[2]
    if fetch:
        panels = [
            pltpu.with_memory_space_constraint(p, pltpu.HBM) if i in (0, 2) else p for i, p in enumerate(panels)
        ]
    own = [pltpu.VMEM(up.shape, up.dtype), pltpu.VMEM(down.shape, down.dtype), pltpu.SemaphoreType.DMA((2,))]
    in_place = pl.BlockSpec(memory_space=pltpu.HBM)
    specs = [in_place if fetch and i in (0, 2) else ON_CHIP for i in range(len(panels))]
    return call(
        functools.partial(ffn_kernel, groups, 256, fetch),
        where,
        (*parts, *panels),
        [shape_of((rows, width))] * len(slots),
        scratch=[
            pltpu.VMEM((total, width), jnp.bfloat16),
            pltpu.VMEM((total, 2 * down.shape[0]), jnp.bfloat16),
            *(own if fetch else []),
        ],
        specs=[ON_CHIP] * len(parts) + specs,
        limit=VMEM_LIMIT + 8 * 1024 * 1024 if fetch else VMEM_LIMIT,
    )


def add_kernel(always, where_ref, a_ref, b_ref, out_ref):
    b = b_ref[...].astype(jnp.float32)
    if not always:
        b = jnp.where(where_ref[MID] == 1, b, 0.0)
    out_ref[...] = (a_ref[...].astype(jnp.float32) + b).astype(jnp.bfloat16)


def add(where, a, b, always=False, flops=0):
    return call(functools.partial(add_kernel, always), where, (a, b), [shape_of(a.shape)], flops=flops)[0]


def out_kernel(begin, always, where_ref, own_ref, near_ref, far_ref, tokens_ref, gate_ref, bias_ref, *refs):
    out_ref, kept_ref, sent_ref = refs[-3:]
    far = far_ref[...].astype(jnp.float32)
    if not always:
        far = jnp.where(where_ref[MID] == 1, far, 0.0)
    summed = own_ref[...].astype(jnp.float32) + near_ref[...].astype(jnp.float32) + far
    rows = summed.shape[0]
    tokens = tokens_ref[begin : begin + rows, :].astype(jnp.float32)
    gate = gate_ref[pl.ds(where_ref[IMAGE], 1), :]
    value = (tokens + gate * (summed + bias_ref[...])).astype(jnp.bfloat16)
    if len(refs) > 3:
        out_ref[0:begin, :] = refs[0][...]
        out_ref[begin : begin + rows, :] = value
    else:
        out_ref[...] = value
    half = rows // 2
    lower = where_ref[UPPER] == 0
    kept_ref[...] = jnp.where(lower, value[:half], value[half:])
    sent_ref[...] = jnp.where(lower, value[half:], value[:half])


def block_rows(where, begin, always, own, near, far, tokens, gate, bias, earlier=()):
    rows, width = own.shape
    full = rows + begin if earlier else rows
    return call(
        functools.partial(out_kernel, begin, always),
        where,
        (own, near, far, tokens, gate, bias, *earlier),
        [shape_of((full, width)), shape_of((rows // 2, width)), shape_of((rows // 2, width))],
    )


def mix_kernel(where_ref, kept_ref, came_ref, ada_ref, twin_ref, out_ref):
    image = where_ref[IMAGE]
    kept, came = modulated(kept_ref[...], ada_ref, image), modulated(came_ref[...], twin_ref, image)
    lower = where_ref[UPPER] == 0
    share = jnp.where(lower, 1.0 + GUIDE, -GUIDE)
    other = jnp.where(lower, -GUIDE, 1.0 + GUIDE)
    out_ref[...] = (share * kept + other * came).astype(jnp.bfloat16)


def mix_twins(where, kept, came, ada, twin):
    return call(mix_kernel, where, (kept, came, ada, twin), [shape_of(kept.shape)])[0]


def head_kernel(
    begin, where_ref, own_ref, near_ref, far_ref, last_ref, weight_a, weight_b, bias_a, bias_b, code_a, code_b,
    noise_own, noise_core, noise_twin, noise_both, stats_ref, x_ref
):
    step = own_ref.shape[0]
    for r, ref in enumerate((own_ref, near_ref, far_ref, last_ref)):
        x_ref[r * step : (r + 1) * step, :] = ref[...]
    x = x_ref[...]
    odd = where_ref[ODD]
    even = 1 - odd
    same = where_ref[SAME] == 1
    scores = []
    for weight, bias, ours, theirs in (
        (weight_a, bias_a, noise_own, noise_twin),
        (weight_b, bias_b, noise_core, noise_both),
    ):
        picked = []
        for first in (True, False):
            for block in (odd, even):
                a, b = ours[block, begin : begin + step, :], theirs[block, begin : begin + step, :]
                picked.append(jnp.where(same, a, b) if first else jnp.where(same, b, a))
        logits = jnp.dot(x, weight[...], preferred_element_type=jnp.float32)
        scores.append(logits + bias[:, bias.shape[1] - weight.shape[1] :] + jnp.concatenate(picked, axis=0))
    peak = jnp.max(jnp.maximum(scores[0], scores[1]), axis=1, keepdims=True)
    sums = 0.0
    total = 0.0
    for score, code in zip(scores, (code_a, code_b)):
        weights = jnp.exp(score - peak).astype(jnp.bfloat16)
        total = total + jnp.sum(weights.astype(jnp.float32), axis=1, keepdims=True)
        sums = sums + lax.dot_general(
            weights, code[...], (((1,), (1,)), ((), ())), preferred_element_type=jnp.float32
        )
    channels = code_a.shape[0]
    pad = jnp.zeros((4 * step, 128 - channels), jnp.float32)
    table = jnp.concatenate([sums, pad], axis=1)
    lane = lax.broadcasted_iota(jnp.int32, table.shape, 1)
    table = jnp.where(lane == channels, total, table)
    table = jnp.where(lane == channels + 1, peak, table)
    stats_ref[...] = jnp.transpose(table)[: stats_ref.shape[0], :]


def head_stats(where, begin, slots, heads, noises, flops=0):
    step, width = slots[0].shape
    height = -(-(heads[-1].shape[0] + 2) // 8) * 8
    return call(
        functools.partial(head_kernel, begin),
        where,
        (*slots, *heads, *noises),
        [shape_of((height, 4 * step), jnp.float32)],
        scratch=[pltpu.VMEM((4 * step, width), jnp.bfloat16)],
        flops=flops,
    )[0]


def soft_kernel(channels, where_ref, *refs):
    parts, out_ref = refs[:-1], refs[-1]
    tops = [part[channels + 1 : channels + 2, :] for part in parts]
    top = functools.reduce(jnp.maximum, tops)
    code = 0.0
    total = 0.0
    for part, peak in zip(parts, tops):
        factor = jnp.exp(peak - top)
        code = code + part[0:channels, :] * factor
        total = total + part[channels : channels + 1, :] * factor
    out_ref[...] = code / total


def soft_codes(where, parts, channels):
    outs = [shape_of((channels, parts[0].shape[1]), jnp.float32)]
    return call(functools.partial(soft_kernel, channels), where, tuple(parts), outs)[0]


def refine_kernel(where_ref, first_ref, second_ref, halo_ref, phi_ref, bias_ref, map_ref, out_ref):
    first, second, halo = first_ref[...], second_ref[...], halo_ref[...]
    cells = first.shape[1]
    half = cells // 2
    lane = lax.broadcasted_iota(jnp.int32, first.shape, 1)
    shift = lambda value, by: pltpu.roll(value, by % cells, 1)
    early = where_ref[CORE] == 0
    lower, higher = jnp.where(early, first, second), jnp.where(early, second, first)
    centre = jnp.where(
        early,
        jnp.where(lane < half, lower, shift(higher, half)),
        jnp.where(lane < half, shift(lower, half), higher),
    )
    above = jnp.where(early, shift(halo, SIDE), shift(higher, SIDE - half))
    below = jnp.where(early, shift(lower, half - SIDE), shift(halo, -SIDE))
    rows = (
        jnp.where(lane < SIDE, above, shift(centre, SIDE)),
        centre,
        jnp.where(lane >= cells - SIDE, below, shift(centre, -SIDE)),
    )
    column = lane % SIDE
    conv = jnp.zeros(out_ref.shape, jnp.float32) + bias_ref[...]
    for i, row in enumerate(rows):
        left = jnp.where(column == 0, 0.0, shift(row, 1))
        right = jnp.where(column == SIDE - 1, 0.0, shift(row, -1))
        for j, tap in enumerate((left, row, right)):
            conv = conv + jnp.dot(
                phi_ref[i, j], tap, precision=lax.Precision.HIGHEST, preferred_element_type=jnp.float32
            )
    out_ref[...] = map_ref[...] + 0.5 * centre + 0.5 * conv


def line_body(
    tokens,
    ada_ffn,
    ffn_gate,
    up_weight,
    up_bias,
    down_weight,
    down_bias,
    ada_head,
    head_weight,
    head_bias,
    gumbel_noise,
    codebook,
    phi_weight,
    phi_bias,
    f_hat,
):
    rows = tokens.shape[0]
    dp, mp = lax.axis_size("dp"), lax.axis_size("mp")
    d_index, m_index = lax.axis_index("dp"), lax.axis_index("mp")
    channels = f_hat.shape[1]
    half_dp = dp // 2
    upper = d_index // half_dp
    z_index, core = m_index // 2, m_index % 2
    where = jnp.stack(
        [
            (z_index == 1) | (z_index == 2),
            upper,
            (m_index * rows) // NEW,
            z_index % 2,
            z_index // 2 == upper,
            core,
        ]
    ).astype(jnp.int32)

    def along_z(value, target):
        def to(d, m):
            z = target(m // 2)
            return None if z is None else (d, 2 * z + m % 2)

        return permute_devices(value, dp, mp, to)

    def near(value):
        return along_z(value, lambda z: z ^ 1)

    def across(value):
        return along_z(value, lambda z: z ^ 2)

    def middle(value):
        return along_z(value, lambda z: 3 - z if z in (1, 2) else z)

    def outward(value):
        return along_z(value, lambda z: {1: 0, 2: 3}.get(z))

    def inward(value):
        return along_z(value, lambda z: {0: 1, 3: 2}.get(z))

    def swap_cores(value):
        return permute_devices(value, dp, mp, lambda d, m: (d, m ^ 1))

    def swap_twins(value):
        return permute_devices(value, dp, mp, lambda d, m: ((d + half_dp) % dp, m))

    def swap_both(value):
        return permute_devices(value, dp, mp, lambda d, m: ((d + half_dp) % dp, m ^ 1))

    step = rows // CHUNKS
    half = step // 2
    voc = head_bias.shape[0]
    noise = gumbel_noise.reshape(2, 2, CHUNKS, 2, half, voc)

    def noise_for(to_core, to_upper):
        picked = lax.dynamic_slice(
            noise, (0, to_core, 0, to_upper, 0, 0), (2, 1, CHUNKS, 1, half, voc)
        )
        return picked.reshape(2, CHUNKS * half, voc)

    gate, bias_out = ffn_gate, down_bias[None]
    up_other, down_other = swap_cores(up_weight), swap_cores(down_weight)
    biases = jnp.concatenate([up_bias, head_bias])[None]
    codes = codebook.T
    bias_other = swap_cores(biases)

    barrier = lax.optimization_barrier
    own_a = norm_part(where, tokens, ada_ffn, 0, step)
    near_a, mid_a = near(own_a), middle(own_a)
    own_b = norm_part(where, tokens, ada_ffn, step, step)
    noise_own, noise_twin, noise_core, noise_both = (
        noise_for(core, upper),
        noise_for(core, 1 - upper),
        noise_for(1 - core, upper),
        noise_for(1 - core, 1 - upper),
    )
    noise_twin, noise_core, noise_both, _ = barrier((noise_twin, noise_core, noise_both, own_b))
    noise_twin = swap_twins(noise_twin)
    up_other, down_other, bias_other, near_a, own_b = barrier((up_other, down_other, bias_other, near_a, own_b))
    panels = (up_weight, up_other, down_weight, down_other, biases, bias_other)
    far_mid_a = middle(near_a)
    near_b = near(after(own_b, near_a))
    mid_a = after(mid_a, near_a)
    far_end_a = outward(mid_a)
    sum_own_a, sum_near_a = ffn(where, [[own_a], [after(near_a, mid_a)]], panels, fetch=True)
    far_mid_a = after(far_mid_a, sum_near_a)
    last_end_a = outward(far_mid_a)
    mid_b = middle(after(own_b, far_mid_a))
    noise_core = swap_cores(after(noise_core, far_mid_a))
    head_twin = swap_twins(after(ada_head, far_mid_a))
    (sum_far_a,) = ffn(where, [[far_mid_a, far_end_a]], panels)
    came_far_a = inward(sum_far_a)
    near_b, mid_b = barrier((near_b, mid_b, sum_far_a))[:2]
    far_mid_b, far_end_b = middle(near_b), outward(mid_b)
    (sum_last_a,) = ffn(where, [[mid_a, after(last_end_a, near_b, mid_b, noise_twin, head_twin)]], panels)
    came_last_a = inward(sum_last_a)
    noise_both = swap_both(after(noise_both, noise_twin))
    sum_own_b, sum_near_b = ffn(where, [[after(own_b, sum_last_a, noise_core)], [near_b]], panels)
    both_last_a = add(where, after(sum_last_a, sum_near_b), came_far_a)
    went_last_a = middle(both_last_a)
    far_mid_b, far_end_b = barrier((far_mid_b, far_end_b, both_last_a))[:2]
    last_end_b = outward(far_mid_b)
    (sum_far_b,) = ffn(where, [[far_mid_b, far_end_b]], panels)
    both_far_a = add(where, after(sum_far_a, sum_far_b), came_last_a)
    went_far_a = middle(both_far_a)
    (sum_last_b,) = ffn(where, [[after(mid_b, both_far_a, went_last_a), last_end_b]], panels)
    came_last_b = near(sum_last_b)
    head_other = swap_cores(after(head_weight, sum_last_b))
    code_other = swap_cores(after(codes, sum_last_b))
    came_near_b = near(after(sum_near_b, last_end_b))
    both_near_a = add(where, sum_near_a, after(went_far_a, went_last_a, came_near_b), flops=AHEAD)
    came_near_a = near(both_near_a)
    both_far_b = add(where, after(sum_far_b, both_near_a), came_last_b, True)
    went_far_b = across(both_far_b)
    out_a, kept_a, sent_a = block_rows(
        where, 0, False, sum_own_a, after(came_near_a, noise_both), went_last_a, tokens, gate, bias_out
    )
    came_a = swap_twins(sent_a)
    mixed_a = mix_twins(where, kept_a, came_a, ada_head, head_twin)
    mix_near_a, mix_far_a = near(mixed_a), across(mixed_a)
    block_out, kept_b, sent_b = block_rows(
        where, step, True, sum_own_b, after(came_near_b, mixed_a, head_other, code_other), went_far_b, tokens, gate, bias_out, (out_a,)
    )
    came_b = after(swap_twins(sent_b), mix_far_a)
    mix_last_a = near(mix_far_a)
    mixed_b = mix_twins(where, kept_b, came_b, ada_head, head_twin)
    mix_near_b, mix_far_b = near(mixed_b), across(mixed_b)
    heads = (head_weight, head_other, biases, bias_other, codes, code_other)
    noises = (noise_own, noise_core, noise_twin, noise_both)
    stats_a = head_stats(
        where, 0, (after(mixed_a, mixed_b), mix_near_a, mix_far_a, mix_last_a), heads, noises, flops=AHEAD
    )
    mix_last_b = near(after(mix_far_b, stats_a))
    stats_b = head_stats(where, half, (after(mixed_b, stats_a), mix_near_b, mix_far_b, mix_last_b), heads, noises)

    slots = [
        jnp.concatenate([part[:, r * half : (r + 1) * half] for part in (stats_a, stats_b)], axis=1) for r in range(4)
    ]
    parts = [slots[0]] + [along_z(slots[r], lambda z, r=r: z ^ r) for r in (1, 2, 3)]
    soft = soft_codes(where, parts, channels)

    def to_cells(d, m, core_of):
        y, x = d // half_dp, d % half_dp
        z, c = m // 2, m % 2
        return ((z // 2) * half_dp + x, 2 * (2 * (z % 2) + c) + core_of(y))

    def to_halo(d, m):
        y, x = d // half_dp, d % half_dp
        z, c = m // 2, m % 2
        block = 2 * (z % 2) + c + (1 if y == 1 else -1)
        if block < 0 or block > 3:
            return None
        return ((z // 2) * half_dp + x, 2 * block + (0 if y == 1 else 1))

    first = permute_devices(soft, dp, mp, lambda d, m: to_cells(d, m, lambda y: y))
    second = permute_devices(soft, dp, mp, lambda d, m: to_cells(d, m, lambda y: 1 - y))
    halo = permute_devices(soft, dp, mp, to_halo)
    f_hat_out = call(
        refine_kernel,
        where,
        (first, second, halo, jnp.transpose(phi_weight, (2, 3, 0, 1)), phi_bias[:, None], f_hat[0]),
        [shape_of(f_hat.shape[1:], jnp.float32)],
    )[0]
    return (block_out, f_hat_out[None])


def solution(mesh):
    in_specs = (
        P(("dp", "mp"), None),
        P("dp", None, None),
        P("dp", None),
        P(None, "mp"),
        P("mp"),
        P("mp", None),
        P(),
        P("dp", None, None),
        P(None, "mp"),
        P("mp"),
        P("dp", None, "mp"),
        P("mp", None),
        P(),
        P(),
        P("dp", None, "mp"),
    )
    out_specs = (P(("dp", "mp"), None), P("dp", None, "mp"))
    line = mesh.shape["dp"] == 4 and mesh.shape["mp"] == 8
    body = line_body if line else general_body
    return jax.shard_map(body, mesh=mesh, in_specs=in_specs, out_specs=out_specs, check_vma=False)
```

```python
import functools

import jax
import jax.numpy as jnp
from jax import lax
from jax.experimental import pallas as pl
from jax.experimental.pallas import tpu as pltpu
from jax.sharding import PartitionSpec as P

SIDE = 32
NEW = 1024
GUIDE = 1.5
CHUNKS = 2
FLOWS = 4
HEAD_FLOWS = 2


def norm_rows(values):
    row_mean = jnp.mean(values, axis=-1, keepdims=True)
    centred = values - row_mean
    spread = jnp.mean(centred * centred, axis=-1, keepdims=True)
    return centred * lax.rsqrt(spread + 1e-06)


def modulate(values, ada):
    return norm_rows(values.astype(jnp.float32)) * (1.0 + ada[1]) + ada[0]


def permute_devices(value, dp, mp, target):
    pairs = []
    for d in range(dp):
        for m in range(mp):
            to = target(d, m)
            if to is not None:
                pairs.append((d * mp + m, to[0] * mp + to[1]))
    return lax.ppermute(value, ("dp", "mp"), pairs)


def general_body(
    tokens,
    ada_ffn,
    ffn_gate,
    up_weight,
    up_bias,
    down_weight,
    down_bias,
    ada_head,
    head_weight,
    head_bias,
    gumbel_noise,
    codebook,
    phi_weight,
    phi_bias,
    f_hat,
):
    rows, width = tokens.shape
    dp, mp = lax.axis_size("dp"), lax.axis_size("mp")
    d_index, m_index = lax.axis_index("dp"), lax.axis_index("mp")
    images = ada_ffn.shape[0]
    pairs = f_hat.shape[0]
    channels = f_hat.shape[1]
    vocab = head_weight.shape[1]
    own_image = (m_index * rows) // NEW
    ada_own = lax.dynamic_index_in_dim(ada_ffn, own_image, 0, keepdims=False)
    gate_own = lax.dynamic_index_in_dim(ffn_gate, own_image, 0, keepdims=False)
    head_own = lax.dynamic_index_in_dim(ada_head, own_image, 0, keepdims=False)
    half_dp, half_mp = dp // 2, mp // 2
    upper = d_index // half_dp

    def swap(d, m):
        return ((d + half_dp) % dp, m)

    def cross(d, m):
        if d // half_dp == m // half_mp:
            return None
        return ((d + half_dp) % dp, (m + half_mp) % mp)

    stays = upper == m_index // half_mp
    head_twin = permute_devices(head_own, dp, mp, swap)
    head_cond = jnp.where(upper == 0, head_own, head_twin)
    head_uncond = jnp.where(upper == 0, head_twin, head_own)

    step = rows // FLOWS
    normed = modulate(tokens, ada_own).astype(jnp.bfloat16)
    outs = []
    for c in range(FLOWS):
        part = lax.slice_in_dim(normed, c * step, (c + 1) * step, axis=0)
        gathered = lax.all_gather(part, "mp", axis=0, tiled=True)
        hidden = jax.nn.gelu(
            jnp.dot(gathered, up_weight, preferred_element_type=jnp.float32) + up_bias,
            approximate=True,
        ).astype(jnp.bfloat16)
        partial = jnp.dot(hidden, down_weight, preferred_element_type=jnp.float32).astype(jnp.bfloat16)
        summed = lax.psum_scatter(partial, "mp", scatter_dimension=0, tiled=True).astype(jnp.float32)
        own = lax.slice_in_dim(tokens, c * step, (c + 1) * step, axis=0).astype(jnp.float32)
        outs.append((own + gate_own * (summed + down_bias)).astype(jnp.bfloat16))
    block_out = jnp.concatenate(outs, axis=0)

    group = FLOWS // HEAD_FLOWS
    half = rows // HEAD_FLOWS // 2
    noise = gumbel_noise.reshape(pairs, NEW // rows, HEAD_FLOWS, 2, half, vocab)
    peaks, totals, codes = [], [], []
    for c in range(HEAD_FLOWS):
        part = jnp.concatenate(outs[c * group : (c + 1) * group], axis=0)
        first, second = part[:half], part[half:]
        kept = jnp.where(upper == 0, first, second)
        sent = jnp.where(upper == 0, second, first)
        came = permute_devices(sent, dp, mp, swap)
        cond = jnp.where(upper == 0, kept, came)
        uncond = jnp.where(upper == 0, came, kept)
        mixed = (
            (1.0 + GUIDE) * modulate(cond, head_cond) - GUIDE * modulate(uncond, head_uncond)
        ).astype(jnp.bfloat16)
        crossed = permute_devices(mixed, dp, mp, cross)
        mixed = jnp.where(stays, mixed, crossed)
        gathered = lax.all_gather(mixed, "mp", axis=0, tiled=True)
        logits = jnp.dot(gathered, head_weight, preferred_element_type=jnp.float32) + head_bias
        logits = logits.reshape(2, half_mp, half, vocab)
        order = jnp.transpose(logits, (1, 0, 2, 3)).reshape(pairs, NEW // rows, 2, half, vocab)
        scores = order + noise[:, :, c]
        peak = jnp.max(scores, axis=-1)
        weights = jnp.exp(scores - peak[..., None]).astype(jnp.bfloat16)
        totals.append(jnp.sum(weights.astype(jnp.float32), axis=-1))
        codes.append(jnp.dot(weights, codebook, preferred_element_type=jnp.float32))
        peaks.append(peak)
    stack = lambda parts: jnp.stack(parts, axis=2)
    peak = stack(peaks).reshape(pairs, 1, NEW)
    total = stack(totals).reshape(pairs, 1, NEW)
    code = stack(codes).reshape(pairs, NEW, channels).transpose(0, 2, 1)
    stats = jnp.concatenate([code, total, peak], axis=1)

    cells = f_hat.shape[2]
    band = cells // SIDE
    padded = jnp.pad(stats, ((0, 0), (0, 0), (SIDE, SIDE)))
    windows = jnp.stack(
        [padded[:, :, m * cells : m * cells + cells + 2 * SIDE] for m in range(mp)], axis=0
    )
    parts = lax.all_to_all(windows, "mp", 0, 0, tiled=True)
    top = jnp.max(parts[:, :, channels + 1], axis=0)
    factor = jnp.exp(parts[:, :, channels + 1] - top[None])[:, :, None]
    sums = jnp.sum(parts[:, :, : channels + 1] * factor, axis=0)
    cell_index = m_index * cells - SIDE + jnp.arange(cells + 2 * SIDE)
    inside = (cell_index >= 0) & (cell_index < NEW)
    soft = jnp.where(inside, sums[:, :channels] / jnp.where(inside, sums[:, channels:], 1.0), 0.0)
    code_map = soft.reshape(pairs, channels, band + 2, SIDE)
    wide = jnp.pad(code_map, ((0, 0), (0, 0), (0, 0), (1, 1)))
    taps = jnp.stack(
        [wide[:, :, i : i + band, j : j + SIDE] for i in range(3) for j in range(3)], axis=2
    ).reshape(pairs, channels * 9, cells)
    conv = jnp.einsum(
        "ok,pkn->pon",
        phi_weight.reshape(channels, channels * 9),
        taps,
        precision=lax.Precision.HIGHEST,
        preferred_element_type=jnp.float32,
    ) + phi_bias[None, :, None]
    f_hat_out = f_hat + 0.5 * soft[:, :, SIDE : SIDE + cells] + 0.5 * conv
    return (block_out, f_hat_out)


SCALARS = pl.BlockSpec(memory_space=pltpu.SMEM)
ON_CHIP = pl.BlockSpec(memory_space=pltpu.VMEM)
VMEM_LIMIT = 16 * 1024 * 1024
AHEAD = 40_000_000_000
MID, UPPER, IMAGE, ODD, SAME, CORE = range(6)


def call(kernel, where, args, outs, scratch=(), flops=0, specs=None, limit=VMEM_LIMIT):
    return pl.pallas_call(
        kernel,
        out_shape=outs,
        in_specs=[SCALARS] + (specs or [ON_CHIP] * len(args)),
        out_specs=[ON_CHIP] * len(outs),
        scratch_shapes=scratch,
        compiler_params=pltpu.CompilerParams(vmem_limit_bytes=limit),
        cost_estimate=pl.CostEstimate(flops=flops, bytes_accessed=0, transcendentals=0),
    )(where, *args)


def shape_of(shape, kind=jnp.bfloat16):
    return jax.ShapeDtypeStruct(shape, kind)


def after(value, *others):
    return lax.optimization_barrier((value, *others))[0]


def modulated(values, ada_ref, image):
    shift, scale = ada_ref[image, 0:1, :], ada_ref[image, 1:2, :]
    return norm_rows(values.astype(jnp.float32)) * (1.0 + scale) + shift


def norm_kernel(begin, where_ref, tokens_ref, ada_ref, out_ref):
    values = tokens_ref[begin : begin + out_ref.shape[0], :]
    out_ref[...] = modulated(values, ada_ref, where_ref[IMAGE]).astype(jnp.bfloat16)


def norm_part(where, tokens, ada, begin, size):
    outs = [shape_of((size, tokens.shape[1]))]
    return call(functools.partial(norm_kernel, begin), where, (tokens, ada), outs)[0]


def ffn_kernel(groups, tile, fetch, where_ref, *refs):
    count = sum(groups)
    parts = refs[:count]
    up_a, up_b, down_a, down_b, bias_a, bias_b = refs[count : count + 6]
    outs = refs[count + 6 : count + 6 + len(groups)]
    x_ref, hidden_ref, *own = refs[count + 6 + len(groups) :]
    order = list(range(0, 2 * down_a.shape[0], tile))
    copies = []
    if fetch:
        up_own, down_own, sems = own
        copies = [
            pltpu.make_async_copy(up_a, up_own, sems.at[0]),
            pltpu.make_async_copy(down_a, down_own, sems.at[1]),
        ]
        for copy in copies:
            copy.start()
        up_a, down_a = up_own, down_own
        order = [t for t in order if t >= down_a.shape[0]] + [t for t in order if t < down_a.shape[0]]
    panel, width = down_a.shape
    step = outs[0].shape[0]
    place = 0
    for g, size in enumerate(groups):
        if size == 1:
            value = parts[place][...]
        else:
            value = jnp.where(where_ref[MID] == 1, parts[place][...], parts[place + 1][...])
        x_ref[g * step : (g + 1) * step, :] = value
        place += size

    def columns(first, second, begin, end):
        if end <= panel:
            return first[:, begin:end]
        if begin >= panel:
            return second[:, begin - panel : end - panel]
        return jnp.concatenate([first[:, begin:panel], second[:, : end - panel]], axis=1)

    for begin in order:
        end = begin + tile
        if fetch and begin == 0:
            copies[0].wait()
        v = jnp.dot(x_ref[...], columns(up_a, up_b, begin, end), preferred_element_type=jnp.float32)
        v = v + columns(bias_a, bias_b, begin, end)
        hidden_ref[:, begin:end] = jax.nn.gelu(v, approximate=True).astype(jnp.bfloat16)
    if fetch:
        copies[1].wait()
    for begin in range(0, width, tile):
        cols = slice(begin, begin + tile)
        weight = jnp.concatenate([down_a[:, cols], down_b[:, cols]], axis=0)
        result = jnp.dot(hidden_ref[...], weight, preferred_element_type=jnp.float32)
        for g in range(len(groups)):
            outs[g][:, cols] = result[g * step : (g + 1) * step].astype(jnp.bfloat16)


def ffn(where, slots, panels, fetch=False):
    groups = tuple(len(slot) for slot in slots)
    parts = [part for slot in slots for part in slot]
    rows, width = parts[0].shape
    total = rows * len(slots)
    up, down = panels[0], panels[2]
    if fetch:
        panels = [
            pltpu.with_memory_space_constraint(p, pltpu.HBM) if i in (0, 2) else p for i, p in enumerate(panels)
        ]
    own = [pltpu.VMEM(up.shape, up.dtype), pltpu.VMEM(down.shape, down.dtype), pltpu.SemaphoreType.DMA((2,))]
    in_place = pl.BlockSpec(memory_space=pltpu.HBM)
    specs = [in_place if fetch and i in (0, 2) else ON_CHIP for i in range(len(panels))]
    return call(
        functools.partial(ffn_kernel, groups, 256, fetch),
        where,
        (*parts, *panels),
        [shape_of((rows, width))] * len(slots),
        scratch=[
            pltpu.VMEM((total, width), jnp.bfloat16),
            pltpu.VMEM((total, 2 * down.shape[0]), jnp.bfloat16),
            *(own if fetch else []),
        ],
        specs=[ON_CHIP] * len(parts) + specs,
        limit=VMEM_LIMIT + 8 * 1024 * 1024 if fetch else VMEM_LIMIT,
    )


def add_kernel(begin, always, where_ref, *refs):
    out_ref = refs[-1]
    rows = refs[0].shape[0]
    for place, (a_ref, b_ref) in enumerate(zip(refs[:-1:2], refs[1:-1:2])):
        b = b_ref[begin : begin + rows, :].astype(jnp.float32)
        if not always:
            b = jnp.where(where_ref[MID] == 1, b, 0.0)
        total = (a_ref[...].astype(jnp.float32) + b).astype(jnp.bfloat16)
        out_ref[place * rows : (place + 1) * rows, :] = total


def add(where, *parts, begin=0, always=False, flops=0):
    rows, width = parts[0].shape
    outs = [shape_of((rows * len(parts) // 2, width))]
    return call(functools.partial(add_kernel, begin, always), where, parts, outs, flops=flops)[0]


def out_kernel(begin, always, where_ref, own_ref, near_ref, far_ref, tokens_ref, gate_ref, bias_ref, *refs):
    out_ref, kept_ref, sent_ref = refs[-3:]
    far = far_ref[0 : own_ref.shape[0], :].astype(jnp.float32)
    if not always:
        far = jnp.where(where_ref[MID] == 1, far, 0.0)
    summed = own_ref[...].astype(jnp.float32) + near_ref[...].astype(jnp.float32) + far
    rows = summed.shape[0]
    tokens = tokens_ref[begin : begin + rows, :].astype(jnp.float32)
    gate = gate_ref[pl.ds(where_ref[IMAGE], 1), :]
    value = (tokens + gate * (summed + bias_ref[...])).astype(jnp.bfloat16)
    if len(refs) > 3:
        out_ref[0:begin, :] = refs[0][...]
        out_ref[begin : begin + rows, :] = value
    else:
        out_ref[...] = value
    half = rows // 2
    lower = where_ref[UPPER] == 0
    kept_ref[...] = jnp.where(lower, value[:half], value[half:])
    sent_ref[...] = jnp.where(lower, value[half:], value[:half])


def block_rows(where, begin, always, own, near, far, tokens, gate, bias, earlier=()):
    rows, width = own.shape
    full = rows + begin if earlier else rows
    return call(
        functools.partial(out_kernel, begin, always),
        where,
        (own, near, far, tokens, gate, bias, *earlier),
        [shape_of((full, width)), shape_of((rows // 2, width)), shape_of((rows // 2, width))],
    )


def mix_kernel(where_ref, kept_ref, came_ref, ada_ref, twin_ref, out_ref):
    image = where_ref[IMAGE]
    kept, came = modulated(kept_ref[...], ada_ref, image), modulated(came_ref[...], twin_ref, image)
    lower = where_ref[UPPER] == 0
    share = jnp.where(lower, 1.0 + GUIDE, -GUIDE)
    other = jnp.where(lower, -GUIDE, 1.0 + GUIDE)
    out_ref[...] = (share * kept + other * came).astype(jnp.bfloat16)


def mix_twins(where, kept, came, ada, twin):
    return call(mix_kernel, where, (kept, came, ada, twin), [shape_of(kept.shape)])[0]


def head_kernel(
    begin, where_ref, own_ref, near_ref, far_ref, last_ref, weight_a, weight_b, bias_a, bias_b, code_a, code_b,
    noise_own, noise_core, noise_twin, noise_both, stats_ref, x_ref
):
    step = own_ref.shape[0]
    for r, ref in enumerate((own_ref, near_ref, far_ref, last_ref)):
        x_ref[r * step : (r + 1) * step, :] = ref[...]
    x = x_ref[...]
    odd = where_ref[ODD]
    even = 1 - odd
    same = where_ref[SAME] == 1
    scores = []
    for weight, bias, ours, theirs in (
        (weight_a, bias_a, noise_own, noise_twin),
        (weight_b, bias_b, noise_core, noise_both),
    ):
        picked = []
        for first in (True, False):
            for block in (odd, even):
                a, b = ours[block, begin : begin + step, :], theirs[block, begin : begin + step, :]
                picked.append(jnp.where(same, a, b) if first else jnp.where(same, b, a))
        logits = jnp.dot(x, weight[...], preferred_element_type=jnp.float32)
        scores.append(logits + bias[:, bias.shape[1] - weight.shape[1] :] + jnp.concatenate(picked, axis=0))
    peak = jnp.max(jnp.maximum(scores[0], scores[1]), axis=1, keepdims=True)
    sums = 0.0
    total = 0.0
    for score, code in zip(scores, (code_a, code_b)):
        weights = jnp.exp(score - peak).astype(jnp.bfloat16)
        total = total + jnp.sum(weights.astype(jnp.float32), axis=1, keepdims=True)
        sums = sums + lax.dot_general(
            weights, code[...], (((1,), (1,)), ((), ())), preferred_element_type=jnp.float32
        )
    channels = code_a.shape[0]
    pad = jnp.zeros((4 * step, 128 - channels), jnp.float32)
    table = jnp.concatenate([sums, pad], axis=1)
    lane = lax.broadcasted_iota(jnp.int32, table.shape, 1)
    table = jnp.where(lane == channels, total, table)
    table = jnp.where(lane == channels + 1, peak, table)
    stats_ref[...] = jnp.transpose(table)[: stats_ref.shape[0], :]


def head_stats(where, begin, slots, heads, noises, flops=0):
    step, width = slots[0].shape
    height = -(-(heads[-1].shape[0] + 2) // 8) * 8
    return call(
        functools.partial(head_kernel, begin),
        where,
        (*slots, *heads, *noises),
        [shape_of((height, 4 * step), jnp.float32)],
        scratch=[pltpu.VMEM((4 * step, width), jnp.bfloat16)],
        flops=flops,
    )[0]


def soft_kernel(channels, where_ref, *refs):
    parts, out_ref = refs[:-1], refs[-1]
    tops = [part[channels + 1 : channels + 2, :] for part in parts]
    top = functools.reduce(jnp.maximum, tops)
    code = 0.0
    total = 0.0
    for part, peak in zip(parts, tops):
        factor = jnp.exp(peak - top)
        code = code + part[0:channels, :] * factor
        total = total + part[channels : channels + 1, :] * factor
    out_ref[...] = code / total


def soft_codes(where, parts, channels):
    outs = [shape_of((channels, parts[0].shape[1]), jnp.float32)]
    return call(functools.partial(soft_kernel, channels), where, tuple(parts), outs)[0]


def refine_kernel(where_ref, first_ref, second_ref, halo_ref, phi_ref, bias_ref, map_ref, out_ref):
    first, second, halo = first_ref[...], second_ref[...], halo_ref[...]
    cells = first.shape[1]
    half = cells // 2
    lane = lax.broadcasted_iota(jnp.int32, first.shape, 1)
    shift = lambda value, by: pltpu.roll(value, by % cells, 1)
    early = where_ref[CORE] == 0
    lower, higher = jnp.where(early, first, second), jnp.where(early, second, first)
    centre = jnp.where(
        early,
        jnp.where(lane < half, lower, shift(higher, half)),
        jnp.where(lane < half, shift(lower, half), higher),
    )
    above = jnp.where(early, shift(halo, SIDE), shift(higher, SIDE - half))
    below = jnp.where(early, shift(lower, half - SIDE), shift(halo, -SIDE))
    rows = (
        jnp.where(lane < SIDE, above, shift(centre, SIDE)),
        centre,
        jnp.where(lane >= cells - SIDE, below, shift(centre, -SIDE)),
    )
    column = lane % SIDE
    conv = jnp.zeros(out_ref.shape, jnp.float32) + bias_ref[...]
    for i, row in enumerate(rows):
        left = jnp.where(column == 0, 0.0, shift(row, 1))
        right = jnp.where(column == SIDE - 1, 0.0, shift(row, -1))
        for j, tap in enumerate((left, row, right)):
            conv = conv + jnp.dot(
                phi_ref[i, j], tap, precision=lax.Precision.HIGHEST, preferred_element_type=jnp.float32
            )
    out_ref[...] = map_ref[...] + 0.5 * centre + 0.5 * conv


def line_body(
    tokens,
    ada_ffn,
    ffn_gate,
    up_weight,
    up_bias,
    down_weight,
    down_bias,
    ada_head,
    head_weight,
    head_bias,
    gumbel_noise,
    codebook,
    phi_weight,
    phi_bias,
    f_hat,
):
    rows = tokens.shape[0]
    dp, mp = lax.axis_size("dp"), lax.axis_size("mp")
    d_index, m_index = lax.axis_index("dp"), lax.axis_index("mp")
    channels = f_hat.shape[1]
    half_dp = dp // 2
    upper = d_index // half_dp
    z_index, core = m_index // 2, m_index % 2
    where = jnp.stack(
        [
            (z_index == 1) | (z_index == 2),
            upper,
            (m_index * rows) // NEW,
            z_index % 2,
            z_index // 2 == upper,
            core,
        ]
    ).astype(jnp.int32)

    def along_z(value, target):
        def to(d, m):
            z = target(m // 2)
            return None if z is None else (d, 2 * z + m % 2)

        return permute_devices(value, dp, mp, to)

    def near(value):
        return along_z(value, lambda z: z ^ 1)

    def across(value):
        return along_z(value, lambda z: z ^ 2)

    def middle(value):
        return along_z(value, lambda z: 3 - z if z in (1, 2) else z)

    def outward(value):
        return along_z(value, lambda z: {1: 0, 2: 3}.get(z))

    def inward(value):
        return along_z(value, lambda z: {0: 1, 3: 2}.get(z))

    def swap_cores(value):
        return permute_devices(value, dp, mp, lambda d, m: (d, m ^ 1))

    def swap_twins(value):
        return permute_devices(value, dp, mp, lambda d, m: ((d + half_dp) % dp, m))

    def swap_both(value):
        return permute_devices(value, dp, mp, lambda d, m: ((d + half_dp) % dp, m ^ 1))

    step = rows // CHUNKS
    half = step // 2
    voc = head_bias.shape[0]
    noise = gumbel_noise.reshape(2, 2, CHUNKS, 2, half, voc)

    def noise_for(to_core, to_upper):
        picked = lax.dynamic_slice(
            noise, (0, to_core, 0, to_upper, 0, 0), (2, 1, CHUNKS, 1, half, voc)
        )
        return picked.reshape(2, CHUNKS * half, voc)

    gate, bias_out = ffn_gate, down_bias[None]
    up_other, down_other = swap_cores(up_weight), swap_cores(down_weight)
    biases = jnp.concatenate([up_bias, head_bias])[None]
    codes = codebook.T
    bias_other = swap_cores(biases)

    barrier = lax.optimization_barrier
    own_a = norm_part(where, tokens, ada_ffn, 0, step)
    near_a, mid_a = near(own_a), middle(own_a)
    own_b = norm_part(where, tokens, ada_ffn, step, step)
    noise_own, noise_twin, noise_core, noise_both = (
        noise_for(core, upper),
        noise_for(core, 1 - upper),
        noise_for(1 - core, upper),
        noise_for(1 - core, 1 - upper),
    )
    head_twin = swap_twins(after(ada_head, own_a))
    up_other, down_other, bias_other, near_a, own_b, head_twin = barrier(
        (up_other, down_other, bias_other, near_a, own_b, head_twin)
    )
    panels = (up_weight, up_other, down_weight, down_other, biases, bias_other)
    far_mid_a = middle(near_a)
    near_b = near(after(own_b, near_a))
    mid_a = after(mid_a, near_a)
    far_end_a = outward(mid_a)
    noise_twin = swap_twins(after(noise_twin, near_a))
    sum_own_a, sum_near_a = ffn(where, [[own_a], [after(near_a, mid_a)]], panels, fetch=True)
    far_mid_a = after(far_mid_a, sum_near_a)
    last_end_a = outward(far_mid_a)
    mid_b = middle(after(own_b, far_mid_a))
    noise_core = swap_cores(after(noise_core, far_mid_a))
    (sum_far_a,) = ffn(where, [[far_mid_a, far_end_a]], panels)
    came_far_a = inward(sum_far_a)
    near_b, mid_b = barrier((near_b, mid_b, sum_far_a))[:2]
    far_mid_b, far_end_b = middle(near_b), outward(mid_b)
    sum_own_b, sum_near_b = ffn(where, [[after(own_b, sum_far_a)], [after(near_b, mid_b, noise_twin)]], panels)
    (sum_last_a,) = ffn(where, [[mid_a, after(last_end_a, sum_near_b, noise_core)]], panels)
    came_last_a = inward(sum_last_a)
    far_mid_b, far_end_b = barrier((far_mid_b, far_end_b, sum_last_a))[:2]
    last_end_b = outward(far_mid_b)
    noise_both = swap_both(after(noise_both, noise_twin))
    both_a = add(where, sum_last_a, after(came_far_a, far_mid_b), sum_far_a, came_last_a)
    went_a = middle(both_a)
    sum_far_b, sum_last_b = ffn(
        where, [[after(far_mid_b, both_a), far_end_b], [mid_b, last_end_b]], panels
    )
    came_last_b = near(sum_last_b)
    head_other = swap_cores(after(head_weight, sum_last_b))
    code_other = swap_cores(after(codes, sum_last_b))
    came_near_b = near(after(sum_near_b, last_end_b))
    both_near_a = add(where, sum_near_a, after(went_a, came_near_b), begin=step, flops=AHEAD)
    came_near_a = near(both_near_a)
    both_far_b = add(where, after(sum_far_b, both_near_a), came_last_b, always=True)
    went_far_b = across(both_far_b)
    out_a, kept_a, sent_a = block_rows(
        where, 0, False, sum_own_a, after(came_near_a, noise_both), went_a, tokens, gate, bias_out
    )
    came_a = swap_twins(sent_a)
    mixed_a = mix_twins(where, kept_a, came_a, ada_head, head_twin)
    mix_near_a, mix_far_a = near(mixed_a), across(mixed_a)
    block_out, kept_b, sent_b = block_rows(
        where, step, True, sum_own_b, after(came_near_b, mixed_a, head_other, code_other), went_far_b, tokens, gate, bias_out, (out_a,)
    )
    came_b = after(swap_twins(sent_b), mix_far_a)
    mix_last_a = near(mix_far_a)
    mixed_b = mix_twins(where, kept_b, came_b, ada_head, head_twin)
    mix_near_b, mix_far_b = near(mixed_b), across(mixed_b)
    heads = (head_weight, head_other, biases, bias_other, codes, code_other)
    noises = (noise_own, noise_core, noise_twin, noise_both)
    stats_a = head_stats(
        where, 0, (after(mixed_a, mixed_b), mix_near_a, mix_far_a, mix_last_a), heads, noises, flops=AHEAD
    )
    mix_last_b = near(after(mix_far_b, stats_a))
    stats_b = head_stats(where, half, (after(mixed_b, stats_a), mix_near_b, mix_far_b, mix_last_b), heads, noises)

    slots = [
        jnp.concatenate([part[:, r * half : (r + 1) * half] for part in (stats_a, stats_b)], axis=1) for r in range(4)
    ]
    parts = [slots[0]] + [along_z(slots[r], lambda z, r=r: z ^ r) for r in (1, 2, 3)]
    soft = soft_codes(where, parts, channels)

    def to_cells(d, m, core_of):
        y, x = d // half_dp, d % half_dp
        z, c = m // 2, m % 2
        return ((z // 2) * half_dp + x, 2 * (2 * (z % 2) + c) + core_of(y))

    def to_halo(d, m):
        y, x = d // half_dp, d % half_dp
        z, c = m // 2, m % 2
        block = 2 * (z % 2) + c + (1 if y == 1 else -1)
        if block < 0 or block > 3:
            return None
        return ((z // 2) * half_dp + x, 2 * block + (0 if y == 1 else 1))

    first = permute_devices(soft, dp, mp, lambda d, m: to_cells(d, m, lambda y: y))
    second = permute_devices(soft, dp, mp, lambda d, m: to_cells(d, m, lambda y: 1 - y))
    halo = permute_devices(soft, dp, mp, to_halo)
    f_hat_out = call(
        refine_kernel,
        where,
        (first, second, halo, jnp.transpose(phi_weight, (2, 3, 0, 1)), phi_bias[:, None], f_hat[0]),
        [shape_of(f_hat.shape[1:], jnp.float32)],
    )[0]
    return (block_out, f_hat_out[None])


def solution(mesh):
    in_specs = (
        P(("dp", "mp"), None),
        P("dp", None, None),
        P("dp", None),
        P(None, "mp"),
        P("mp"),
        P("mp", None),
        P(),
        P("dp", None, None),
        P(None, "mp"),
        P("mp"),
        P("dp", None, "mp"),
        P("mp", None),
        P(),
        P(),
        P("dp", None, "mp"),
    )
    out_specs = (P(("dp", "mp"), None), P("dp", None, "mp"))
    line = mesh.shape["dp"] == 4 and mesh.shape["mp"] == 8
    body = line_body if line else general_body
    return jax.shard_map(body, mesh=mesh, in_specs=in_specs, out_specs=out_specs, check_vma=False)
```

```python
import functools

import jax
import jax.numpy as jnp
from jax import lax
from jax.experimental import pallas as pl
from jax.experimental.pallas import tpu as pltpu
from jax.sharding import PartitionSpec as P

SIDE = 32
NEW = 1024
GUIDE = 1.5
CHUNKS = 2
FLOWS = 4
HEAD_FLOWS = 2


def norm_rows(values):
    row_mean = jnp.mean(values, axis=-1, keepdims=True)
    centred = values - row_mean
    spread = jnp.mean(centred * centred, axis=-1, keepdims=True)
    return centred * lax.rsqrt(spread + 1e-06)


def modulate(values, ada):
    return norm_rows(values.astype(jnp.float32)) * (1.0 + ada[1]) + ada[0]


def permute_devices(value, dp, mp, target):
    pairs = []
    for d in range(dp):
        for m in range(mp):
            to = target(d, m)
            if to is not None:
                pairs.append((d * mp + m, to[0] * mp + to[1]))
    return lax.ppermute(value, ("dp", "mp"), pairs)


def general_body(
    tokens,
    ada_ffn,
    ffn_gate,
    up_weight,
    up_bias,
    down_weight,
    down_bias,
    ada_head,
    head_weight,
    head_bias,
    gumbel_noise,
    codebook,
    phi_weight,
    phi_bias,
    f_hat,
):
    rows, width = tokens.shape
    dp, mp = lax.axis_size("dp"), lax.axis_size("mp")
    d_index, m_index = lax.axis_index("dp"), lax.axis_index("mp")
    images = ada_ffn.shape[0]
    pairs = f_hat.shape[0]
    channels = f_hat.shape[1]
    vocab = head_weight.shape[1]
    own_image = (m_index * rows) // NEW
    ada_own = lax.dynamic_index_in_dim(ada_ffn, own_image, 0, keepdims=False)
    gate_own = lax.dynamic_index_in_dim(ffn_gate, own_image, 0, keepdims=False)
    head_own = lax.dynamic_index_in_dim(ada_head, own_image, 0, keepdims=False)
    half_dp, half_mp = dp // 2, mp // 2
    upper = d_index // half_dp

    def swap(d, m):
        return ((d + half_dp) % dp, m)

    def cross(d, m):
        if d // half_dp == m // half_mp:
            return None
        return ((d + half_dp) % dp, (m + half_mp) % mp)

    stays = upper == m_index // half_mp
    head_twin = permute_devices(head_own, dp, mp, swap)
    head_cond = jnp.where(upper == 0, head_own, head_twin)
    head_uncond = jnp.where(upper == 0, head_twin, head_own)

    step = rows // FLOWS
    normed = modulate(tokens, ada_own).astype(jnp.bfloat16)
    outs = []
    for c in range(FLOWS):
        part = lax.slice_in_dim(normed, c * step, (c + 1) * step, axis=0)
        gathered = lax.all_gather(part, "mp", axis=0, tiled=True)
        hidden = jax.nn.gelu(
            jnp.dot(gathered, up_weight, preferred_element_type=jnp.float32) + up_bias,
            approximate=True,
        ).astype(jnp.bfloat16)
        partial = jnp.dot(hidden, down_weight, preferred_element_type=jnp.float32).astype(jnp.bfloat16)
        summed = lax.psum_scatter(partial, "mp", scatter_dimension=0, tiled=True).astype(jnp.float32)
        own = lax.slice_in_dim(tokens, c * step, (c + 1) * step, axis=0).astype(jnp.float32)
        outs.append((own + gate_own * (summed + down_bias)).astype(jnp.bfloat16))
    block_out = jnp.concatenate(outs, axis=0)

    group = FLOWS // HEAD_FLOWS
    half = rows // HEAD_FLOWS // 2
    noise = gumbel_noise.reshape(pairs, NEW // rows, HEAD_FLOWS, 2, half, vocab)
    peaks, totals, codes = [], [], []
    for c in range(HEAD_FLOWS):
        part = jnp.concatenate(outs[c * group : (c + 1) * group], axis=0)
        first, second = part[:half], part[half:]
        kept = jnp.where(upper == 0, first, second)
        sent = jnp.where(upper == 0, second, first)
        came = permute_devices(sent, dp, mp, swap)
        cond = jnp.where(upper == 0, kept, came)
        uncond = jnp.where(upper == 0, came, kept)
        mixed = (
            (1.0 + GUIDE) * modulate(cond, head_cond) - GUIDE * modulate(uncond, head_uncond)
        ).astype(jnp.bfloat16)
        crossed = permute_devices(mixed, dp, mp, cross)
        mixed = jnp.where(stays, mixed, crossed)
        gathered = lax.all_gather(mixed, "mp", axis=0, tiled=True)
        logits = jnp.dot(gathered, head_weight, preferred_element_type=jnp.float32) + head_bias
        logits = logits.reshape(2, half_mp, half, vocab)
        order = jnp.transpose(logits, (1, 0, 2, 3)).reshape(pairs, NEW // rows, 2, half, vocab)
        scores = order + noise[:, :, c]
        peak = jnp.max(scores, axis=-1)
        weights = jnp.exp(scores - peak[..., None]).astype(jnp.bfloat16)
        totals.append(jnp.sum(weights.astype(jnp.float32), axis=-1))
        codes.append(jnp.dot(weights, codebook, preferred_element_type=jnp.float32))
        peaks.append(peak)
    stack = lambda parts: jnp.stack(parts, axis=2)
    peak = stack(peaks).reshape(pairs, 1, NEW)
    total = stack(totals).reshape(pairs, 1, NEW)
    code = stack(codes).reshape(pairs, NEW, channels).transpose(0, 2, 1)
    stats = jnp.concatenate([code, total, peak], axis=1)

    cells = f_hat.shape[2]
    band = cells // SIDE
    padded = jnp.pad(stats, ((0, 0), (0, 0), (SIDE, SIDE)))
    windows = jnp.stack(
        [padded[:, :, m * cells : m * cells + cells + 2 * SIDE] for m in range(mp)], axis=0
    )
    parts = lax.all_to_all(windows, "mp", 0, 0, tiled=True)
    top = jnp.max(parts[:, :, channels + 1], axis=0)
    factor = jnp.exp(parts[:, :, channels + 1] - top[None])[:, :, None]
    sums = jnp.sum(parts[:, :, : channels + 1] * factor, axis=0)
    cell_index = m_index * cells - SIDE + jnp.arange(cells + 2 * SIDE)
    inside = (cell_index >= 0) & (cell_index < NEW)
    soft = jnp.where(inside, sums[:, :channels] / jnp.where(inside, sums[:, channels:], 1.0), 0.0)
    code_map = soft.reshape(pairs, channels, band + 2, SIDE)
    wide = jnp.pad(code_map, ((0, 0), (0, 0), (0, 0), (1, 1)))
    taps = jnp.stack(
        [wide[:, :, i : i + band, j : j + SIDE] for i in range(3) for j in range(3)], axis=2
    ).reshape(pairs, channels * 9, cells)
    conv = jnp.einsum(
        "ok,pkn->pon",
        phi_weight.reshape(channels, channels * 9),
        taps,
        precision=lax.Precision.HIGHEST,
        preferred_element_type=jnp.float32,
    ) + phi_bias[None, :, None]
    f_hat_out = f_hat + 0.5 * soft[:, :, SIDE : SIDE + cells] + 0.5 * conv
    return (block_out, f_hat_out)


SCALARS = pl.BlockSpec(memory_space=pltpu.SMEM)
ON_CHIP = pl.BlockSpec(memory_space=pltpu.VMEM)
VMEM_LIMIT = 16 * 1024 * 1024
AHEAD = 40_000_000_000
MID, UPPER, IMAGE, ODD, SAME, CORE = range(6)


def call(kernel, where, args, outs, scratch=(), flops=0, specs=None, limit=VMEM_LIMIT):
    return pl.pallas_call(
        kernel,
        out_shape=outs,
        in_specs=[SCALARS] + (specs or [ON_CHIP] * len(args)),
        out_specs=[ON_CHIP] * len(outs),
        scratch_shapes=scratch,
        compiler_params=pltpu.CompilerParams(vmem_limit_bytes=limit),
        cost_estimate=pl.CostEstimate(flops=flops, bytes_accessed=0, transcendentals=0),
    )(where, *args)


def shape_of(shape, kind=jnp.bfloat16):
    return jax.ShapeDtypeStruct(shape, kind)


def after(value, *others):
    return lax.optimization_barrier((value, *others))[0]


def modulated(values, ada_ref, image):
    shift, scale = ada_ref[image, 0:1, :], ada_ref[image, 1:2, :]
    return norm_rows(values.astype(jnp.float32)) * (1.0 + scale) + shift


def norm_kernel(begin, where_ref, tokens_ref, ada_ref, out_ref):
    values = tokens_ref[begin : begin + out_ref.shape[0], :]
    out_ref[...] = modulated(values, ada_ref, where_ref[IMAGE]).astype(jnp.bfloat16)


def norm_part(where, tokens, ada, begin, size):
    outs = [shape_of((size, tokens.shape[1]))]
    return call(functools.partial(norm_kernel, begin), where, (tokens, ada), outs)[0]


def ffn_kernel(groups, tile, fetch, where_ref, *refs):
    count = sum(groups)
    parts = refs[:count]
    up_a, up_b, down_a, down_b, bias_a, bias_b = refs[count : count + 6]
    outs = refs[count + 6 : count + 6 + len(groups)]
    x_ref, hidden_ref, *own = refs[count + 6 + len(groups) :]
    order = list(range(0, 2 * down_a.shape[0], tile))
    copies = []
    if fetch:
        up_own, down_own, sems = own
        copies = [
            pltpu.make_async_copy(up_a, up_own, sems.at[0]),
            pltpu.make_async_copy(down_a, down_own, sems.at[1]),
        ]
        for copy in copies:
            copy.start()
        up_a, down_a = up_own, down_own
        order = [t for t in order if t >= down_a.shape[0]] + [t for t in order if t < down_a.shape[0]]
    panel, width = down_a.shape
    step = outs[0].shape[0]
    place = 0
    for g, size in enumerate(groups):
        if size == 1:
            value = parts[place][...]
        else:
            value = jnp.where(where_ref[MID] == 1, parts[place][...], parts[place + 1][...])
        x_ref[g * step : (g + 1) * step, :] = value
        place += size

    def columns(first, second, begin, end):
        if end <= panel:
            return first[:, begin:end]
        if begin >= panel:
            return second[:, begin - panel : end - panel]
        return jnp.concatenate([first[:, begin:panel], second[:, : end - panel]], axis=1)

    for begin in order:
        end = begin + tile
        if fetch and begin == 0:
            copies[0].wait()
        v = jnp.dot(x_ref[...], columns(up_a, up_b, begin, end), preferred_element_type=jnp.float32)
        v = v + columns(bias_a, bias_b, begin, end)
        hidden_ref[:, begin:end] = jax.nn.gelu(v, approximate=True).astype(jnp.bfloat16)
    if fetch:
        copies[1].wait()
    for begin in range(0, width, tile):
        cols = slice(begin, begin + tile)
        weight = jnp.concatenate([down_a[:, cols], down_b[:, cols]], axis=0)
        result = jnp.dot(hidden_ref[...], weight, preferred_element_type=jnp.float32)
        for g in range(len(groups)):
            outs[g][:, cols] = result[g * step : (g + 1) * step].astype(jnp.bfloat16)


def ffn(where, slots, panels, fetch=False):
    groups = tuple(len(slot) for slot in slots)
    parts = [part for slot in slots for part in slot]
    rows, width = parts[0].shape
    total = rows * len(slots)
    up, down = panels[0], panels[2]
    if fetch:
        panels = [
            pltpu.with_memory_space_constraint(p, pltpu.HBM) if i in (0, 2) else p for i, p in enumerate(panels)
        ]
    own = [pltpu.VMEM(up.shape, up.dtype), pltpu.VMEM(down.shape, down.dtype), pltpu.SemaphoreType.DMA((2,))]
    in_place = pl.BlockSpec(memory_space=pltpu.HBM)
    specs = [in_place if fetch and i in (0, 2) else ON_CHIP for i in range(len(panels))]
    return call(
        functools.partial(ffn_kernel, groups, 256, fetch),
        where,
        (*parts, *panels),
        [shape_of((rows, width))] * len(slots),
        scratch=[
            pltpu.VMEM((total, width), jnp.bfloat16),
            pltpu.VMEM((total, 2 * down.shape[0]), jnp.bfloat16),
            *(own if fetch else []),
        ],
        specs=[ON_CHIP] * len(parts) + specs,
        limit=VMEM_LIMIT + 8 * 1024 * 1024 if fetch else VMEM_LIMIT,
    )


def add_kernel(always, where_ref, a_ref, b_ref, out_ref):
    b = b_ref[...].astype(jnp.float32)
    if not always:
        b = jnp.where(where_ref[MID] == 1, b, 0.0)
    out_ref[...] = (a_ref[...].astype(jnp.float32) + b).astype(jnp.bfloat16)


def add(where, a, b, always=False, flops=0):
    return call(functools.partial(add_kernel, always), where, (a, b), [shape_of(a.shape)], flops=flops)[0]


def out_kernel(begin, always, where_ref, own_ref, near_ref, far_ref, tokens_ref, gate_ref, bias_ref, ada_ref, *refs):
    out_ref, kept_ref, sent_ref = refs[-3:]
    far = far_ref[...].astype(jnp.float32)
    if not always:
        far = jnp.where(where_ref[MID] == 1, far, 0.0)
    summed = own_ref[...].astype(jnp.float32) + near_ref[...].astype(jnp.float32) + far
    rows = summed.shape[0]
    tokens = tokens_ref[begin : begin + rows, :].astype(jnp.float32)
    gate = gate_ref[pl.ds(where_ref[IMAGE], 1), :]
    value = (tokens + gate * (summed + bias_ref[...])).astype(jnp.bfloat16)
    if len(refs) > 3:
        out_ref[0:begin, :] = refs[0][...]
        out_ref[begin : begin + rows, :] = value
    else:
        out_ref[...] = value
    half = rows // 2
    lower = where_ref[UPPER] == 0
    kept_ref[...] = jnp.where(lower, value[:half], value[half:])
    sent = jnp.where(lower, value[half:], value[:half])
    sent_ref[...] = modulated(sent, ada_ref, where_ref[IMAGE]).astype(jnp.bfloat16)


def block_rows(where, begin, always, own, near, far, tokens, gate, bias, ada, earlier=()):
    rows, width = own.shape
    full = rows + begin if earlier else rows
    return call(
        functools.partial(out_kernel, begin, always),
        where,
        (own, near, far, tokens, gate, bias, ada, *earlier),
        [shape_of((full, width)), shape_of((rows // 2, width)), shape_of((rows // 2, width))],
    )


def mix_kernel(where_ref, kept_ref, came_ref, ada_ref, out_ref):
    kept, came = modulated(kept_ref[...], ada_ref, where_ref[IMAGE]), came_ref[...].astype(jnp.float32)
    lower = where_ref[UPPER] == 0
    share = jnp.where(lower, 1.0 + GUIDE, -GUIDE)
    other = jnp.where(lower, -GUIDE, 1.0 + GUIDE)
    out_ref[...] = (share * kept + other * came).astype(jnp.bfloat16)


def mix_twins(where, kept, came, ada):
    return call(mix_kernel, where, (kept, came, ada), [shape_of(kept.shape)])[0]


def head_kernel(
    begin, where_ref, own_ref, near_ref, far_ref, last_ref, weight_a, weight_b, bias_a, bias_b, code_a, code_b,
    noise_own, noise_core, noise_twin, noise_both, stats_ref, x_ref
):
    step = own_ref.shape[0]
    for r, ref in enumerate((own_ref, near_ref, far_ref, last_ref)):
        x_ref[r * step : (r + 1) * step, :] = ref[...]
    x = x_ref[...]
    odd = where_ref[ODD]
    even = 1 - odd
    same = where_ref[SAME] == 1
    scores = []
    for weight, bias, ours, theirs in (
        (weight_a, bias_a, noise_own, noise_twin),
        (weight_b, bias_b, noise_core, noise_both),
    ):
        picked = []
        for first in (True, False):
            for block in (odd, even):
                a, b = ours[block, begin : begin + step, :], theirs[block, begin : begin + step, :]
                picked.append(jnp.where(same, a, b) if first else jnp.where(same, b, a))
        logits = jnp.dot(x, weight[...], preferred_element_type=jnp.float32)
        scores.append(logits + bias[:, bias.shape[1] - weight.shape[1] :] + jnp.concatenate(picked, axis=0))
    peak = jnp.max(jnp.maximum(scores[0], scores[1]), axis=1, keepdims=True)
    sums = 0.0
    total = 0.0
    for score, code in zip(scores, (code_a, code_b)):
        weights = jnp.exp(score - peak).astype(jnp.bfloat16)
        total = total + jnp.sum(weights.astype(jnp.float32), axis=1, keepdims=True)
        sums = sums + lax.dot_general(
            weights, code[...], (((1,), (1,)), ((), ())), preferred_element_type=jnp.float32
        )
    channels = code_a.shape[0]
    pad = jnp.zeros((4 * step, 128 - channels), jnp.float32)
    table = jnp.concatenate([sums, pad], axis=1)
    lane = lax.broadcasted_iota(jnp.int32, table.shape, 1)
    table = jnp.where(lane == channels, total, table)
    table = jnp.where(lane == channels + 1, peak, table)
    stats_ref[...] = jnp.transpose(table)[: stats_ref.shape[0], :]


def head_stats(where, begin, slots, heads, noises, flops=0):
    step, width = slots[0].shape
    height = -(-(heads[-1].shape[0] + 2) // 8) * 8
    return call(
        functools.partial(head_kernel, begin),
        where,
        (*slots, *heads, *noises),
        [shape_of((height, 4 * step), jnp.float32)],
        scratch=[pltpu.VMEM((4 * step, width), jnp.bfloat16)],
        flops=flops,
    )[0]


def soft_kernel(channels, where_ref, *refs):
    parts, out_ref = refs[:-1], refs[-1]
    tops = [part[channels + 1 : channels + 2, :] for part in parts]
    top = functools.reduce(jnp.maximum, tops)
    code = 0.0
    total = 0.0
    for part, peak in zip(parts, tops):
        factor = jnp.exp(peak - top)
        code = code + part[0:channels, :] * factor
        total = total + part[channels : channels + 1, :] * factor
    out_ref[...] = code / total


def soft_codes(where, parts, channels):
    outs = [shape_of((channels, parts[0].shape[1]), jnp.float32)]
    return call(functools.partial(soft_kernel, channels), where, tuple(parts), outs)[0]


def refine_kernel(where_ref, first_ref, second_ref, halo_ref, phi_ref, bias_ref, map_ref, out_ref):
    first, second, halo = first_ref[...], second_ref[...], halo_ref[...]
    cells = first.shape[1]
    half = cells // 2
    lane = lax.broadcasted_iota(jnp.int32, first.shape, 1)
    shift = lambda value, by: pltpu.roll(value, by % cells, 1)
    early = where_ref[CORE] == 0
    lower, higher = jnp.where(early, first, second), jnp.where(early, second, first)
    centre = jnp.where(
        early,
        jnp.where(lane < half, lower, shift(higher, half)),
        jnp.where(lane < half, shift(lower, half), higher),
    )
    above = jnp.where(early, shift(halo, SIDE), shift(higher, SIDE - half))
    below = jnp.where(early, shift(lower, half - SIDE), shift(halo, -SIDE))
    rows = (
        jnp.where(lane < SIDE, above, shift(centre, SIDE)),
        centre,
        jnp.where(lane >= cells - SIDE, below, shift(centre, -SIDE)),
    )
    column = lane % SIDE
    conv = jnp.zeros(out_ref.shape, jnp.float32) + bias_ref[...]
    for i, row in enumerate(rows):
        left = jnp.where(column == 0, 0.0, shift(row, 1))
        right = jnp.where(column == SIDE - 1, 0.0, shift(row, -1))
        for j, tap in enumerate((left, row, right)):
            conv = conv + jnp.dot(
                phi_ref[i, j], tap, precision=lax.Precision.HIGHEST, preferred_element_type=jnp.float32
            )
    out_ref[...] = map_ref[...] + 0.5 * centre + 0.5 * conv


def line_body(
    tokens,
    ada_ffn,
    ffn_gate,
    up_weight,
    up_bias,
    down_weight,
    down_bias,
    ada_head,
    head_weight,
    head_bias,
    gumbel_noise,
    codebook,
    phi_weight,
    phi_bias,
    f_hat,
):
    rows = tokens.shape[0]
    dp, mp = lax.axis_size("dp"), lax.axis_size("mp")
    d_index, m_index = lax.axis_index("dp"), lax.axis_index("mp")
    channels = f_hat.shape[1]
    half_dp = dp // 2
    upper = d_index // half_dp
    z_index, core = m_index // 2, m_index % 2
    where = jnp.stack(
        [
            (z_index == 1) | (z_index == 2),
            upper,
            (m_index * rows) // NEW,
            z_index % 2,
            z_index // 2 == upper,
            core,
        ]
    ).astype(jnp.int32)

    def along_z(value, target):
        def to(d, m):
            z = target(m // 2)
            return None if z is None else (d, 2 * z + m % 2)

        return permute_devices(value, dp, mp, to)

    def near(value):
        return along_z(value, lambda z: z ^ 1)

    def across(value):
        return along_z(value, lambda z: z ^ 2)

    def middle(value):
        return along_z(value, lambda z: 3 - z if z in (1, 2) else z)

    def outward(value):
        return along_z(value, lambda z: {1: 0, 2: 3}.get(z))

    def inward(value):
        return along_z(value, lambda z: {0: 1, 3: 2}.get(z))

    def swap_cores(value):
        return permute_devices(value, dp, mp, lambda d, m: (d, m ^ 1))

    def swap_twins(value):
        return permute_devices(value, dp, mp, lambda d, m: ((d + half_dp) % dp, m))

    def swap_both(value):
        return permute_devices(value, dp, mp, lambda d, m: ((d + half_dp) % dp, m ^ 1))

    step = rows // CHUNKS
    half = step // 2
    voc = head_bias.shape[0]
    noise = gumbel_noise.reshape(2, 2, CHUNKS, 2, half, voc)

    def noise_for(to_core, to_upper):
        picked = lax.dynamic_slice(
            noise, (0, to_core, 0, to_upper, 0, 0), (2, 1, CHUNKS, 1, half, voc)
        )
        return picked.reshape(2, CHUNKS * half, voc)

    gate, bias_out = ffn_gate, down_bias[None]
    up_other, down_other = swap_cores(up_weight), swap_cores(down_weight)
    biases = jnp.concatenate([up_bias, head_bias])[None]
    codes = codebook.T
    bias_other = swap_cores(biases)

    barrier = lax.optimization_barrier
    own_a = norm_part(where, tokens, ada_ffn, 0, step)
    near_a, mid_a = near(own_a), middle(own_a)
    own_b = norm_part(where, tokens, ada_ffn, step, step)
    noise_own, noise_twin, noise_core, noise_both = (
        noise_for(core, upper),
        noise_for(core, 1 - upper),
        noise_for(1 - core, upper),
        noise_for(1 - core, 1 - upper),
    )
    up_other, down_other, bias_other, near_a, own_b = barrier((up_other, down_other, bias_other, near_a, own_b))
    panels = (up_weight, up_other, down_weight, down_other, biases, bias_other)
    far_mid_a = middle(near_a)
    near_b = near(after(own_b, near_a))
    mid_a = after(mid_a, near_a)
    far_end_a = outward(mid_a)
    noise_twin = swap_twins(after(noise_twin, near_a))
    sum_own_a, sum_near_a = ffn(where, [[own_a], [after(near_a, mid_a)]], panels, fetch=True)
    far_mid_a = after(far_mid_a, sum_near_a)
    last_end_a = outward(far_mid_a)
    mid_b = middle(after(own_b, far_mid_a))
    noise_core = swap_cores(after(noise_core, far_mid_a))
    (sum_far_a,) = ffn(where, [[far_mid_a, far_end_a]], panels)
    came_far_a = inward(sum_far_a)
    near_b, mid_b = barrier((near_b, mid_b, sum_far_a))[:2]
    far_mid_b, far_end_b = middle(near_b), outward(mid_b)
    sum_own_b, sum_near_b = ffn(where, [[after(own_b, sum_far_a)], [after(near_b, mid_b)]], panels)
    (sum_last_a,) = ffn(where, [[mid_a, after(last_end_a, sum_near_b, noise_twin, far_mid_b)]], panels)
    came_last_a = inward(sum_last_a)
    last_end_b = outward(after(far_mid_b, sum_near_b))
    noise_both = swap_both(after(noise_both, noise_twin))
    both_last_a = add(where, sum_last_a, came_far_a)
    went_last_a = middle(both_last_a)
    sum_far_b, sum_last_b = ffn(
        where, [[after(far_mid_b, sum_last_a, both_last_a), far_end_b], [mid_b, last_end_b]], panels
    )
    both_far_a = add(where, after(sum_far_a, went_last_a, sum_far_b), came_last_a)
    went_far_a = middle(both_far_a)
    came_last_b = near(sum_last_b)
    head_other = swap_cores(after(head_weight, sum_last_b))
    code_other = swap_cores(after(codes, sum_last_b))
    came_near_b = near(after(sum_near_b, last_end_b))
    both_near_a = add(where, sum_near_a, after(went_far_a, came_near_b), flops=AHEAD)
    came_near_a = near(both_near_a)
    both_far_b = add(where, after(sum_far_b, both_near_a), came_last_b, always=True)
    went_far_b = across(both_far_b)
    out_a, kept_a, sent_a = block_rows(
        where, 0, False, sum_own_a, after(came_near_a, noise_both, noise_core), went_last_a, tokens, gate, bias_out, ada_head
    )
    came_a = swap_twins(sent_a)
    mixed_a = mix_twins(where, kept_a, came_a, ada_head)
    mix_near_a, mix_far_a = near(mixed_a), across(mixed_a)
    block_out, kept_b, sent_b = block_rows(
        where, step, True, sum_own_b, after(came_near_b, mixed_a, head_other, code_other), went_far_b, tokens, gate, bias_out, ada_head, (out_a,)
    )
    came_b = after(swap_twins(sent_b), mix_far_a)
    mix_last_a = near(mix_far_a)
    mixed_b = mix_twins(where, kept_b, came_b, ada_head)
    mix_near_b, mix_far_b = near(mixed_b), across(mixed_b)
    heads = (head_weight, head_other, biases, bias_other, codes, code_other)
    noises = (noise_own, noise_core, noise_twin, noise_both)
    stats_a = head_stats(
        where, 0, (after(mixed_a, mixed_b), mix_near_a, mix_far_a, mix_last_a), heads, noises, flops=AHEAD
    )
    mix_last_b = near(after(mix_far_b, stats_a))
    stats_b = head_stats(where, half, (after(mixed_b, stats_a), mix_near_b, mix_far_b, mix_last_b), heads, noises)

    slots = [
        jnp.concatenate([part[:, r * half : (r + 1) * half] for part in (stats_a, stats_b)], axis=1) for r in range(4)
    ]
    parts = [slots[0]] + [along_z(slots[r], lambda z, r=r: z ^ r) for r in (1, 2, 3)]
    soft = soft_codes(where, parts, channels)

    def to_cells(d, m, core_of):
        y, x = d // half_dp, d % half_dp
        z, c = m // 2, m % 2
        return ((z // 2) * half_dp + x, 2 * (2 * (z % 2) + c) + core_of(y))

    def to_halo(d, m):
        y, x = d // half_dp, d % half_dp
        z, c = m // 2, m % 2
        block = 2 * (z % 2) + c + (1 if y == 1 else -1)
        if block < 0 or block > 3:
            return None
        return ((z // 2) * half_dp + x, 2 * block + (0 if y == 1 else 1))

    first = permute_devices(soft, dp, mp, lambda d, m: to_cells(d, m, lambda y: y))
    second = permute_devices(soft, dp, mp, lambda d, m: to_cells(d, m, lambda y: 1 - y))
    halo = permute_devices(soft, dp, mp, to_halo)
    f_hat_out = call(
        refine_kernel,
        where,
        (first, second, halo, jnp.transpose(phi_weight, (2, 3, 0, 1)), phi_bias[:, None], f_hat[0]),
        [shape_of(f_hat.shape[1:], jnp.float32)],
    )[0]
    return (block_out, f_hat_out[None])


def solution(mesh):
    in_specs = (
        P(("dp", "mp"), None),
        P("dp", None, None),
        P("dp", None),
        P(None, "mp"),
        P("mp"),
        P("mp", None),
        P(),
        P("dp", None, None),
        P(None, "mp"),
        P("mp"),
        P("dp", None, "mp"),
        P("mp", None),
        P(),
        P(),
        P("dp", None, "mp"),
    )
    out_specs = (P(("dp", "mp"), None), P("dp", None, "mp"))
    line = mesh.shape["dp"] == 4 and mesh.shape["mp"] == 8
    body = line_body if line else general_body
    return jax.shard_map(body, mesh=mesh, in_specs=in_specs, out_specs=out_specs, check_vma=False)
```

```python
import functools

import jax
import jax.numpy as jnp
from jax import lax
from jax.experimental import pallas as pl
from jax.experimental.pallas import tpu as pltpu
from jax.sharding import PartitionSpec as P

SIDE = 32
NEW = 1024
GUIDE = 1.5
CHUNKS = 2
FLOWS = 4
HEAD_FLOWS = 2


def norm_rows(values):
    row_mean = jnp.mean(values, axis=-1, keepdims=True)
    centred = values - row_mean
    spread = jnp.mean(centred * centred, axis=-1, keepdims=True)
    return centred * lax.rsqrt(spread + 1e-06)


def modulate(values, ada):
    return norm_rows(values.astype(jnp.float32)) * (1.0 + ada[1]) + ada[0]


def permute_devices(value, dp, mp, target):
    pairs = []
    for d in range(dp):
        for m in range(mp):
            to = target(d, m)
            if to is not None:
                pairs.append((d * mp + m, to[0] * mp + to[1]))
    return lax.ppermute(value, ("dp", "mp"), pairs)


def general_body(
    tokens,
    ada_ffn,
    ffn_gate,
    up_weight,
    up_bias,
    down_weight,
    down_bias,
    ada_head,
    head_weight,
    head_bias,
    gumbel_noise,
    codebook,
    phi_weight,
    phi_bias,
    f_hat,
):
    rows, width = tokens.shape
    dp, mp = lax.axis_size("dp"), lax.axis_size("mp")
    d_index, m_index = lax.axis_index("dp"), lax.axis_index("mp")
    images = ada_ffn.shape[0]
    pairs = f_hat.shape[0]
    channels = f_hat.shape[1]
    vocab = head_weight.shape[1]
    own_image = (m_index * rows) // NEW
    ada_own = lax.dynamic_index_in_dim(ada_ffn, own_image, 0, keepdims=False)
    gate_own = lax.dynamic_index_in_dim(ffn_gate, own_image, 0, keepdims=False)
    head_own = lax.dynamic_index_in_dim(ada_head, own_image, 0, keepdims=False)
    half_dp, half_mp = dp // 2, mp // 2
    upper = d_index // half_dp

    def swap(d, m):
        return ((d + half_dp) % dp, m)

    def cross(d, m):
        if d // half_dp == m // half_mp:
            return None
        return ((d + half_dp) % dp, (m + half_mp) % mp)

    stays = upper == m_index // half_mp
    head_twin = permute_devices(head_own, dp, mp, swap)
    head_cond = jnp.where(upper == 0, head_own, head_twin)
    head_uncond = jnp.where(upper == 0, head_twin, head_own)

    step = rows // FLOWS
    normed = modulate(tokens, ada_own).astype(jnp.bfloat16)
    outs = []
    for c in range(FLOWS):
        part = lax.slice_in_dim(normed, c * step, (c + 1) * step, axis=0)
        gathered = lax.all_gather(part, "mp", axis=0, tiled=True)
        hidden = jax.nn.gelu(
            jnp.dot(gathered, up_weight, preferred_element_type=jnp.float32) + up_bias,
            approximate=True,
        ).astype(jnp.bfloat16)
        partial = jnp.dot(hidden, down_weight, preferred_element_type=jnp.float32).astype(jnp.bfloat16)
        summed = lax.psum_scatter(partial, "mp", scatter_dimension=0, tiled=True).astype(jnp.float32)
        own = lax.slice_in_dim(tokens, c * step, (c + 1) * step, axis=0).astype(jnp.float32)
        outs.append((own + gate_own * (summed + down_bias)).astype(jnp.bfloat16))
    block_out = jnp.concatenate(outs, axis=0)

    group = FLOWS // HEAD_FLOWS
    half = rows // HEAD_FLOWS // 2
    noise = gumbel_noise.reshape(pairs, NEW // rows, HEAD_FLOWS, 2, half, vocab)
    peaks, totals, codes = [], [], []
    for c in range(HEAD_FLOWS):
        part = jnp.concatenate(outs[c * group : (c + 1) * group], axis=0)
        first, second = part[:half], part[half:]
        kept = jnp.where(upper == 0, first, second)
        sent = jnp.where(upper == 0, second, first)
        came = permute_devices(sent, dp, mp, swap)
        cond = jnp.where(upper == 0, kept, came)
        uncond = jnp.where(upper == 0, came, kept)
        mixed = (
            (1.0 + GUIDE) * modulate(cond, head_cond) - GUIDE * modulate(uncond, head_uncond)
        ).astype(jnp.bfloat16)
        crossed = permute_devices(mixed, dp, mp, cross)
        mixed = jnp.where(stays, mixed, crossed)
        gathered = lax.all_gather(mixed, "mp", axis=0, tiled=True)
        logits = jnp.dot(gathered, head_weight, preferred_element_type=jnp.float32) + head_bias
        logits = logits.reshape(2, half_mp, half, vocab)
        order = jnp.transpose(logits, (1, 0, 2, 3)).reshape(pairs, NEW // rows, 2, half, vocab)
        scores = order + noise[:, :, c]
        peak = jnp.max(scores, axis=-1)
        weights = jnp.exp(scores - peak[..., None]).astype(jnp.bfloat16)
        totals.append(jnp.sum(weights.astype(jnp.float32), axis=-1))
        codes.append(jnp.dot(weights, codebook, preferred_element_type=jnp.float32))
        peaks.append(peak)
    stack = lambda parts: jnp.stack(parts, axis=2)
    peak = stack(peaks).reshape(pairs, 1, NEW)
    total = stack(totals).reshape(pairs, 1, NEW)
    code = stack(codes).reshape(pairs, NEW, channels).transpose(0, 2, 1)
    stats = jnp.concatenate([code, total, peak], axis=1)

    cells = f_hat.shape[2]
    band = cells // SIDE
    padded = jnp.pad(stats, ((0, 0), (0, 0), (SIDE, SIDE)))
    windows = jnp.stack(
        [padded[:, :, m * cells : m * cells + cells + 2 * SIDE] for m in range(mp)], axis=0
    )
    parts = lax.all_to_all(windows, "mp", 0, 0, tiled=True)
    top = jnp.max(parts[:, :, channels + 1], axis=0)
    factor = jnp.exp(parts[:, :, channels + 1] - top[None])[:, :, None]
    sums = jnp.sum(parts[:, :, : channels + 1] * factor, axis=0)
    cell_index = m_index * cells - SIDE + jnp.arange(cells + 2 * SIDE)
    inside = (cell_index >= 0) & (cell_index < NEW)
    soft = jnp.where(inside, sums[:, :channels] / jnp.where(inside, sums[:, channels:], 1.0), 0.0)
    code_map = soft.reshape(pairs, channels, band + 2, SIDE)
    wide = jnp.pad(code_map, ((0, 0), (0, 0), (0, 0), (1, 1)))
    taps = jnp.stack(
        [wide[:, :, i : i + band, j : j + SIDE] for i in range(3) for j in range(3)], axis=2
    ).reshape(pairs, channels * 9, cells)
    conv = jnp.einsum(
        "ok,pkn->pon",
        phi_weight.reshape(channels, channels * 9),
        taps,
        precision=lax.Precision.HIGHEST,
        preferred_element_type=jnp.float32,
    ) + phi_bias[None, :, None]
    f_hat_out = f_hat + 0.5 * soft[:, :, SIDE : SIDE + cells] + 0.5 * conv
    return (block_out, f_hat_out)


SCALARS = pl.BlockSpec(memory_space=pltpu.SMEM)
ON_CHIP = pl.BlockSpec(memory_space=pltpu.VMEM)
VMEM_LIMIT = 16 * 1024 * 1024
AHEAD = 40_000_000_000
MID, UPPER, IMAGE, ODD, SAME, CORE = range(6)


def call(kernel, where, args, outs, scratch=(), flops=0, specs=None, limit=VMEM_LIMIT):
    return pl.pallas_call(
        kernel,
        out_shape=outs,
        in_specs=[SCALARS] + (specs or [ON_CHIP] * len(args)),
        out_specs=[ON_CHIP] * len(outs),
        scratch_shapes=scratch,
        compiler_params=pltpu.CompilerParams(vmem_limit_bytes=limit),
        cost_estimate=pl.CostEstimate(flops=flops, bytes_accessed=0, transcendentals=0),
    )(where, *args)


def shape_of(shape, kind=jnp.bfloat16):
    return jax.ShapeDtypeStruct(shape, kind)


def after(value, *others):
    return lax.optimization_barrier((value, *others))[0]


def modulated(values, ada_ref, image):
    shift, scale = ada_ref[image, 0:1, :], ada_ref[image, 1:2, :]
    return norm_rows(values.astype(jnp.float32)) * (1.0 + scale) + shift


def norm_kernel(begin, where_ref, tokens_ref, ada_ref, out_ref):
    values = tokens_ref[begin : begin + out_ref.shape[0], :]
    out_ref[...] = modulated(values, ada_ref, where_ref[IMAGE]).astype(jnp.bfloat16)


def norm_part(where, tokens, ada, begin, size):
    outs = [shape_of((size, tokens.shape[1]))]
    return call(functools.partial(norm_kernel, begin), where, (tokens, ada), outs)[0]


def ffn_kernel(groups, tile, fetch, where_ref, *refs):
    count = sum(groups)
    parts = refs[:count]
    up_a, up_b, down_a, down_b, bias_a, bias_b = refs[count : count + 6]
    outs = refs[count + 6 : count + 6 + len(groups)]
    x_ref, hidden_ref, *own = refs[count + 6 + len(groups) :]
    order = list(range(0, 2 * down_a.shape[0], tile))
    copies = []
    if fetch:
        up_own, down_own, sems = own
        copies = [
            pltpu.make_async_copy(up_a, up_own, sems.at[0]),
            pltpu.make_async_copy(down_a, down_own, sems.at[1]),
        ]
        for copy in copies:
            copy.start()
        up_a, down_a = up_own, down_own
        order = [t for t in order if t >= down_a.shape[0]] + [t for t in order if t < down_a.shape[0]]
    panel, width = down_a.shape
    step = outs[0].shape[0]
    place = 0
    for g, size in enumerate(groups):
        if size == 1:
            value = parts[place][...]
        else:
            value = jnp.where(where_ref[MID] == 1, parts[place][...], parts[place + 1][...])
        x_ref[g * step : (g + 1) * step, :] = value
        place += size

    def columns(first, second, begin, end):
        if end <= panel:
            return first[:, begin:end]
        if begin >= panel:
            return second[:, begin - panel : end - panel]
        return jnp.concatenate([first[:, begin:panel], second[:, : end - panel]], axis=1)

    for begin in order:
        end = begin + tile
        if fetch and begin == 0:
            copies[0].wait()
        v = jnp.dot(x_ref[...], columns(up_a, up_b, begin, end), preferred_element_type=jnp.float32)
        v = v + columns(bias_a, bias_b, begin, end)
        hidden_ref[:, begin:end] = jax.nn.gelu(v, approximate=True).astype(jnp.bfloat16)
    if fetch:
        copies[1].wait()
    for begin in range(0, width, tile):
        cols = slice(begin, begin + tile)
        weight = jnp.concatenate([down_a[:, cols], down_b[:, cols]], axis=0)
        result = jnp.dot(hidden_ref[...], weight, preferred_element_type=jnp.float32)
        for g in range(len(groups)):
            outs[g][:, cols] = result[g * step : (g + 1) * step].astype(jnp.bfloat16)


def ffn(where, slots, panels, fetch=False):
    groups = tuple(len(slot) for slot in slots)
    parts = [part for slot in slots for part in slot]
    rows, width = parts[0].shape
    total = rows * len(slots)
    up, down = panels[0], panels[2]
    if fetch:
        panels = [
            pltpu.with_memory_space_constraint(p, pltpu.HBM) if i in (0, 2) else p for i, p in enumerate(panels)
        ]
    own = [pltpu.VMEM(up.shape, up.dtype), pltpu.VMEM(down.shape, down.dtype), pltpu.SemaphoreType.DMA((2,))]
    in_place = pl.BlockSpec(memory_space=pltpu.HBM)
    specs = [in_place if fetch and i in (0, 2) else ON_CHIP for i in range(len(panels))]
    return call(
        functools.partial(ffn_kernel, groups, 256, fetch),
        where,
        (*parts, *panels),
        [shape_of((rows, width))] * len(slots),
        scratch=[
            pltpu.VMEM((total, width), jnp.bfloat16),
            pltpu.VMEM((total, 2 * down.shape[0]), jnp.bfloat16),
            *(own if fetch else []),
        ],
        specs=[ON_CHIP] * len(parts) + specs,
        limit=VMEM_LIMIT + 8 * 1024 * 1024 if fetch else VMEM_LIMIT,
    )


def add_kernel(always, where_ref, a_ref, b_ref, out_ref):
    b = b_ref[...].astype(jnp.float32)
    if not always:
        b = jnp.where(where_ref[MID] == 1, b, 0.0)
    out_ref[...] = (a_ref[...].astype(jnp.float32) + b).astype(jnp.bfloat16)


def add(where, a, b, always=False, flops=0):
    return call(functools.partial(add_kernel, always), where, (a, b), [shape_of(a.shape)], flops=flops)[0]


def out_kernel(begin, always, where_ref, own_ref, near_ref, far_ref, tokens_ref, gate_ref, bias_ref, ada_ref, *refs):
    out_ref, kept_ref, sent_ref = refs[-3:]
    far = far_ref[...].astype(jnp.float32)
    if not always:
        far = jnp.where(where_ref[MID] == 1, far, 0.0)
    summed = own_ref[...].astype(jnp.float32) + near_ref[...].astype(jnp.float32) + far
    rows = summed.shape[0]
    tokens = tokens_ref[begin : begin + rows, :].astype(jnp.float32)
    gate = gate_ref[pl.ds(where_ref[IMAGE], 1), :]
    value = (tokens + gate * (summed + bias_ref[...])).astype(jnp.bfloat16)
    if len(refs) > 3:
        out_ref[0:begin, :] = refs[0][...]
        out_ref[begin : begin + rows, :] = value
    else:
        out_ref[...] = value
    half = rows // 2
    lower = where_ref[UPPER] == 0
    kept_ref[...] = jnp.where(lower, value[:half], value[half:])
    sent = jnp.where(lower, value[half:], value[:half])
    sent_ref[...] = modulated(sent, ada_ref, where_ref[IMAGE]).astype(jnp.bfloat16)


def block_rows(where, begin, always, own, near, far, tokens, gate, bias, ada, earlier=()):
    rows, width = own.shape
    full = rows + begin if earlier else rows
    return call(
        functools.partial(out_kernel, begin, always),
        where,
        (own, near, far, tokens, gate, bias, ada, *earlier),
        [shape_of((full, width)), shape_of((rows // 2, width)), shape_of((rows // 2, width))],
    )


def mix_kernel(where_ref, kept_ref, came_ref, ada_ref, out_ref):
    kept, came = modulated(kept_ref[...], ada_ref, where_ref[IMAGE]), came_ref[...].astype(jnp.float32)
    lower = where_ref[UPPER] == 0
    share = jnp.where(lower, 1.0 + GUIDE, -GUIDE)
    other = jnp.where(lower, -GUIDE, 1.0 + GUIDE)
    out_ref[...] = (share * kept + other * came).astype(jnp.bfloat16)


def mix_twins(where, kept, came, ada):
    return call(mix_kernel, where, (kept, came, ada), [shape_of(kept.shape)])[0]


def head_kernel(
    begin, where_ref, own_ref, near_ref, far_ref, last_ref, weight_a, weight_b, bias_a, bias_b, code_a, code_b,
    noise_own, noise_core, noise_twin, noise_both, stats_ref, x_ref
):
    step = own_ref.shape[0]
    for r, ref in enumerate((own_ref, near_ref, far_ref, last_ref)):
        x_ref[r * step : (r + 1) * step, :] = ref[...]
    x = x_ref[...]
    odd = where_ref[ODD]
    even = 1 - odd
    same = where_ref[SAME] == 1
    scores = []
    for weight, bias, ours, theirs in (
        (weight_a, bias_a, noise_own, noise_twin),
        (weight_b, bias_b, noise_core, noise_both),
    ):
        picked = []
        for first in (True, False):
            for block in (odd, even):
                a, b = ours[block, begin : begin + step, :], theirs[block, begin : begin + step, :]
                picked.append(jnp.where(same, a, b) if first else jnp.where(same, b, a))
        logits = jnp.dot(x, weight[...], preferred_element_type=jnp.float32)
        scores.append(logits + bias[:, bias.shape[1] - weight.shape[1] :] + jnp.concatenate(picked, axis=0))
    peak = jnp.max(jnp.maximum(scores[0], scores[1]), axis=1, keepdims=True)
    sums = 0.0
    total = 0.0
    for score, code in zip(scores, (code_a, code_b)):
        weights = jnp.exp(score - peak).astype(jnp.bfloat16)
        total = total + jnp.sum(weights.astype(jnp.float32), axis=1, keepdims=True)
        sums = sums + lax.dot_general(
            weights, code[...], (((1,), (1,)), ((), ())), preferred_element_type=jnp.float32
        )
    channels = code_a.shape[0]
    pad = jnp.zeros((4 * step, 128 - channels), jnp.float32)
    table = jnp.concatenate([sums, pad], axis=1)
    lane = lax.broadcasted_iota(jnp.int32, table.shape, 1)
    table = jnp.where(lane == channels, total, table)
    table = jnp.where(lane == channels + 1, peak, table)
    stats_ref[...] = jnp.transpose(table)[: stats_ref.shape[0], :]


def head_stats(where, begin, slots, heads, noises, flops=0):
    step, width = slots[0].shape
    height = -(-(heads[-1].shape[0] + 2) // 8) * 8
    return call(
        functools.partial(head_kernel, begin),
        where,
        (*slots, *heads, *noises),
        [shape_of((height, 4 * step), jnp.float32)],
        scratch=[pltpu.VMEM((4 * step, width), jnp.bfloat16)],
        flops=flops,
    )[0]


def soft_kernel(channels, where_ref, *refs):
    parts, out_ref = refs[:-1], refs[-1]
    tops = [part[channels + 1 : channels + 2, :] for part in parts]
    top = functools.reduce(jnp.maximum, tops)
    code = 0.0
    total = 0.0
    for part, peak in zip(parts, tops):
        factor = jnp.exp(peak - top)
        code = code + part[0:channels, :] * factor
        total = total + part[channels : channels + 1, :] * factor
    out_ref[...] = code / total


def soft_codes(where, parts, channels):
    outs = [shape_of((channels, parts[0].shape[1]), jnp.float32)]
    return call(functools.partial(soft_kernel, channels), where, tuple(parts), outs)[0]


def refine_kernel(where_ref, first_ref, second_ref, halo_ref, phi_ref, bias_ref, map_ref, out_ref):
    first, second, halo = first_ref[...], second_ref[...], halo_ref[...]
    cells = first.shape[1]
    half = cells // 2
    lane = lax.broadcasted_iota(jnp.int32, first.shape, 1)
    shift = lambda value, by: pltpu.roll(value, by % cells, 1)
    early = where_ref[CORE] == 0
    lower, higher = jnp.where(early, first, second), jnp.where(early, second, first)
    centre = jnp.where(
        early,
        jnp.where(lane < half, lower, shift(higher, half)),
        jnp.where(lane < half, shift(lower, half), higher),
    )
    above = jnp.where(early, shift(halo, SIDE), shift(higher, SIDE - half))
    below = jnp.where(early, shift(lower, half - SIDE), shift(halo, -SIDE))
    rows = (
        jnp.where(lane < SIDE, above, shift(centre, SIDE)),
        centre,
        jnp.where(lane >= cells - SIDE, below, shift(centre, -SIDE)),
    )
    column = lane % SIDE
    conv = jnp.zeros(out_ref.shape, jnp.float32) + bias_ref[...]
    for i, row in enumerate(rows):
        left = jnp.where(column == 0, 0.0, shift(row, 1))
        right = jnp.where(column == SIDE - 1, 0.0, shift(row, -1))
        for j, tap in enumerate((left, row, right)):
            conv = conv + jnp.dot(
                phi_ref[i, j], tap, precision=lax.Precision.HIGHEST, preferred_element_type=jnp.float32
            )
    out_ref[...] = map_ref[...] + 0.5 * centre + 0.5 * conv


def line_body(
    tokens,
    ada_ffn,
    ffn_gate,
    up_weight,
    up_bias,
    down_weight,
    down_bias,
    ada_head,
    head_weight,
    head_bias,
    gumbel_noise,
    codebook,
    phi_weight,
    phi_bias,
    f_hat,
):
    rows = tokens.shape[0]
    dp, mp = lax.axis_size("dp"), lax.axis_size("mp")
    d_index, m_index = lax.axis_index("dp"), lax.axis_index("mp")
    channels = f_hat.shape[1]
    half_dp = dp // 2
    upper = d_index // half_dp
    z_index, core = m_index // 2, m_index % 2
    where = jnp.stack(
        [
            (z_index == 1) | (z_index == 2),
            upper,
            (m_index * rows) // NEW,
            z_index % 2,
            z_index // 2 == upper,
            core,
        ]
    ).astype(jnp.int32)

    def along_z(value, target):
        def to(d, m):
            z = target(m // 2)
            return None if z is None else (d, 2 * z + m % 2)

        return permute_devices(value, dp, mp, to)

    def near(value):
        return along_z(value, lambda z: z ^ 1)

    def across(value):
        return along_z(value, lambda z: z ^ 2)

    def middle(value):
        return along_z(value, lambda z: 3 - z if z in (1, 2) else z)

    def outward(value):
        return along_z(value, lambda z: {1: 0, 2: 3}.get(z))

    def inward(value):
        return along_z(value, lambda z: {0: 1, 3: 2}.get(z))

    def swap_cores(value):
        return permute_devices(value, dp, mp, lambda d, m: (d, m ^ 1))

    def swap_twins(value):
        return permute_devices(value, dp, mp, lambda d, m: ((d + half_dp) % dp, m))

    def swap_both(value):
        return permute_devices(value, dp, mp, lambda d, m: ((d + half_dp) % dp, m ^ 1))

    step = rows // CHUNKS
    half = step // 2
    voc = head_bias.shape[0]
    noise = gumbel_noise.reshape(2, 2, CHUNKS, 2, half, voc)

    def noise_for(to_core, to_upper):
        picked = lax.dynamic_slice(
            noise, (0, to_core, 0, to_upper, 0, 0), (2, 1, CHUNKS, 1, half, voc)
        )
        return picked.reshape(2, CHUNKS * half, voc)

    gate, bias_out = ffn_gate, down_bias[None]
    up_other, down_other = swap_cores(up_weight), swap_cores(down_weight)
    biases = jnp.concatenate([up_bias, head_bias])[None]
    codes = codebook.T
    bias_other = swap_cores(biases)

    barrier = lax.optimization_barrier
    own_a = norm_part(where, tokens, ada_ffn, 0, step)
    near_a, mid_a = near(own_a), middle(own_a)
    own_b = norm_part(where, tokens, ada_ffn, step, step)
    noise_own, noise_twin, noise_core, noise_both = (
        noise_for(core, upper),
        noise_for(core, 1 - upper),
        noise_for(1 - core, upper),
        noise_for(1 - core, 1 - upper),
    )
    up_other, down_other, bias_other, near_a, own_b = barrier((up_other, down_other, bias_other, near_a, own_b))
    panels = (up_weight, up_other, down_weight, down_other, biases, bias_other)
    far_mid_a = middle(near_a)
    near_b = near(after(own_b, near_a))
    mid_a = after(mid_a, near_a)
    far_end_a = outward(mid_a)
    noise_twin = swap_twins(after(noise_twin, near_a))
    sum_own_a, sum_near_a = ffn(where, [[own_a], [after(near_a, mid_a)]], panels, fetch=True)
    far_mid_a = after(far_mid_a, sum_near_a)
    last_end_a = outward(far_mid_a)
    mid_b = middle(after(own_b, far_mid_a))
    noise_core = swap_cores(after(noise_core, far_mid_a))
    (sum_far_a,) = ffn(where, [[far_mid_a, far_end_a]], panels)
    came_far_a = inward(sum_far_a)
    near_b, mid_b = barrier((near_b, mid_b, sum_far_a))[:2]
    far_mid_b, far_end_b = middle(near_b), outward(mid_b)
    (sum_last_a,) = ffn(where, [[mid_a, after(last_end_a, near_b, mid_b)]], panels)
    came_last_a = inward(sum_last_a)
    far_mid_b = after(far_mid_b, sum_last_a)
    last_end_b = outward(far_mid_b)
    both_last_a = add(where, after(sum_last_a, far_mid_b), came_far_a)
    went_last_a = middle(both_last_a)
    sum_own_b, sum_near_b = ffn(where, [[after(own_b, both_last_a, far_end_b)], [near_b]], panels)
    noise_both = swap_both(after(noise_both, noise_twin))
    both_far_a = add(where, after(sum_far_a, went_last_a, sum_near_b), came_last_a)
    went_far_a = middle(both_far_a)
    sum_far_b, sum_last_b = ffn(
        where, [[after(far_mid_b, both_far_a), far_end_b], [mid_b, last_end_b]], panels
    )
    came_last_b = near(sum_last_b)
    head_other = swap_cores(after(head_weight, sum_last_b))
    code_other = swap_cores(after(codes, sum_last_b))
    came_near_b = near(after(sum_near_b, last_end_b))
    both_near_a = add(where, sum_near_a, after(went_far_a, came_near_b, noise_twin), flops=AHEAD)
    came_near_a = near(both_near_a)
    both_far_b = add(where, after(sum_far_b, both_near_a), came_last_b, always=True)
    went_far_b = across(both_far_b)
    out_a, kept_a, sent_a = block_rows(
        where, 0, False, sum_own_a, after(came_near_a, noise_both, noise_core), went_last_a, tokens, gate, bias_out, ada_head
    )
    came_a = swap_twins(sent_a)
    mixed_a = mix_twins(where, kept_a, came_a, ada_head)
    mix_near_a, mix_far_a = near(mixed_a), across(mixed_a)
    block_out, kept_b, sent_b = block_rows(
        where, step, True, sum_own_b, after(came_near_b, mixed_a, head_other, code_other), went_far_b, tokens, gate, bias_out, ada_head, (out_a,)
    )
    came_b = after(swap_twins(sent_b), mix_far_a)
    mix_last_a = near(mix_far_a)
    mixed_b = mix_twins(where, kept_b, came_b, ada_head)
    mix_near_b, mix_far_b = near(mixed_b), across(mixed_b)
    heads = (head_weight, head_other, biases, bias_other, codes, code_other)
    noises = (noise_own, noise_core, noise_twin, noise_both)
    stats_a = head_stats(
        where, 0, (after(mixed_a, mixed_b), mix_near_a, mix_far_a, mix_last_a), heads, noises, flops=AHEAD
    )
    mix_last_b = near(after(mix_far_b, stats_a))
    stats_b = head_stats(where, half, (after(mixed_b, stats_a), mix_near_b, mix_far_b, mix_last_b), heads, noises)

    slots = [
        jnp.concatenate([part[:, r * half : (r + 1) * half] for part in (stats_a, stats_b)], axis=1) for r in range(4)
    ]
    parts = [slots[0]] + [along_z(slots[r], lambda z, r=r: z ^ r) for r in (1, 2, 3)]
    soft = soft_codes(where, parts, channels)

    def to_cells(d, m, core_of):
        y, x = d // half_dp, d % half_dp
        z, c = m // 2, m % 2
        return ((z // 2) * half_dp + x, 2 * (2 * (z % 2) + c) + core_of(y))

    def to_halo(d, m):
        y, x = d // half_dp, d % half_dp
        z, c = m // 2, m % 2
        block = 2 * (z % 2) + c + (1 if y == 1 else -1)
        if block < 0 or block > 3:
            return None
        return ((z // 2) * half_dp + x, 2 * block + (0 if y == 1 else 1))

    first = permute_devices(soft, dp, mp, lambda d, m: to_cells(d, m, lambda y: y))
    second = permute_devices(soft, dp, mp, lambda d, m: to_cells(d, m, lambda y: 1 - y))
    halo = permute_devices(soft, dp, mp, to_halo)
    f_hat_out = call(
        refine_kernel,
        where,
        (first, second, halo, jnp.transpose(phi_weight, (2, 3, 0, 1)), phi_bias[:, None], f_hat[0]),
        [shape_of(f_hat.shape[1:], jnp.float32)],
    )[0]
    return (block_out, f_hat_out[None])


def solution(mesh):
    in_specs = (
        P(("dp", "mp"), None),
        P("dp", None, None),
        P("dp", None),
        P(None, "mp"),
        P("mp"),
        P("mp", None),
        P(),
        P("dp", None, None),
        P(None, "mp"),
        P("mp"),
        P("dp", None, "mp"),
        P("mp", None),
        P(),
        P(),
        P("dp", None, "mp"),
    )
    out_specs = (P(("dp", "mp"), None), P("dp", None, "mp"))
    line = mesh.shape["dp"] == 4 and mesh.shape["mp"] == 8
    body = line_body if line else general_body
    return jax.shard_map(body, mesh=mesh, in_specs=in_specs, out_specs=out_specs, check_vma=False)
```

```python
import functools

import jax
import jax.numpy as jnp
from jax import lax
from jax.experimental import pallas as pl
from jax.experimental.pallas import tpu as pltpu
from jax.sharding import PartitionSpec as P

SIDE = 32
NEW = 1024
GUIDE = 1.5
CHUNKS = 2
FLOWS = 4
HEAD_FLOWS = 2


def norm_rows(values):
    row_mean = jnp.mean(values, axis=-1, keepdims=True)
    centred = values - row_mean
    spread = jnp.mean(centred * centred, axis=-1, keepdims=True)
    return centred * lax.rsqrt(spread + 1e-06)


def modulate(values, ada):
    return norm_rows(values.astype(jnp.float32)) * (1.0 + ada[1]) + ada[0]


def permute_devices(value, dp, mp, target):
    pairs = []
    for d in range(dp):
        for m in range(mp):
            to = target(d, m)
            if to is not None:
                pairs.append((d * mp + m, to[0] * mp + to[1]))
    return lax.ppermute(value, ("dp", "mp"), pairs)


def general_body(
    tokens,
    ada_ffn,
    ffn_gate,
    up_weight,
    up_bias,
    down_weight,
    down_bias,
    ada_head,
    head_weight,
    head_bias,
    gumbel_noise,
    codebook,
    phi_weight,
    phi_bias,
    f_hat,
):
    rows, width = tokens.shape
    dp, mp = lax.axis_size("dp"), lax.axis_size("mp")
    d_index, m_index = lax.axis_index("dp"), lax.axis_index("mp")
    images = ada_ffn.shape[0]
    pairs = f_hat.shape[0]
    channels = f_hat.shape[1]
    vocab = head_weight.shape[1]
    own_image = (m_index * rows) // NEW
    ada_own = lax.dynamic_index_in_dim(ada_ffn, own_image, 0, keepdims=False)
    gate_own = lax.dynamic_index_in_dim(ffn_gate, own_image, 0, keepdims=False)
    head_own = lax.dynamic_index_in_dim(ada_head, own_image, 0, keepdims=False)
    half_dp, half_mp = dp // 2, mp // 2
    upper = d_index // half_dp

    def swap(d, m):
        return ((d + half_dp) % dp, m)

    def cross(d, m):
        if d // half_dp == m // half_mp:
            return None
        return ((d + half_dp) % dp, (m + half_mp) % mp)

    stays = upper == m_index // half_mp
    head_twin = permute_devices(head_own, dp, mp, swap)
    head_cond = jnp.where(upper == 0, head_own, head_twin)
    head_uncond = jnp.where(upper == 0, head_twin, head_own)

    step = rows // FLOWS
    normed = modulate(tokens, ada_own).astype(jnp.bfloat16)
    outs = []
    for c in range(FLOWS):
        part = lax.slice_in_dim(normed, c * step, (c + 1) * step, axis=0)
        gathered = lax.all_gather(part, "mp", axis=0, tiled=True)
        hidden = jax.nn.gelu(
            jnp.dot(gathered, up_weight, preferred_element_type=jnp.float32) + up_bias,
            approximate=True,
        ).astype(jnp.bfloat16)
        partial = jnp.dot(hidden, down_weight, preferred_element_type=jnp.float32).astype(jnp.bfloat16)
        summed = lax.psum_scatter(partial, "mp", scatter_dimension=0, tiled=True).astype(jnp.float32)
        own = lax.slice_in_dim(tokens, c * step, (c + 1) * step, axis=0).astype(jnp.float32)
        outs.append((own + gate_own * (summed + down_bias)).astype(jnp.bfloat16))
    block_out = jnp.concatenate(outs, axis=0)

    group = FLOWS // HEAD_FLOWS
    half = rows // HEAD_FLOWS // 2
    noise = gumbel_noise.reshape(pairs, NEW // rows, HEAD_FLOWS, 2, half, vocab)
    peaks, totals, codes = [], [], []
    for c in range(HEAD_FLOWS):
        part = jnp.concatenate(outs[c * group : (c + 1) * group], axis=0)
        first, second = part[:half], part[half:]
        kept = jnp.where(upper == 0, first, second)
        sent = jnp.where(upper == 0, second, first)
        came = permute_devices(sent, dp, mp, swap)
        cond = jnp.where(upper == 0, kept, came)
        uncond = jnp.where(upper == 0, came, kept)
        mixed = (
            (1.0 + GUIDE) * modulate(cond, head_cond) - GUIDE * modulate(uncond, head_uncond)
        ).astype(jnp.bfloat16)
        crossed = permute_devices(mixed, dp, mp, cross)
        mixed = jnp.where(stays, mixed, crossed)
        gathered = lax.all_gather(mixed, "mp", axis=0, tiled=True)
        logits = jnp.dot(gathered, head_weight, preferred_element_type=jnp.float32) + head_bias
        logits = logits.reshape(2, half_mp, half, vocab)
        order = jnp.transpose(logits, (1, 0, 2, 3)).reshape(pairs, NEW // rows, 2, half, vocab)
        scores = order + noise[:, :, c]
        peak = jnp.max(scores, axis=-1)
        weights = jnp.exp(scores - peak[..., None]).astype(jnp.bfloat16)
        totals.append(jnp.sum(weights.astype(jnp.float32), axis=-1))
        codes.append(jnp.dot(weights, codebook, preferred_element_type=jnp.float32))
        peaks.append(peak)
    stack = lambda parts: jnp.stack(parts, axis=2)
    peak = stack(peaks).reshape(pairs, 1, NEW)
    total = stack(totals).reshape(pairs, 1, NEW)
    code = stack(codes).reshape(pairs, NEW, channels).transpose(0, 2, 1)
    stats = jnp.concatenate([code, total, peak], axis=1)

    cells = f_hat.shape[2]
    band = cells // SIDE
    padded = jnp.pad(stats, ((0, 0), (0, 0), (SIDE, SIDE)))
    windows = jnp.stack(
        [padded[:, :, m * cells : m * cells + cells + 2 * SIDE] for m in range(mp)], axis=0
    )
    parts = lax.all_to_all(windows, "mp", 0, 0, tiled=True)
    top = jnp.max(parts[:, :, channels + 1], axis=0)
    factor = jnp.exp(parts[:, :, channels + 1] - top[None])[:, :, None]
    sums = jnp.sum(parts[:, :, : channels + 1] * factor, axis=0)
    cell_index = m_index * cells - SIDE + jnp.arange(cells + 2 * SIDE)
    inside = (cell_index >= 0) & (cell_index < NEW)
    soft = jnp.where(inside, sums[:, :channels] / jnp.where(inside, sums[:, channels:], 1.0), 0.0)
    code_map = soft.reshape(pairs, channels, band + 2, SIDE)
    wide = jnp.pad(code_map, ((0, 0), (0, 0), (0, 0), (1, 1)))
    taps = jnp.stack(
        [wide[:, :, i : i + band, j : j + SIDE] for i in range(3) for j in range(3)], axis=2
    ).reshape(pairs, channels * 9, cells)
    conv = jnp.einsum(
        "ok,pkn->pon",
        phi_weight.reshape(channels, channels * 9),
        taps,
        precision=lax.Precision.HIGHEST,
        preferred_element_type=jnp.float32,
    ) + phi_bias[None, :, None]
    f_hat_out = f_hat + 0.5 * soft[:, :, SIDE : SIDE + cells] + 0.5 * conv
    return (block_out, f_hat_out)


SCALARS = pl.BlockSpec(memory_space=pltpu.SMEM)
ON_CHIP = pl.BlockSpec(memory_space=pltpu.VMEM)
VMEM_LIMIT = 16 * 1024 * 1024
AHEAD = 40_000_000_000
MID, UPPER, IMAGE, ODD, SAME, CORE = range(6)


def call(kernel, where, args, outs, scratch=(), flops=0, specs=None, limit=VMEM_LIMIT):
    return pl.pallas_call(
        kernel,
        out_shape=outs,
        in_specs=[SCALARS] + (specs or [ON_CHIP] * len(args)),
        out_specs=[ON_CHIP] * len(outs),
        scratch_shapes=scratch,
        compiler_params=pltpu.CompilerParams(vmem_limit_bytes=limit),
        cost_estimate=pl.CostEstimate(flops=flops, bytes_accessed=0, transcendentals=0),
    )(where, *args)


def shape_of(shape, kind=jnp.bfloat16):
    return jax.ShapeDtypeStruct(shape, kind)


def after(value, *others):
    return lax.optimization_barrier((value, *others))[0]


def modulated(values, ada_ref, image):
    shift, scale = ada_ref[image, 0:1, :], ada_ref[image, 1:2, :]
    return norm_rows(values.astype(jnp.float32)) * (1.0 + scale) + shift


def norm_kernel(begin, where_ref, tokens_ref, ada_ref, out_ref):
    values = tokens_ref[begin : begin + out_ref.shape[0], :]
    out_ref[...] = modulated(values, ada_ref, where_ref[IMAGE]).astype(jnp.bfloat16)


def norm_part(where, tokens, ada, begin, size):
    outs = [shape_of((size, tokens.shape[1]))]
    return call(functools.partial(norm_kernel, begin), where, (tokens, ada), outs)[0]


def ffn_kernel(groups, tile, fetch, where_ref, *refs):
    count = sum(groups)
    parts = refs[:count]
    up_a, up_b, down_a, down_b, bias_a, bias_b = refs[count : count + 6]
    outs = refs[count + 6 : count + 6 + len(groups)]
    x_ref, hidden_ref, *own = refs[count + 6 + len(groups) :]
    order = list(range(0, 2 * down_a.shape[0], tile))
    copies = []
    if fetch:
        up_own, down_own, sems = own
        copies = [
            pltpu.make_async_copy(up_a, up_own, sems.at[0]),
            pltpu.make_async_copy(down_a, down_own, sems.at[1]),
        ]
        for copy in copies:
            copy.start()
        up_a, down_a = up_own, down_own
        order = [t for t in order if t >= down_a.shape[0]] + [t for t in order if t < down_a.shape[0]]
    panel, width = down_a.shape
    step = outs[0].shape[0]
    place = 0
    for g, size in enumerate(groups):
        if size == 1:
            value = parts[place][...]
        else:
            value = jnp.where(where_ref[MID] == 1, parts[place][...], parts[place + 1][...])
        x_ref[g * step : (g + 1) * step, :] = value
        place += size

    def columns(first, second, begin, end):
        if end <= panel:
            return first[:, begin:end]
        if begin >= panel:
            return second[:, begin - panel : end - panel]
        return jnp.concatenate([first[:, begin:panel], second[:, : end - panel]], axis=1)

    for begin in order:
        end = begin + tile
        if fetch and begin == 0:
            copies[0].wait()
        v = jnp.dot(x_ref[...], columns(up_a, up_b, begin, end), preferred_element_type=jnp.float32)
        v = v + columns(bias_a, bias_b, begin, end)
        hidden_ref[:, begin:end] = jax.nn.gelu(v, approximate=True).astype(jnp.bfloat16)
    if fetch:
        copies[1].wait()
    for begin in range(0, width, tile):
        cols = slice(begin, begin + tile)
        weight = jnp.concatenate([down_a[:, cols], down_b[:, cols]], axis=0)
        result = jnp.dot(hidden_ref[...], weight, preferred_element_type=jnp.float32)
        for g in range(len(groups)):
            outs[g][:, cols] = result[g * step : (g + 1) * step].astype(jnp.bfloat16)


def ffn(where, slots, panels, fetch=False):
    groups = tuple(len(slot) for slot in slots)
    parts = [part for slot in slots for part in slot]
    rows, width = parts[0].shape
    total = rows * len(slots)
    up, down = panels[0], panels[2]
    if fetch:
        panels = [
            pltpu.with_memory_space_constraint(p, pltpu.HBM) if i in (0, 2) else p for i, p in enumerate(panels)
        ]
    own = [pltpu.VMEM(up.shape, up.dtype), pltpu.VMEM(down.shape, down.dtype), pltpu.SemaphoreType.DMA((2,))]
    in_place = pl.BlockSpec(memory_space=pltpu.HBM)
    specs = [in_place if fetch and i in (0, 2) else ON_CHIP for i in range(len(panels))]
    return call(
        functools.partial(ffn_kernel, groups, 256, fetch),
        where,
        (*parts, *panels),
        [shape_of((rows, width))] * len(slots),
        scratch=[
            pltpu.VMEM((total, width), jnp.bfloat16),
            pltpu.VMEM((total, 2 * down.shape[0]), jnp.bfloat16),
            *(own if fetch else []),
        ],
        specs=[ON_CHIP] * len(parts) + specs,
        limit=VMEM_LIMIT + 8 * 1024 * 1024 if fetch else VMEM_LIMIT,
    )


def add_kernel(always, where_ref, a_ref, b_ref, out_ref):
    b = b_ref[...].astype(jnp.float32)
    if not always:
        b = jnp.where(where_ref[MID] == 1, b, 0.0)
    out_ref[...] = (a_ref[...].astype(jnp.float32) + b).astype(jnp.bfloat16)


def add(where, a, b, always=False, flops=0):
    return call(functools.partial(add_kernel, always), where, (a, b), [shape_of(a.shape)], flops=flops)[0]


def out_kernel(begin, always, where_ref, own_ref, near_ref, far_ref, tokens_ref, gate_ref, bias_ref, ada_ref, *refs):
    out_ref, kept_ref, sent_ref = refs[-3:]
    far = far_ref[...].astype(jnp.float32)
    if not always:
        far = jnp.where(where_ref[MID] == 1, far, 0.0)
    summed = own_ref[...].astype(jnp.float32) + near_ref[...].astype(jnp.float32) + far
    rows = summed.shape[0]
    tokens = tokens_ref[begin : begin + rows, :].astype(jnp.float32)
    gate = gate_ref[pl.ds(where_ref[IMAGE], 1), :]
    value = (tokens + gate * (summed + bias_ref[...])).astype(jnp.bfloat16)
    if len(refs) > 3:
        out_ref[0:begin, :] = refs[0][...]
        out_ref[begin : begin + rows, :] = value
    else:
        out_ref[...] = value
    half = rows // 2
    lower = where_ref[UPPER] == 0
    kept_ref[...] = jnp.where(lower, value[:half], value[half:])
    sent = jnp.where(lower, value[half:], value[:half])
    sent_ref[...] = modulated(sent, ada_ref, where_ref[IMAGE]).astype(jnp.bfloat16)


def block_rows(where, begin, always, own, near, far, tokens, gate, bias, ada, earlier=()):
    rows, width = own.shape
    full = rows + begin if earlier else rows
    return call(
        functools.partial(out_kernel, begin, always),
        where,
        (own, near, far, tokens, gate, bias, ada, *earlier),
        [shape_of((full, width)), shape_of((rows // 2, width)), shape_of((rows // 2, width))],
    )


def mix_kernel(where_ref, kept_ref, came_ref, ada_ref, out_ref):
    kept, came = modulated(kept_ref[...], ada_ref, where_ref[IMAGE]), came_ref[...].astype(jnp.float32)
    lower = where_ref[UPPER] == 0
    share = jnp.where(lower, 1.0 + GUIDE, -GUIDE)
    other = jnp.where(lower, -GUIDE, 1.0 + GUIDE)
    out_ref[...] = (share * kept + other * came).astype(jnp.bfloat16)


def mix_twins(where, kept, came, ada):
    return call(mix_kernel, where, (kept, came, ada), [shape_of(kept.shape)])[0]


def head_kernel(
    begin, where_ref, own_ref, near_ref, far_ref, last_ref, weight_a, weight_b, bias_a, bias_b, code_a, code_b,
    noise_own, noise_core, noise_twin, noise_both, stats_ref, x_ref
):
    step = own_ref.shape[0]
    for r, ref in enumerate((own_ref, near_ref, far_ref, last_ref)):
        x_ref[r * step : (r + 1) * step, :] = ref[...]
    x = x_ref[...]
    odd = where_ref[ODD]
    even = 1 - odd
    same = where_ref[SAME] == 1
    scores = []
    for weight, bias, ours, theirs in (
        (weight_a, bias_a, noise_own, noise_twin),
        (weight_b, bias_b, noise_core, noise_both),
    ):
        picked = []
        for first in (True, False):
            for block in (odd, even):
                a, b = ours[block, begin : begin + step, :], theirs[block, begin : begin + step, :]
                picked.append(jnp.where(same, a, b) if first else jnp.where(same, b, a))
        logits = jnp.dot(x, weight[...], preferred_element_type=jnp.float32)
        scores.append(logits + bias[:, bias.shape[1] - weight.shape[1] :] + jnp.concatenate(picked, axis=0))
    peak = jnp.max(jnp.maximum(scores[0], scores[1]), axis=1, keepdims=True)
    sums = 0.0
    total = 0.0
    for score, code in zip(scores, (code_a, code_b)):
        weights = jnp.exp(score - peak).astype(jnp.bfloat16)
        total = total + jnp.sum(weights.astype(jnp.float32), axis=1, keepdims=True)
        sums = sums + lax.dot_general(
            weights, code[...], (((1,), (1,)), ((), ())), preferred_element_type=jnp.float32
        )
    channels = code_a.shape[0]
    pad = jnp.zeros((4 * step, 128 - channels), jnp.float32)
    table = jnp.concatenate([sums, pad], axis=1)
    lane = lax.broadcasted_iota(jnp.int32, table.shape, 1)
    table = jnp.where(lane == channels, total, table)
    table = jnp.where(lane == channels + 1, peak, table)
    stats_ref[...] = jnp.transpose(table)[: stats_ref.shape[0], :]


def head_stats(where, begin, slots, heads, noises, flops=0):
    step, width = slots[0].shape
    height = -(-(heads[-1].shape[0] + 2) // 8) * 8
    return call(
        functools.partial(head_kernel, begin),
        where,
        (*slots, *heads, *noises),
        [shape_of((height, 4 * step), jnp.float32)],
        scratch=[pltpu.VMEM((4 * step, width), jnp.bfloat16)],
        flops=flops,
    )[0]


def soft_kernel(channels, where_ref, *refs):
    parts, out_ref = refs[:-1], refs[-1]
    tops = [part[channels + 1 : channels + 2, :] for part in parts]
    top = functools.reduce(jnp.maximum, tops)
    code = 0.0
    total = 0.0
    for part, peak in zip(parts, tops):
        factor = jnp.exp(peak - top)
        code = code + part[0:channels, :] * factor
        total = total + part[channels : channels + 1, :] * factor
    out_ref[...] = code / total


def soft_codes(where, parts, channels):
    outs = [shape_of((channels, parts[0].shape[1]), jnp.float32)]
    return call(functools.partial(soft_kernel, channels), where, tuple(parts), outs)[0]


def refine_kernel(where_ref, first_ref, second_ref, halo_ref, phi_ref, bias_ref, map_ref, out_ref):
    first, second, halo = first_ref[...], second_ref[...], halo_ref[...]
    cells = first.shape[1]
    half = cells // 2
    lane = lax.broadcasted_iota(jnp.int32, first.shape, 1)
    shift = lambda value, by: pltpu.roll(value, by % cells, 1)
    early = where_ref[CORE] == 0
    lower, higher = jnp.where(early, first, second), jnp.where(early, second, first)
    centre = jnp.where(
        early,
        jnp.where(lane < half, lower, shift(higher, half)),
        jnp.where(lane < half, shift(lower, half), higher),
    )
    above = jnp.where(early, shift(halo, SIDE), shift(higher, SIDE - half))
    below = jnp.where(early, shift(lower, half - SIDE), shift(halo, -SIDE))
    rows = (
        jnp.where(lane < SIDE, above, shift(centre, SIDE)),
        centre,
        jnp.where(lane >= cells - SIDE, below, shift(centre, -SIDE)),
    )
    column = lane % SIDE
    conv = jnp.zeros(out_ref.shape, jnp.float32) + bias_ref[...]
    for i, row in enumerate(rows):
        left = jnp.where(column == 0, 0.0, shift(row, 1))
        right = jnp.where(column == SIDE - 1, 0.0, shift(row, -1))
        for j, tap in enumerate((left, row, right)):
            conv = conv + jnp.dot(
                phi_ref[i, j], tap, precision=lax.Precision.HIGHEST, preferred_element_type=jnp.float32
            )
    out_ref[...] = map_ref[...] + 0.5 * centre + 0.5 * conv


def line_body(
    tokens,
    ada_ffn,
    ffn_gate,
    up_weight,
    up_bias,
    down_weight,
    down_bias,
    ada_head,
    head_weight,
    head_bias,
    gumbel_noise,
    codebook,
    phi_weight,
    phi_bias,
    f_hat,
):
    rows = tokens.shape[0]
    dp, mp = lax.axis_size("dp"), lax.axis_size("mp")
    d_index, m_index = lax.axis_index("dp"), lax.axis_index("mp")
    channels = f_hat.shape[1]
    half_dp = dp // 2
    upper = d_index // half_dp
    z_index, core = m_index // 2, m_index % 2
    where = jnp.stack(
        [
            (z_index == 1) | (z_index == 2),
            upper,
            (m_index * rows) // NEW,
            z_index % 2,
            z_index // 2 == upper,
            core,
        ]
    ).astype(jnp.int32)

    def along_z(value, target):
        def to(d, m):
            z = target(m // 2)
            return None if z is None else (d, 2 * z + m % 2)

        return permute_devices(value, dp, mp, to)

    def near(value):
        return along_z(value, lambda z: z ^ 1)

    def across(value):
        return along_z(value, lambda z: z ^ 2)

    def middle(value):
        return along_z(value, lambda z: 3 - z if z in (1, 2) else z)

    def outward(value):
        return along_z(value, lambda z: {1: 0, 2: 3}.get(z))

    def inward(value):
        return along_z(value, lambda z: {0: 1, 3: 2}.get(z))

    def swap_cores(value):
        return permute_devices(value, dp, mp, lambda d, m: (d, m ^ 1))

    def swap_twins(value):
        return permute_devices(value, dp, mp, lambda d, m: ((d + half_dp) % dp, m))

    def swap_both(value):
        return permute_devices(value, dp, mp, lambda d, m: ((d + half_dp) % dp, m ^ 1))

    step = rows // CHUNKS
    half = step // 2
    voc = head_bias.shape[0]
    noise = gumbel_noise.reshape(2, 2, CHUNKS, 2, half, voc)

    def noise_for(to_core, to_upper):
        picked = lax.dynamic_slice(
            noise, (0, to_core, 0, to_upper, 0, 0), (2, 1, CHUNKS, 1, half, voc)
        )
        return picked.reshape(2, CHUNKS * half, voc)

    gate, bias_out = ffn_gate, down_bias[None]
    up_other, down_other = swap_cores(up_weight), swap_cores(down_weight)
    biases = jnp.concatenate([up_bias, head_bias])[None]
    codes = codebook.T
    bias_other = swap_cores(biases)

    barrier = lax.optimization_barrier
    own_a = norm_part(where, tokens, ada_ffn, 0, step)
    near_a, mid_a = near(own_a), middle(own_a)
    own_b = norm_part(where, tokens, ada_ffn, step, step)
    noise_own, noise_twin, noise_core, noise_both = (
        noise_for(core, upper),
        noise_for(core, 1 - upper),
        noise_for(1 - core, upper),
        noise_for(1 - core, 1 - upper),
    )
    (
        up_other, down_other, bias_other, near_a, own_b, noise_own, noise_twin, noise_core, noise_both
    ) = barrier(
        (up_other, down_other, bias_other, near_a, own_b, noise_own, noise_twin, noise_core, noise_both)
    )
    panels = (up_weight, up_other, down_weight, down_other, biases, bias_other)
    far_mid_a = middle(near_a)
    near_b = near(after(own_b, near_a))
    mid_a = after(mid_a, near_a)
    far_end_a = outward(mid_a)
    noise_twin = swap_twins(after(noise_twin, near_a))
    sum_own_a, sum_near_a = ffn(where, [[own_a], [after(near_a, mid_a)]], panels, fetch=True)
    far_mid_a = after(far_mid_a, sum_near_a)
    last_end_a = outward(far_mid_a)
    mid_b = middle(after(own_b, far_mid_a))
    noise_core = swap_cores(after(noise_core, far_mid_a))
    (sum_far_a,) = ffn(where, [[far_mid_a, far_end_a]], panels)
    came_far_a = inward(sum_far_a)
    near_b, mid_b = barrier((near_b, mid_b, sum_far_a))[:2]
    far_mid_b, far_end_b = middle(near_b), outward(mid_b)
    (sum_last_a,) = ffn(where, [[mid_a, after(last_end_a, near_b, mid_b)]], panels)
    came_last_a = inward(sum_last_a)
    far_mid_b = after(far_mid_b, sum_last_a)
    last_end_b = outward(far_mid_b)
    both_last_a = add(where, after(sum_last_a, far_mid_b), came_far_a)
    went_last_a = middle(both_last_a)
    sum_own_b, sum_near_b = ffn(where, [[after(own_b, both_last_a, far_end_b)], [near_b]], panels)
    noise_both = swap_both(after(noise_both, noise_twin))
    both_far_a = add(where, after(sum_far_a, went_last_a, sum_near_b), came_last_a)
    went_far_a = middle(both_far_a)
    sum_far_b, sum_last_b = ffn(
        where, [[after(far_mid_b, both_far_a), far_end_b], [mid_b, last_end_b]], panels
    )
    came_last_b = near(sum_last_b)
    head_other = swap_cores(after(head_weight, sum_last_b))
    code_other = swap_cores(after(codes, sum_last_b))
    came_near_b = near(after(sum_near_b, last_end_b))
    both_near_a = add(where, sum_near_a, after(went_far_a, came_near_b, noise_twin), flops=AHEAD)
    came_near_a = near(both_near_a)
    both_far_b = add(where, after(sum_far_b, both_near_a), came_last_b, always=True)
    went_far_b = across(both_far_b)
    out_a, kept_a, sent_a = block_rows(
        where, 0, False, sum_own_a, after(came_near_a, noise_both, noise_core), went_last_a, tokens, gate, bias_out, ada_head
    )
    came_a = swap_twins(sent_a)
    mixed_a = mix_twins(where, kept_a, came_a, ada_head)
    mix_near_a, mix_far_a = near(mixed_a), across(mixed_a)
    block_out, kept_b, sent_b = block_rows(
        where, step, True, sum_own_b, after(came_near_b, mixed_a, head_other, code_other), went_far_b, tokens, gate, bias_out, ada_head, (out_a,)
    )
    came_b = after(swap_twins(sent_b), mix_far_a)
    mix_last_a = near(mix_far_a)
    mixed_b = mix_twins(where, kept_b, came_b, ada_head)
    mix_near_b, mix_far_b = near(mixed_b), across(mixed_b)
    heads = (head_weight, head_other, biases, bias_other, codes, code_other)
    noises = (noise_own, noise_core, noise_twin, noise_both)
    stats_a = head_stats(
        where, 0, (after(mixed_a, mixed_b), mix_near_a, mix_far_a, mix_last_a), heads, noises, flops=AHEAD
    )
    mix_last_b = near(after(mix_far_b, stats_a))
    stats_b = head_stats(where, half, (after(mixed_b, stats_a), mix_near_b, mix_far_b, mix_last_b), heads, noises)

    slots = [
        jnp.concatenate([part[:, r * half : (r + 1) * half] for part in (stats_a, stats_b)], axis=1) for r in range(4)
    ]
    parts = [slots[0]] + [along_z(slots[r], lambda z, r=r: z ^ r) for r in (1, 2, 3)]
    soft = soft_codes(where, parts, channels)

    def to_cells(d, m, core_of):
        y, x = d // half_dp, d % half_dp
        z, c = m // 2, m % 2
        return ((z // 2) * half_dp + x, 2 * (2 * (z % 2) + c) + core_of(y))

    def to_halo(d, m):
        y, x = d // half_dp, d % half_dp
        z, c = m // 2, m % 2
        block = 2 * (z % 2) + c + (1 if y == 1 else -1)
        if block < 0 or block > 3:
            return None
        return ((z // 2) * half_dp + x, 2 * block + (0 if y == 1 else 1))

    first = permute_devices(soft, dp, mp, lambda d, m: to_cells(d, m, lambda y: y))
    second = permute_devices(soft, dp, mp, lambda d, m: to_cells(d, m, lambda y: 1 - y))
    halo = permute_devices(soft, dp, mp, to_halo)
    f_hat_out = call(
        refine_kernel,
        where,
        (first, second, halo, jnp.transpose(phi_weight, (2, 3, 0, 1)), phi_bias[:, None], f_hat[0]),
        [shape_of(f_hat.shape[1:], jnp.float32)],
    )[0]
    return (block_out, f_hat_out[None])


def solution(mesh):
    in_specs = (
        P(("dp", "mp"), None),
        P("dp", None, None),
        P("dp", None),
        P(None, "mp"),
        P("mp"),
        P("mp", None),
        P(),
        P("dp", None, None),
        P(None, "mp"),
        P("mp"),
        P("dp", None, "mp"),
        P("mp", None),
        P(),
        P(),
        P("dp", None, "mp"),
    )
    out_specs = (P(("dp", "mp"), None), P("dp", None, "mp"))
    line = mesh.shape["dp"] == 4 and mesh.shape["mp"] == 8
    body = line_body if line else general_body
    return jax.shard_map(body, mesh=mesh, in_specs=in_specs, out_specs=out_specs, check_vma=False)
```

```python
import functools

import jax
import jax.numpy as jnp
from jax import lax
from jax.experimental import pallas as pl
from jax.experimental.pallas import tpu as pltpu
from jax.sharding import PartitionSpec as P

SIDE = 32
NEW = 1024
GUIDE = 1.5
CHUNKS = 2
FLOWS = 4
HEAD_FLOWS = 2


def norm_rows(values):
    row_mean = jnp.mean(values, axis=-1, keepdims=True)
    centred = values - row_mean
    spread = jnp.mean(centred * centred, axis=-1, keepdims=True)
    return centred * lax.rsqrt(spread + 1e-06)


def modulate(values, ada):
    return norm_rows(values.astype(jnp.float32)) * (1.0 + ada[1]) + ada[0]


def permute_devices(value, dp, mp, target):
    pairs = []
    for d in range(dp):
        for m in range(mp):
            to = target(d, m)
            if to is not None:
                pairs.append((d * mp + m, to[0] * mp + to[1]))
    return lax.ppermute(value, ("dp", "mp"), pairs)


def general_body(
    tokens,
    ada_ffn,
    ffn_gate,
    up_weight,
    up_bias,
    down_weight,
    down_bias,
    ada_head,
    head_weight,
    head_bias,
    gumbel_noise,
    codebook,
    phi_weight,
    phi_bias,
    f_hat,
):
    rows, width = tokens.shape
    dp, mp = lax.axis_size("dp"), lax.axis_size("mp")
    d_index, m_index = lax.axis_index("dp"), lax.axis_index("mp")
    images = ada_ffn.shape[0]
    pairs = f_hat.shape[0]
    channels = f_hat.shape[1]
    vocab = head_weight.shape[1]
    own_image = (m_index * rows) // NEW
    ada_own = lax.dynamic_index_in_dim(ada_ffn, own_image, 0, keepdims=False)
    gate_own = lax.dynamic_index_in_dim(ffn_gate, own_image, 0, keepdims=False)
    head_own = lax.dynamic_index_in_dim(ada_head, own_image, 0, keepdims=False)
    half_dp, half_mp = dp // 2, mp // 2
    upper = d_index // half_dp

    def swap(d, m):
        return ((d + half_dp) % dp, m)

    def cross(d, m):
        if d // half_dp == m // half_mp:
            return None
        return ((d + half_dp) % dp, (m + half_mp) % mp)

    stays = upper == m_index // half_mp
    head_twin = permute_devices(head_own, dp, mp, swap)
    head_cond = jnp.where(upper == 0, head_own, head_twin)
    head_uncond = jnp.where(upper == 0, head_twin, head_own)

    step = rows // FLOWS
    normed = modulate(tokens, ada_own).astype(jnp.bfloat16)
    outs = []
    for c in range(FLOWS):
        part = lax.slice_in_dim(normed, c * step, (c + 1) * step, axis=0)
        gathered = lax.all_gather(part, "mp", axis=0, tiled=True)
        hidden = jax.nn.gelu(
            jnp.dot(gathered, up_weight, preferred_element_type=jnp.float32) + up_bias,
            approximate=True,
        ).astype(jnp.bfloat16)
        partial = jnp.dot(hidden, down_weight, preferred_element_type=jnp.float32).astype(jnp.bfloat16)
        summed = lax.psum_scatter(partial, "mp", scatter_dimension=0, tiled=True).astype(jnp.float32)
        own = lax.slice_in_dim(tokens, c * step, (c + 1) * step, axis=0).astype(jnp.float32)
        outs.append((own + gate_own * (summed + down_bias)).astype(jnp.bfloat16))
    block_out = jnp.concatenate(outs, axis=0)

    group = FLOWS // HEAD_FLOWS
    half = rows // HEAD_FLOWS // 2
    noise = gumbel_noise.reshape(pairs, NEW // rows, HEAD_FLOWS, 2, half, vocab)
    peaks, totals, codes = [], [], []
    for c in range(HEAD_FLOWS):
        part = jnp.concatenate(outs[c * group : (c + 1) * group], axis=0)
        first, second = part[:half], part[half:]
        kept = jnp.where(upper == 0, first, second)
        sent = jnp.where(upper == 0, second, first)
        came = permute_devices(sent, dp, mp, swap)
        cond = jnp.where(upper == 0, kept, came)
        uncond = jnp.where(upper == 0, came, kept)
        mixed = (
            (1.0 + GUIDE) * modulate(cond, head_cond) - GUIDE * modulate(uncond, head_uncond)
        ).astype(jnp.bfloat16)
        crossed = permute_devices(mixed, dp, mp, cross)
        mixed = jnp.where(stays, mixed, crossed)
        gathered = lax.all_gather(mixed, "mp", axis=0, tiled=True)
        logits = jnp.dot(gathered, head_weight, preferred_element_type=jnp.float32) + head_bias
        logits = logits.reshape(2, half_mp, half, vocab)
        order = jnp.transpose(logits, (1, 0, 2, 3)).reshape(pairs, NEW // rows, 2, half, vocab)
        scores = order + noise[:, :, c]
        peak = jnp.max(scores, axis=-1)
        weights = jnp.exp(scores - peak[..., None]).astype(jnp.bfloat16)
        totals.append(jnp.sum(weights.astype(jnp.float32), axis=-1))
        codes.append(jnp.dot(weights, codebook, preferred_element_type=jnp.float32))
        peaks.append(peak)
    stack = lambda parts: jnp.stack(parts, axis=2)
    peak = stack(peaks).reshape(pairs, 1, NEW)
    total = stack(totals).reshape(pairs, 1, NEW)
    code = stack(codes).reshape(pairs, NEW, channels).transpose(0, 2, 1)
    stats = jnp.concatenate([code, total, peak], axis=1)

    cells = f_hat.shape[2]
    band = cells // SIDE
    padded = jnp.pad(stats, ((0, 0), (0, 0), (SIDE, SIDE)))
    windows = jnp.stack(
        [padded[:, :, m * cells : m * cells + cells + 2 * SIDE] for m in range(mp)], axis=0
    )
    parts = lax.all_to_all(windows, "mp", 0, 0, tiled=True)
    top = jnp.max(parts[:, :, channels + 1], axis=0)
    factor = jnp.exp(parts[:, :, channels + 1] - top[None])[:, :, None]
    sums = jnp.sum(parts[:, :, : channels + 1] * factor, axis=0)
    cell_index = m_index * cells - SIDE + jnp.arange(cells + 2 * SIDE)
    inside = (cell_index >= 0) & (cell_index < NEW)
    soft = jnp.where(inside, sums[:, :channels] / jnp.where(inside, sums[:, channels:], 1.0), 0.0)
    code_map = soft.reshape(pairs, channels, band + 2, SIDE)
    wide = jnp.pad(code_map, ((0, 0), (0, 0), (0, 0), (1, 1)))
    taps = jnp.stack(
        [wide[:, :, i : i + band, j : j + SIDE] for i in range(3) for j in range(3)], axis=2
    ).reshape(pairs, channels * 9, cells)
    conv = jnp.einsum(
        "ok,pkn->pon",
        phi_weight.reshape(channels, channels * 9),
        taps,
        precision=lax.Precision.HIGHEST,
        preferred_element_type=jnp.float32,
    ) + phi_bias[None, :, None]
    f_hat_out = f_hat + 0.5 * soft[:, :, SIDE : SIDE + cells] + 0.5 * conv
    return (block_out, f_hat_out)


SCALARS = pl.BlockSpec(memory_space=pltpu.SMEM)
ON_CHIP = pl.BlockSpec(memory_space=pltpu.VMEM)
VMEM_LIMIT = 16 * 1024 * 1024
AHEAD = 40_000_000_000
MID, UPPER, IMAGE, ODD, SAME, CORE, FIRST, LAST = range(8)


def call(kernel, where, args, outs, scratch=(), flops=0, specs=None, limit=VMEM_LIMIT):
    return pl.pallas_call(
        kernel,
        out_shape=outs,
        in_specs=[SCALARS] + (specs or [ON_CHIP] * len(args)),
        out_specs=[ON_CHIP] * len(outs),
        scratch_shapes=scratch,
        compiler_params=pltpu.CompilerParams(vmem_limit_bytes=limit),
        cost_estimate=pl.CostEstimate(flops=flops, bytes_accessed=0, transcendentals=0),
    )(where, *args)


def shape_of(shape, kind=jnp.bfloat16):
    return jax.ShapeDtypeStruct(shape, kind)


def after(value, *others):
    return lax.optimization_barrier((value, *others))[0]


def modulated(values, ada_ref, image):
    shift, scale = ada_ref[image, 0:1, :], ada_ref[image, 1:2, :]
    return norm_rows(values.astype(jnp.float32)) * (1.0 + scale) + shift


def norm_kernel(begin, where_ref, tokens_ref, ada_ref, out_ref):
    values = tokens_ref[begin : begin + out_ref.shape[0], :]
    out_ref[...] = modulated(values, ada_ref, where_ref[IMAGE]).astype(jnp.bfloat16)


def norm_part(where, tokens, ada, begin, size):
    outs = [shape_of((size, tokens.shape[1]))]
    return call(functools.partial(norm_kernel, begin), where, (tokens, ada), outs)[0]


def ffn_kernel(groups, tile, fetch, where_ref, *refs):
    count = sum(groups)
    parts = refs[:count]
    up_a, up_b, down_a, down_b, bias_a, bias_b = refs[count : count + 6]
    outs = refs[count + 6 : count + 6 + len(groups)]
    x_ref, hidden_ref, *own = refs[count + 6 + len(groups) :]
    order = list(range(0, 2 * down_a.shape[0], tile))
    copies = []
    if fetch:
        up_own, down_own, sems = own
        copies = [
            pltpu.make_async_copy(up_a, up_own, sems.at[0]),
            pltpu.make_async_copy(down_a, down_own, sems.at[1]),
        ]
        for copy in copies:
            copy.start()
        up_a, down_a = up_own, down_own
        order = [t for t in order if t >= down_a.shape[0]] + [t for t in order if t < down_a.shape[0]]
    panel, width = down_a.shape
    step = outs[0].shape[0]
    place = 0
    for g, size in enumerate(groups):
        if size == 1:
            value = parts[place][...]
        else:
            value = jnp.where(where_ref[MID] == 1, parts[place][...], parts[place + 1][...])
        x_ref[g * step : (g + 1) * step, :] = value
        place += size

    def columns(first, second, begin, end):
        if end <= panel:
            return first[:, begin:end]
        if begin >= panel:
            return second[:, begin - panel : end - panel]
        return jnp.concatenate([first[:, begin:panel], second[:, : end - panel]], axis=1)

    for begin in order:
        end = begin + tile
        if fetch and begin == 0:
            copies[0].wait()
        v = jnp.dot(x_ref[...], columns(up_a, up_b, begin, end), preferred_element_type=jnp.float32)
        v = v + columns(bias_a, bias_b, begin, end)
        hidden_ref[:, begin:end] = jax.nn.gelu(v, approximate=True).astype(jnp.bfloat16)
    if fetch:
        copies[1].wait()
    for begin in range(0, width, tile):
        cols = slice(begin, begin + tile)
        weight = jnp.concatenate([down_a[:, cols], down_b[:, cols]], axis=0)
        result = jnp.dot(hidden_ref[...], weight, preferred_element_type=jnp.float32)
        for g in range(len(groups)):
            outs[g][:, cols] = result[g * step : (g + 1) * step].astype(jnp.bfloat16)


def ffn(where, slots, panels, fetch=False):
    groups = tuple(len(slot) for slot in slots)
    parts = [part for slot in slots for part in slot]
    rows, width = parts[0].shape
    total = rows * len(slots)
    up, down = panels[0], panels[2]
    if fetch:
        panels = [
            pltpu.with_memory_space_constraint(p, pltpu.HBM) if i in (0, 2) else p for i, p in enumerate(panels)
        ]
    own = [pltpu.VMEM(up.shape, up.dtype), pltpu.VMEM(down.shape, down.dtype), pltpu.SemaphoreType.DMA((2,))]
    in_place = pl.BlockSpec(memory_space=pltpu.HBM)
    specs = [in_place if fetch and i in (0, 2) else ON_CHIP for i in range(len(panels))]
    return call(
        functools.partial(ffn_kernel, groups, 256, fetch),
        where,
        (*parts, *panels),
        [shape_of((rows, width))] * len(slots),
        scratch=[
            pltpu.VMEM((total, width), jnp.bfloat16),
            pltpu.VMEM((total, 2 * down.shape[0]), jnp.bfloat16),
            *(own if fetch else []),
        ],
        specs=[ON_CHIP] * len(parts) + specs,
        limit=VMEM_LIMIT + 8 * 1024 * 1024 if fetch else VMEM_LIMIT,
    )


def add_kernel(always, where_ref, a_ref, b_ref, out_ref):
    b = b_ref[...].astype(jnp.float32)
    if not always:
        b = jnp.where(where_ref[MID] == 1, b, 0.0)
    out_ref[...] = (a_ref[...].astype(jnp.float32) + b).astype(jnp.bfloat16)


def add(where, a, b, always=False, flops=0):
    return call(functools.partial(add_kernel, always), where, (a, b), [shape_of(a.shape)], flops=flops)[0]


def out_kernel(begin, always, where_ref, own_ref, near_ref, far_ref, tokens_ref, gate_ref, bias_ref, ada_ref, *refs):
    out_ref, kept_ref, sent_ref = refs[-3:]
    far = far_ref[...].astype(jnp.float32)
    if not always:
        far = jnp.where(where_ref[MID] == 1, far, 0.0)
    summed = own_ref[...].astype(jnp.float32) + near_ref[...].astype(jnp.float32) + far
    rows = summed.shape[0]
    tokens = tokens_ref[begin : begin + rows, :].astype(jnp.float32)
    gate = gate_ref[pl.ds(where_ref[IMAGE], 1), :]
    value = (tokens + gate * (summed + bias_ref[...])).astype(jnp.bfloat16)
    if len(refs) > 3:
        out_ref[0:begin, :] = refs[0][...]
        out_ref[begin : begin + rows, :] = value
    else:
        out_ref[...] = value
    half = rows // 2
    lower = where_ref[UPPER] == 0
    kept_ref[...] = jnp.where(lower, value[:half], value[half:])
    sent = jnp.where(lower, value[half:], value[:half])
    sent_ref[...] = modulated(sent, ada_ref, where_ref[IMAGE]).astype(jnp.bfloat16)


def block_rows(where, begin, always, own, near, far, tokens, gate, bias, ada, earlier=()):
    rows, width = own.shape
    full = rows + begin if earlier else rows
    return call(
        functools.partial(out_kernel, begin, always),
        where,
        (own, near, far, tokens, gate, bias, ada, *earlier),
        [shape_of((full, width)), shape_of((rows // 2, width)), shape_of((rows // 2, width))],
    )


def mix_kernel(where_ref, kept_ref, came_ref, ada_ref, out_ref):
    kept, came = modulated(kept_ref[...], ada_ref, where_ref[IMAGE]), came_ref[...].astype(jnp.float32)
    lower = where_ref[UPPER] == 0
    share = jnp.where(lower, 1.0 + GUIDE, -GUIDE)
    other = jnp.where(lower, -GUIDE, 1.0 + GUIDE)
    out_ref[...] = (share * kept + other * came).astype(jnp.bfloat16)


def mix_twins(where, kept, came, ada):
    return call(mix_kernel, where, (kept, came, ada), [shape_of(kept.shape)])[0]


def head_kernel(
    begin, where_ref, own_ref, near_ref, far_ref, last_ref, weight_a, weight_b, bias_a, bias_b, code_a, code_b,
    noise_own, noise_core, noise_twin, noise_both, stats_ref, x_ref
):
    step = own_ref.shape[0]
    for r, ref in enumerate((own_ref, near_ref, far_ref, last_ref)):
        x_ref[r * step : (r + 1) * step, :] = ref[...]
    x = x_ref[...]
    odd = where_ref[ODD]
    even = 1 - odd
    same = where_ref[SAME] == 1
    scores = []
    for weight, bias, ours, theirs in (
        (weight_a, bias_a, noise_own, noise_twin),
        (weight_b, bias_b, noise_core, noise_both),
    ):
        picked = []
        for first in (True, False):
            for block in (odd, even):
                a, b = ours[block, begin : begin + step, :], theirs[block, begin : begin + step, :]
                picked.append(jnp.where(same, a, b) if first else jnp.where(same, b, a))
        logits = jnp.dot(x, weight[...], preferred_element_type=jnp.float32)
        scores.append(logits + bias[:, bias.shape[1] - weight.shape[1] :] + jnp.concatenate(picked, axis=0))
    peak = jnp.max(jnp.maximum(scores[0], scores[1]), axis=1, keepdims=True)
    sums = 0.0
    total = 0.0
    for score, code in zip(scores, (code_a, code_b)):
        weights = jnp.exp(score - peak).astype(jnp.bfloat16)
        total = total + jnp.sum(weights.astype(jnp.float32), axis=1, keepdims=True)
        sums = sums + lax.dot_general(
            weights, code[...], (((1,), (1,)), ((), ())), preferred_element_type=jnp.float32
        )
    channels = code_a.shape[0]
    pad = jnp.zeros((4 * step, 128 - channels), jnp.float32)
    table = jnp.concatenate([sums, pad], axis=1)
    lane = lax.broadcasted_iota(jnp.int32, table.shape, 1)
    table = jnp.where(lane == channels, total, table)
    table = jnp.where(lane == channels + 1, peak, table)
    stats_ref[...] = jnp.transpose(table)[: stats_ref.shape[0], :]


def head_stats(where, begin, slots, heads, noises, flops=0):
    step, width = slots[0].shape
    height = -(-(heads[-1].shape[0] + 2) // 8) * 8
    return call(
        functools.partial(head_kernel, begin),
        where,
        (*slots, *heads, *noises),
        [shape_of((height, 4 * step), jnp.float32)],
        scratch=[pltpu.VMEM((4 * step, width), jnp.bfloat16)],
        flops=flops,
    )[0]


def soft_kernel(channels, where_ref, *refs):
    parts, out_ref = refs[:-1], refs[-1]
    tops = [part[channels + 1 : channels + 2, :] for part in parts]
    top = functools.reduce(jnp.maximum, tops)
    code = 0.0
    total = 0.0
    for part, peak in zip(parts, tops):
        factor = jnp.exp(peak - top)
        code = code + part[0:channels, :] * factor
        total = total + part[channels : channels + 1, :] * factor
    out_ref[...] = code / total


def soft_codes(where, parts, channels):
    outs = [shape_of((channels, parts[0].shape[1]), jnp.float32)]
    return call(functools.partial(soft_kernel, channels), where, tuple(parts), outs)[0]


def refine_kernel(where_ref, first_ref, second_ref, halo_ref, phi_ref, bias_ref, map_ref, out_ref):
    first, second, halo = first_ref[...], second_ref[...], halo_ref[...]
    cells = first.shape[1]
    half = cells // 2
    lane = lax.broadcasted_iota(jnp.int32, first.shape, 1)
    shift = lambda value, by: pltpu.roll(value, by % cells, 1)
    early = where_ref[CORE] == 0
    lower, higher = jnp.where(early, first, second), jnp.where(early, second, first)
    centre = jnp.where(
        early,
        jnp.where(lane < half, lower, shift(higher, half)),
        jnp.where(lane < half, shift(lower, half), higher),
    )
    before = jnp.where(where_ref[FIRST] == 1, 0.0, shift(halo, SIDE))
    behind = jnp.where(where_ref[LAST] == 1, 0.0, shift(halo, -SIDE))
    above = jnp.where(early, before, shift(higher, SIDE - half))
    below = jnp.where(early, shift(lower, half - SIDE), behind)
    rows = (
        jnp.where(lane < SIDE, above, shift(centre, SIDE)),
        centre,
        jnp.where(lane >= cells - SIDE, below, shift(centre, -SIDE)),
    )
    column = lane % SIDE
    conv = jnp.zeros(out_ref.shape, jnp.float32) + bias_ref[...]
    for i, row in enumerate(rows):
        left = jnp.where(column == 0, 0.0, shift(row, 1))
        right = jnp.where(column == SIDE - 1, 0.0, shift(row, -1))
        for j, tap in enumerate((left, row, right)):
            conv = conv + jnp.dot(
                phi_ref[i, j], tap, precision=lax.Precision.HIGHEST, preferred_element_type=jnp.float32
            )
    out_ref[...] = map_ref[...] + 0.5 * centre + 0.5 * conv


def line_body(
    tokens,
    ada_ffn,
    ffn_gate,
    up_weight,
    up_bias,
    down_weight,
    down_bias,
    ada_head,
    head_weight,
    head_bias,
    gumbel_noise,
    codebook,
    phi_weight,
    phi_bias,
    f_hat,
):
    rows = tokens.shape[0]
    dp, mp = lax.axis_size("dp"), lax.axis_size("mp")
    d_index, m_index = lax.axis_index("dp"), lax.axis_index("mp")
    channels = f_hat.shape[1]
    half_dp = dp // 2
    upper = d_index // half_dp
    z_index, core = m_index // 2, m_index % 2
    where = jnp.stack(
        [
            (z_index == 1) | (z_index == 2),
            upper,
            (m_index * rows) // NEW,
            z_index % 2,
            z_index // 2 == upper,
            core,
            z_index == 0,
            z_index == mp // 2 - 1,
        ]
    ).astype(jnp.int32)

    def along_z(value, target):
        def to(d, m):
            z = target(m // 2)
            return None if z is None else (d, 2 * z + m % 2)

        return permute_devices(value, dp, mp, to)

    def near(value):
        return along_z(value, lambda z: z ^ 1)

    def across(value):
        return along_z(value, lambda z: z ^ 2)

    def middle(value):
        return along_z(value, lambda z: 3 - z if z in (1, 2) else z)

    def outward(value):
        return along_z(value, lambda z: {1: 0, 2: 3}.get(z))

    def inward(value):
        return along_z(value, lambda z: {0: 1, 3: 2}.get(z))

    def swap_cores(value):
        return permute_devices(value, dp, mp, lambda d, m: (d, m ^ 1))

    def swap_twins(value):
        return permute_devices(value, dp, mp, lambda d, m: ((d + half_dp) % dp, m))

    def swap_both(value):
        return permute_devices(value, dp, mp, lambda d, m: ((d + half_dp) % dp, m ^ 1))

    step = rows // CHUNKS
    half = step // 2
    voc = head_bias.shape[0]
    noise = gumbel_noise.reshape(2, 2, CHUNKS, 2, half, voc)

    def noise_for(to_core, to_upper):
        picked = lax.dynamic_slice(
            noise, (0, to_core, 0, to_upper, 0, 0), (2, 1, CHUNKS, 1, half, voc)
        )
        return picked.reshape(2, CHUNKS * half, voc)

    gate, bias_out = ffn_gate, down_bias[None]
    up_other, down_other = swap_cores(up_weight), swap_cores(down_weight)
    biases = jnp.concatenate([up_bias, head_bias])[None]
    codes = codebook.T
    bias_other = swap_cores(biases)

    barrier = lax.optimization_barrier
    own_a = norm_part(where, tokens, ada_ffn, 0, step)
    near_a, mid_a = near(own_a), middle(own_a)
    own_b = norm_part(where, tokens, ada_ffn, step, step)
    noise_own, noise_twin, noise_core, noise_both = (
        noise_for(core, upper),
        noise_for(core, 1 - upper),
        noise_for(1 - core, upper),
        noise_for(1 - core, 1 - upper),
    )
    (
        up_other, down_other, bias_other, near_a, own_b, noise_own, noise_twin, noise_core, noise_both
    ) = barrier(
        (up_other, down_other, bias_other, near_a, own_b, noise_own, noise_twin, noise_core, noise_both)
    )
    panels = (up_weight, up_other, down_weight, down_other, biases, bias_other)
    far_mid_a = middle(near_a)
    near_b = near(after(own_b, near_a))
    mid_a = after(mid_a, near_a)
    far_end_a = outward(mid_a)
    noise_twin = swap_twins(after(noise_twin, near_a))
    sum_own_a, sum_near_a = ffn(where, [[own_a], [after(near_a, mid_a)]], panels, fetch=True)
    far_mid_a = after(far_mid_a, sum_near_a)
    last_end_a = outward(far_mid_a)
    mid_b = middle(after(own_b, far_mid_a))
    noise_core = swap_cores(after(noise_core, far_mid_a))
    (sum_far_a,) = ffn(where, [[far_mid_a, far_end_a]], panels)
    came_far_a = inward(sum_far_a)
    near_b, mid_b = barrier((near_b, mid_b, sum_far_a))[:2]
    far_mid_b, far_end_b = middle(near_b), outward(mid_b)
    (sum_last_a,) = ffn(where, [[mid_a, after(last_end_a, near_b, mid_b)]], panels)
    came_last_a = inward(sum_last_a)
    far_mid_b = after(far_mid_b, sum_last_a)
    last_end_b = outward(far_mid_b)
    both_last_a = add(where, after(sum_last_a, far_mid_b), came_far_a)
    went_last_a = middle(both_last_a)
    sum_own_b, sum_near_b = ffn(where, [[after(own_b, both_last_a, far_end_b)], [near_b]], panels)
    noise_both = swap_both(after(noise_both, noise_twin))
    both_far_a = add(where, after(sum_far_a, went_last_a, sum_near_b), came_last_a)
    went_far_a = middle(both_far_a)
    sum_far_b, sum_last_b = ffn(
        where, [[after(far_mid_b, both_far_a), far_end_b], [mid_b, last_end_b]], panels
    )
    came_last_b = near(sum_last_b)
    head_other = swap_cores(after(head_weight, sum_last_b))
    code_other = swap_cores(after(codes, sum_last_b))
    came_near_b = near(after(sum_near_b, last_end_b))
    both_near_a = add(where, sum_near_a, after(went_far_a, came_near_b, noise_twin), flops=AHEAD)
    both_far_b = add(where, after(sum_far_b, both_near_a), came_last_b, always=True)
    went_far_b = across(both_far_b)
    came_near_a = near(after(both_near_a, both_far_b))
    out_a, kept_a, sent_a = block_rows(
        where, 0, False, sum_own_a, after(came_near_a, noise_both, noise_core), went_last_a, tokens, gate, bias_out, ada_head
    )
    came_a = swap_twins(sent_a)
    mixed_a = mix_twins(where, kept_a, came_a, ada_head)
    mix_near_a, mix_far_a = near(mixed_a), across(mixed_a)
    block_out, kept_b, sent_b = block_rows(
        where, step, True, sum_own_b, after(came_near_b, mixed_a, head_other, code_other), went_far_b, tokens, gate, bias_out, ada_head, (out_a,)
    )
    came_b = after(swap_twins(sent_b), mix_far_a)
    mix_last_a = near(mix_far_a)
    mixed_b = mix_twins(where, kept_b, came_b, ada_head)
    mix_near_b, mix_far_b = near(mixed_b), across(mixed_b)
    heads = (head_weight, head_other, biases, bias_other, codes, code_other)
    noises = (noise_own, noise_core, noise_twin, noise_both)
    stats_a = head_stats(
        where, 0, (after(mixed_a, mixed_b), mix_near_a, mix_far_a, mix_last_a), heads, noises, flops=AHEAD
    )
    mix_last_b = near(after(mix_far_b, stats_a))
    stats_b = head_stats(where, half, (after(mixed_b, stats_a), mix_near_b, mix_far_b, mix_last_b), heads, noises)

    slots = [
        jnp.concatenate([part[:, r * half : (r + 1) * half] for part in (stats_a, stats_b)], axis=1) for r in range(4)
    ]
    parts = [slots[0]] + [along_z(slots[r], lambda z, r=r: z ^ r) for r in (1, 2, 3)]
    soft = soft_codes(where, parts, channels)

    def to_cells(d, m, core_of):
        y, x = d // half_dp, d % half_dp
        z, c = m // 2, m % 2
        return ((z // 2) * half_dp + x, 2 * (2 * (z % 2) + c) + core_of(y))

    def to_halo(d, m):
        y, x = d // half_dp, d % half_dp
        z, c = m // 2, m % 2
        block = (2 * (z % 2) + c + (1 if y == 1 else -1)) % 4
        return ((z // 2) * half_dp + x, 2 * block + (0 if y == 1 else 1))

    first = permute_devices(soft, dp, mp, lambda d, m: to_cells(d, m, lambda y: y))
    second = permute_devices(soft, dp, mp, lambda d, m: to_cells(d, m, lambda y: 1 - y))
    halo = permute_devices(soft, dp, mp, to_halo)
    f_hat_out = call(
        refine_kernel,
        where,
        (first, second, halo, jnp.transpose(phi_weight, (2, 3, 0, 1)), phi_bias[:, None], f_hat[0]),
        [shape_of(f_hat.shape[1:], jnp.float32)],
    )[0]
    return (block_out, f_hat_out[None])


def solution(mesh):
    in_specs = (
        P(("dp", "mp"), None),
        P("dp", None, None),
        P("dp", None),
        P(None, "mp"),
        P("mp"),
        P("mp", None),
        P(),
        P("dp", None, None),
        P(None, "mp"),
        P("mp"),
        P("dp", None, "mp"),
        P("mp", None),
        P(),
        P(),
        P("dp", None, "mp"),
    )
    out_specs = (P(("dp", "mp"), None), P("dp", None, "mp"))
    line = mesh.shape["dp"] == 4 and mesh.shape["mp"] == 8
    body = line_body if line else general_body
    return jax.shard_map(body, mesh=mesh, in_specs=in_specs, out_specs=out_specs, check_vma=False)
```

```python
import functools

import jax
import jax.numpy as jnp
from jax import lax
from jax.experimental import pallas as pl
from jax.experimental.pallas import tpu as pltpu
from jax.sharding import PartitionSpec as P

SIDE = 32
NEW = 1024
GUIDE = 1.5
CHUNKS = 2
FLOWS = 4
HEAD_FLOWS = 2


def norm_rows(values):
    row_mean = jnp.mean(values, axis=-1, keepdims=True)
    centred = values - row_mean
    spread = jnp.mean(centred * centred, axis=-1, keepdims=True)
    return centred * lax.rsqrt(spread + 1e-06)


def modulate(values, ada):
    return norm_rows(values.astype(jnp.float32)) * (1.0 + ada[1]) + ada[0]


def permute_devices(value, dp, mp, target):
    pairs = []
    for d in range(dp):
        for m in range(mp):
            to = target(d, m)
            if to is not None:
                pairs.append((d * mp + m, to[0] * mp + to[1]))
    return lax.ppermute(value, ("dp", "mp"), pairs)


def general_body(
    tokens,
    ada_ffn,
    ffn_gate,
    up_weight,
    up_bias,
    down_weight,
    down_bias,
    ada_head,
    head_weight,
    head_bias,
    gumbel_noise,
    codebook,
    phi_weight,
    phi_bias,
    f_hat,
):
    rows, width = tokens.shape
    dp, mp = lax.axis_size("dp"), lax.axis_size("mp")
    d_index, m_index = lax.axis_index("dp"), lax.axis_index("mp")
    images = ada_ffn.shape[0]
    pairs = f_hat.shape[0]
    channels = f_hat.shape[1]
    vocab = head_weight.shape[1]
    own_image = (m_index * rows) // NEW
    ada_own = lax.dynamic_index_in_dim(ada_ffn, own_image, 0, keepdims=False)
    gate_own = lax.dynamic_index_in_dim(ffn_gate, own_image, 0, keepdims=False)
    head_own = lax.dynamic_index_in_dim(ada_head, own_image, 0, keepdims=False)
    half_dp, half_mp = dp // 2, mp // 2
    upper = d_index // half_dp

    def swap(d, m):
        return ((d + half_dp) % dp, m)

    def cross(d, m):
        if d // half_dp == m // half_mp:
            return None
        return ((d + half_dp) % dp, (m + half_mp) % mp)

    stays = upper == m_index // half_mp
    head_twin = permute_devices(head_own, dp, mp, swap)
    head_cond = jnp.where(upper == 0, head_own, head_twin)
    head_uncond = jnp.where(upper == 0, head_twin, head_own)

    step = rows // FLOWS
    normed = modulate(tokens, ada_own).astype(jnp.bfloat16)
    outs = []
    for c in range(FLOWS):
        part = lax.slice_in_dim(normed, c * step, (c + 1) * step, axis=0)
        gathered = lax.all_gather(part, "mp", axis=0, tiled=True)
        hidden = jax.nn.gelu(
            jnp.dot(gathered, up_weight, preferred_element_type=jnp.float32) + up_bias,
            approximate=True,
        ).astype(jnp.bfloat16)
        partial = jnp.dot(hidden, down_weight, preferred_element_type=jnp.float32).astype(jnp.bfloat16)
        summed = lax.psum_scatter(partial, "mp", scatter_dimension=0, tiled=True).astype(jnp.float32)
        own = lax.slice_in_dim(tokens, c * step, (c + 1) * step, axis=0).astype(jnp.float32)
        outs.append((own + gate_own * (summed + down_bias)).astype(jnp.bfloat16))
    block_out = jnp.concatenate(outs, axis=0)

    group = FLOWS // HEAD_FLOWS
    half = rows // HEAD_FLOWS // 2
    noise = gumbel_noise.reshape(pairs, NEW // rows, HEAD_FLOWS, 2, half, vocab)
    peaks, totals, codes = [], [], []
    for c in range(HEAD_FLOWS):
        part = jnp.concatenate(outs[c * group : (c + 1) * group], axis=0)
        first, second = part[:half], part[half:]
        kept = jnp.where(upper == 0, first, second)
        sent = jnp.where(upper == 0, second, first)
        came = permute_devices(sent, dp, mp, swap)
        cond = jnp.where(upper == 0, kept, came)
        uncond = jnp.where(upper == 0, came, kept)
        mixed = (
            (1.0 + GUIDE) * modulate(cond, head_cond) - GUIDE * modulate(uncond, head_uncond)
        ).astype(jnp.bfloat16)
        crossed = permute_devices(mixed, dp, mp, cross)
        mixed = jnp.where(stays, mixed, crossed)
        gathered = lax.all_gather(mixed, "mp", axis=0, tiled=True)
        logits = jnp.dot(gathered, head_weight, preferred_element_type=jnp.float32) + head_bias
        logits = logits.reshape(2, half_mp, half, vocab)
        order = jnp.transpose(logits, (1, 0, 2, 3)).reshape(pairs, NEW // rows, 2, half, vocab)
        scores = order + noise[:, :, c]
        peak = jnp.max(scores, axis=-1)
        weights = jnp.exp(scores - peak[..., None]).astype(jnp.bfloat16)
        totals.append(jnp.sum(weights.astype(jnp.float32), axis=-1))
        codes.append(jnp.dot(weights, codebook, preferred_element_type=jnp.float32))
        peaks.append(peak)
    stack = lambda parts: jnp.stack(parts, axis=2)
    peak = stack(peaks).reshape(pairs, 1, NEW)
    total = stack(totals).reshape(pairs, 1, NEW)
    code = stack(codes).reshape(pairs, NEW, channels).transpose(0, 2, 1)
    stats = jnp.concatenate([code, total, peak], axis=1)

    cells = f_hat.shape[2]
    band = cells // SIDE
    padded = jnp.pad(stats, ((0, 0), (0, 0), (SIDE, SIDE)))
    windows = jnp.stack(
        [padded[:, :, m * cells : m * cells + cells + 2 * SIDE] for m in range(mp)], axis=0
    )
    parts = lax.all_to_all(windows, "mp", 0, 0, tiled=True)
    top = jnp.max(parts[:, :, channels + 1], axis=0)
    factor = jnp.exp(parts[:, :, channels + 1] - top[None])[:, :, None]
    sums = jnp.sum(parts[:, :, : channels + 1] * factor, axis=0)
    cell_index = m_index * cells - SIDE + jnp.arange(cells + 2 * SIDE)
    inside = (cell_index >= 0) & (cell_index < NEW)
    soft = jnp.where(inside, sums[:, :channels] / jnp.where(inside, sums[:, channels:], 1.0), 0.0)
    code_map = soft.reshape(pairs, channels, band + 2, SIDE)
    wide = jnp.pad(code_map, ((0, 0), (0, 0), (0, 0), (1, 1)))
    taps = jnp.stack(
        [wide[:, :, i : i + band, j : j + SIDE] for i in range(3) for j in range(3)], axis=2
    ).reshape(pairs, channels * 9, cells)
    conv = jnp.einsum(
        "ok,pkn->pon",
        phi_weight.reshape(channels, channels * 9),
        taps,
        precision=lax.Precision.HIGHEST,
        preferred_element_type=jnp.float32,
    ) + phi_bias[None, :, None]
    f_hat_out = f_hat + 0.5 * soft[:, :, SIDE : SIDE + cells] + 0.5 * conv
    return (block_out, f_hat_out)


SCALARS = pl.BlockSpec(memory_space=pltpu.SMEM)
ON_CHIP = pl.BlockSpec(memory_space=pltpu.VMEM)
VMEM_LIMIT = 16 * 1024 * 1024
AHEAD = 40_000_000_000
MID, UPPER, IMAGE, ODD, SAME, CORE = range(6)


def call(kernel, where, args, outs, scratch=(), flops=0, specs=None, limit=VMEM_LIMIT):
    return pl.pallas_call(
        kernel,
        out_shape=outs,
        in_specs=[SCALARS] + (specs or [ON_CHIP] * len(args)),
        out_specs=[ON_CHIP] * len(outs),
        scratch_shapes=scratch,
        compiler_params=pltpu.CompilerParams(vmem_limit_bytes=limit),
        cost_estimate=pl.CostEstimate(flops=flops, bytes_accessed=0, transcendentals=0),
    )(where, *args)


def shape_of(shape, kind=jnp.bfloat16):
    return jax.ShapeDtypeStruct(shape, kind)


def after(value, *others):
    return lax.optimization_barrier((value, *others))[0]


def modulated(values, ada_ref, image):
    shift, scale = ada_ref[image, 0:1, :], ada_ref[image, 1:2, :]
    return norm_rows(values.astype(jnp.float32)) * (1.0 + scale) + shift


def norm_kernel(begin, where_ref, tokens_ref, ada_ref, out_ref):
    values = tokens_ref[begin : begin + out_ref.shape[0], :]
    out_ref[...] = modulated(values, ada_ref, where_ref[IMAGE]).astype(jnp.bfloat16)


def norm_part(where, tokens, ada, begin, size):
    outs = [shape_of((size, tokens.shape[1]))]
    return call(functools.partial(norm_kernel, begin), where, (tokens, ada), outs)[0]


def ffn_kernel(groups, tile, fetch, where_ref, *refs):
    count = sum(groups)
    parts = refs[:count]
    up_a, up_b, down_a, down_b, bias_a, bias_b = refs[count : count + 6]
    outs = refs[count + 6 : count + 6 + len(groups)]
    x_ref, hidden_ref, *own = refs[count + 6 + len(groups) :]
    order = list(range(0, 2 * down_a.shape[0], tile))
    copies = []
    if fetch:
        up_own, down_own, sems = own
        copies = [
            pltpu.make_async_copy(up_a, up_own, sems.at[0]),
            pltpu.make_async_copy(down_a, down_own, sems.at[1]),
        ]
        for copy in copies:
            copy.start()
        up_a, down_a = up_own, down_own
        order = [t for t in order if t >= down_a.shape[0]] + [t for t in order if t < down_a.shape[0]]
    panel, width = down_a.shape
    step = outs[0].shape[0]
    place = 0
    for g, size in enumerate(groups):
        if size == 1:
            value = parts[place][...]
        else:
            value = jnp.where(where_ref[MID] == 1, parts[place][...], parts[place + 1][...])
        x_ref[g * step : (g + 1) * step, :] = value
        place += size

    def columns(first, second, begin, end):
        if end <= panel:
            return first[:, begin:end]
        if begin >= panel:
            return second[:, begin - panel : end - panel]
        return jnp.concatenate([first[:, begin:panel], second[:, : end - panel]], axis=1)

    for begin in order:
        end = begin + tile
        if fetch and begin == 0:
            copies[0].wait()
        v = jnp.dot(x_ref[...], columns(up_a, up_b, begin, end), preferred_element_type=jnp.float32)
        v = v + columns(bias_a, bias_b, begin, end)
        hidden_ref[:, begin:end] = jax.nn.gelu(v, approximate=True).astype(jnp.bfloat16)
    if fetch:
        copies[1].wait()
    for begin in range(0, width, tile):
        cols = slice(begin, begin + tile)
        weight = jnp.concatenate([down_a[:, cols], down_b[:, cols]], axis=0)
        result = jnp.dot(hidden_ref[...], weight, preferred_element_type=jnp.float32)
        for g in range(len(groups)):
            outs[g][:, cols] = result[g * step : (g + 1) * step].astype(jnp.bfloat16)


def ffn(where, slots, panels, fetch=False):
    groups = tuple(len(slot) for slot in slots)
    parts = [part for slot in slots for part in slot]
    rows, width = parts[0].shape
    total = rows * len(slots)
    up, down = panels[0], panels[2]
    if fetch:
        panels = [
            pltpu.with_memory_space_constraint(p, pltpu.HBM) if i in (0, 2) else p for i, p in enumerate(panels)
        ]
    own = [pltpu.VMEM(up.shape, up.dtype), pltpu.VMEM(down.shape, down.dtype), pltpu.SemaphoreType.DMA((2,))]
    in_place = pl.BlockSpec(memory_space=pltpu.HBM)
    specs = [in_place if fetch and i in (0, 2) else ON_CHIP for i in range(len(panels))]
    return call(
        functools.partial(ffn_kernel, groups, 768, fetch),
        where,
        (*parts, *panels),
        [shape_of((rows, width))] * len(slots),
        scratch=[
            pltpu.VMEM((total, width), jnp.bfloat16),
            pltpu.VMEM((total, 2 * down.shape[0]), jnp.bfloat16),
            *(own if fetch else []),
        ],
        specs=[ON_CHIP] * len(parts) + specs,
        limit=VMEM_LIMIT + 8 * 1024 * 1024 if fetch else VMEM_LIMIT,
    )


def add_kernel(always, where_ref, a_ref, b_ref, out_ref):
    b = b_ref[...].astype(jnp.float32)
    if not always:
        b = jnp.where(where_ref[MID] == 1, b, 0.0)
    out_ref[...] = (a_ref[...].astype(jnp.float32) + b).astype(jnp.bfloat16)


def add(where, a, b, always=False, flops=0):
    return call(functools.partial(add_kernel, always), where, (a, b), [shape_of(a.shape)], flops=flops)[0]


def out_kernel(begin, always, where_ref, own_ref, near_ref, far_ref, tokens_ref, gate_ref, bias_ref, ada_ref, *refs):
    out_ref, kept_ref, sent_ref = refs[-3:]
    far = far_ref[...].astype(jnp.float32)
    if not always:
        far = jnp.where(where_ref[MID] == 1, far, 0.0)
    summed = own_ref[...].astype(jnp.float32) + near_ref[...].astype(jnp.float32) + far
    rows = summed.shape[0]
    tokens = tokens_ref[begin : begin + rows, :].astype(jnp.float32)
    gate = gate_ref[pl.ds(where_ref[IMAGE], 1), :]
    value = (tokens + gate * (summed + bias_ref[...])).astype(jnp.bfloat16)
    if len(refs) > 3:
        out_ref[0:begin, :] = refs[0][...]
        out_ref[begin : begin + rows, :] = value
    else:
        out_ref[...] = value
    half = rows // 2
    lower = where_ref[UPPER] == 0
    kept_ref[...] = jnp.where(lower, value[:half], value[half:])
    sent = jnp.where(lower, value[half:], value[:half])
    sent_ref[...] = modulated(sent, ada_ref, where_ref[IMAGE]).astype(jnp.bfloat16)


def block_rows(where, begin, always, own, near, far, tokens, gate, bias, ada, earlier=()):
    rows, width = own.shape
    full = rows + begin if earlier else rows
    return call(
        functools.partial(out_kernel, begin, always),
        where,
        (own, near, far, tokens, gate, bias, ada, *earlier),
        [shape_of((full, width)), shape_of((rows // 2, width)), shape_of((rows // 2, width))],
    )


def mix_kernel(where_ref, kept_ref, came_ref, ada_ref, out_ref):
    kept, came = modulated(kept_ref[...], ada_ref, where_ref[IMAGE]), came_ref[...].astype(jnp.float32)
    lower = where_ref[UPPER] == 0
    share = jnp.where(lower, 1.0 + GUIDE, -GUIDE)
    other = jnp.where(lower, -GUIDE, 1.0 + GUIDE)
    out_ref[...] = (share * kept + other * came).astype(jnp.bfloat16)


def mix_twins(where, kept, came, ada):
    return call(mix_kernel, where, (kept, came, ada), [shape_of(kept.shape)])[0]


def head_kernel(
    begin, where_ref, own_ref, near_ref, far_ref, last_ref, weight_a, weight_b, bias_a, bias_b, code_a, code_b,
    noise_own, noise_core, noise_twin, noise_both, stats_ref, x_ref
):
    step = own_ref.shape[0]
    for r, ref in enumerate((own_ref, near_ref, far_ref, last_ref)):
        x_ref[r * step : (r + 1) * step, :] = ref[...]
    x = x_ref[...]
    odd = where_ref[ODD]
    even = 1 - odd
    same = where_ref[SAME] == 1
    scores = []
    for weight, bias, ours, theirs in (
        (weight_a, bias_a, noise_own, noise_twin),
        (weight_b, bias_b, noise_core, noise_both),
    ):
        picked = []
        for first in (True, False):
            for block in (odd, even):
                a, b = ours[block, begin : begin + step, :], theirs[block, begin : begin + step, :]
                picked.append(jnp.where(same, a, b) if first else jnp.where(same, b, a))
        logits = jnp.dot(x, weight[...], preferred_element_type=jnp.float32)
        scores.append(logits + bias[:, bias.shape[1] - weight.shape[1] :] + jnp.concatenate(picked, axis=0))
    peak = jnp.max(jnp.maximum(scores[0], scores[1]), axis=1, keepdims=True)
    sums = 0.0
    total = 0.0
    for score, code in zip(scores, (code_a, code_b)):
        weights = jnp.exp(score - peak).astype(jnp.bfloat16)
        total = total + jnp.sum(weights.astype(jnp.float32), axis=1, keepdims=True)
        sums = sums + lax.dot_general(
            weights, code[...], (((1,), (1,)), ((), ())), preferred_element_type=jnp.float32
        )
    channels = code_a.shape[0]
    pad = jnp.zeros((4 * step, 128 - channels), jnp.float32)
    table = jnp.concatenate([sums, pad], axis=1)
    lane = lax.broadcasted_iota(jnp.int32, table.shape, 1)
    table = jnp.where(lane == channels, total, table)
    table = jnp.where(lane == channels + 1, peak, table)
    stats_ref[...] = jnp.transpose(table)[: stats_ref.shape[0], :]


def head_stats(where, begin, slots, heads, noises, flops=0):
    step, width = slots[0].shape
    height = -(-(heads[-1].shape[0] + 2) // 8) * 8
    return call(
        functools.partial(head_kernel, begin),
        where,
        (*slots, *heads, *noises),
        [shape_of((height, 4 * step), jnp.float32)],
        scratch=[pltpu.VMEM((4 * step, width), jnp.bfloat16)],
        flops=flops,
    )[0]


def soft_kernel(channels, where_ref, *refs):
    parts, out_ref = refs[:-1], refs[-1]
    tops = [part[channels + 1 : channels + 2, :] for part in parts]
    top = functools.reduce(jnp.maximum, tops)
    code = 0.0
    total = 0.0
    for part, peak in zip(parts, tops):
        factor = jnp.exp(peak - top)
        code = code + part[0:channels, :] * factor
        total = total + part[channels : channels + 1, :] * factor
    out_ref[...] = code / total


def soft_codes(where, parts, channels):
    outs = [shape_of((channels, parts[0].shape[1]), jnp.float32)]
    return call(functools.partial(soft_kernel, channels), where, tuple(parts), outs)[0]


def refine_kernel(where_ref, first_ref, second_ref, halo_ref, phi_ref, bias_ref, map_ref, out_ref):
    first, second, halo = first_ref[...], second_ref[...], halo_ref[...]
    cells = first.shape[1]
    half = cells // 2
    lane = lax.broadcasted_iota(jnp.int32, first.shape, 1)
    shift = lambda value, by: pltpu.roll(value, by % cells, 1)
    early = where_ref[CORE] == 0
    lower, higher = jnp.where(early, first, second), jnp.where(early, second, first)
    centre = jnp.where(
        early,
        jnp.where(lane < half, lower, shift(higher, half)),
        jnp.where(lane < half, shift(lower, half), higher),
    )
    above = jnp.where(early, shift(halo, SIDE), shift(higher, SIDE - half))
    below = jnp.where(early, shift(lower, half - SIDE), shift(halo, -SIDE))
    rows = (
        jnp.where(lane < SIDE, above, shift(centre, SIDE)),
        centre,
        jnp.where(lane >= cells - SIDE, below, shift(centre, -SIDE)),
    )
    column = lane % SIDE
    conv = jnp.zeros(out_ref.shape, jnp.float32) + bias_ref[...]
    for i, row in enumerate(rows):
        left = jnp.where(column == 0, 0.0, shift(row, 1))
        right = jnp.where(column == SIDE - 1, 0.0, shift(row, -1))
        for j, tap in enumerate((left, row, right)):
            conv = conv + jnp.dot(
                phi_ref[i, j], tap, precision=lax.Precision.HIGHEST, preferred_element_type=jnp.float32
            )
    out_ref[...] = map_ref[...] + 0.5 * centre + 0.5 * conv


def line_body(
    tokens,
    ada_ffn,
    ffn_gate,
    up_weight,
    up_bias,
    down_weight,
    down_bias,
    ada_head,
    head_weight,
    head_bias,
    gumbel_noise,
    codebook,
    phi_weight,
    phi_bias,
    f_hat,
):
    rows = tokens.shape[0]
    dp, mp = lax.axis_size("dp"), lax.axis_size("mp")
    d_index, m_index = lax.axis_index("dp"), lax.axis_index("mp")
    channels = f_hat.shape[1]
    half_dp = dp // 2
    upper = d_index // half_dp
    z_index, core = m_index // 2, m_index % 2
    where = jnp.stack(
        [
            (z_index == 1) | (z_index == 2),
            upper,
            (m_index * rows) // NEW,
            z_index % 2,
            z_index // 2 == upper,
            core,
        ]
    ).astype(jnp.int32)

    def along_z(value, target):
        def to(d, m):
            z = target(m // 2)
            return None if z is None else (d, 2 * z + m % 2)

        return permute_devices(value, dp, mp, to)

    def near(value):
        return along_z(value, lambda z: z ^ 1)

    def across(value):
        return along_z(value, lambda z: z ^ 2)

    def middle(value):
        return along_z(value, lambda z: 3 - z if z in (1, 2) else z)

    def outward(value):
        return along_z(value, lambda z: {1: 0, 2: 3}.get(z))

    def inward(value):
        return along_z(value, lambda z: {0: 1, 3: 2}.get(z))

    def swap_cores(value):
        return permute_devices(value, dp, mp, lambda d, m: (d, m ^ 1))

    def swap_twins(value):
        return permute_devices(value, dp, mp, lambda d, m: ((d + half_dp) % dp, m))

    def swap_both(value):
        return permute_devices(value, dp, mp, lambda d, m: ((d + half_dp) % dp, m ^ 1))

    step = rows // CHUNKS
    half = step // 2
    voc = head_bias.shape[0]
    noise = gumbel_noise.reshape(2, 2, CHUNKS, 2, half, voc)

    def noise_for(to_core, to_upper):
        picked = lax.dynamic_slice(
            noise, (0, to_core, 0, to_upper, 0, 0), (2, 1, CHUNKS, 1, half, voc)
        )
        return picked.reshape(2, CHUNKS * half, voc)

    gate, bias_out = ffn_gate, down_bias[None]
    up_other, down_other = swap_cores(up_weight), swap_cores(down_weight)
    biases = jnp.concatenate([up_bias, head_bias])[None]
    codes = codebook.T
    bias_other = swap_cores(biases)

    barrier = lax.optimization_barrier
    own_a = norm_part(where, tokens, ada_ffn, 0, step)
    near_a, mid_a = near(own_a), middle(own_a)
    own_b = norm_part(where, tokens, ada_ffn, step, step)
    noise_own, noise_twin, noise_core, noise_both = (
        noise_for(core, upper),
        noise_for(core, 1 - upper),
        noise_for(1 - core, upper),
        noise_for(1 - core, 1 - upper),
    )
    (
        up_other, down_other, bias_other, near_a, own_b, noise_own, noise_twin, noise_core, noise_both
    ) = barrier(
        (up_other, down_other, bias_other, near_a, own_b, noise_own, noise_twin, noise_core, noise_both)
    )
    panels = (up_weight, up_other, down_weight, down_other, biases, bias_other)
    far_mid_a = middle(near_a)
    near_b = near(after(own_b, near_a))
    mid_a = after(mid_a, near_a)
    far_end_a = outward(mid_a)
    noise_twin = swap_twins(after(noise_twin, near_a))
    sum_own_a, sum_near_a = ffn(where, [[own_a], [after(near_a, mid_a)]], panels, fetch=True)
    far_mid_a = after(far_mid_a, sum_near_a)
    last_end_a = outward(far_mid_a)
    mid_b = middle(after(own_b, far_mid_a))
    noise_core = swap_cores(after(noise_core, far_mid_a))
    (sum_far_a,) = ffn(where, [[far_mid_a, far_end_a]], panels)
    came_far_a = inward(sum_far_a)
    near_b, mid_b = barrier((near_b, mid_b, sum_far_a))[:2]
    far_mid_b, far_end_b = middle(near_b), outward(mid_b)
    (sum_last_a,) = ffn(where, [[mid_a, after(last_end_a, near_b, mid_b)]], panels)
    came_last_a = inward(sum_last_a)
    far_mid_b = after(far_mid_b, sum_last_a)
    last_end_b = outward(far_mid_b)
    both_last_a = add(where, after(sum_last_a, far_mid_b), came_far_a)
    went_last_a = middle(both_last_a)
    sum_own_b, sum_near_b = ffn(where, [[after(own_b, both_last_a, far_end_b)], [near_b]], panels)
    noise_both = swap_both(after(noise_both, noise_twin))
    both_far_a = add(where, after(sum_far_a, went_last_a, sum_near_b), came_last_a)
    went_far_a = middle(both_far_a)
    sum_far_b, sum_last_b = ffn(
        where, [[after(far_mid_b, both_far_a), far_end_b], [mid_b, last_end_b]], panels
    )
    came_last_b = near(sum_last_b)
    head_other = swap_cores(after(head_weight, sum_last_b))
    code_other = swap_cores(after(codes, sum_last_b))
    came_near_b = near(after(sum_near_b, last_end_b))
    both_near_a = add(where, sum_near_a, after(went_far_a, came_near_b, noise_twin), flops=AHEAD)
    came_near_a = near(both_near_a)
    both_far_b = add(where, after(sum_far_b, both_near_a), came_last_b, always=True)
    went_far_b = across(both_far_b)
    out_a, kept_a, sent_a = block_rows(
        where, 0, False, sum_own_a, after(came_near_a, noise_both, noise_core), went_last_a, tokens, gate, bias_out, ada_head
    )
    came_a = swap_twins(sent_a)
    mixed_a = mix_twins(where, kept_a, came_a, ada_head)
    mix_near_a, mix_far_a = near(mixed_a), across(mixed_a)
    block_out, kept_b, sent_b = block_rows(
        where, step, True, sum_own_b, after(came_near_b, mixed_a, head_other, code_other), went_far_b, tokens, gate, bias_out, ada_head, (out_a,)
    )
    came_b = after(swap_twins(sent_b), mix_far_a)
    mix_last_a = near(mix_far_a)
    mixed_b = mix_twins(where, kept_b, came_b, ada_head)
    mix_near_b, mix_far_b = near(mixed_b), across(mixed_b)
    heads = (head_weight, head_other, biases, bias_other, codes, code_other)
    noises = (noise_own, noise_core, noise_twin, noise_both)
    stats_a = head_stats(
        where, 0, (after(mixed_a, mixed_b), mix_near_a, mix_far_a, mix_last_a), heads, noises, flops=AHEAD
    )
    mix_last_b = near(after(mix_far_b, stats_a))
    stats_b = head_stats(where, half, (after(mixed_b, stats_a), mix_near_b, mix_far_b, mix_last_b), heads, noises)

    slots = [
        jnp.concatenate([part[:, r * half : (r + 1) * half] for part in (stats_a, stats_b)], axis=1) for r in range(4)
    ]
    parts = [slots[0]] + [along_z(slots[r], lambda z, r=r: z ^ r) for r in (1, 2, 3)]
    soft = soft_codes(where, parts, channels)

    def to_cells(d, m, core_of):
        y, x = d // half_dp, d % half_dp
        z, c = m // 2, m % 2
        return ((z // 2) * half_dp + x, 2 * (2 * (z % 2) + c) + core_of(y))

    def to_halo(d, m):
        y, x = d // half_dp, d % half_dp
        z, c = m // 2, m % 2
        block = 2 * (z % 2) + c + (1 if y == 1 else -1)
        if block < 0 or block > 3:
            return None
        return ((z // 2) * half_dp + x, 2 * block + (0 if y == 1 else 1))

    first = permute_devices(soft, dp, mp, lambda d, m: to_cells(d, m, lambda y: y))
    second = permute_devices(soft, dp, mp, lambda d, m: to_cells(d, m, lambda y: 1 - y))
    halo = permute_devices(soft, dp, mp, to_halo)
    f_hat_out = call(
        refine_kernel,
        where,
        (first, second, halo, jnp.transpose(phi_weight, (2, 3, 0, 1)), phi_bias[:, None], f_hat[0]),
        [shape_of(f_hat.shape[1:], jnp.float32)],
    )[0]
    return (block_out, f_hat_out[None])


def solution(mesh):
    in_specs = (
        P(("dp", "mp"), None),
        P("dp", None, None),
        P("dp", None),
        P(None, "mp"),
        P("mp"),
        P("mp", None),
        P(),
        P("dp", None, None),
        P(None, "mp"),
        P("mp"),
        P("dp", None, "mp"),
        P("mp", None),
        P(),
        P(),
        P("dp", None, "mp"),
    )
    out_specs = (P(("dp", "mp"), None), P("dp", None, "mp"))
    line = mesh.shape["dp"] == 4 and mesh.shape["mp"] == 8
    body = line_body if line else general_body
    return jax.shard_map(body, mesh=mesh, in_specs=in_specs, out_specs=out_specs, check_vma=False)
```

```python
import functools

import jax
import jax.numpy as jnp
from jax import lax
from jax.experimental import pallas as pl
from jax.experimental.pallas import tpu as pltpu
from jax.sharding import PartitionSpec as P

SIDE = 32
NEW = 1024
GUIDE = 1.5
CHUNKS = 2
FLOWS = 4
HEAD_FLOWS = 2


def norm_rows(values):
    row_mean = jnp.mean(values, axis=-1, keepdims=True)
    centred = values - row_mean
    spread = jnp.mean(centred * centred, axis=-1, keepdims=True)
    return centred * lax.rsqrt(spread + 1e-06)


def modulate(values, ada):
    return norm_rows(values.astype(jnp.float32)) * (1.0 + ada[1]) + ada[0]


def permute_devices(value, dp, mp, target):
    pairs = []
    for d in range(dp):
        for m in range(mp):
            to = target(d, m)
            if to is not None:
                pairs.append((d * mp + m, to[0] * mp + to[1]))
    return lax.ppermute(value, ("dp", "mp"), pairs)


def general_body(
    tokens,
    ada_ffn,
    ffn_gate,
    up_weight,
    up_bias,
    down_weight,
    down_bias,
    ada_head,
    head_weight,
    head_bias,
    gumbel_noise,
    codebook,
    phi_weight,
    phi_bias,
    f_hat,
):
    rows, width = tokens.shape
    dp, mp = lax.axis_size("dp"), lax.axis_size("mp")
    d_index, m_index = lax.axis_index("dp"), lax.axis_index("mp")
    images = ada_ffn.shape[0]
    pairs = f_hat.shape[0]
    channels = f_hat.shape[1]
    vocab = head_weight.shape[1]
    own_image = (m_index * rows) // NEW
    ada_own = lax.dynamic_index_in_dim(ada_ffn, own_image, 0, keepdims=False)
    gate_own = lax.dynamic_index_in_dim(ffn_gate, own_image, 0, keepdims=False)
    head_own = lax.dynamic_index_in_dim(ada_head, own_image, 0, keepdims=False)
    half_dp, half_mp = dp // 2, mp // 2
    upper = d_index // half_dp

    def swap(d, m):
        return ((d + half_dp) % dp, m)

    def cross(d, m):
        if d // half_dp == m // half_mp:
            return None
        return ((d + half_dp) % dp, (m + half_mp) % mp)

    stays = upper == m_index // half_mp
    head_twin = permute_devices(head_own, dp, mp, swap)
    head_cond = jnp.where(upper == 0, head_own, head_twin)
    head_uncond = jnp.where(upper == 0, head_twin, head_own)

    step = rows // FLOWS
    normed = modulate(tokens, ada_own).astype(jnp.bfloat16)
    outs = []
    for c in range(FLOWS):
        part = lax.slice_in_dim(normed, c * step, (c + 1) * step, axis=0)
        gathered = lax.all_gather(part, "mp", axis=0, tiled=True)
        hidden = jax.nn.gelu(
            jnp.dot(gathered, up_weight, preferred_element_type=jnp.float32) + up_bias,
            approximate=True,
        ).astype(jnp.bfloat16)
        partial = jnp.dot(hidden, down_weight, preferred_element_type=jnp.float32).astype(jnp.bfloat16)
        summed = lax.psum_scatter(partial, "mp", scatter_dimension=0, tiled=True).astype(jnp.float32)
        own = lax.slice_in_dim(tokens, c * step, (c + 1) * step, axis=0).astype(jnp.float32)
        outs.append((own + gate_own * (summed + down_bias)).astype(jnp.bfloat16))
    block_out = jnp.concatenate(outs, axis=0)

    group = FLOWS // HEAD_FLOWS
    half = rows // HEAD_FLOWS // 2
    noise = gumbel_noise.reshape(pairs, NEW // rows, HEAD_FLOWS, 2, half, vocab)
    peaks, totals, codes = [], [], []
    for c in range(HEAD_FLOWS):
        part = jnp.concatenate(outs[c * group : (c + 1) * group], axis=0)
        first, second = part[:half], part[half:]
        kept = jnp.where(upper == 0, first, second)
        sent = jnp.where(upper == 0, second, first)
        came = permute_devices(sent, dp, mp, swap)
        cond = jnp.where(upper == 0, kept, came)
        uncond = jnp.where(upper == 0, came, kept)
        mixed = (
            (1.0 + GUIDE) * modulate(cond, head_cond) - GUIDE * modulate(uncond, head_uncond)
        ).astype(jnp.bfloat16)
        crossed = permute_devices(mixed, dp, mp, cross)
        mixed = jnp.where(stays, mixed, crossed)
        gathered = lax.all_gather(mixed, "mp", axis=0, tiled=True)
        logits = jnp.dot(gathered, head_weight, preferred_element_type=jnp.float32) + head_bias
        logits = logits.reshape(2, half_mp, half, vocab)
        order = jnp.transpose(logits, (1, 0, 2, 3)).reshape(pairs, NEW // rows, 2, half, vocab)
        scores = order + noise[:, :, c]
        peak = jnp.max(scores, axis=-1)
        weights = jnp.exp(scores - peak[..., None]).astype(jnp.bfloat16)
        totals.append(jnp.sum(weights.astype(jnp.float32), axis=-1))
        codes.append(jnp.dot(weights, codebook, preferred_element_type=jnp.float32))
        peaks.append(peak)
    stack = lambda parts: jnp.stack(parts, axis=2)
    peak = stack(peaks).reshape(pairs, 1, NEW)
    total = stack(totals).reshape(pairs, 1, NEW)
    code = stack(codes).reshape(pairs, NEW, channels).transpose(0, 2, 1)
    stats = jnp.concatenate([code, total, peak], axis=1)

    cells = f_hat.shape[2]
    band = cells // SIDE
    padded = jnp.pad(stats, ((0, 0), (0, 0), (SIDE, SIDE)))
    windows = jnp.stack(
        [padded[:, :, m * cells : m * cells + cells + 2 * SIDE] for m in range(mp)], axis=0
    )
    parts = lax.all_to_all(windows, "mp", 0, 0, tiled=True)
    top = jnp.max(parts[:, :, channels + 1], axis=0)
    factor = jnp.exp(parts[:, :, channels + 1] - top[None])[:, :, None]
    sums = jnp.sum(parts[:, :, : channels + 1] * factor, axis=0)
    cell_index = m_index * cells - SIDE + jnp.arange(cells + 2 * SIDE)
    inside = (cell_index >= 0) & (cell_index < NEW)
    soft = jnp.where(inside, sums[:, :channels] / jnp.where(inside, sums[:, channels:], 1.0), 0.0)
    code_map = soft.reshape(pairs, channels, band + 2, SIDE)
    wide = jnp.pad(code_map, ((0, 0), (0, 0), (0, 0), (1, 1)))
    taps = jnp.stack(
        [wide[:, :, i : i + band, j : j + SIDE] for i in range(3) for j in range(3)], axis=2
    ).reshape(pairs, channels * 9, cells)
    conv = jnp.einsum(
        "ok,pkn->pon",
        phi_weight.reshape(channels, channels * 9),
        taps,
        precision=lax.Precision.HIGHEST,
        preferred_element_type=jnp.float32,
    ) + phi_bias[None, :, None]
    f_hat_out = f_hat + 0.5 * soft[:, :, SIDE : SIDE + cells] + 0.5 * conv
    return (block_out, f_hat_out)


SCALARS = pl.BlockSpec(memory_space=pltpu.SMEM)
ON_CHIP = pl.BlockSpec(memory_space=pltpu.VMEM)
VMEM_LIMIT = 16 * 1024 * 1024
AHEAD = 40_000_000_000
MID, UPPER, IMAGE, ODD, SAME, CORE = range(6)


def call(kernel, where, args, outs, scratch=(), flops=0, specs=None, limit=VMEM_LIMIT):
    return pl.pallas_call(
        kernel,
        out_shape=outs,
        in_specs=[SCALARS] + (specs or [ON_CHIP] * len(args)),
        out_specs=[ON_CHIP] * len(outs),
        scratch_shapes=scratch,
        compiler_params=pltpu.CompilerParams(vmem_limit_bytes=limit),
        cost_estimate=pl.CostEstimate(flops=flops, bytes_accessed=0, transcendentals=0),
    )(where, *args)


def shape_of(shape, kind=jnp.bfloat16):
    return jax.ShapeDtypeStruct(shape, kind)


def after(value, *others):
    return lax.optimization_barrier((value, *others))[0]


def modulated(values, ada_ref, image):
    shift, scale = ada_ref[image, 0:1, :], ada_ref[image, 1:2, :]
    return norm_rows(values.astype(jnp.float32)) * (1.0 + scale) + shift


def norm_kernel(begin, where_ref, tokens_ref, ada_ref, out_ref):
    values = tokens_ref[begin : begin + out_ref.shape[0], :]
    out_ref[...] = modulated(values, ada_ref, where_ref[IMAGE]).astype(jnp.bfloat16)


def norm_part(where, tokens, ada, begin, size):
    outs = [shape_of((size, tokens.shape[1]))]
    return call(functools.partial(norm_kernel, begin), where, (tokens, ada), outs)[0]


def ffn_kernel(groups, tile, fetch, where_ref, *refs):
    count = sum(groups)
    parts = refs[:count]
    up_a, up_b, down_a, down_b, bias_a, bias_b = refs[count : count + 6]
    outs = refs[count + 6 : count + 6 + len(groups)]
    x_ref, hidden_ref, *own = refs[count + 6 + len(groups) :]
    order = list(range(0, 2 * down_a.shape[0], tile))
    copies = []
    if fetch:
        up_own, down_own, sems = own
        copies = [
            pltpu.make_async_copy(up_a, up_own, sems.at[0]),
            pltpu.make_async_copy(down_a, down_own, sems.at[1]),
        ]
        for copy in copies:
            copy.start()
        up_a, down_a = up_own, down_own
        order = [t for t in order if t >= down_a.shape[0]] + [t for t in order if t < down_a.shape[0]]
    panel, width = down_a.shape
    step = outs[0].shape[0]
    place = 0
    for g, size in enumerate(groups):
        if size == 1:
            value = parts[place][...]
        else:
            value = jnp.where(where_ref[MID] == 1, parts[place][...], parts[place + 1][...])
        x_ref[g * step : (g + 1) * step, :] = value
        place += size

    def columns(first, second, begin, end):
        if end <= panel:
            return first[:, begin:end]
        if begin >= panel:
            return second[:, begin - panel : end - panel]
        return jnp.concatenate([first[:, begin:panel], second[:, : end - panel]], axis=1)

    for begin in order:
        end = begin + tile
        if fetch and begin == 0:
            copies[0].wait()
        v = jnp.dot(x_ref[...], columns(up_a, up_b, begin, end), preferred_element_type=jnp.float32)
        v = v + columns(bias_a, bias_b, begin, end)
        hidden_ref[:, begin:end] = jax.nn.gelu(v, approximate=True).astype(jnp.bfloat16)
    if fetch:
        copies[1].wait()
    for begin in range(0, width, tile):
        cols = slice(begin, begin + tile)
        weight = jnp.concatenate([down_a[:, cols], down_b[:, cols]], axis=0)
        result = jnp.dot(hidden_ref[...], weight, preferred_element_type=jnp.float32)
        for g in range(len(groups)):
            outs[g][:, cols] = result[g * step : (g + 1) * step].astype(jnp.bfloat16)


def ffn(where, slots, panels, fetch=False):
    groups = tuple(len(slot) for slot in slots)
    parts = [part for slot in slots for part in slot]
    rows, width = parts[0].shape
    total = rows * len(slots)
    up, down = panels[0], panels[2]
    if fetch:
        panels = [
            pltpu.with_memory_space_constraint(p, pltpu.HBM) if i in (0, 2) else p for i, p in enumerate(panels)
        ]
    own = [pltpu.VMEM(up.shape, up.dtype), pltpu.VMEM(down.shape, down.dtype), pltpu.SemaphoreType.DMA((2,))]
    in_place = pl.BlockSpec(memory_space=pltpu.HBM)
    specs = [in_place if fetch and i in (0, 2) else ON_CHIP for i in range(len(panels))]
    return call(
        functools.partial(ffn_kernel, groups, 256, fetch),
        where,
        (*parts, *panels),
        [shape_of((rows, width))] * len(slots),
        scratch=[
            pltpu.VMEM((total, width), jnp.bfloat16),
            pltpu.VMEM((total, 2 * down.shape[0]), jnp.bfloat16),
            *(own if fetch else []),
        ],
        specs=[ON_CHIP] * len(parts) + specs,
        limit=VMEM_LIMIT + 8 * 1024 * 1024 if fetch else VMEM_LIMIT,
    )


def add_kernel(always, where_ref, a_ref, b_ref, out_ref):
    b = b_ref[...].astype(jnp.float32)
    if not always:
        b = jnp.where(where_ref[MID] == 1, b, 0.0)
    out_ref[...] = (a_ref[...].astype(jnp.float32) + b).astype(jnp.bfloat16)


def add(where, a, b, always=False, flops=0):
    return call(functools.partial(add_kernel, always), where, (a, b), [shape_of(a.shape)], flops=flops)[0]


def out_kernel(begin, always, where_ref, own_ref, near_ref, far_ref, tokens_ref, gate_ref, bias_ref, ada_ref, *refs):
    out_ref, kept_ref, sent_ref = refs[-3:]
    far = far_ref[...].astype(jnp.float32)
    if not always:
        far = jnp.where(where_ref[MID] == 1, far, 0.0)
    summed = own_ref[...].astype(jnp.float32) + near_ref[...].astype(jnp.float32) + far
    rows = summed.shape[0]
    tokens = tokens_ref[begin : begin + rows, :].astype(jnp.float32)
    gate = gate_ref[pl.ds(where_ref[IMAGE], 1), :]
    value = (tokens + gate * (summed + bias_ref[...])).astype(jnp.bfloat16)
    if len(refs) > 3:
        out_ref[0:begin, :] = refs[0][...]
        out_ref[begin : begin + rows, :] = value
    else:
        out_ref[...] = value
    half = rows // 2
    lower = where_ref[UPPER] == 0
    kept_ref[...] = jnp.where(lower, value[:half], value[half:])
    sent = jnp.where(lower, value[half:], value[:half])
    sent_ref[...] = modulated(sent, ada_ref, where_ref[IMAGE]).astype(jnp.bfloat16)


def block_rows(where, begin, always, own, near, far, tokens, gate, bias, ada, earlier=()):
    rows, width = own.shape
    full = rows + begin if earlier else rows
    return call(
        functools.partial(out_kernel, begin, always),
        where,
        (own, near, far, tokens, gate, bias, ada, *earlier),
        [shape_of((full, width)), shape_of((rows // 2, width)), shape_of((rows // 2, width))],
    )


def mix_kernel(where_ref, kept_ref, came_ref, ada_ref, out_ref):
    kept, came = modulated(kept_ref[...], ada_ref, where_ref[IMAGE]), came_ref[...].astype(jnp.float32)
    lower = where_ref[UPPER] == 0
    share = jnp.where(lower, 1.0 + GUIDE, -GUIDE)
    other = jnp.where(lower, -GUIDE, 1.0 + GUIDE)
    out_ref[...] = (share * kept + other * came).astype(jnp.bfloat16)


def mix_twins(where, kept, came, ada):
    return call(mix_kernel, where, (kept, came, ada), [shape_of(kept.shape)])[0]


def head_kernel(
    begin, where_ref, own_ref, near_ref, far_ref, last_ref, weight_a, weight_b, bias_a, bias_b, code_a, code_b,
    noise_own, noise_core, noise_twin, noise_both, stats_ref, x_ref
):
    step = own_ref.shape[0]
    for r, ref in enumerate((own_ref, near_ref, far_ref, last_ref)):
        x_ref[r * step : (r + 1) * step, :] = ref[...]
    x = x_ref[...]
    odd = where_ref[ODD]
    even = 1 - odd
    same = where_ref[SAME] == 1
    scores = []
    for weight, bias, ours, theirs in (
        (weight_a, bias_a, noise_own, noise_twin),
        (weight_b, bias_b, noise_core, noise_both),
    ):
        picked = []
        for first in (True, False):
            for block in (odd, even):
                a, b = ours[block, begin : begin + step, :], theirs[block, begin : begin + step, :]
                picked.append(jnp.where(same, a, b) if first else jnp.where(same, b, a))
        logits = jnp.dot(x, weight[...], preferred_element_type=jnp.float32)
        scores.append(logits + bias[:, bias.shape[1] - weight.shape[1] :] + jnp.concatenate(picked, axis=0))
    peak = jnp.max(jnp.maximum(scores[0], scores[1]), axis=1, keepdims=True)
    sums = 0.0
    total = 0.0
    for score, code in zip(scores, (code_a, code_b)):
        weights = jnp.exp(score - peak).astype(jnp.bfloat16)
        total = total + jnp.sum(weights.astype(jnp.float32), axis=1, keepdims=True)
        sums = sums + lax.dot_general(
            weights, code[...], (((1,), (1,)), ((), ())), preferred_element_type=jnp.float32
        )
    channels = code_a.shape[0]
    pad = jnp.zeros((4 * step, 128 - channels), jnp.float32)
    table = jnp.concatenate([sums, pad], axis=1)
    lane = lax.broadcasted_iota(jnp.int32, table.shape, 1)
    table = jnp.where(lane == channels, total, table)
    table = jnp.where(lane == channels + 1, peak, table)
    stats_ref[...] = jnp.transpose(table)[: stats_ref.shape[0], :]


def head_stats(where, begin, slots, heads, noises, flops=0):
    step, width = slots[0].shape
    height = -(-(heads[-1].shape[0] + 2) // 8) * 8
    return call(
        functools.partial(head_kernel, begin),
        where,
        (*slots, *heads, *noises),
        [shape_of((height, 4 * step), jnp.float32)],
        scratch=[pltpu.VMEM((4 * step, width), jnp.bfloat16)],
        flops=flops,
    )[0]


def soft_kernel(channels, where_ref, *refs):
    parts, out_ref = refs[:-1], refs[-1]
    tops = [part[channels + 1 : channels + 2, :] for part in parts]
    top = functools.reduce(jnp.maximum, tops)
    code = 0.0
    total = 0.0
    for part, peak in zip(parts, tops):
        factor = jnp.exp(peak - top)
        code = code + part[0:channels, :] * factor
        total = total + part[channels : channels + 1, :] * factor
    out_ref[...] = code / total


def soft_codes(where, parts, channels):
    outs = [shape_of((channels, parts[0].shape[1]), jnp.float32)]
    return call(functools.partial(soft_kernel, channels), where, tuple(parts), outs)[0]


def refine_kernel(where_ref, first_ref, second_ref, halo_ref, phi_ref, bias_ref, map_ref, out_ref):
    first, second, halo = first_ref[...], second_ref[...], halo_ref[...]
    cells = first.shape[1]
    half = cells // 2
    lane = lax.broadcasted_iota(jnp.int32, first.shape, 1)
    shift = lambda value, by: pltpu.roll(value, by % cells, 1)
    early = where_ref[CORE] == 0
    lower, higher = jnp.where(early, first, second), jnp.where(early, second, first)
    centre = jnp.where(
        early,
        jnp.where(lane < half, lower, shift(higher, half)),
        jnp.where(lane < half, shift(lower, half), higher),
    )
    above = jnp.where(early, shift(halo, SIDE), shift(higher, SIDE - half))
    below = jnp.where(early, shift(lower, half - SIDE), shift(halo, -SIDE))
    rows = (
        jnp.where(lane < SIDE, above, shift(centre, SIDE)),
        centre,
        jnp.where(lane >= cells - SIDE, below, shift(centre, -SIDE)),
    )
    column = lane % SIDE
    conv = jnp.zeros(out_ref.shape, jnp.float32) + bias_ref[...]
    for i, row in enumerate(rows):
        left = jnp.where(column == 0, 0.0, shift(row, 1))
        right = jnp.where(column == SIDE - 1, 0.0, shift(row, -1))
        for j, tap in enumerate((left, row, right)):
            conv = conv + jnp.dot(
                phi_ref[i, j], tap, precision=lax.Precision.HIGHEST, preferred_element_type=jnp.float32
            )
    out_ref[...] = map_ref[...] + 0.5 * centre + 0.5 * conv


def line_body(
    tokens,
    ada_ffn,
    ffn_gate,
    up_weight,
    up_bias,
    down_weight,
    down_bias,
    ada_head,
    head_weight,
    head_bias,
    gumbel_noise,
    codebook,
    phi_weight,
    phi_bias,
    f_hat,
):
    rows = tokens.shape[0]
    dp, mp = lax.axis_size("dp"), lax.axis_size("mp")
    d_index, m_index = lax.axis_index("dp"), lax.axis_index("mp")
    channels = f_hat.shape[1]
    half_dp = dp // 2
    upper = d_index // half_dp
    z_index, core = m_index // 2, m_index % 2
    where = jnp.stack(
        [
            (z_index == 1) | (z_index == 2),
            upper,
            (m_index * rows) // NEW,
            z_index % 2,
            z_index // 2 == upper,
            core,
        ]
    ).astype(jnp.int32)

    def along_z(value, target):
        def to(d, m):
            z = target(m // 2)
            return None if z is None else (d, 2 * z + m % 2)

        return permute_devices(value, dp, mp, to)

    def near(value):
        return along_z(value, lambda z: z ^ 1)

    def across(value):
        return along_z(value, lambda z: z ^ 2)

    def middle(value):
        return along_z(value, lambda z: 3 - z if z in (1, 2) else z)

    def outward(value):
        return along_z(value, lambda z: {1: 0, 2: 3}.get(z))

    def inward(value):
        return along_z(value, lambda z: {0: 1, 3: 2}.get(z))

    def swap_cores(value):
        return permute_devices(value, dp, mp, lambda d, m: (d, m ^ 1))

    def swap_twins(value):
        return permute_devices(value, dp, mp, lambda d, m: ((d + half_dp) % dp, m))

    def swap_both(value):
        return permute_devices(value, dp, mp, lambda d, m: ((d + half_dp) % dp, m ^ 1))

    step = rows // CHUNKS
    half = step // 2
    voc = head_bias.shape[0]
    noise = gumbel_noise.reshape(2, 2, CHUNKS, 2, half, voc)

    def noise_for(to_core, to_upper):
        picked = lax.dynamic_slice(
            noise, (0, to_core, 0, to_upper, 0, 0), (2, 1, CHUNKS, 1, half, voc)
        )
        return picked.reshape(2, CHUNKS * half, voc)

    gate, bias_out = ffn_gate, down_bias[None]
    up_other, down_other = swap_cores(up_weight), swap_cores(down_weight)
    biases = jnp.concatenate([up_bias, head_bias])[None]
    codes = codebook.T
    bias_other = swap_cores(biases)

    barrier = lax.optimization_barrier
    own_a = norm_part(where, tokens, ada_ffn, 0, step)
    near_a, mid_a = near(own_a), middle(own_a)
    own_b = norm_part(where, tokens, ada_ffn, step, step)
    noise_own, noise_twin, noise_core, noise_both = (
        noise_for(core, upper),
        noise_for(core, 1 - upper),
        noise_for(1 - core, upper),
        noise_for(1 - core, 1 - upper),
    )
    (
        up_other, down_other, bias_other, near_a, own_b, noise_own, noise_twin, noise_core, noise_both
    ) = barrier(
        (up_other, down_other, bias_other, near_a, own_b, noise_own, noise_twin, noise_core, noise_both)
    )
    panels = (up_weight, up_other, down_weight, down_other, biases, bias_other)
    far_mid_a = middle(near_a)
    near_b = near(after(own_b, near_a))
    mid_a = after(mid_a, near_a)
    far_end_a = outward(mid_a)
    noise_twin = swap_twins(after(noise_twin, near_a))
    sum_own_a, sum_near_a = ffn(where, [[own_a], [after(near_a, mid_a)]], panels, fetch=True)
    far_mid_a = after(far_mid_a, sum_near_a)
    last_end_a = outward(far_mid_a)
    mid_b = middle(after(own_b, far_mid_a))
    noise_core = swap_cores(after(noise_core, far_mid_a))
    (sum_far_a,) = ffn(where, [[far_mid_a, far_end_a]], panels)
    came_far_a = inward(sum_far_a)
    near_b, mid_b = barrier((near_b, mid_b, sum_far_a))[:2]
    far_mid_b, far_end_b = middle(near_b), outward(mid_b)
    (sum_last_a,) = ffn(where, [[mid_a, after(last_end_a, near_b, mid_b)]], panels)
    came_last_a = inward(sum_last_a)
    far_mid_b = after(far_mid_b, sum_last_a)
    last_end_b = outward(far_mid_b)
    both_last_a = add(where, after(sum_last_a, far_mid_b), came_far_a)
    went_last_a = middle(both_last_a)
    sum_own_b, sum_near_b = ffn(where, [[after(own_b, both_last_a, far_end_b)], [near_b]], panels)
    noise_both = swap_both(after(noise_both, noise_twin))
    both_far_a = add(where, after(sum_far_a, went_last_a, sum_near_b), came_last_a)
    went_far_a = middle(both_far_a)
    sum_far_b, sum_last_b = ffn(
        where, [[after(far_mid_b, both_far_a), far_end_b], [mid_b, last_end_b]], panels
    )
    came_last_b = near(sum_last_b)
    head_other = swap_cores(after(head_weight, sum_last_b))
    code_other = swap_cores(after(codes, sum_last_b))
    came_near_b = near(after(sum_near_b, last_end_b))
    both_near_a = add(where, sum_near_a, after(went_far_a, came_near_b, noise_twin), flops=AHEAD)
    came_near_a = near(both_near_a)
    both_far_b = add(where, after(sum_far_b, both_near_a), came_last_b, always=True)
    went_far_b = across(both_far_b)
    out_a, kept_a, sent_a = block_rows(
        where, 0, False, sum_own_a, after(came_near_a, noise_both, noise_core), went_last_a, tokens, gate, bias_out, ada_head
    )
    came_a = swap_twins(sent_a)
    mixed_a = mix_twins(where, kept_a, came_a, ada_head)
    mix_near_a, mix_far_a = near(mixed_a), across(mixed_a)
    block_out, kept_b, sent_b = block_rows(
        where, step, True, sum_own_b, after(came_near_b, mixed_a, head_other, code_other), went_far_b, tokens, gate, bias_out, ada_head, (out_a,)
    )
    came_b = after(swap_twins(sent_b), mix_far_a)
    mix_last_a = near(after(mix_far_a, mix_near_a))
    mixed_b = mix_twins(where, kept_b, came_b, ada_head)
    mix_near_b, mix_far_b = near(mixed_b), across(mixed_b)
    heads = (head_weight, head_other, biases, bias_other, codes, code_other)
    noises = (noise_own, noise_core, noise_twin, noise_both)
    stats_a = head_stats(
        where, 0, (after(mixed_a, mixed_b), mix_near_a, mix_far_a, mix_last_a), heads, noises, flops=AHEAD
    )
    mix_last_b = near(after(mix_far_b, stats_a))
    stats_b = head_stats(where, half, (after(mixed_b, stats_a), mix_near_b, mix_far_b, mix_last_b), heads, noises)

    slots = [
        jnp.concatenate([part[:, r * half : (r + 1) * half] for part in (stats_a, stats_b)], axis=1) for r in range(4)
    ]
    parts = [slots[0]] + [along_z(slots[r], lambda z, r=r: z ^ r) for r in (1, 2, 3)]
    soft = soft_codes(where, parts, channels)

    def to_cells(d, m, core_of):
        y, x = d // half_dp, d % half_dp
        z, c = m // 2, m % 2
        return ((z // 2) * half_dp + x, 2 * (2 * (z % 2) + c) + core_of(y))

    def to_halo(d, m):
        y, x = d // half_dp, d % half_dp
        z, c = m // 2, m % 2
        block = 2 * (z % 2) + c + (1 if y == 1 else -1)
        if block < 0 or block > 3:
            return None
        return ((z // 2) * half_dp + x, 2 * block + (0 if y == 1 else 1))

    first = permute_devices(soft, dp, mp, lambda d, m: to_cells(d, m, lambda y: y))
    second = permute_devices(soft, dp, mp, lambda d, m: to_cells(d, m, lambda y: 1 - y))
    halo = permute_devices(soft, dp, mp, to_halo)
    f_hat_out = call(
        refine_kernel,
        where,
        (first, second, halo, jnp.transpose(phi_weight, (2, 3, 0, 1)), phi_bias[:, None], f_hat[0]),
        [shape_of(f_hat.shape[1:], jnp.float32)],
    )[0]
    return (block_out, f_hat_out[None])


def solution(mesh):
    in_specs = (
        P(("dp", "mp"), None),
        P("dp", None, None),
        P("dp", None),
        P(None, "mp"),
        P("mp"),
        P("mp", None),
        P(),
        P("dp", None, None),
        P(None, "mp"),
        P("mp"),
        P("dp", None, "mp"),
        P("mp", None),
        P(),
        P(),
        P("dp", None, "mp"),
    )
    out_specs = (P(("dp", "mp"), None), P("dp", None, "mp"))
    line = mesh.shape["dp"] == 4 and mesh.shape["mp"] == 8
    body = line_body if line else general_body
    return jax.shard_map(body, mesh=mesh, in_specs=in_specs, out_specs=out_specs, check_vma=False)
```
